32 devices in a mesh: seq: 8 (over z, x), head: 4 (over y, core).
Axes of the slice: x: 2, y: 2, z: 4, core: 2. Of those that a mesh axis runs over, the one named last changes fastest.
Arguments:
- qkv_tokens: bfloat16 [2, 3072, 3, 4096], P(None, ('seq', 'head')), may hold values from -6 to 6
- sign_bits: int32 [32, 2, 3, 128], P('head'), may hold values from 0 to 1
- out_weight: bfloat16 [4096, 4096], P('head'), may hold values from -0.09375 to 0.09375
Outputs:
- layer_out: bfloat16 [2, 3072, 4096], P(None, ('seq', 'head'))
The draws below stay inside these ranges and needn't reach their ends.
Inputs may be any that keep to these rules, and one draw needn't show every extreme that they name: `sign_bits`: 1 stands for the sign +1 and 0 for -1.
All inputs are finite; a program needn't handle non-finite values.
Results may differ from the reference program's by a relative error of at most 0.014.
Values may be sent and summed in bfloat16 or wider, within the bound.
No kernel may reach another device: no remote copies, remote signals or barrier semaphores. Data moves between devices by JAX's collectives and lax.ppermute only.
A program may use at most 256 MiB of HBM per device.

```python
import math
import jax
import jax.numpy as jnp
from jax import lax

D = 4096
HEADS = 32
DH = 128
FB = 2
SEQS = 2
LOCAL_SPAN = 384
SPAN_SIZE = 3072


def with_ends(entries, stream_key, low, top_value):
    index_at = [jax.random.randint(jax.random.fold_in(stream_key, axis), (), 0, length) for axis, length in enumerate(entries.shape)]
    widest = entries.shape.index(max(entries.shape))
    beside = index_at[:widest] + [(index_at[widest] + 1) % entries.shape[widest]] + index_at[widest + 1:]
    return entries.at[tuple(index_at)].set(low).at[tuple(beside)].set(top_value)


def steps_of(key, shape, split, low, top_value):
    factor_of, own = 1.0, jax.random.fold_in(key, 6)
    for position, blocks in split:
        draws = jnp.exp(jax.random.uniform(jax.random.fold_in(own, position), (blocks,), jnp.float32, low / len(split), top_value / len(split)))
        factor_of = factor_of * jnp.repeat(draws, shape[position] // blocks).reshape([-1 if axis == position else 1 for axis in range(len(shape))])
    return factor_of


def noise(stream_key, shape, spread, limit, pieces=(), held_as=jnp.bfloat16):
    entries = jax.random.normal(stream_key, shape, jnp.float32) * spread
    if len(pieces) > 0:
        entries = steps_of(stream_key, shape, pieces, -0.22, 0.18) * entries
    return jnp.clip(entries, min=-limit, max=limit).astype(held_as)


def setup_inputs(seed: int = 0) -> dict:
    streams_of = jax.random.split(jax.random.key(seed), 4)
    qkv_tokens = noise(streams_of[0], (SEQS, SPAN_SIZE, 3, HEADS * DH), 1.0, 6.0, ((1, 32),))
    sign_bits = with_ends(jax.random.randint(streams_of[1], (HEADS, FB, 3, DH), 0, 2), jax.random.fold_in(streams_of[1], 1), 0, 1).astype(jnp.int32)
    out_weight = noise(streams_of[2], (HEADS * DH, D), (HEADS * DH) ** -0.5, 0.09375, ((0, 4),))
    return dict(qkv_tokens=qkv_tokens, sign_bits=sign_bits, out_weight=out_weight)


logit_divisor = 1.3
norm_epsilon = 1e-06

def sylvester(order):
    position_ids = jnp.arange(order, dtype=jnp.int32)
    common_part = position_ids[:, None] & position_ids[None, :]
    table_now = jnp.ones((order, order), jnp.float32)
    stride = 1
    while stride < order:
        table_now = table_now * (1.0 - 2.0 * (common_part // stride % 2).astype(jnp.float32))
        stride = stride * 2
    return table_now / math.sqrt(order)

def random_feature_maps(sign_bits):
    channel_breadth = sign_bits.shape[-1]
    hadamard = sylvester(channel_breadth)
    signed = (2 * sign_bits - 1).astype(jnp.float32)
    matrix = signed[:, :, 2, :, None] * hadamard[None, None]
    matrix = jnp.einsum('ij,hbjk->hbik', hadamard, matrix, precision=lax.Precision.HIGHEST)
    matrix = signed[:, :, 1, :, None] * matrix
    matrix = jnp.einsum('ij,hbjk->hbik', hadamard, matrix, precision=lax.Precision.HIGHEST)
    matrix = signed[:, :, 0, :, None] * matrix
    matrix = matrix * math.sqrt(channel_breadth)
    head_count, block_count = (sign_bits.shape[0], sign_bits.shape[1])
    return matrix.transpose(0, 2, 1, 3).reshape(head_count, channel_breadth, block_count * channel_breadth)

def widen(reduce_dimension):
    return lax.optimization_barrier(reduce_dimension).astype(jnp.float32)

def feature_lift(inputs, projection_transposed):
    channel_breadth = inputs.shape[-1]
    widened = inputs.astype(jnp.float32)
    normalized_source = widened * lax.rsqrt(lax.optimization_barrier(jnp.mean(widened * widened, axis=-1, keepdims=True)) + norm_epsilon)
    normalized_source = normalized_source * (logit_divisor / math.sqrt(math.sqrt(channel_breadth)))
    return jnp.exp(jnp.dot(normalized_source, projection_transposed, precision=lax.Precision.HIGHEST)).astype(jnp.bfloat16)

def attend_one(one_item):
    queries, keys_in, values, projection_transposed = one_item
    blocks = SPAN_SIZE // LOCAL_SPAN
    channel_breadth = queries.shape[-1]
    feat_count = projection_transposed.shape[-1]
    query_feats = widen(feature_lift(queries, projection_transposed)).reshape(blocks, LOCAL_SPAN, feat_count)
    key_features = widen(feature_lift(keys_in, projection_transposed)).reshape(blocks, LOCAL_SPAN, feat_count)
    entry_vectors = values.astype(jnp.float32).reshape(blocks, LOCAL_SPAN, channel_breadth)
    states = jnp.einsum('btf,btd->bfd', key_features, entry_vectors, precision=lax.Precision.HIGHEST)
    totals = lax.optimization_barrier(jnp.sum(key_features, axis=1))
    prior_states = jnp.concatenate([jnp.zeros((1, feat_count, channel_breadth), jnp.float32), jnp.cumsum(states, axis=0)[:-1]], axis=0)
    prior_totals = jnp.concatenate([jnp.zeros((1, feat_count), jnp.float32), jnp.cumsum(totals, axis=0)[:-1]], axis=0)
    prior_rounded = widen(prior_states.astype(jnp.bfloat16))
    scores = jnp.einsum('btf,bsf->bts', query_feats, key_features, precision=lax.Precision.HIGHEST)
    row_index = jnp.arange(LOCAL_SPAN, dtype=jnp.int32)
    causal_masked = row_index[:, None] >= row_index[None, :]
    scores = jnp.where(causal_masked[None], scores, jnp.zeros_like(scores))
    weights = widen(scores.astype(jnp.bfloat16))
    numerator = jnp.einsum('bts,bsd->btd', weights, entry_vectors, precision=lax.Precision.HIGHEST)
    numerator = numerator + jnp.einsum('btf,bfd->btd', query_feats, prior_rounded, precision=lax.Precision.HIGHEST)
    denominator = lax.optimization_barrier(jnp.sum(scores, axis=-1)) + jnp.einsum('btf,bf->bt', query_feats, prior_totals, precision=lax.Precision.HIGHEST)
    attended = (numerator / denominator[..., None]).astype(jnp.bfloat16)
    return attended.reshape(SPAN_SIZE, channel_breadth)

def reference(qkv_tokens, sign_bits, out_weight):
    projection_transposed = random_feature_maps(sign_bits)
    seq_count = qkv_tokens.shape[0]
    grouped = qkv_tokens.reshape(seq_count, SPAN_SIZE, 3, HEADS, DH)

    def per_item(which):
        return grouped[:, :, which].transpose(0, 2, 1, 3).reshape(seq_count * HEADS, SPAN_SIZE, DH)
    tiled = jnp.tile(projection_transposed, (seq_count, 1, 1))
    attended = lax.map(attend_one, (per_item(0), per_item(1), per_item(2), tiled))
    attended = attended.reshape(seq_count, HEADS, SPAN_SIZE, DH).transpose(0, 2, 1, 3).reshape(seq_count, SPAN_SIZE, HEADS * DH)

    def project(seq_rows):
        return jnp.dot(seq_rows, out_weight, preferred_element_type=jnp.float32).astype(jnp.bfloat16)
    return lax.map(project, attended)
```

```python
import functools
import math

import jax
import jax.numpy as jnp
import numpy as np
from jax import lax
from jax.experimental import pallas as pl
from jax.experimental.pallas import tpu as pltpu
from jax.sharding import PartitionSpec as P

logit_divisor = 1.3
norm_epsilon = 1e-06
CHUNKS = 2

bf16, f32 = jnp.bfloat16, jnp.float32
VMEM_LIMIT = 48 * 1024 * 1024
ROW_TILE = 16


def params():
    return pltpu.CompilerParams(vmem_limit_bytes=VMEM_LIMIT)


def full(*shape):
    return pl.BlockSpec(shape, lambda _: (0,) * len(shape))


def cost(flops, nbytes, exps=0):
    return pl.CostEstimate(flops=int(flops), bytes_accessed=int(nbytes), transcendentals=int(exps))


def swap(value, axis, bit):
    return lax.ppermute(value, axis, [(j, j ^ bit) for j in range(lax.axis_size(axis))])


def sign_matrix(order):
    ids = np.arange(order)
    common = ids[:, None] & ids[None, :]
    parity = np.zeros_like(common)
    while common.any():
        parity ^= common & 1
        common = common >> 1
    return (1 - 2 * parity).astype(np.float32)


def integer_maps(sign_bits):
    heads, blocks, _, dh = sign_bits.shape
    had = jnp.asarray(sign_matrix(dh), bf16)
    signed = (2 * sign_bits - 1).astype(bf16)
    inner = jnp.einsum("hbij,jk->hbik", had * signed[:, :, 1, None, :], had, preferred_element_type=f32)
    outer = inner.astype(bf16) * signed[:, :, 2, None, :]
    whole = jnp.einsum("hbij,jk->hbik", outer, had, preferred_element_type=f32)
    whole = whole * signed[:, :, 0, :, None].astype(f32)
    whole = whole.transpose(0, 2, 1, 3).reshape(heads, dh, blocks * dh)
    near = lax.reduce_precision(whole, 8, 7)
    return jnp.concatenate([near, whole - near], axis=1).astype(bf16)


def features(rows, maps):
    dh = rows.shape[-1]
    wide = rows.astype(f32)
    mean = jnp.sum(wide * wide, axis=-1, keepdims=True) * (1.0 / dh)
    scale = lax.rsqrt(mean + norm_epsilon) * (logit_divisor / dh**0.25 / dh)
    twice = jnp.concatenate([rows, rows], axis=1)
    return jnp.exp(jnp.dot(twice, maps, preferred_element_type=f32) * scale).astype(bf16)


def pack_kernel(seq, first, count, width, offset, where_ref, x_ref, *refs):
    outs, sems = refs[:-1], refs[-1]
    me = where_ref[0]
    copies = []
    for k, out in enumerate(outs):
        start = pl.multiple_of((me ^ k) * (len(offset) * width) + offset.index(1) * width, width)
        copies.append(
            pltpu.make_async_copy(
                x_ref.at[seq, pl.ds(first, count), :, pl.ds(start, width)], out, sems.at[k]
            )
        )
    for copy in copies:
        copy.start()
    for copy in copies:
        copy.wait()


def pack(where, x, partners, seq, first, count, parts, part):
    _, _, rows, cols = x.shape
    width = cols // partners // parts
    offset = [int(j == part) for j in range(parts)]
    out = jax.ShapeDtypeStruct((count, rows, width), x.dtype)
    return pl.pallas_call(
        functools.partial(pack_kernel, seq, first, count, width, offset),
        out_shape=[out] * partners,
        in_specs=[pl.BlockSpec(memory_space=pltpu.SMEM), pl.BlockSpec(memory_space=pl.ANY)],
        out_specs=[pl.BlockSpec(memory_space=pl.ANY)] * partners,
        scratch_shapes=[pltpu.SemaphoreType.DMA((partners,))],
        compiler_params=params(),
        cost_estimate=cost(0, 4 * partners * count * rows * width),
        name="pack",
    )(where, x)


def state_kernel(heads, dh, where_ref, maps_ref, *refs):
    *kv_refs, feats_ref, mine_ref, theirs_ref = refs
    half = heads // 2
    states, totals = [], []
    for i in range(heads):
        cut = slice(i * dh, (i + 1) * dh)
        keys = jnp.concatenate([ref[0, :, cut] for ref in kv_refs], axis=0)
        values = jnp.concatenate([ref[1, :, cut] for ref in kv_refs], axis=0)
        feats = features(keys, maps_ref[i])
        feats_ref[i] = feats
        states.append(
            lax.dot_general(values, feats, (((0,), (0,)), ((), ())), preferred_element_type=f32)
        )
        totals.append(jnp.sum(feats.astype(f32), axis=0, keepdims=True))
    low = where_ref[1] == 0
    pad = jnp.zeros((ROW_TILE - half, feats_ref.shape[-1]), f32)
    for j in range(half):
        rows = slice(j * dh, (j + 1) * dh)
        mine_ref[rows, :] = jnp.where(low, states[j], states[half + j])
        theirs_ref[rows, :] = jnp.where(low, states[half + j], states[j]).astype(bf16)
    lows = jnp.concatenate(totals[:half] + [pad], axis=0)
    highs = jnp.concatenate(totals[half:] + [pad], axis=0)
    mine_ref[half * dh :, :] = jnp.where(low, lows, highs)
    theirs_ref[half * dh :, :] = jnp.where(low, highs, lows).astype(bf16)


def block_state(where, maps, kv, part, heads, dh):
    feat = maps.shape[-1]
    rows = len(kv) * kv[0].shape[1]
    height = heads // 2 * dh + ROW_TILE
    return pl.pallas_call(
        functools.partial(state_kernel, heads, dh),
        grid=(1,),
        out_shape=[
            jax.ShapeDtypeStruct((heads, rows, feat), bf16),
            jax.ShapeDtypeStruct((height, feat), f32),
            jax.ShapeDtypeStruct((height, feat), bf16),
        ],
        in_specs=[
            pl.BlockSpec(memory_space=pltpu.SMEM),
            pl.BlockSpec((heads, 2 * dh, feat), lambda _: (part, 0, 0)),
        ]
        + [full(*kv[0].shape)] * len(kv),
        out_specs=[full(heads, rows, feat), full(height, feat), full(height, feat)],
        compiler_params=params(),
        cost_estimate=cost(
            heads * rows * dh * feat * 4, heads * rows * (feat + 2 * dh) * 2, heads * rows * feat
        ),
        name="block_state",
    )(where, maps, *kv)


def prior_sums(mine, theirs, index):
    count = lax.axis_size("seq")
    odd = (index & 1) == 1
    beside = swap(theirs, "seq", 1).astype(f32)
    total = mine + beside
    prior = jnp.zeros_like(mine)
    bit = 2
    while bit < count:
        got = swap(total.astype(bf16), "seq", bit).astype(f32)
        prior = prior + jnp.where((index & bit) > 0, got, 0.0)
        total = total + got
        bit *= 2
    keep = (prior + jnp.where(odd, beside, 0.0)).astype(bf16)
    send = (prior + jnp.where(odd, 0.0, mine)).astype(bf16)
    return keep, swap(send, "seq", 1)


def attend_kernel(partners, heads, dh, where_ref, maps_ref, feats_ref, keep_ref, got_ref, *refs):
    q_refs, v_refs = refs[:partners], refs[partners : 2 * partners]
    stay_ref, leave_ref = refs[2 * partners :]
    piece = q_refs[0].shape[1]
    rows = partners * piece
    half = heads // 2
    me, low = where_ref[0], where_ref[1] == 0

    def places(shape, dim):
        ids = lax.broadcasted_iota(jnp.int32, shape, dim)
        result = ids + (me ^ 0) * piece
        for k in range(1, partners):
            result = jnp.where(ids >= k * piece, ids + ((me ^ k) - k) * piece, result)
        return result

    causal = places((rows, 1), 0) >= places((1, rows), 1)
    ones = jnp.ones((rows, dh), bf16)
    for i in range(heads):
        cut = slice(i * dh, (i + 1) * dh)
        queries = jnp.concatenate([ref[0, :, cut] for ref in q_refs], axis=0)
        values = jnp.concatenate([ref[0, :, cut] for ref in v_refs], axis=0)
        query_feats = features(queries, maps_ref[i])
        scores = lax.dot_general(
            query_feats, feats_ref[i], (((1,), (1,)), ((), ())), preferred_element_type=f32
        )
        weights = jnp.where(causal, scores, 0.0).astype(bf16)
        j = i % half
        state, total = slice(j * dh, (j + 1) * dh), slice(half * dh, half * dh + ROW_TILE)
        own = low if i < half else jnp.logical_not(low)
        prior = jnp.where(own, keep_ref[state, :], got_ref[state, :])
        tail = jnp.where(own, keep_ref[total, :], got_ref[total, :])
        tail = jnp.broadcast_to(tail[j : j + 1, :], prior.shape)
        both = jnp.dot(
            weights, jnp.concatenate([values, ones], axis=1), preferred_element_type=f32
        ) + lax.dot_general(
            query_feats,
            jnp.concatenate([prior, tail], axis=0),
            (((1,), (1,)), ((), ())),
            preferred_element_type=f32,
        )
        attended = (both[:, :dh] / both[:, dh:]).astype(bf16)
        for k in range(partners):
            out = leave_ref if k & 1 else stay_ref
            out[k // 2, :, cut] = attended[k * piece : (k + 1) * piece]


def attend(where, maps, feats, keep, got, queries, kv, part, heads, dh):
    partners, (_, piece, width) = len(kv), kv[0].shape
    feat = maps.shape[-1]
    rows = partners * piece
    out = jax.ShapeDtypeStruct((partners // 2, piece, width), bf16)
    return pl.pallas_call(
        functools.partial(attend_kernel, partners, heads, dh),
        grid=(1,),
        out_shape=[out, out],
        in_specs=[
            pl.BlockSpec(memory_space=pltpu.SMEM),
            pl.BlockSpec((heads, 2 * dh, feat), lambda _: (part, 0, 0)),
            full(*feats.shape),
            full(*keep.shape),
            full(*got.shape),
        ]
        + [pl.BlockSpec((1, piece, width), lambda _: (0, 0, part))] * partners
        + [pl.BlockSpec((1, piece, width), lambda _: (1, 0, 0))] * partners,
        out_specs=[full(*out.shape)] * 2,
        compiler_params=params(),
        cost_estimate=cost(
            2 * heads * rows * (dh * feat + rows * (feat + 2 * dh) + 2 * feat * dh),
            heads * rows * (feat + 3 * dh) * 2,
            heads * rows * feat,
        ),
        name="attend",
    )(where, maps, feats, keep, got, *queries, *kv)


def project_kernel(parts, *refs):
    own_refs, other_refs = refs[:parts], refs[parts : 2 * parts]
    own_w, other_w, stay_ref, *leave_refs = refs[2 * parts :]
    groups, piece, width = own_refs[0].shape
    acc = None
    for lhs_refs, w_ref in ((own_refs, own_w), (other_refs, other_w)):
        for p, ref in enumerate(lhs_refs):
            lhs = ref[...].reshape(groups * piece, width)
            term = jnp.dot(
                lhs, w_ref[p * width : (p + 1) * width, :], preferred_element_type=f32
            )
            acc = term if acc is None else acc + term
    stay_ref[...] = acc[:piece]
    for g, ref in enumerate(leave_refs):
        ref[...] = acc[(g + 1) * piece : (g + 2) * piece].astype(bf16)


def project(own, other, own_w, other_w):
    parts, (groups, piece, width) = len(own), own[0].shape
    depth, cols = own_w.shape
    tile = math.gcd(cols, 512)
    lhs = pl.BlockSpec((groups, piece, width), lambda n: (0, 0, 0))
    weight = pl.BlockSpec((depth, tile), lambda n: (0, n))
    out = pl.BlockSpec((piece, tile), lambda n: (0, n))
    return pl.pallas_call(
        functools.partial(project_kernel, parts),
        grid=(cols // tile,),
        out_shape=[jax.ShapeDtypeStruct((piece, cols), f32)]
        + [jax.ShapeDtypeStruct((piece, cols), bf16)] * (groups - 1),
        in_specs=[lhs] * (2 * parts) + [weight, weight],
        out_specs=[out] * groups,
        compiler_params=params(),
        cost_estimate=cost(4 * groups * piece * depth * cols, 4 * depth * cols),
        name="project",
    )(*own, *other, own_w, other_w)


def body(qkv_tokens, sign_bits, out_weight):
    partners = lax.axis_size("head")
    me, index = lax.axis_index("head"), lax.axis_index("seq")
    seqs = qkv_tokens.shape[0]
    all_heads, dh = sign_bits.shape[0], sign_bits.shape[-1]
    parts = CHUNKS
    heads = all_heads // parts
    x = qkv_tokens.transpose(0, 2, 1, 3)
    where = jnp.stack([me, index & 1]).astype(jnp.int32)

    def spread(pieces):
        return [pieces[0]] + [swap(pieces[k], "head", k) for k in range(1, partners)]

    work = [(s, c) for s in range(seqs) for c in range(parts)]
    kv = {(s, c): spread(pack(where, x, partners, s, 1, 2, parts, c)) for s, c in work}
    queries = {s: spread(pack(where, x, partners, s, 0, 1, 1, 0)) for s in range(seqs)}
    other_weight = swap(out_weight, "head", 1)
    maps = integer_maps(sign_bits)
    priors = {}
    for s, c in work:
        feats, mine, theirs = block_state(where, maps, kv[s, c], c, heads, dh)
        priors[s, c] = (feats, *prior_sums(mine, theirs, index))
    results = []
    for s in range(seqs):
        own, other = [], []
        for c in range(parts):
            stay, leave = attend(where, maps, *priors[s, c], queries[s], kv[s, c], c, heads, dh)
            own.append(stay)
            other.append(swap(leave, "head", 1))
        total, *shares = project(own, other, out_weight, other_weight)
        for g, share in enumerate(shares):
            total = total + swap(share, "head", 2 * (g + 1)).astype(f32)
        results.append(total.astype(bf16))
    return jnp.stack(results)


def solution(mesh):
    return jax.shard_map(
        body,
        mesh=mesh,
        in_specs=(
            P(None, ("seq", "head"), None, None),
            P("head", None, None, None),
            P("head", None),
        ),
        out_specs=P(None, ("seq", "head"), None),
        check_vma=False,
    )
```

```python
import functools
import math

import jax
import jax.numpy as jnp
import numpy as np
from jax import lax
from jax.experimental import pallas as pl
from jax.experimental.pallas import tpu as pltpu
from jax.sharding import PartitionSpec as P

logit_divisor = 1.3
norm_epsilon = 1e-06
CHUNKS = 1

bf16, f32 = jnp.bfloat16, jnp.float32
VMEM_LIMIT = 48 * 1024 * 1024
ROW_TILE = 16


def params():
    return pltpu.CompilerParams(vmem_limit_bytes=VMEM_LIMIT)


def full(*shape):
    return pl.BlockSpec(shape, lambda _: (0,) * len(shape))


def cost(flops, nbytes, exps=0):
    return pl.CostEstimate(flops=int(flops), bytes_accessed=int(nbytes), transcendentals=int(exps))


def swap(value, axis, bit):
    return lax.ppermute(value, axis, [(j, j ^ bit) for j in range(lax.axis_size(axis))])


def sign_matrix(order):
    ids = np.arange(order)
    common = ids[:, None] & ids[None, :]
    parity = np.zeros_like(common)
    while common.any():
        parity ^= common & 1
        common = common >> 1
    return (1 - 2 * parity).astype(np.float32)


def integer_maps(sign_bits):
    heads, blocks, _, dh = sign_bits.shape
    had = jnp.asarray(sign_matrix(dh), bf16)
    signed = (2 * sign_bits - 1).astype(bf16)
    inner = jnp.einsum("hbij,jk->hbik", had * signed[:, :, 1, None, :], had, preferred_element_type=f32)
    outer = inner.astype(bf16) * signed[:, :, 2, None, :]
    whole = jnp.einsum("hbij,jk->hbik", outer, had, preferred_element_type=f32)
    whole = whole * signed[:, :, 0, :, None].astype(f32)
    whole = whole.transpose(0, 2, 1, 3).reshape(heads, dh, blocks * dh)
    near = lax.reduce_precision(whole, 8, 7)
    return jnp.concatenate([near, whole - near], axis=1).astype(bf16)


def features(rows, maps):
    dh = rows.shape[-1]
    wide = rows.astype(f32)
    mean = jnp.sum(wide * wide, axis=-1, keepdims=True) * (1.0 / dh)
    scale = lax.rsqrt(mean + norm_epsilon) * (logit_divisor / dh**0.25 / dh)
    twice = jnp.concatenate([rows, rows], axis=1)
    return jnp.exp(jnp.dot(twice, maps, preferred_element_type=f32) * scale).astype(bf16)


def pack_kernel(seq, first, part, x_ref, out_ref, sems):
    partners, count, _, width = out_ref.shape
    stride = x_ref.shape[-1] // partners
    copies = [
        pltpu.make_async_copy(
            x_ref.at[seq, pl.ds(first, count), :, pl.ds(g * stride + part * width, width)],
            out_ref.at[g],
            sems.at[g],
        )
        for g in range(partners)
    ]
    for copy in copies:
        copy.start()
    for copy in copies:
        copy.wait()


def pack(x, partners, seq, first, count, parts, part):
    _, _, rows, cols = x.shape
    width = cols // partners // parts
    return pl.pallas_call(
        functools.partial(pack_kernel, seq, first, part),
        out_shape=jax.ShapeDtypeStruct((partners, count, rows, width), x.dtype),
        in_specs=[pl.BlockSpec(memory_space=pltpu.HBM)],
        out_specs=pl.BlockSpec(memory_space=pltpu.HBM),
        scratch_shapes=[pltpu.SemaphoreType.DMA((partners,))],
        compiler_params=params(),
        cost_estimate=cost(0, 4 * partners * count * rows * width),
        name="pack",
    )(x)


def exchange(value, axis):
    return lax.all_to_all(value, axis, split_axis=0, concat_axis=0, tiled=True)


def joined(ref, which, cut):
    return jnp.concatenate([ref[p, which, :, cut] for p in range(ref.shape[0])], axis=0)


def state_kernel(heads, dh, maps_ref, kv_ref, feats_ref, state_ref):
    totals = []
    for i in range(heads):
        cut = slice(i * dh, (i + 1) * dh)
        feats = features(joined(kv_ref, 0, cut), maps_ref[i])
        feats_ref[i] = feats
        state_ref[cut, :] = lax.dot_general(
            joined(kv_ref, 1, cut), feats, (((0,), (0,)), ((), ())), preferred_element_type=f32
        ).astype(bf16)
        totals.append(jnp.sum(feats.astype(f32), axis=0, keepdims=True))
    left = state_ref.shape[0] - heads * dh
    totals.append(jnp.zeros((left - heads, state_ref.shape[1]), f32))
    state_ref[heads * dh :, :] = jnp.concatenate(totals, axis=0).astype(bf16)


def block_state(maps, kv, part, heads, dh, height):
    feat = maps.shape[-1]
    partners, _, piece, _ = kv.shape
    rows = partners * piece
    return pl.pallas_call(
        functools.partial(state_kernel, heads, dh),
        grid=(1,),
        out_shape=[
            jax.ShapeDtypeStruct((heads, rows, feat), bf16),
            jax.ShapeDtypeStruct((height, feat), bf16),
        ],
        in_specs=[
            pl.BlockSpec((heads, 2 * dh, feat), lambda _: (part, 0, 0)),
            full(*kv.shape),
        ],
        out_specs=[full(heads, rows, feat), full(height, feat)],
        compiler_params=params(),
        cost_estimate=cost(
            heads * rows * dh * feat * 4, heads * rows * (feat + 2 * dh) * 2, heads * rows * feat
        ),
        name="block_state",
    )(maps, kv)


def prefix_kernel(in_ref, out_ref):
    total = jnp.zeros(in_ref.shape[1:], f32)
    for p in range(in_ref.shape[0]):
        out_ref[p] = total.astype(bf16)
        total = total + in_ref[p].astype(f32)


def prior_sums(state):
    count = lax.axis_size("seq")
    height, feat = state.shape
    shares = exchange(state.reshape(count, height // count, feat), "seq")
    sums = pl.pallas_call(
        prefix_kernel,
        grid=(1,),
        out_shape=jax.ShapeDtypeStruct(shares.shape, bf16),
        in_specs=[full(*shares.shape)],
        out_specs=full(*shares.shape),
        compiler_params=params(),
        cost_estimate=cost(2 * height * feat, 4 * height * feat),
        name="prefix",
    )(shares)
    return exchange(sums, "seq").reshape(height, feat)


def attend_kernel(heads, dh, where_ref, maps_ref, feats_ref, prior_ref, q_ref, v_ref, stay_ref, leave_ref):
    partners, _, piece, _ = q_ref.shape
    rows = partners * piece
    even = where_ref[0] % 2 == 0
    causal = lax.broadcasted_iota(jnp.int32, (rows, rows), 0) >= lax.broadcasted_iota(
        jnp.int32, (rows, rows), 1
    )
    ones = jnp.ones((rows, dh), bf16)
    for i in range(heads):
        cut = slice(i * dh, (i + 1) * dh)
        query_feats = features(joined(q_ref, 0, cut), maps_ref[i])
        scores = lax.dot_general(
            query_feats, feats_ref[i], (((1,), (1,)), ((), ())), preferred_element_type=f32
        )
        weights = jnp.where(causal, scores, 0.0).astype(bf16)
        tails = prior_ref[heads * dh : heads * dh + ROW_TILE, :]
        tails = jnp.broadcast_to(tails[i : i + 1, :], (dh, tails.shape[1]))
        both = jnp.dot(
            weights,
            jnp.concatenate([joined(v_ref, 0, cut), ones], axis=1),
            preferred_element_type=f32,
        ) + lax.dot_general(
            query_feats,
            jnp.concatenate([prior_ref[cut, :], tails], axis=0),
            (((1,), (1,)), ((), ())),
            preferred_element_type=f32,
        )
        attended = (both[:, :dh] / both[:, dh:]).astype(bf16)
        for o in range(partners // 2):
            first = attended[2 * o * piece : (2 * o + 1) * piece]
            second = attended[(2 * o + 1) * piece : (2 * o + 2) * piece]
            stay_ref[o, :, cut] = jnp.where(even, first, second)
            leave_ref[o, :, cut] = jnp.where(even, second, first)


def attend(where, maps, feats, prior, queries, kv, part, heads, dh):
    partners, _, piece, width = kv.shape
    feat = maps.shape[-1]
    rows = partners * piece
    out = jax.ShapeDtypeStruct((partners // 2, piece, width), bf16)
    return pl.pallas_call(
        functools.partial(attend_kernel, heads, dh),
        grid=(1,),
        out_shape=[out, out],
        in_specs=[
            pl.BlockSpec(memory_space=pltpu.SMEM),
            pl.BlockSpec((heads, 2 * dh, feat), lambda _: (part, 0, 0)),
            full(*feats.shape),
            full(*prior.shape),
            pl.BlockSpec((partners, 1, piece, width), lambda _: (0, 0, 0, part)),
            pl.BlockSpec((partners, 1, piece, width), lambda _: (0, 1, 0, 0)),
        ],
        out_specs=[full(*out.shape)] * 2,
        compiler_params=params(),
        cost_estimate=cost(
            2 * heads * rows * (dh * feat + rows * (feat + 2 * dh) + 2 * feat * dh),
            heads * rows * (feat + 3 * dh) * 2,
            heads * rows * feat,
        ),
        name="attend",
    )(where, maps, feats, prior, queries, kv)


def project_kernel(parts, where_ref, *refs):
    own_refs, other_refs = refs[:parts], refs[parts : 2 * parts]
    own_w, other_w, stay_ref, *leave_refs = refs[2 * parts :]
    groups, _, width = own_refs[0].shape
    mine = where_ref[0] // 2
    acc = None
    for lhs_refs, w_ref in ((own_refs, own_w), (other_refs, other_w)):
        for p, ref in enumerate(lhs_refs):
            lhs = jnp.concatenate([ref[mine ^ t] for t in range(groups)], axis=0)
            term = jnp.dot(lhs, w_ref[p * width : (p + 1) * width, :], preferred_element_type=f32)
            acc = term if acc is None else acc + term
    piece = stay_ref.shape[0]
    stay_ref[...] = acc[:piece]
    for t, ref in enumerate(leave_refs):
        ref[...] = acc[(t + 1) * piece : (t + 2) * piece].astype(bf16)


def project(where, own, other, own_w, other_w):
    parts, (groups, piece, width) = len(own), own[0].shape
    depth, cols = own_w.shape
    tile = math.gcd(cols, 512)
    lhs = pl.BlockSpec((groups, piece, width), lambda n: (0, 0, 0))
    weight = pl.BlockSpec((depth, tile), lambda n: (0, n))
    out = pl.BlockSpec((piece, tile), lambda n: (0, n))
    return pl.pallas_call(
        functools.partial(project_kernel, parts),
        grid=(cols // tile,),
        out_shape=[jax.ShapeDtypeStruct((piece, cols), f32)]
        + [jax.ShapeDtypeStruct((piece, cols), bf16)] * (groups - 1),
        in_specs=[pl.BlockSpec(memory_space=pltpu.SMEM)] + [lhs] * (2 * parts) + [weight, weight],
        out_specs=[out] * groups,
        compiler_params=params(),
        cost_estimate=cost(4 * groups * piece * depth * cols, 4 * depth * cols),
        name="project",
    )(where, *own, *other, own_w, other_w)


def body(qkv_tokens, sign_bits, out_weight):
    partners, blocks = lax.axis_size("head"), lax.axis_size("seq")
    seqs = qkv_tokens.shape[0]
    all_heads, dh = sign_bits.shape[0], sign_bits.shape[-1]
    parts = CHUNKS
    heads = all_heads // parts
    unit = ROW_TILE * blocks
    height = -(-heads * (dh + 1) // unit) * unit
    x = qkv_tokens.transpose(0, 2, 1, 3)
    where = lax.axis_index("head").astype(jnp.int32).reshape(1)
    work = [(s, c) for s in range(seqs) for c in range(parts)]
    kv = {(s, c): exchange(pack(x, partners, s, 1, 2, parts, c), "head") for s, c in work}
    queries = {s: exchange(pack(x, partners, s, 0, 1, 1, 0), "head") for s in range(seqs)}
    other_weight = swap(out_weight, "head", 1)
    maps = integer_maps(sign_bits)
    priors = {}
    for s, c in work:
        feats, state = block_state(maps, kv[s, c], c, heads, dh, height)
        priors[s, c] = (feats, prior_sums(state))
    results = []
    for s in range(seqs):
        own, other = [], []
        for c in range(parts):
            stay, leave = attend(where, maps, *priors[s, c], queries[s], kv[s, c], c, heads, dh)
            own.append(stay)
            other.append(swap(leave, "head", 1))
        total, *shares = project(where, own, other, out_weight, other_weight)
        for t, share in enumerate(shares):
            total = total + swap(share, "head", 2 * (t + 1)).astype(f32)
        results.append(total.astype(bf16))
    return jnp.stack(results)


def solution(mesh):
    return jax.shard_map(
        body,
        mesh=mesh,
        in_specs=(
            P(None, ("seq", "head"), None, None),
            P("head", None, None, None),
            P("head", None),
        ),
        out_specs=P(None, ("seq", "head"), None),
        check_vma=False,
    )
```

```python
import functools
import math

import jax
import jax.numpy as jnp
import numpy as np
from jax import lax
from jax.experimental import pallas as pl
from jax.experimental.pallas import tpu as pltpu
from jax.sharding import PartitionSpec as P

logit_divisor = 1.3
norm_epsilon = 1e-06
CHUNKS = 2

SLABS = 2

bf16, f32 = jnp.bfloat16, jnp.float32
ROW_TILE = 16


def params(mebibytes=20):
    return pltpu.CompilerParams(vmem_limit_bytes=mebibytes * 1024 * 1024)


def full(*shape):
    return pl.BlockSpec(shape, lambda _: (0,) * len(shape))


def ordered(kernel, count, skip):
    return lambda *refs: kernel(*refs[:skip], *refs[skip + count :])


def waits(after):
    return [pl.BlockSpec(memory_space=pl.ANY)] * len(after)


def swap(value, axis, bit):
    return lax.ppermute(value, axis, [(j, j ^ bit) for j in range(lax.axis_size(axis))])


def sign_matrix(order):
    ids = np.arange(order)
    common = ids[:, None] & ids[None, :]
    parity = np.zeros_like(common)
    while common.any():
        parity ^= common & 1
        common = common >> 1
    return (1 - 2 * parity).astype(np.float32)


def integer_maps(sign_bits):
    heads, blocks, _, dh = sign_bits.shape
    had = jnp.asarray(sign_matrix(dh), bf16)
    signed = (2 * sign_bits - 1).astype(bf16)
    inner = jnp.einsum("hbij,jk->hbik", had * signed[:, :, 1, None, :], had, preferred_element_type=f32)
    outer = inner.astype(bf16) * signed[:, :, 2, None, :]
    whole = jnp.einsum("hbij,jk->hbik", outer, had, preferred_element_type=f32)
    whole = whole * signed[:, :, 0, :, None].astype(f32)
    whole = whole.transpose(0, 2, 1, 3).reshape(heads, dh, blocks * dh)
    near = lax.reduce_precision(whole, 8, 7)
    return jnp.concatenate([near, whole - near], axis=1).astype(bf16)


def features(rows, maps):
    dh = rows.shape[-1]
    wide = rows.astype(f32)
    mean = jnp.sum(wide * wide, axis=-1, keepdims=True) * (1.0 / dh)
    scale = lax.rsqrt(mean + norm_epsilon) * (logit_divisor / dh**0.25 / dh)
    twice = jnp.concatenate([rows, rows], axis=1)
    return jnp.exp(jnp.dot(twice, maps, preferred_element_type=f32) * scale).astype(bf16)


def pack_kernel(items, partners, *refs):
    refs = refs[1:]
    seqs = sorted({item[0] for item in items})
    ins, outs = refs[: len(seqs) * partners], refs[len(seqs) * partners :]
    for n, (seq, first, count, parts, part) in enumerate(items):
        for k in range(partners):
            out_ref = outs[n * partners + k]
            width = out_ref.shape[-1]
            in_ref = ins[seqs.index(seq) * partners + k]
            out_ref[...] = in_ref[0, first : first + count, :, part * width : (part + 1) * width]


def pack(where, x, partners, items):
    _, kinds, rows, cols = x.shape
    width = cols // partners
    seqs = sorted({item[0] for item in items})

    def columns_of(seq, k):
        return pl.BlockSpec((1, kinds, rows, width), lambda _, where: (seq, 0, 0, where[0] ^ k))

    shapes = [
        (count, rows, width // parts) for _, _, count, parts, _ in items for _ in range(partners)
    ]
    outs = pl.pallas_call(
        functools.partial(pack_kernel, items, partners),
        out_shape=[jax.ShapeDtypeStruct(shape, x.dtype) for shape in shapes],
        grid_spec=pltpu.PrefetchScalarGridSpec(
            num_scalar_prefetch=1,
            grid=(1,),
            in_specs=[columns_of(seq, k) for seq in seqs for k in range(partners)],
            out_specs=[pl.BlockSpec(shape, lambda _, where: (0, 0, 0)) for shape in shapes],
        ),
        compiler_params=params(60),
        cost_estimate=pl.CostEstimate(flops=0, bytes_accessed=0, transcendentals=0),
        name="pack",
    )(where, *[x] * (partners * len(seqs)))
    return [outs[n * partners : (n + 1) * partners] for n in range(len(items))]


def state_kernel(heads, dh, where_ref, maps_ref, *refs):
    *kv_refs, feats_ref, mine_ref, theirs_ref = refs
    half = heads // 2
    states, totals = [], []
    for i in range(heads):
        cut = slice(i * dh, (i + 1) * dh)
        keys = jnp.concatenate([ref[0, :, cut] for ref in kv_refs], axis=0)
        values = jnp.concatenate([ref[1, :, cut] for ref in kv_refs], axis=0)
        feats = features(keys, maps_ref[i])
        feats_ref[i] = feats
        states.append(
            lax.dot_general(values, feats, (((0,), (0,)), ((), ())), preferred_element_type=f32)
        )
        totals.append(jnp.sum(feats.astype(f32), axis=0, keepdims=True))
    low = where_ref[1] == 0
    pad = jnp.zeros((ROW_TILE - half, feats_ref.shape[-1]), f32)
    for j in range(half):
        rows = slice(j * dh, (j + 1) * dh)
        mine_ref[rows, :] = jnp.where(low, states[j], states[half + j])
        theirs_ref[rows, :] = jnp.where(low, states[half + j], states[j]).astype(bf16)
    lows = jnp.concatenate(totals[:half] + [pad], axis=0)
    highs = jnp.concatenate(totals[half:] + [pad], axis=0)
    mine_ref[half * dh :, :] = jnp.where(low, lows, highs)
    theirs_ref[half * dh :, :] = jnp.where(low, highs, lows).astype(bf16)


def block_state(where, maps, kv, part, heads, dh, after):
    feat = maps.shape[-1]
    rows = len(kv) * kv[0].shape[1]
    height = heads // 2 * dh + ROW_TILE
    return pl.pallas_call(
        ordered(functools.partial(state_kernel, heads, dh), len(after), 0),
        grid=(1,),
        out_shape=[
            jax.ShapeDtypeStruct((heads, rows, feat), bf16),
            jax.ShapeDtypeStruct((height, feat), f32),
            jax.ShapeDtypeStruct((height, feat), bf16),
        ],
        in_specs=waits(after)
        + [
            pl.BlockSpec(memory_space=pltpu.SMEM),
            pl.BlockSpec((heads, 2 * dh, feat), lambda _: (part, 0, 0)),
        ]
        + [full(*kv[0].shape)] * len(kv),
        out_specs=[full(heads, rows, feat), full(height, feat), full(height, feat)],
        compiler_params=params(),
        cost_estimate=pl.CostEstimate(flops=0, bytes_accessed=0, transcendentals=0),
        name="block_state",
    )(*after, where, maps, *kv)


def chain_values(levels, where_ref, refs):
    mine, beside = refs[0][...], refs[1][...].astype(f32)
    got = [ref[...].astype(f32) for ref in refs[2:]]
    if len(got) < levels:
        total = mine + beside
        for value in got:
            total = total + value
        return [total]
    odd = where_ref[1] == 1
    prior = jnp.zeros_like(mine)
    for level, value in enumerate(got):
        prior = prior + jnp.where(where_ref[2 + level] == 1, value, 0.0)
    return [prior + jnp.where(odd, 0.0, mine), prior + jnp.where(odd, beside, 0.0)]


def round_kernel(levels, counts, where_ref, *refs):
    ins, outs = list(refs[: sum(counts)]), list(refs[sum(counts) :])
    for count in counts:
        for value in chain_values(levels, where_ref, ins[:count]):
            outs.pop(0)[...] = value.astype(bf16)
        del ins[:count]


def round_step(where, levels, chains, after):
    counts = [len(chain) for chain in chains]
    results = [2 if count == levels + 2 else 1 for count in counts]
    values = [value for chain in chains for value in chain]
    shape = values[0].shape
    outs = list(pl.pallas_call(
        ordered(functools.partial(round_kernel, levels, counts), len(after), 0),
        grid=(1,),
        out_shape=[jax.ShapeDtypeStruct(shape, bf16)] * sum(results),
        in_specs=waits(after)
        + [pl.BlockSpec(memory_space=pltpu.SMEM)]
        + [full(*shape)] * len(values),
        out_specs=[full(*shape)] * sum(results),
        compiler_params=params(),
        cost_estimate=pl.CostEstimate(flops=0, bytes_accessed=0, transcendentals=0),
        name="round_step",
    )(*after, where, *values))
    return [[outs.pop(0) for _ in range(result)] for result in results]


def local_kernel(partners, heads, dh, where_ref, maps_ref, feats_ref, *refs):
    q_refs, v_refs = refs[:partners], refs[partners : 2 * partners]
    query_feats_ref, local_ref = refs[2 * partners :]
    piece = q_refs[0].shape[1]
    rows = partners * piece
    me = where_ref[0]

    def places(shape, dim):
        ids = lax.broadcasted_iota(jnp.int32, shape, dim)
        result = ids + (me ^ 0) * piece
        for k in range(1, partners):
            result = jnp.where(ids >= k * piece, ids + ((me ^ k) - k) * piece, result)
        return result

    causal = places((rows, 1), 0) >= places((1, rows), 1)
    ones = jnp.ones((rows, dh), bf16)
    for i in range(heads):
        cut = slice(i * dh, (i + 1) * dh)
        queries = jnp.concatenate([ref[0, :, cut] for ref in q_refs], axis=0)
        values = jnp.concatenate([ref[0, :, cut] for ref in v_refs], axis=0)
        query_feats = features(queries, maps_ref[i])
        query_feats_ref[i] = query_feats
        scores = lax.dot_general(
            query_feats, feats_ref[i], (((1,), (1,)), ((), ())), preferred_element_type=f32
        )
        weights = jnp.where(causal, scores, 0.0).astype(bf16)
        local_ref[i] = jnp.dot(
            weights, jnp.concatenate([values, ones], axis=1), preferred_element_type=f32
        )


def attend_local(where, maps, feats, queries, kv, part, heads, dh, after):
    partners, (_, piece, width) = len(kv), kv[0].shape
    feat = maps.shape[-1]
    rows = partners * piece
    return pl.pallas_call(
        ordered(functools.partial(local_kernel, partners, heads, dh), len(after), 0),
        grid=(1,),
        out_shape=[
            jax.ShapeDtypeStruct((heads, rows, feat), bf16),
            jax.ShapeDtypeStruct((heads, rows, 2 * dh), f32),
        ],
        in_specs=waits(after)
        + [
            pl.BlockSpec(memory_space=pltpu.SMEM),
            pl.BlockSpec((heads, 2 * dh, feat), lambda _: (part, 0, 0)),
            full(*feats.shape),
        ]
        + [pl.BlockSpec((1, piece, width), lambda _: (0, 0, part))] * partners
        + [pl.BlockSpec((1, piece, width), lambda _: (1, 0, 0))] * partners,
        out_specs=[full(heads, rows, feat), full(heads, rows, 2 * dh)],
        compiler_params=params(),
        cost_estimate=pl.CostEstimate(flops=0, bytes_accessed=0, transcendentals=0),
        name="attend_local",
    )(*after, where, maps, feats, *queries, *kv)


def prior_kernel(partners, heads, dh, where_ref, query_feats_ref, local_ref, keep_ref, got_ref, *refs):
    stay_ref, leave_ref = refs
    piece = query_feats_ref.shape[1] // partners
    half = heads // 2
    low = where_ref[1] == 0
    for i in range(heads):
        j = i % half
        state, total = slice(j * dh, (j + 1) * dh), slice(half * dh, half * dh + ROW_TILE)
        own = low if i < half else jnp.logical_not(low)
        prior = jnp.where(own, keep_ref[state, :], got_ref[state, :])
        tail = jnp.where(own, keep_ref[total, :], got_ref[total, :])
        tail = jnp.broadcast_to(tail[j : j + 1, :], prior.shape)
        both = local_ref[i] + lax.dot_general(
            query_feats_ref[i],
            jnp.concatenate([prior, tail], axis=0),
            (((1,), (1,)), ((), ())),
            preferred_element_type=f32,
        )
        attended = (both[:, :dh] / both[:, dh:]).astype(bf16)
        for k in range(partners):
            out = leave_ref if k & 1 else stay_ref
            out[k // 2, :, i * dh : (i + 1) * dh] = attended[k * piece : (k + 1) * piece]


def attend_prior(where, query_feats, local, keep, got, partners, dh, after):
    heads, rows, feat = query_feats.shape
    out = jax.ShapeDtypeStruct((partners // 2, rows // partners, heads * dh), bf16)
    return pl.pallas_call(
        ordered(functools.partial(prior_kernel, partners, heads, dh), len(after), 0),
        grid=(1,),
        out_shape=[out, out],
        in_specs=waits(after)
        + [pl.BlockSpec(memory_space=pltpu.SMEM)]
        + [full(*value.shape) for value in (query_feats, local, keep, got)],
        out_specs=[full(*out.shape)] * 2,
        compiler_params=params(),
        cost_estimate=pl.CostEstimate(flops=0, bytes_accessed=0, transcendentals=0),
        name="attend_prior",
    )(*after, where, query_feats, local, keep, got)


def project_kernel(parts, *refs):
    own_refs, other_refs = refs[:parts], refs[parts : 2 * parts]
    own_w, other_w, stay_ref, *leave_refs = refs[2 * parts :]
    groups, piece, width = own_refs[0].shape
    acc = None
    for lhs_refs, w_ref in ((own_refs, own_w), (other_refs, other_w)):
        for p, ref in enumerate(lhs_refs):
            lhs = ref[...].reshape(groups * piece, width)
            term = jnp.dot(
                lhs, w_ref[p * width : (p + 1) * width, :], preferred_element_type=f32
            )
            acc = term if acc is None else acc + term
    stay_ref[...] = acc[:piece]
    for g, ref in enumerate(leave_refs):
        ref[...] = acc[(g + 1) * piece : (g + 2) * piece].astype(bf16)


def project(own, other, own_w, other_w, slabs, slab, after):
    parts, (groups, piece, width) = len(own), own[0].shape
    depth, cols = own_w.shape
    cols = cols // slabs
    tile = math.gcd(cols, 512)
    first = slab * (cols // tile)
    lhs = pl.BlockSpec((groups, piece, width), lambda n: (0, 0, 0))
    weight = pl.BlockSpec((depth, tile), lambda n: (0, first + n))
    out = pl.BlockSpec((piece, tile), lambda n: (0, n))
    return pl.pallas_call(
        ordered(functools.partial(project_kernel, parts), len(after), 0),
        grid=(cols // tile,),
        out_shape=[jax.ShapeDtypeStruct((piece, cols), f32)]
        + [jax.ShapeDtypeStruct((piece, cols), bf16)] * (groups - 1),
        in_specs=waits(after) + [lhs] * (2 * parts) + [weight, weight],
        out_specs=[out] * groups,
        compiler_params=params(),
        cost_estimate=pl.CostEstimate(flops=0, bytes_accessed=0, transcendentals=0),
        name="project",
    )(*after, *own, *other, own_w, other_w)


def body(qkv_tokens, sign_bits, out_weight):
    partners, blocks = lax.axis_size("head"), lax.axis_size("seq")
    me, index = lax.axis_index("head"), lax.axis_index("seq")
    seqs = qkv_tokens.shape[0]
    all_heads, dh = sign_bits.shape[0], sign_bits.shape[-1]
    parts = CHUNKS
    heads = all_heads // parts
    levels = blocks.bit_length() - 2
    x = qkv_tokens.transpose(0, 2, 1, 3)
    where = jnp.stack([me] + [(index >> l) & 1 for l in range(levels + 1)]).astype(jnp.int32)

    def spread(pieces):
        return [pieces[0]] + [swap(pieces[k], "head", k) for k in range(1, partners)]

    work = [(s, c) for s in range(seqs) for c in range(parts)]
    items = [(s, 1, 2, parts, c) for s, c in work] + [(s, 0, 1, 1, 0) for s in range(seqs)]
    packed = pack(where, x, partners, items[:1]) + pack(where, x, partners, items[1:])
    packed = [spread(pieces) for pieces in packed]
    kv, queries = packed[: len(work)], packed[len(work) :]
    late_weight, _ = lax.optimization_barrier((out_weight, kv[-1]))
    other_weight = swap(late_weight, "head", 1)
    maps = integer_maps(sign_bits)

    last = []

    def state(n):
        feats[n], mine, theirs = block_state(where, maps, kv[n], work[n][1], heads, dh, last)
        chains[n] = [mine, swap(theirs, "seq", 1)]
        last[:] = [mine]

    def step():
        moving = [n for n in chains if n not in ends]
        for n, outs in zip(moving, round_step(where, levels, [chains[n] for n in moving], last)):
            last[:] = [outs[0]]
            if len(outs) == 2:
                ends[n] = (outs[1], swap(outs[0], "seq", 1))
            else:
                chains[n] = chains[n] + [swap(outs[0], "seq", 2 ** (len(chains[n]) - 1))]

    def local(n):
        s, c = work[n]
        locals_[n] = attend_local(where, maps, feats[n], queries[s], kv[n], c, heads, dh, last)
        last[:] = [locals_[n][0]]

    def attend(n):
        stay, leave = attend_prior(where, *locals_[n], *ends[n], partners, dh, last)
        own.setdefault(work[n][0], []).append(stay)
        other.setdefault(work[n][0], []).append(swap(leave, "head", 1))
        last[:] = [stay]

    def multiply(s, slab):
        total, *shares = project(own[s], other[s], out_weight, other_weight, SLABS, slab, last)
        totals[s, slab] = total, [swap(v, "head", 2 * (g + 1)) for g, v in enumerate(shares)]
        last[:] = [total]

    feats, chains, ends, locals_, own, other, totals = {}, {}, {}, {}, {}, {}, {}
    early, late = [[n for n, (s, _) in enumerate(work) if (s == seqs - 1) == end] for end in (False, True)]
    state(0)
    for n in range(1, len(work)):
        step()
        state(n)
    step()
    for n in early:
        local(n)
    while len(ends) < len(work):
        step()
        if len(ends) == len(work) - 1:
            for n in early:
                attend(n)
            for n in late:
                local(n)
    for s in range(seqs - 1):
        multiply(s, 0)
    for n in late:
        attend(n)
    for s in range(seqs - 1):
        for slab in range(1, SLABS):
            multiply(s, slab)
    for slab in range(SLABS):
        multiply(seqs - 1, slab)

    def finished(s, slab):
        total, shares = totals[s, slab]
        for share in shares:
            total = total + share.astype(f32)
        return total.astype(bf16)

    return jnp.stack(
        [jnp.concatenate([finished(s, n) for n in range(SLABS)], axis=1) for s in range(seqs)]
    )


def solution(mesh):
    return jax.shard_map(
        body,
        mesh=mesh,
        in_specs=(
            P(None, ("seq", "head"), None, None),
            P("head", None, None, None),
            P("head", None),
        ),
        out_specs=P(None, ("seq", "head"), None),
        check_vma=False,
    )
```

```python
import functools
import math

import jax
import jax.numpy as jnp
import numpy as np
from jax import lax
from jax.experimental import pallas as pl
from jax.experimental.pallas import tpu as pltpu
from jax.sharding import PartitionSpec as P

logit_divisor = 1.3
norm_epsilon = 1e-06
CHUNKS = 2

SLABS = 2
LOCAL_US = 0

bf16, f32 = jnp.bfloat16, jnp.float32
ROW_TILE = 16


def params(mebibytes=20):
    return pltpu.CompilerParams(vmem_limit_bytes=mebibytes * 1024 * 1024)


def full(*shape):
    return pl.BlockSpec(shape, lambda _: (0,) * len(shape))


def ordered(kernel, count, skip):
    return lambda *refs: kernel(*refs[:skip], *refs[skip + count :])


def busy(microseconds):
    return pl.CostEstimate(flops=int(microseconds * 1e9), bytes_accessed=0, transcendentals=0)


def waits(after):
    return [pl.BlockSpec(memory_space=pl.ANY)] * len(after)


def swap(value, axis, bit):
    return lax.ppermute(value, axis, [(j, j ^ bit) for j in range(lax.axis_size(axis))])


def sign_matrix(order):
    ids = np.arange(order)
    common = ids[:, None] & ids[None, :]
    parity = np.zeros_like(common)
    while common.any():
        parity ^= common & 1
        common = common >> 1
    return (1 - 2 * parity).astype(np.float32)


def integer_maps(sign_bits):
    heads, blocks, _, dh = sign_bits.shape
    had = jnp.asarray(sign_matrix(dh), bf16)
    signed = (2 * sign_bits - 1).astype(bf16)
    inner = jnp.einsum("hbij,jk->hbik", had * signed[:, :, 1, None, :], had, preferred_element_type=f32)
    outer = inner.astype(bf16) * signed[:, :, 2, None, :]
    whole = jnp.einsum("hbij,jk->hbik", outer, had, preferred_element_type=f32)
    whole = whole * signed[:, :, 0, :, None].astype(f32)
    whole = whole.transpose(0, 2, 1, 3).reshape(heads, dh, blocks * dh)
    near = lax.reduce_precision(whole, 8, 7)
    return jnp.concatenate([near, whole - near], axis=1).astype(bf16)


def features(rows, maps):
    dh = rows.shape[-1]
    wide = rows.astype(f32)
    mean = jnp.sum(wide * wide, axis=-1, keepdims=True) * (1.0 / dh)
    scale = lax.rsqrt(mean + norm_epsilon) * (logit_divisor / dh**0.25 / dh)
    twice = jnp.concatenate([rows, rows], axis=1)
    return jnp.exp(jnp.dot(twice, maps, preferred_element_type=f32) * scale).astype(bf16)


def pack_kernel(places, where_ref, *refs):
    for ref, (out, index) in zip(refs, places):
        refs[len(places) + out][index] = ref[0, 0]


def pack(where, x, partners, wanted):
    _, _, rows, cols = x.shape
    ins, places, shapes = [], [], []
    for out, (lead, kinds, part, parts) in enumerate(wanted):
        width = cols // partners // parts
        shapes.append((len(lead), len(kinds), rows, width))
        for i, (seq, k) in enumerate(lead):
            for j, kind in enumerate(kinds):
                places.append((out, (i, j)))
                ins.append(
                    pl.BlockSpec(
                        (1, 1, rows, width),
                        lambda _, where, seq=seq, kind=kind, k=k, part=part, parts=parts: (
                            seq,
                            kind,
                            0,
                            (where[0] ^ k) * parts + part,
                        ),
                    )
                )
    return pl.pallas_call(
        functools.partial(pack_kernel, places),
        out_shape=[jax.ShapeDtypeStruct(shape, x.dtype) for shape in shapes],
        grid_spec=pltpu.PrefetchScalarGridSpec(
            num_scalar_prefetch=1,
            grid=(1,),
            in_specs=ins,
            out_specs=[pl.BlockSpec(shape, lambda _, where: (0, 0, 0, 0)) for shape in shapes],
        ),
        compiler_params=params(60),
        cost_estimate=busy(0),
        name="pack",
    )(where, *[x] * len(ins))


def operands(pieces, rows, width):
    specs = [
        pl.BlockSpec((1, 1, rows, width), lambda _, at=(lead, kind, 0, col): at)
        for _, lead, kind, col in pieces
    ]
    return [piece[0] for piece in pieces], specs


def joined(refs, cut):
    return jnp.concatenate([ref[0, 0, :, cut] for ref in refs], axis=0)


def state_kernel(partners, heads, dh, where_ref, maps_ref, *refs):
    k_refs, v_refs = refs[:partners], refs[partners : 2 * partners]
    feats_ref, mine_ref, theirs_ref = refs[2 * partners :]
    half = heads // 2
    states, totals = [], []
    for i in range(heads):
        cut = slice(i * dh, (i + 1) * dh)
        keys, values = joined(k_refs, cut), joined(v_refs, cut)
        feats = features(keys, maps_ref[i])
        feats_ref[i] = feats
        states.append(
            lax.dot_general(values, feats, (((0,), (0,)), ((), ())), preferred_element_type=f32)
        )
        totals.append(jnp.sum(feats.astype(f32), axis=0, keepdims=True))
    low = where_ref[1] == 0
    pad = jnp.zeros((ROW_TILE - half, feats_ref.shape[-1]), f32)
    for j in range(half):
        rows = slice(j * dh, (j + 1) * dh)
        mine_ref[rows, :] = jnp.where(low, states[j], states[half + j])
        theirs_ref[rows, :] = jnp.where(low, states[half + j], states[j]).astype(bf16)
    lows = jnp.concatenate(totals[:half] + [pad], axis=0)
    highs = jnp.concatenate(totals[half:] + [pad], axis=0)
    mine_ref[half * dh :, :] = jnp.where(low, lows, highs)
    theirs_ref[half * dh :, :] = jnp.where(low, highs, lows).astype(bf16)


def block_state(where, maps, keys, values, part, heads, dh, piece, after):
    feat = maps.shape[-1]
    rows = len(keys) * piece
    height = heads // 2 * dh + ROW_TILE
    arrays, specs = operands(keys + values, piece, heads * dh)
    return pl.pallas_call(
        ordered(functools.partial(state_kernel, len(keys), heads, dh), len(after), 0),
        grid=(1,),
        out_shape=[
            jax.ShapeDtypeStruct((heads, rows, feat), bf16),
            jax.ShapeDtypeStruct((height, feat), f32),
            jax.ShapeDtypeStruct((height, feat), bf16),
        ],
        in_specs=waits(after)
        + [
            pl.BlockSpec(memory_space=pltpu.SMEM),
            pl.BlockSpec((heads, 2 * dh, feat), lambda _: (part, 0, 0)),
        ]
        + specs,
        out_specs=[full(heads, rows, feat), full(height, feat), full(height, feat)],
        compiler_params=params(),
        cost_estimate=busy(0),
        name="block_state",
    )(*after, where, maps, *arrays)


def chain_values(levels, where_ref, refs):
    mine, beside = refs[0][...], refs[1][...].astype(f32)
    got = [ref[...].astype(f32) for ref in refs[2:]]
    if len(got) < levels:
        total = mine + beside
        for value in got:
            total = total + value
        return [total]
    odd = where_ref[1] == 1
    prior = jnp.zeros_like(mine)
    for level, value in enumerate(got):
        prior = prior + jnp.where(where_ref[2 + level] == 1, value, 0.0)
    return [prior + jnp.where(odd, 0.0, mine), prior + jnp.where(odd, beside, 0.0)]


def round_kernel(levels, counts, where_ref, *refs):
    ins, outs = list(refs[: sum(counts)]), list(refs[sum(counts) :])
    for count in counts:
        for value in chain_values(levels, where_ref, ins[:count]):
            outs.pop(0)[...] = value.astype(bf16)
        del ins[:count]


def round_step(where, levels, chains, after):
    counts = [len(chain) for chain in chains]
    results = [2 if count == levels + 2 else 1 for count in counts]
    values = [value for chain in chains for value in chain]
    shape = values[0].shape
    outs = list(pl.pallas_call(
        ordered(functools.partial(round_kernel, levels, counts), len(after), 0),
        grid=(1,),
        out_shape=[jax.ShapeDtypeStruct(shape, bf16)] * sum(results),
        in_specs=waits(after)
        + [pl.BlockSpec(memory_space=pltpu.SMEM)]
        + [full(*shape)] * len(values),
        out_specs=[full(*shape)] * sum(results),
        compiler_params=params(),
        cost_estimate=busy(0),
        name="round_step",
    )(*after, where, *values))
    return [[outs.pop(0) for _ in range(result)] for result in results]


def local_kernel(partners, heads, dh, where_ref, maps_ref, feats_ref, *refs):
    q_refs, v_refs = refs[:partners], refs[partners : 2 * partners]
    query_feats_ref, local_ref = refs[2 * partners :]
    piece = q_refs[0].shape[2]
    rows = partners * piece
    me = where_ref[0]

    def places(shape, dim):
        ids = lax.broadcasted_iota(jnp.int32, shape, dim)
        result = ids + (me ^ 0) * piece
        for k in range(1, partners):
            result = jnp.where(ids >= k * piece, ids + ((me ^ k) - k) * piece, result)
        return result

    causal = places((rows, 1), 0) >= places((1, rows), 1)
    ones = jnp.ones((rows, dh), bf16)
    for i in range(heads):
        cut = slice(i * dh, (i + 1) * dh)
        queries, values = joined(q_refs, cut), joined(v_refs, cut)
        query_feats = features(queries, maps_ref[i])
        query_feats_ref[i] = query_feats
        scores = lax.dot_general(
            query_feats, feats_ref[i], (((1,), (1,)), ((), ())), preferred_element_type=f32
        )
        weights = jnp.where(causal, scores, 0.0).astype(bf16)
        local_ref[i] = jnp.dot(
            weights, jnp.concatenate([values, ones], axis=1), preferred_element_type=f32
        )


def attend_local(where, maps, feats, queries, values, part, heads, dh, piece, after):
    partners = len(queries)
    feat = maps.shape[-1]
    rows = partners * piece
    arrays, specs = operands(queries + values, piece, heads * dh)
    return pl.pallas_call(
        ordered(functools.partial(local_kernel, partners, heads, dh), len(after), 0),
        grid=(1,),
        out_shape=[
            jax.ShapeDtypeStruct((heads, rows, feat), bf16),
            jax.ShapeDtypeStruct((heads, rows, 2 * dh), f32),
        ],
        in_specs=waits(after)
        + [
            pl.BlockSpec(memory_space=pltpu.SMEM),
            pl.BlockSpec((heads, 2 * dh, feat), lambda _: (part, 0, 0)),
            full(*feats.shape),
        ]
        + specs,
        out_specs=[full(heads, rows, feat), full(heads, rows, 2 * dh)],
        compiler_params=params(),
        cost_estimate=busy(LOCAL_US),
        name="attend_local",
    )(*after, where, maps, feats, *arrays)


def prior_kernel(partners, heads, dh, where_ref, query_feats_ref, local_ref, keep_ref, got_ref, *refs):
    stay_ref, leave_ref = refs
    piece = query_feats_ref.shape[1] // partners
    half = heads // 2
    low = where_ref[1] == 0
    for i in range(heads):
        j = i % half
        state, total = slice(j * dh, (j + 1) * dh), slice(half * dh, half * dh + ROW_TILE)
        own = low if i < half else jnp.logical_not(low)
        prior = jnp.where(own, keep_ref[state, :], got_ref[state, :])
        tail = jnp.where(own, keep_ref[total, :], got_ref[total, :])
        tail = jnp.broadcast_to(tail[j : j + 1, :], prior.shape)
        both = local_ref[i] + lax.dot_general(
            query_feats_ref[i],
            jnp.concatenate([prior, tail], axis=0),
            (((1,), (1,)), ((), ())),
            preferred_element_type=f32,
        )
        attended = (both[:, :dh] / both[:, dh:]).astype(bf16)
        for k in range(partners):
            out = leave_ref if k & 1 else stay_ref
            out[k // 2, :, i * dh : (i + 1) * dh] = attended[k * piece : (k + 1) * piece]


def attend_prior(where, query_feats, local, keep, got, partners, dh, after):
    heads, rows, feat = query_feats.shape
    out = jax.ShapeDtypeStruct((partners // 2, rows // partners, heads * dh), bf16)
    return pl.pallas_call(
        ordered(functools.partial(prior_kernel, partners, heads, dh), len(after), 0),
        grid=(1,),
        out_shape=[out, out],
        in_specs=waits(after)
        + [pl.BlockSpec(memory_space=pltpu.SMEM)]
        + [full(*value.shape) for value in (query_feats, local, keep, got)],
        out_specs=[full(*out.shape)] * 2,
        compiler_params=params(),
        cost_estimate=busy(0),
        name="attend_prior",
    )(*after, where, query_feats, local, keep, got)


def project_kernel(parts, *refs):
    own_refs, other_refs = refs[:parts], refs[parts : 2 * parts]
    own_w, other_w, stay_ref, *leave_refs = refs[2 * parts :]
    groups, piece, width = own_refs[0].shape
    acc = None
    for lhs_refs, w_ref in ((own_refs, own_w), (other_refs, other_w)):
        for p, ref in enumerate(lhs_refs):
            lhs = ref[...].reshape(groups * piece, width)
            term = jnp.dot(
                lhs, w_ref[p * width : (p + 1) * width, :], preferred_element_type=f32
            )
            acc = term if acc is None else acc + term
    stay_ref[...] = acc[:piece]
    for g, ref in enumerate(leave_refs):
        ref[...] = acc[(g + 1) * piece : (g + 2) * piece].astype(bf16)


def project(own, other, own_w, other_w, slabs, slab, after):
    parts, (groups, piece, width) = len(own), own[0].shape
    depth, cols = own_w.shape
    cols = cols // slabs
    tile = math.gcd(cols, 512)
    first = slab * (cols // tile)
    lhs = pl.BlockSpec((groups, piece, width), lambda n: (0, 0, 0))
    weight = pl.BlockSpec((depth, tile), lambda n: (0, first + n))
    out = pl.BlockSpec((piece, tile), lambda n: (0, n))
    return pl.pallas_call(
        ordered(functools.partial(project_kernel, parts), len(after), 0),
        grid=(cols // tile,),
        out_shape=[jax.ShapeDtypeStruct((piece, cols), f32)]
        + [jax.ShapeDtypeStruct((piece, cols), bf16)] * (groups - 1),
        in_specs=waits(after) + [lhs] * (2 * parts) + [weight, weight],
        out_specs=[out] * groups,
        compiler_params=params(),
        cost_estimate=busy(0),
        name="project",
    )(*after, *own, *other, own_w, other_w)


def body(qkv_tokens, sign_bits, out_weight):
    partners, blocks = lax.axis_size("head"), lax.axis_size("seq")
    me, index = lax.axis_index("head"), lax.axis_index("seq")
    seqs = qkv_tokens.shape[0]
    all_heads, dh = sign_bits.shape[0], sign_bits.shape[-1]
    parts = CHUNKS
    heads = all_heads // parts
    levels = blocks.bit_length() - 2
    x = qkv_tokens.transpose(0, 2, 1, 3)
    piece = x.shape[2]
    where = jnp.stack([me] + [(index >> l) & 1 for l in range(levels + 1)]).astype(jnp.int32)
    work = [(s, c) for s in range(seqs) for c in range(parts)]

    messages = [(s, c, (1, 2), parts) for s, c in work] + [(s, 0, (0,), 1) for s in range(seqs)]
    wanted = [
        ([(s, k), (s, k + 1)], kinds, c, cuts)
        for s, c, kinds, cuts in messages
        for k in range(2, partners, 2)
    ]
    beside = [([(s, k) for s in range(seqs)], (0, 1, 2), 0, 1) for k in (0, 1)]
    outer = partners // 2 - 1
    packed = pack(where, x, partners, wanted[:outer]) if outer else []
    *rest, own_rows, near = pack(where, x, partners, wanted[outer:] + beside)
    packed = [*packed, *rest]
    near = swap(near, "head", 1)
    far = []
    for n in range(len(messages)):
        for t in range(outer):
            got_far = swap(packed[n * outer + t], "head", 2 * (t + 1))
            far.append((got_far, swap(got_far[1:], "head", 1)))

    def pieces(n, kind):
        s, c = work[n]
        message, at, col = (len(work) + s, 0, c) if kind == 0 else (n, kind - 1, 0)
        found = [(own_rows, s, kind, c), (near, s, kind, c)]
        for t in range(outer):
            direct, forwarded = far[message * outer + t]
            found += [(direct, 0, at, col), (forwarded, 0, at, col)]
        return found

    late_weight, _ = lax.optimization_barrier((out_weight, packed))
    other_weight = swap(late_weight, "head", 1)
    maps = integer_maps(sign_bits)

    last = []

    def state(n):
        feats[n], mine, theirs = block_state(
            where, maps, pieces(n, 1), pieces(n, 2), work[n][1], heads, dh, piece, last
        )
        chains[n] = [mine, swap(theirs, "seq", 1)]
        last[:] = [mine]

    def step():
        moving = [n for n in chains if n not in ends]
        for n, outs in zip(moving, round_step(where, levels, [chains[n] for n in moving], last)):
            last[:] = [outs[0]]
            if len(outs) == 2:
                ends[n] = (outs[1], swap(outs[0], "seq", 1))
            else:
                chains[n] = chains[n] + [swap(outs[0], "seq", 2 ** (len(chains[n]) - 1))]

    def local(n):
        locals_[n] = attend_local(
            where, maps, feats[n], pieces(n, 0), pieces(n, 2), work[n][1], heads, dh, piece, last
        )
        last[:] = [locals_[n][0]]

    def attend(n):
        stay, leave = attend_prior(where, *locals_[n], *ends[n], partners, dh, last)
        own.setdefault(work[n][0], []).append(stay)
        other.setdefault(work[n][0], []).append(swap(leave, "head", 1))
        last[:] = [stay]

    def multiply(s, slab):
        if s == seqs - 1:
            last.extend(share for early_s in range(s) for share in totals[early_s, slab][1])
        total, *shares = project(own[s], other[s], out_weight, other_weight, SLABS, slab, last)
        totals[s, slab] = total, [swap(v, "head", 2 * (g + 1)) for g, v in enumerate(shares)]
        last[:] = [total]

    feats, chains, ends, locals_, own, other, totals = {}, {}, {}, {}, {}, {}, {}
    early, late = [[n for n, (s, _) in enumerate(work) if (s == seqs - 1) == end] for end in (False, True)]
    state(0)
    for n in range(1, len(work)):
        step()
        state(n)
    step()
    for n in early:
        local(n)
    while len(ends) < len(work):
        step()
        if len(ends) == len(work) - 1:
            for n in early:
                attend(n)
            for n in late:
                local(n)
    for s in range(seqs - 1):
        multiply(s, 0)
    for n in late:
        attend(n)
    for s in range(seqs - 1):
        for slab in range(1, SLABS):
            multiply(s, slab)
    for slab in range(SLABS):
        multiply(seqs - 1, slab)

    def finished(s, slab):
        total, shares = totals[s, slab]
        for share in shares:
            total = total + share.astype(f32)
        return total.astype(bf16)

    return jnp.stack(
        [jnp.concatenate([finished(s, n) for n in range(SLABS)], axis=1) for s in range(seqs)]
    )


def solution(mesh):
    return jax.shard_map(
        body,
        mesh=mesh,
        in_specs=(
            P(None, ("seq", "head"), None, None),
            P("head", None, None, None),
            P("head", None),
        ),
        out_specs=P(None, ("seq", "head"), None),
        check_vma=False,
    )
```

```python
import functools
import math

import jax
import jax.numpy as jnp
import numpy as np
from jax import lax
from jax.experimental import pallas as pl
from jax.experimental.pallas import tpu as pltpu
from jax.sharding import PartitionSpec as P

logit_divisor = 1.3
norm_epsilon = 1e-06
CHUNKS = 2

SLABS = (4, 3, 1)
PACK_STEPS = 4

bf16, f32 = jnp.bfloat16, jnp.float32
ROW_TILE = 16


def params(mebibytes=20):
    return pltpu.CompilerParams(vmem_limit_bytes=mebibytes * 1024 * 1024)


def full(*shape):
    return pl.BlockSpec(shape, lambda *_: (0,) * len(shape))


def ordered(kernel, count, skip):
    return lambda *refs: kernel(*refs[:skip], *refs[skip + count :])


def busy(microseconds):
    return pl.CostEstimate(flops=int(microseconds * 1e9), bytes_accessed=0, transcendentals=0)


def waits(after):
    return [pl.BlockSpec(memory_space=pl.ANY)] * len(after)


def swap(value, axis, bit):
    return lax.ppermute(value, axis, [(j, j ^ bit) for j in range(lax.axis_size(axis))])


def sign_matrix(order):
    ids = np.arange(order)
    common = ids[:, None] & ids[None, :]
    parity = np.zeros_like(common)
    while common.any():
        parity ^= common & 1
        common = common >> 1
    return (1 - 2 * parity).astype(np.float32)


def integer_maps(sign_bits):
    heads, blocks, _, dh = sign_bits.shape
    had = jnp.asarray(sign_matrix(dh), bf16)
    signed = (2 * sign_bits - 1).astype(bf16)
    inner = jnp.einsum("hbij,jk->hbik", had * signed[:, :, 1, None, :], had, preferred_element_type=f32)
    outer = inner.astype(bf16) * signed[:, :, 2, None, :]
    whole = jnp.einsum("hbij,jk->hbik", outer, had, preferred_element_type=f32)
    whole = whole * signed[:, :, 0, :, None].astype(f32)
    whole = whole.transpose(0, 2, 1, 3).reshape(heads, dh, blocks * dh)
    near = lax.reduce_precision(whole, 8, 7)
    return jnp.concatenate([near, whole - near], axis=1).astype(bf16)


def features(rows, maps):
    dh = rows.shape[-1]
    wide = rows.astype(f32)
    mean = jnp.sum(wide * wide, axis=-1, keepdims=True) * (1.0 / dh)
    scale = lax.rsqrt(mean + norm_epsilon) * (logit_divisor / dh**0.25 / dh)
    twice = jnp.concatenate([rows, rows], axis=1)
    return jnp.exp(jnp.dot(twice, maps, preferred_element_type=f32) * scale).astype(bf16)


def pack_kernel(places, where_ref, *refs):
    for ref, (out, index) in zip(refs, places):
        refs[len(places) + out][index] = ref[0, 0]


def pack(where, partners, wanted, shape, mebibytes):
    rows, cols = shape
    arrays, ins, outs, places, shapes = [], [], [], [], []
    for out, (lead, kinds, part, parts) in enumerate(wanted):
        width = cols // parts
        shapes.append((len(lead), len(kinds), rows, width))
        outs.append(
            pl.BlockSpec((*shapes[-1][:3], width // PACK_STEPS), lambda n, where: (0, 0, 0, n))
        )
        for i, (array, first, k) in enumerate(lead):
            for j, kind in enumerate(kinds):

                def at(n, where, first=first, kind=kind, k=k, part=part, parts=parts):
                    group = 0 if k is None else where[0] ^ k
                    return (first, kind, 0, (group * parts + part) * PACK_STEPS + n)

                places.append((out, (i, j)))
                arrays.append(array)
                ins.append(pl.BlockSpec((1, 1, rows, width // PACK_STEPS), at))
    return pl.pallas_call(
        functools.partial(pack_kernel, places),
        out_shape=[jax.ShapeDtypeStruct(shape, bf16) for shape in shapes],
        grid_spec=pltpu.PrefetchScalarGridSpec(
            num_scalar_prefetch=1, grid=(PACK_STEPS,), in_specs=ins, out_specs=outs
        ),
        compiler_params=params(mebibytes),
        cost_estimate=busy(0),
        name="pack",
    )(where, *arrays)


def copy_kernel(in_ref, out_ref):
    out_ref[...] = in_ref[...]


def second_half(value, after):
    shape = (1, *value.shape[1:])
    return pl.pallas_call(
        ordered(copy_kernel, len(after), 0),
        grid=(1,),
        out_shape=jax.ShapeDtypeStruct(shape, value.dtype),
        in_specs=waits(after) + [pl.BlockSpec(shape, lambda _: (1, 0, 0, 0))],
        out_specs=full(*shape),
        compiler_params=params(),
        cost_estimate=busy(0),
        name="second_half",
    )(*after, value)


def operands(pieces, rows, width):
    specs = []
    for _, lead, kind, col in pieces:
        if callable(col):
            at = lambda _, where, lead=lead, kind=kind, col=col: (lead, kind, 0, col(where))
        else:
            at = lambda _, where, at=(lead, kind, 0, col): at
        specs.append(pl.BlockSpec((1, 1, rows, width), at))
    return [piece[0] for piece in pieces], specs


def joined(refs, cut):
    return jnp.concatenate([ref[0, 0, :, cut] for ref in refs], axis=0)


def state_kernel(partners, heads, dh, where_ref, maps_ref, *refs):
    k_refs, v_refs = refs[:partners], refs[partners : 2 * partners]
    feats_ref, mine_ref, theirs_ref = refs[2 * partners :]
    half = heads // 2
    states, totals = [], []
    for i in range(heads):
        cut = slice(i * dh, (i + 1) * dh)
        keys, values = joined(k_refs, cut), joined(v_refs, cut)
        feats = features(keys, maps_ref[i])
        feats_ref[i] = feats
        states.append(
            lax.dot_general(values, feats, (((0,), (0,)), ((), ())), preferred_element_type=f32)
        )
        totals.append(jnp.sum(feats.astype(f32), axis=0, keepdims=True))
    low = where_ref[1] == 0
    pad = jnp.zeros((ROW_TILE - half, feats_ref.shape[-1]), f32)
    for j in range(half):
        rows = slice(j * dh, (j + 1) * dh)
        mine_ref[rows, :] = jnp.where(low, states[j], states[half + j])
        theirs_ref[rows, :] = jnp.where(low, states[half + j], states[j]).astype(bf16)
    lows = jnp.concatenate(totals[:half] + [pad], axis=0)
    highs = jnp.concatenate(totals[half:] + [pad], axis=0)
    mine_ref[half * dh :, :] = jnp.where(low, lows, highs)
    theirs_ref[half * dh :, :] = jnp.where(low, highs, lows).astype(bf16)


def block_state(where, maps, keys, values, part, heads, dh, piece, after):
    feat = maps.shape[-1]
    rows = len(keys) * piece
    height = heads // 2 * dh + ROW_TILE
    arrays, specs = operands(keys + values, piece, heads * dh)
    return pl.pallas_call(
        ordered(functools.partial(state_kernel, len(keys), heads, dh), len(after), 1),
        out_shape=[
            jax.ShapeDtypeStruct((heads, rows, feat), bf16),
            jax.ShapeDtypeStruct((height, feat), f32),
            jax.ShapeDtypeStruct((height, feat), bf16),
        ],
        grid_spec=pltpu.PrefetchScalarGridSpec(
            num_scalar_prefetch=1,
            grid=(1,),
            in_specs=waits(after)
            + [
                pl.BlockSpec((heads, 2 * dh, feat), lambda *_: (part, 0, 0)),
            ]
            + specs,
            out_specs=[full(heads, rows, feat), full(height, feat), full(height, feat)],
        ),
        compiler_params=params(),
        cost_estimate=busy(0),
        name="block_state",
    )(where, *after, maps, *arrays)


def chain_values(levels, where_ref, refs):
    mine, beside = refs[0][...], refs[1][...].astype(f32)
    got = [ref[...].astype(f32) for ref in refs[2:]]
    if len(got) < levels:
        total = mine + beside
        for value in got:
            total = total + value
        return [total]
    odd = where_ref[1] == 1
    prior = jnp.zeros_like(mine)
    for level, value in enumerate(got):
        prior = prior + jnp.where(where_ref[2 + level] == 1, value, 0.0)
    return [prior + jnp.where(odd, 0.0, mine), prior + jnp.where(odd, beside, 0.0)]


def round_kernel(levels, counts, where_ref, *refs):
    ins, outs = list(refs[: sum(counts)]), list(refs[sum(counts) :])
    for count in counts:
        for value in chain_values(levels, where_ref, ins[:count]):
            outs.pop(0)[...] = value.astype(bf16)
        del ins[:count]


def round_step(where, levels, chains, after):
    counts = [len(chain) for chain in chains]
    results = [2 if count == levels + 2 else 1 for count in counts]
    values = [value for chain in chains for value in chain]
    shape = values[0].shape
    outs = list(pl.pallas_call(
        ordered(functools.partial(round_kernel, levels, counts), len(after), 0),
        grid=(1,),
        out_shape=[jax.ShapeDtypeStruct(shape, bf16)] * sum(results),
        in_specs=waits(after)
        + [pl.BlockSpec(memory_space=pltpu.SMEM)]
        + [full(*shape)] * len(values),
        out_specs=[full(*shape)] * sum(results),
        compiler_params=params(),
        cost_estimate=busy(0),
        name="round_step",
    )(*after, where, *values))
    return [[outs.pop(0) for _ in range(result)] for result in results]


def local_kernel(partners, heads, dh, where_ref, maps_ref, feats_ref, *refs):
    q_refs, v_refs = refs[:partners], refs[partners : 2 * partners]
    query_feats_ref, local_ref = refs[2 * partners :]
    piece = q_refs[0].shape[2]
    rows = partners * piece
    me = where_ref[0]

    def places(shape, dim):
        ids = lax.broadcasted_iota(jnp.int32, shape, dim)
        result = ids + (me ^ 0) * piece
        for k in range(1, partners):
            result = jnp.where(ids >= k * piece, ids + ((me ^ k) - k) * piece, result)
        return result

    causal = places((rows, 1), 0) >= places((1, rows), 1)
    ones = jnp.ones((rows, dh), bf16)
    for i in range(heads):
        cut = slice(i * dh, (i + 1) * dh)
        queries, values = joined(q_refs, cut), joined(v_refs, cut)
        query_feats = features(queries, maps_ref[i])
        query_feats_ref[i] = query_feats
        scores = lax.dot_general(
            query_feats, feats_ref[i], (((1,), (1,)), ((), ())), preferred_element_type=f32
        )
        weights = jnp.where(causal, scores, 0.0).astype(bf16)
        local_ref[i] = jnp.dot(
            weights, jnp.concatenate([values, ones], axis=1), preferred_element_type=f32
        )


def attend_local(where, maps, feats, queries, values, part, heads, dh, piece, after):
    partners = len(queries)
    feat = maps.shape[-1]
    rows = partners * piece
    arrays, specs = operands(queries + values, piece, heads * dh)
    return pl.pallas_call(
        ordered(functools.partial(local_kernel, partners, heads, dh), len(after), 1),
        out_shape=[
            jax.ShapeDtypeStruct((heads, rows, feat), bf16),
            jax.ShapeDtypeStruct((heads, rows, 2 * dh), f32),
        ],
        grid_spec=pltpu.PrefetchScalarGridSpec(
            num_scalar_prefetch=1,
            grid=(1,),
            in_specs=waits(after)
            + [
                pl.BlockSpec((heads, 2 * dh, feat), lambda *_: (part, 0, 0)),
                full(*feats.shape),
            ]
            + specs,
            out_specs=[full(heads, rows, feat), full(heads, rows, 2 * dh)],
        ),
        compiler_params=params(),
        cost_estimate=busy(0),
        name="attend_local",
    )(where, *after, maps, feats, *arrays)


def prior_kernel(partners, heads, dh, where_ref, query_feats_ref, local_ref, keep_ref, got_ref, *refs):
    stay_ref, leave_ref = refs
    piece = query_feats_ref.shape[1] // partners
    half = heads // 2
    low = where_ref[1] == 0
    for i in range(heads):
        j = i % half
        state, total = slice(j * dh, (j + 1) * dh), slice(half * dh, half * dh + ROW_TILE)
        own = low if i < half else jnp.logical_not(low)
        prior = jnp.where(own, keep_ref[state, :], got_ref[state, :])
        tail = jnp.where(own, keep_ref[total, :], got_ref[total, :])
        tail = jnp.broadcast_to(tail[j : j + 1, :], prior.shape)
        both = local_ref[i] + lax.dot_general(
            query_feats_ref[i],
            jnp.concatenate([prior, tail], axis=0),
            (((1,), (1,)), ((), ())),
            preferred_element_type=f32,
        )
        attended = (both[:, :dh] / both[:, dh:]).astype(bf16)
        for k in range(partners):
            out = leave_ref if k & 1 else stay_ref
            out[k // 2, :, i * dh : (i + 1) * dh] = attended[k * piece : (k + 1) * piece]


def attend_prior(where, query_feats, local, keep, got, partners, dh, after):
    heads, rows, feat = query_feats.shape
    out = jax.ShapeDtypeStruct((partners // 2, rows // partners, heads * dh), bf16)
    return pl.pallas_call(
        ordered(functools.partial(prior_kernel, partners, heads, dh), len(after), 0),
        grid=(1,),
        out_shape=[out, out],
        in_specs=waits(after)
        + [pl.BlockSpec(memory_space=pltpu.SMEM)]
        + [full(*value.shape) for value in (query_feats, local, keep, got)],
        out_specs=[full(*out.shape)] * 2,
        compiler_params=params(),
        cost_estimate=busy(0),
        name="attend_prior",
    )(*after, where, query_feats, local, keep, got)


def project_kernel(parts, *refs):
    own_refs, other_refs = refs[:parts], refs[parts : 2 * parts]
    own_w, other_w, stay_ref, *leave_refs = refs[2 * parts :]
    groups, piece, width = own_refs[0].shape
    acc = None
    for lhs_refs, w_ref in ((own_refs, own_w), (other_refs, other_w)):
        for p, ref in enumerate(lhs_refs):
            lhs = ref[...].reshape(groups * piece, width)
            term = jnp.dot(
                lhs, w_ref[p * width : (p + 1) * width, :], preferred_element_type=f32
            )
            acc = term if acc is None else acc + term
    stay_ref[...] = acc[:piece]
    for g, ref in enumerate(leave_refs):
        ref[...] = acc[(g + 1) * piece : (g + 2) * piece].astype(bf16)


def project(own, other, own_w, other_w, slab, after):
    parts, (groups, piece, width) = len(own), own[0].shape
    depth, cols = own_w.shape
    unit = cols // sum(SLABS)
    tile = math.gcd(unit, 512)
    first, cols = sum(SLABS[:slab]) * unit // tile, SLABS[slab] * unit
    lhs = pl.BlockSpec((groups, piece, width), lambda n: (0, 0, 0))
    weight = pl.BlockSpec((depth, tile), lambda n: (0, first + n))
    out = pl.BlockSpec((piece, tile), lambda n: (0, n))
    return pl.pallas_call(
        ordered(functools.partial(project_kernel, parts), len(after), 0),
        grid=(cols // tile,),
        out_shape=[jax.ShapeDtypeStruct((piece, cols), f32)]
        + [jax.ShapeDtypeStruct((piece, cols), bf16)] * (groups - 1),
        in_specs=waits(after) + [lhs] * (2 * parts) + [weight, weight],
        out_specs=[out] * groups,
        compiler_params=params(),
        cost_estimate=busy(0),
        name="project",
    )(*after, *own, *other, own_w, other_w)


def finish_kernel(counts, *refs):
    refs = list(refs)
    out_ref = refs.pop()
    for s, slabs in enumerate(counts):
        at = 0
        for shares in slabs:
            total = refs.pop(0)[...]
            for _ in range(shares):
                total = total + refs.pop(0)[...].astype(f32)
            width = total.shape[1]
            out_ref[s, :, at : at + width] = total.astype(bf16)
            at += width


def finish(sums, piece):
    counts = [[len(shares) for _, shares in slabs] for slabs in sums]
    values = [value for slabs in sums for total, shares in slabs for value in (total, *shares)]
    out = (len(sums), piece, sum(total.shape[1] for total, _ in sums[0]))
    return pl.pallas_call(
        functools.partial(finish_kernel, counts),
        grid=(1,),
        out_shape=jax.ShapeDtypeStruct(out, bf16),
        in_specs=[full(*value.shape) for value in values],
        out_specs=full(*out),
        compiler_params=params(),
        cost_estimate=busy(0),
        name="finish",
    )(*values)


def nothing(*refs):
    pass


def later_than(value, after):
    anywhere = pl.BlockSpec(memory_space=pl.ANY)
    return pl.pallas_call(
        nothing,
        out_shape=jax.ShapeDtypeStruct(value.shape, value.dtype),
        in_specs=[anywhere] * (1 + len(after)),
        out_specs=anywhere,
        input_output_aliases={0: 0},
        cost_estimate=busy(0),
        name="later_than",
    )(value, *after)


def body(qkv_tokens, sign_bits, out_weight):
    partners, blocks = lax.axis_size("head"), lax.axis_size("seq")
    me, index = lax.axis_index("head"), lax.axis_index("seq")
    seqs = qkv_tokens.shape[0]
    all_heads, dh = sign_bits.shape[0], sign_bits.shape[-1]
    parts = CHUNKS
    heads = all_heads // parts
    levels = blocks.bit_length() - 2
    x = qkv_tokens.transpose(0, 2, 1, 3)
    piece = x.shape[2]
    where = jnp.stack([me] + [(index >> l) & 1 for l in range(levels + 1)]).astype(jnp.int32)
    work = [(s, c) for s in range(seqs) for c in range(parts)]

    messages = [(s, c, (1, 2), parts) for s, c in work if s > 0]
    messages += [(s, 0, (0,), 1) for s in range(seqs)]
    outer, shape = range(2, partners, 2), (piece, x.shape[3] // partners)
    lead = [(x, s, k + 1) for s in range(seqs) for k in range(0, partners, 2)]
    wanted = [([(x, 0, k), (x, 0, k + 1)], (1, 2), 0, 1) for k in outer]
    *first, near = pack(where, partners, wanted + [(lead, (0, 1, 2), 0, 1)], shape, 60)
    first = [swap(value, "head", k) for value, k in zip(first, outer)]
    near = swap(near, "head", 1)
    wanted = [
        ([(x, s, k), (near, s * (partners // 2) + k // 2, None)], kinds, c, cuts)
        for s, c, kinds, cuts in messages
        for k in outer
    ]
    wanted.append(([(x, s, 0) for s in range(seqs)], (0, 1, 2), 0, 1))
    *packed, own_rows = pack(where, partners, wanted, shape, 20)
    hops = [swap(second_half(value, [own_rows]), "head", 1) for value in first]
    later = [swap(value, "head", k) for value, k in zip(packed, list(outer) * len(messages))]

    def pieces(n, kind):
        s, c = work[n]
        found = [(own_rows, s, kind, c), (near, s * (partners // 2), kind, c)]
        for t in range(len(outer)):
            if kind > 0 and s == 0:
                found += [(first[t], 0, kind - 1, c), (hops[t], 0, kind - 1, c)]
            else:
                message = n - parts if kind > 0 else len(work) - parts + s
                both = later[message * len(outer) + t]
                at, col = (kind - 1, 0) if kind > 0 else (0, c)
                found += [(both, 0, at, col), (both, 1, at, col)]
        return found

    maps = integer_maps(sign_bits)

    last = [own_rows]
    feats, chains, ends, locals_, own, other, totals = {}, {}, {}, {}, {}, {}, {}

    def state(n):
        feats[n], mine, theirs = block_state(
            where, maps, pieces(n, 1), pieces(n, 2), work[n][1], heads, dh, piece, last
        )
        chains[n] = [mine, swap(theirs, "seq", 1)]
        last[:] = [mine]

    def step(n):
        (outs,) = round_step(where, levels, [chains[n]], last)
        last[:] = [outs[0]]
        if len(outs) == 2:
            ends[n] = (outs[1], swap(outs[0], "seq", 1))
        else:
            chains[n] = chains[n] + [swap(outs[0], "seq", 2 ** (len(chains[n]) - 1))]

    def local(n):
        locals_[n] = attend_local(
            where, maps, feats[n], pieces(n, 0), pieces(n, 2), work[n][1], heads, dh, piece, last
        )
        last[:] = [locals_[n][0]]

    def attend(n):
        stay, leave = attend_prior(where, *locals_[n], *ends[n], partners, dh, last)
        own.setdefault(work[n][0], []).append(stay)
        other.setdefault(work[n][0], []).append(swap(leave, "head", 1))
        last[:] = [stay]

    def multiply(s, slab):
        if s > 0:
            last.extend(totals[s - 1, slab][1])
        total, *shares = project(own[s], other[s], out_weight, other_weight, slab, last)
        totals[s, slab] = total, [swap(v, "head", 2 * (g + 1)) for g, v in enumerate(shares)]
        last[:] = [total]

    every = 2.4 / parts
    plan = []
    for n, (s, c) in enumerate(work):
        came = every * (n - parts + 1) if s > 0 else 0.3 * c
        asked = every * (len(work) - parts + 1) + 1.2 * s
        end = came + 1.1 * (levels + 1) + 1
        plan.append((came, state, n))
        plan += [(came + 1 + 1.1 * j, step, n) for j in range(levels + 1)]
        plan.append((max(asked, end - 1), local, n))
        plan.append((max(asked, end) + 0.1, attend, n))
        if c == parts - 1:
            plan += [(max(asked, end) + 0.6 + 0.8 * j, multiply, s, j) for j in range(len(SLABS))]
    plan = sorted(plan, key=lambda entry: entry[0])
    state(0)
    other_weight = swap(later_than(out_weight, last), "head", 1)
    for _, act, *which in plan:
        if (act, which) != (state, [0]):
            act(*which)

    return finish([[totals[s, n] for n in range(len(SLABS))] for s in range(seqs)], piece)


def solution(mesh):
    return jax.shard_map(
        body,
        mesh=mesh,
        in_specs=(
            P(None, ("seq", "head"), None, None),
            P("head", None, None, None),
            P("head", None),
        ),
        out_specs=P(None, ("seq", "head"), None),
        check_vma=False,
    )
```

```python
import functools
import math

import jax
import jax.numpy as jnp
import numpy as np
from jax import lax
from jax.experimental import pallas as pl
from jax.experimental.pallas import tpu as pltpu
from jax.sharding import PartitionSpec as P

logit_divisor = 1.3
norm_epsilon = 1e-06
CHUNKS = 1

SLABS = (4, 4), (4, 3, 1)

bf16, f32 = jnp.bfloat16, jnp.float32
ROW_TILE = 16


def params(mebibytes=20):
    return pltpu.CompilerParams(vmem_limit_bytes=mebibytes * 1024 * 1024)


def full(*shape):
    return pl.BlockSpec(shape, lambda *_: (0,) * len(shape))


def ordered(kernel, count, skip):
    return lambda *refs: kernel(*refs[:skip], *refs[skip + count :])


def busy(microseconds):
    return pl.CostEstimate(flops=int(microseconds * 1e9), bytes_accessed=0, transcendentals=0)


def waits(after):
    return [pl.BlockSpec(memory_space=pl.ANY)] * len(after)


def swap(value, axis, bit):
    return lax.ppermute(value, axis, [(j, j ^ bit) for j in range(lax.axis_size(axis))])


def sign_matrix(order):
    ids = np.arange(order)
    common = ids[:, None] & ids[None, :]
    parity = np.zeros_like(common)
    while common.any():
        parity ^= common & 1
        common = common >> 1
    return (1 - 2 * parity).astype(np.float32)


def integer_maps(sign_bits):
    heads, blocks, _, dh = sign_bits.shape
    had = jnp.asarray(sign_matrix(dh), bf16)
    signed = (2 * sign_bits - 1).astype(bf16)
    inner = jnp.einsum("hbij,jk->hbik", had * signed[:, :, 1, None, :], had, preferred_element_type=f32)
    outer = inner.astype(bf16) * signed[:, :, 2, None, :]
    whole = jnp.einsum("hbij,jk->hbik", outer, had, preferred_element_type=f32)
    whole = whole * signed[:, :, 0, :, None].astype(f32)
    whole = whole.transpose(0, 2, 1, 3).reshape(heads, dh, blocks * dh)
    near = lax.reduce_precision(whole, 8, 7)
    return jnp.concatenate([near, whole - near], axis=1).astype(bf16)


def features(rows, maps):
    dh = rows.shape[-1]
    wide = rows.astype(f32)
    mean = jnp.sum(wide * wide, axis=-1, keepdims=True) * (1.0 / dh)
    scale = lax.rsqrt(mean + norm_epsilon) * (logit_divisor / dh**0.25 / dh)
    twice = jnp.concatenate([rows, rows], axis=1)
    return jnp.exp(jnp.dot(twice, maps, preferred_element_type=f32) * scale).astype(bf16)


def pack_kernel(places, arrays, where_ref, *refs):
    ins, outs, sems = refs[:arrays], refs[arrays:-1], refs[-1]
    copies = []
    for n, (which, first, kind, k, part, parts, out, index) in enumerate(places):
        width = outs[out].shape[-1]
        group = 0 if k is None else where_ref[0] ^ k
        start = pl.multiple_of((group * parts + part) * width, width)
        source = ins[which].at[first, kind, :, pl.ds(start, width)]
        copies.append(pltpu.make_async_copy(source, outs[out].at[index], sems.at[n]))
    for copy in copies:
        copy.start()
    for copy in copies:
        copy.wait()


def pack(where, partners, wanted, shape, mebibytes):
    rows, cols = shape
    arrays, places, shapes = [], [], []
    for out, (lead, kinds, part, parts) in enumerate(wanted):
        shapes.append((len(lead), len(kinds), rows, cols // parts))
        for i, (array, first, k) in enumerate(lead):
            if not any(array is known for known in arrays):
                arrays.append(array)
            which = [array is known for known in arrays].index(True)
            for j, kind in enumerate(kinds):
                places.append((which, first, kind, k, part, parts, out, (i, j)))
    return pl.pallas_call(
        functools.partial(pack_kernel, places, len(arrays)),
        out_shape=[jax.ShapeDtypeStruct(shape, bf16) for shape in shapes],
        in_specs=[pl.BlockSpec(memory_space=pltpu.SMEM)]
        + [pl.BlockSpec(memory_space=pl.ANY)] * len(arrays),
        out_specs=[pl.BlockSpec(memory_space=pltpu.VMEM)] * len(shapes),
        scratch_shapes=[pltpu.SemaphoreType.DMA((len(places),))],
        compiler_params=params(mebibytes),
        cost_estimate=busy(0),
        name="pack",
    )(where, *arrays)


def copy_kernel(in_ref, out_ref):
    out_ref[...] = in_ref[...]


def second_half(value, after):
    shape = (1, *value.shape[1:])
    return pl.pallas_call(
        ordered(copy_kernel, len(after), 0),
        grid=(1,),
        out_shape=jax.ShapeDtypeStruct(shape, value.dtype),
        in_specs=waits(after) + [pl.BlockSpec(shape, lambda _: (1, 0, 0, 0))],
        out_specs=full(*shape),
        compiler_params=params(),
        cost_estimate=busy(0),
        name="second_half",
    )(*after, value)


def operands(pieces, rows, width):
    specs = []
    for _, lead, kind, col in pieces:
        if callable(col):
            at = lambda _, where, lead=lead, kind=kind, col=col: (lead, kind, 0, col(where))
        else:
            at = lambda _, where, at=(lead, kind, 0, col): at
        specs.append(pl.BlockSpec((1, 1, rows, width), at))
    return [piece[0] for piece in pieces], specs


def joined(refs, cut):
    return jnp.concatenate([ref[0, 0, :, cut] for ref in refs], axis=0)


def state_kernel(partners, heads, dh, where_ref, maps_ref, *refs):
    k_refs, v_refs = refs[:partners], refs[partners : 2 * partners]
    feats_ref, mine_ref, theirs_ref = refs[2 * partners :]
    half = heads // 2
    states, totals = [], []
    for i in range(heads):
        cut = slice(i * dh, (i + 1) * dh)
        keys, values = joined(k_refs, cut), joined(v_refs, cut)
        feats = features(keys, maps_ref[i])
        feats_ref[i] = feats
        states.append(
            lax.dot_general(values, feats, (((0,), (0,)), ((), ())), preferred_element_type=f32)
        )
        totals.append(jnp.sum(feats.astype(f32), axis=0, keepdims=True))
    low = where_ref[1] == 0
    pad = jnp.zeros((ROW_TILE - half, feats_ref.shape[-1]), f32)
    for j in range(half):
        rows = slice(j * dh, (j + 1) * dh)
        mine_ref[rows, :] = jnp.where(low, states[j], states[half + j])
        theirs_ref[rows, :] = jnp.where(low, states[half + j], states[j]).astype(bf16)
    lows = jnp.concatenate(totals[:half] + [pad], axis=0)
    highs = jnp.concatenate(totals[half:] + [pad], axis=0)
    mine_ref[half * dh :, :] = jnp.where(low, lows, highs)
    theirs_ref[half * dh :, :] = jnp.where(low, highs, lows).astype(bf16)


def block_state(where, maps, keys, values, part, heads, dh, piece, after):
    feat = maps.shape[-1]
    rows = len(keys) * piece
    height = heads // 2 * dh + ROW_TILE
    arrays, specs = operands(keys + values, piece, heads * dh)
    return pl.pallas_call(
        ordered(functools.partial(state_kernel, len(keys), heads, dh), len(after), 1),
        out_shape=[
            jax.ShapeDtypeStruct((heads, rows, feat), bf16),
            jax.ShapeDtypeStruct((height, feat), f32),
            jax.ShapeDtypeStruct((height, feat), bf16),
        ],
        grid_spec=pltpu.PrefetchScalarGridSpec(
            num_scalar_prefetch=1,
            grid=(1,),
            in_specs=waits(after)
            + [
                pl.BlockSpec((heads, 2 * dh, feat), lambda *_: (part, 0, 0)),
            ]
            + specs,
            out_specs=[full(heads, rows, feat), full(height, feat), full(height, feat)],
        ),
        compiler_params=params(),
        cost_estimate=busy(0),
        name="block_state",
    )(where, *after, maps, *arrays)


def chain_values(levels, where_ref, refs):
    mine, beside = refs[0][...], refs[1][...].astype(f32)
    got = [ref[...].astype(f32) for ref in refs[2:]]
    if len(got) < levels:
        total = mine + beside
        for value in got:
            total = total + value
        return [total]
    odd = where_ref[1] == 1
    prior = jnp.zeros_like(mine)
    for level, value in enumerate(got):
        prior = prior + jnp.where(where_ref[2 + level] == 1, value, 0.0)
    return [prior + jnp.where(odd, 0.0, mine), prior + jnp.where(odd, beside, 0.0)]


def round_kernel(levels, counts, where_ref, *refs):
    ins, outs = list(refs[: sum(counts)]), list(refs[sum(counts) :])
    for count in counts:
        for value in chain_values(levels, where_ref, ins[:count]):
            outs.pop(0)[...] = value.astype(bf16)
        del ins[:count]


def round_step(where, levels, chains, after):
    counts = [len(chain) for chain in chains]
    results = [2 if count == levels + 2 else 1 for count in counts]
    values = [value for chain in chains for value in chain]
    shape = values[0].shape
    outs = list(pl.pallas_call(
        ordered(functools.partial(round_kernel, levels, counts), len(after), 0),
        grid=(1,),
        out_shape=[jax.ShapeDtypeStruct(shape, bf16)] * sum(results),
        in_specs=waits(after)
        + [pl.BlockSpec(memory_space=pltpu.SMEM)]
        + [full(*shape)] * len(values),
        out_specs=[full(*shape)] * sum(results),
        compiler_params=params(),
        cost_estimate=busy(0),
        name="round_step",
    )(*after, where, *values))
    return [[outs.pop(0) for _ in range(result)] for result in results]


def local_kernel(partners, heads, dh, where_ref, maps_ref, feats_ref, *refs):
    q_refs, v_refs = refs[:partners], refs[partners : 2 * partners]
    query_feats_ref, local_ref = refs[2 * partners :]
    piece = q_refs[0].shape[2]
    rows = partners * piece
    me = where_ref[0]

    def places(shape, dim):
        ids = lax.broadcasted_iota(jnp.int32, shape, dim)
        result = ids + (me ^ 0) * piece
        for k in range(1, partners):
            result = jnp.where(ids >= k * piece, ids + ((me ^ k) - k) * piece, result)
        return result

    causal = places((rows, 1), 0) >= places((1, rows), 1)
    ones = jnp.ones((rows, dh), bf16)
    for i in range(heads):
        cut = slice(i * dh, (i + 1) * dh)
        queries, values = joined(q_refs, cut), joined(v_refs, cut)
        query_feats = features(queries, maps_ref[i])
        query_feats_ref[i] = query_feats
        scores = lax.dot_general(
            query_feats, feats_ref[i], (((1,), (1,)), ((), ())), preferred_element_type=f32
        )
        weights = jnp.where(causal, scores, 0.0).astype(bf16)
        local_ref[i] = jnp.dot(
            weights, jnp.concatenate([values, ones], axis=1), preferred_element_type=f32
        )


def attend_local(where, maps, feats, queries, values, part, heads, dh, piece, after):
    partners = len(queries)
    feat = maps.shape[-1]
    rows = partners * piece
    arrays, specs = operands(queries + values, piece, heads * dh)
    return pl.pallas_call(
        ordered(functools.partial(local_kernel, partners, heads, dh), len(after), 1),
        out_shape=[
            jax.ShapeDtypeStruct((heads, rows, feat), bf16),
            jax.ShapeDtypeStruct((heads, rows, 2 * dh), f32),
        ],
        grid_spec=pltpu.PrefetchScalarGridSpec(
            num_scalar_prefetch=1,
            grid=(1,),
            in_specs=waits(after)
            + [
                pl.BlockSpec((heads, 2 * dh, feat), lambda *_: (part, 0, 0)),
                full(*feats.shape),
            ]
            + specs,
            out_specs=[full(heads, rows, feat), full(heads, rows, 2 * dh)],
        ),
        compiler_params=params(),
        cost_estimate=busy(0),
        name="attend_local",
    )(where, *after, maps, feats, *arrays)


def prior_kernel(partners, heads, dh, where_ref, query_feats_ref, local_ref, keep_ref, got_ref, *refs):
    stay_ref, leave_ref = refs
    piece = query_feats_ref.shape[1] // partners
    half = heads // 2
    low = where_ref[1] == 0
    for i in range(heads):
        j = i % half
        state, total = slice(j * dh, (j + 1) * dh), slice(half * dh, half * dh + ROW_TILE)
        own = low if i < half else jnp.logical_not(low)
        prior = jnp.where(own, keep_ref[state, :], got_ref[state, :])
        tail = jnp.where(own, keep_ref[total, :], got_ref[total, :])
        tail = jnp.broadcast_to(tail[j : j + 1, :], prior.shape)
        both = local_ref[i] + lax.dot_general(
            query_feats_ref[i],
            jnp.concatenate([prior, tail], axis=0),
            (((1,), (1,)), ((), ())),
            preferred_element_type=f32,
        )
        attended = (both[:, :dh] / both[:, dh:]).astype(bf16)
        for k in range(partners):
            out = leave_ref if k & 1 else stay_ref
            out[k // 2, :, i * dh : (i + 1) * dh] = attended[k * piece : (k + 1) * piece]


def attend_prior(where, query_feats, local, keep, got, partners, dh, after):
    heads, rows, feat = query_feats.shape
    out = jax.ShapeDtypeStruct((partners // 2, rows // partners, heads * dh), bf16)
    return pl.pallas_call(
        ordered(functools.partial(prior_kernel, partners, heads, dh), len(after), 0),
        grid=(1,),
        out_shape=[out, out],
        in_specs=waits(after)
        + [pl.BlockSpec(memory_space=pltpu.SMEM)]
        + [full(*value.shape) for value in (query_feats, local, keep, got)],
        out_specs=[full(*out.shape)] * 2,
        compiler_params=params(),
        cost_estimate=busy(0),
        name="attend_prior",
    )(*after, where, query_feats, local, keep, got)


def project_kernel(parts, *refs):
    own_refs, other_refs = refs[:parts], refs[parts : 2 * parts]
    own_w, other_w, stay_ref, *leave_refs = refs[2 * parts :]
    groups, piece, width = own_refs[0].shape
    acc = None
    for lhs_refs, w_ref in ((own_refs, own_w), (other_refs, other_w)):
        for p, ref in enumerate(lhs_refs):
            lhs = ref[...].reshape(groups * piece, width)
            term = jnp.dot(
                lhs, w_ref[p * width : (p + 1) * width, :], preferred_element_type=f32
            )
            acc = term if acc is None else acc + term
    stay_ref[...] = acc[:piece]
    for g, ref in enumerate(leave_refs):
        ref[...] = acc[(g + 1) * piece : (g + 2) * piece].astype(bf16)


def project(own, other, own_w, other_w, slabs, slab, after):
    parts, (groups, piece, width) = len(own), own[0].shape
    depth, cols = own_w.shape
    unit = cols // sum(slabs)
    tile = math.gcd(unit, 512)
    first, cols = sum(slabs[:slab]) * unit // tile, slabs[slab] * unit
    lhs = pl.BlockSpec((groups, piece, width), lambda n: (0, 0, 0))
    weight = pl.BlockSpec((depth, tile), lambda n: (0, first + n))
    out = pl.BlockSpec((piece, tile), lambda n: (0, n))
    return pl.pallas_call(
        ordered(functools.partial(project_kernel, parts), len(after), 0),
        grid=(cols // tile,),
        out_shape=[jax.ShapeDtypeStruct((piece, cols), f32)]
        + [jax.ShapeDtypeStruct((piece, cols), bf16)] * (groups - 1),
        in_specs=waits(after) + [lhs] * (2 * parts) + [weight, weight],
        out_specs=[out] * groups,
        compiler_params=params(),
        cost_estimate=busy(0),
        name="project",
    )(*after, *own, *other, own_w, other_w)


def finish_kernel(counts, *refs):
    refs = list(refs)
    out_ref = refs.pop()
    for s, slabs in enumerate(counts):
        at = 0
        for shares in slabs:
            total = refs.pop(0)[...]
            for _ in range(shares):
                total = total + refs.pop(0)[...].astype(f32)
            width = total.shape[1]
            out_ref[s, :, at : at + width] = total.astype(bf16)
            at += width


def finish(sums, piece):
    counts = [[len(shares) for _, shares in slabs] for slabs in sums]
    values = [value for slabs in sums for total, shares in slabs for value in (total, *shares)]
    out = (len(sums), piece, sum(total.shape[1] for total, _ in sums[0]))
    return pl.pallas_call(
        functools.partial(finish_kernel, counts),
        grid=(1,),
        out_shape=jax.ShapeDtypeStruct(out, bf16),
        in_specs=[full(*value.shape) for value in values],
        out_specs=full(*out),
        compiler_params=params(),
        cost_estimate=busy(0),
        name="finish",
    )(*values)


def nothing(*refs):
    pass


def later_than(value, after):
    anywhere = pl.BlockSpec(memory_space=pl.ANY)
    return pl.pallas_call(
        nothing,
        out_shape=jax.ShapeDtypeStruct(value.shape, value.dtype),
        in_specs=[anywhere] * (1 + len(after)),
        out_specs=anywhere,
        input_output_aliases={0: 0},
        compiler_params=params(1),
        cost_estimate=busy(0),
        name="later_than",
    )(value, *after)


def body(qkv_tokens, sign_bits, out_weight):
    partners, blocks = lax.axis_size("head"), lax.axis_size("seq")
    me, index = lax.axis_index("head"), lax.axis_index("seq")
    seqs = qkv_tokens.shape[0]
    all_heads, dh = sign_bits.shape[0], sign_bits.shape[-1]
    parts = CHUNKS
    heads = all_heads // parts
    levels = blocks.bit_length() - 2
    x = qkv_tokens.transpose(0, 2, 1, 3)
    piece = x.shape[2]
    where = jnp.stack([me] + [(index >> l) & 1 for l in range(levels + 1)]).astype(jnp.int32)
    work = [(s, c) for s in range(seqs) for c in range(parts)]

    messages = [(s, c, (1, 2), parts) for s, c in work if s > 0]
    messages += [(s, 0, (0,), 1) for s in range(seqs)]
    outer, shape = range(2, partners, 2), (piece, x.shape[3] // partners)
    lead = [(x, s, k + 1) for s in range(seqs) for k in range(0, partners, 2)]
    wanted = [([(x, 0, k), (x, 0, k + 1)], (1, 2), 0, 1) for k in outer]
    *first, near = pack(where, partners, wanted + [(lead, (0, 1, 2), 0, 1)], shape, 60)
    first = [swap(value, "head", k) for value, k in zip(first, outer)]
    near = swap(near, "head", 1)
    wanted = [
        ([(x, s, k), (near, s * (partners // 2) + k // 2, None)], kinds, c, cuts)
        for s, c, kinds, cuts in messages
        for k in outer
    ]
    wanted.append(([(x, s, 0) for s in range(seqs)], (0, 1, 2), 0, 1))
    *packed, own_rows = pack(where, partners, wanted, shape, 20)
    hops = [swap(second_half(value, [own_rows]), "head", 1) for value in first]
    later = [swap(value, "head", k) for value, k in zip(packed, list(outer) * len(messages))]

    def pieces(n, kind):
        s, c = work[n]
        found = [(own_rows, s, kind, c), (near, s * (partners // 2), kind, c)]
        for t in range(len(outer)):
            if kind > 0 and s == 0:
                found += [(first[t], 0, kind - 1, c), (hops[t], 0, kind - 1, c)]
            else:
                message = n - parts if kind > 0 else len(work) - parts + s
                both = later[message * len(outer) + t]
                at, col = (kind - 1, 0) if kind > 0 else (0, c)
                found += [(both, 0, at, col), (both, 1, at, col)]
        return found

    maps = integer_maps(sign_bits)

    last = [own_rows]
    feats, chains, ends, locals_, own, other, totals = {}, {}, {}, {}, {}, {}, {}

    def state(n):
        feats[n], mine, theirs = block_state(
            where, maps, pieces(n, 1), pieces(n, 2), work[n][1], heads, dh, piece, last
        )
        chains[n] = [mine, swap(theirs, "seq", 1)]
        last[:] = [mine]

    def step(n):
        (outs,) = round_step(where, levels, [chains[n]], last)
        last[:] = [outs[0]]
        if len(outs) == 2:
            ends[n] = (outs[1], swap(outs[0], "seq", 1))
        else:
            chains[n] = chains[n] + [swap(outs[0], "seq", 2 ** (len(chains[n]) - 1))]

    def local(n):
        locals_[n] = attend_local(
            where, maps, feats[n], pieces(n, 0), pieces(n, 2), work[n][1], heads, dh, piece, last
        )
        last[:] = [locals_[n][0]]

    def attend(n):
        if (work[n][0] - 1, 0) in totals:
            last.extend(totals[work[n][0] - 1, 0][1])
        stay, leave = attend_prior(where, *locals_[n], *ends[n], partners, dh, last)
        own.setdefault(work[n][0], []).append(stay)
        other.setdefault(work[n][0], []).append(swap(leave, "head", 1))
        last[:] = [stay]

    def multiply(s, slab):
        if slab > 0 and (s - 1, slab) in totals:
            last.extend(totals[s - 1, slab][1])
        total, *shares = project(own[s], other[s], out_weight, other_weight, slabs[s], slab, last)
        totals[s, slab] = total, [swap(v, "head", 2 * (g + 1)) for g, v in enumerate(shares)]
        last[:] = [total]

    slabs = [SLABS[0]] * (seqs - 1) + [SLABS[1]]
    plan = []
    for n, (s, c) in enumerate(work):
        came = 15 * s + 8 * c / parts
        last_step = came + 17 + 8.5 * levels
        plan.append((came, state, n))
        plan += [(came + 11 + 8.5 * j, step, n) for j in range(levels)] + [(last_step, step, n)]
        plan.append((max(last_step - 4, 18 * s), local, n))
        plan.append((last_step + 8.5, attend, n))
        if c == parts - 1:
            plan += [(last_step + 13 + 4.5 * j, multiply, s, j) for j in range(len(slabs[s]))]
    plan = sorted(plan, key=lambda entry: entry[0])
    state(0)
    other_weight = swap(later_than(out_weight, last), "head", 1)
    for _, act, *which in plan:
        if (act, which) != (state, [0]):
            act(*which)

    return finish([[totals[s, n] for n in range(len(slabs[s]))] for s in range(seqs)], piece)


def solution(mesh):
    return jax.shard_map(
        body,
        mesh=mesh,
        in_specs=(
            P(None, ("seq", "head"), None, None),
            P("head", None, None, None),
            P("head", None),
        ),
        out_specs=P(None, ("seq", "head"), None),
        check_vma=False,
    )
```

```python
import functools
import math

import jax
import jax.numpy as jnp
import numpy as np
from jax import lax
from jax.experimental import pallas as pl
from jax.experimental.pallas import tpu as pltpu
from jax.sharding import PartitionSpec as P

logit_divisor = 1.3
norm_epsilon = 1e-06
CHUNKS = 1

SLABS = (4, 4), (4, 3, 1)

bf16, f32 = jnp.bfloat16, jnp.float32
ROW_TILE = 16
GROUP = 4


def params(mebibytes=20):
    return pltpu.CompilerParams(vmem_limit_bytes=mebibytes * 1024 * 1024)


def full(*shape):
    return pl.BlockSpec(shape, lambda *_: (0,) * len(shape))


def ordered(kernel, count, skip):
    return lambda *refs: kernel(*refs[:skip], *refs[skip + count :])


def busy(microseconds):
    return pl.CostEstimate(flops=int(microseconds * 1e9), bytes_accessed=0, transcendentals=0)


def waits(after):
    return [pl.BlockSpec(memory_space=pl.ANY)] * len(after)


def swap(value, axis, bit):
    return lax.ppermute(value, axis, [(j, j ^ bit) for j in range(lax.axis_size(axis))])


def sign_matrix(order):
    ids = np.arange(order)
    common = ids[:, None] & ids[None, :]
    parity = np.zeros_like(common)
    while common.any():
        parity ^= common & 1
        common = common >> 1
    return (1 - 2 * parity).astype(np.float32)


def integer_maps(sign_bits):
    heads, blocks, _, dh = sign_bits.shape
    had = jnp.asarray(sign_matrix(dh), bf16)
    signed = (2 * sign_bits - 1).astype(bf16)
    inner = jnp.einsum("hbij,jk->hbik", had * signed[:, :, 1, None, :], had, preferred_element_type=f32)
    outer = inner.astype(bf16) * signed[:, :, 2, None, :]
    whole = jnp.einsum("hbij,jk->hbik", outer, had, preferred_element_type=f32)
    whole = whole * signed[:, :, 0, :, None].astype(f32)
    whole = whole.transpose(0, 2, 1, 3).reshape(heads, dh, blocks * dh)
    near = lax.reduce_precision(whole, 8, 7)
    return jnp.concatenate([near, whole - near], axis=1).astype(bf16)


def features(rows, maps):
    dh = rows.shape[-1]
    wide = rows.astype(f32)
    mean = jnp.sum(wide * wide, axis=-1, keepdims=True) * (1.0 / dh)
    scale = lax.rsqrt(mean + norm_epsilon) * (logit_divisor / dh**0.25 / dh)
    twice = jnp.concatenate([rows, rows], axis=1)
    return jnp.exp(jnp.dot(twice, maps, preferred_element_type=f32) * scale).astype(bf16)


def pack_kernel(places, arrays, where_ref, *refs):
    ins, outs, sems = refs[:arrays], refs[arrays:-1], refs[-1]
    copies = []
    for n, (which, first, kind, k, part, parts, out, index) in enumerate(places):
        width = outs[out].shape[-1]
        group = 0 if k is None else where_ref[0] ^ k
        start = pl.multiple_of((group * parts + part) * width, width)
        source = ins[which].at[first, kind, :, pl.ds(start, width)]
        copies.append(pltpu.make_async_copy(source, outs[out].at[index], sems.at[n]))
    for copy in copies:
        copy.start()
    for copy in copies:
        copy.wait()


def pack(where, partners, wanted, shape, mebibytes):
    rows, cols = shape
    arrays, places, shapes = [], [], []
    for out, (lead, kinds, part, parts) in enumerate(wanted):
        shapes.append((len(lead), len(kinds), rows, cols // parts))
        for i, (array, first, k) in enumerate(lead):
            if not any(array is known for known in arrays):
                arrays.append(array)
            which = [array is known for known in arrays].index(True)
            for j, kind in enumerate(kinds):
                places.append((which, first, kind, k, part, parts, out, (i, j)))
    return pl.pallas_call(
        functools.partial(pack_kernel, places, len(arrays)),
        out_shape=[jax.ShapeDtypeStruct(shape, bf16) for shape in shapes],
        in_specs=[pl.BlockSpec(memory_space=pltpu.SMEM)]
        + [pl.BlockSpec(memory_space=pl.ANY)] * len(arrays),
        out_specs=[pl.BlockSpec(memory_space=pltpu.VMEM)] * len(shapes),
        scratch_shapes=[pltpu.SemaphoreType.DMA((len(places),))],
        compiler_params=params(mebibytes),
        cost_estimate=busy(0),
        name="pack",
    )(where, *arrays)


def copy_kernel(in_ref, out_ref):
    out_ref[...] = in_ref[...]


def second_half(value, after):
    shape = (1, *value.shape[1:])
    return pl.pallas_call(
        ordered(copy_kernel, len(after), 0),
        grid=(1,),
        out_shape=jax.ShapeDtypeStruct(shape, value.dtype),
        in_specs=waits(after) + [pl.BlockSpec(shape, lambda _: (1, 0, 0, 0))],
        out_specs=full(*shape),
        compiler_params=params(),
        cost_estimate=busy(0),
        name="second_half",
    )(*after, value)


def operands(pieces, rows, width):
    specs = []
    for _, lead, kind, col in pieces:
        if callable(col):
            at = lambda _, where, lead=lead, kind=kind, col=col: (lead, kind, 0, col(where))
        else:
            at = lambda _, where, at=(lead, kind, 0, col): at
        specs.append(pl.BlockSpec((1, 1, rows, width), at))
    return [piece[0] for piece in pieces], specs


def joined(refs, cut):
    return jnp.concatenate([ref[0, 0, :, cut] for ref in refs], axis=0)


def state_kernel(partners, heads, dh, where_ref, maps_ref, *refs):
    k_refs, v_refs = refs[:partners], refs[partners : 2 * partners]
    feats_ref, *share_refs = refs[2 * partners :]
    share = heads // GROUP
    states, totals = [], []
    for i in range(heads):
        cut = slice(i * dh, (i + 1) * dh)
        keys, values = joined(k_refs, cut), joined(v_refs, cut)
        feats = features(keys, maps_ref[i])
        feats_ref[i] = feats
        states.append(
            lax.dot_general(values, feats, (((0,), (0,)), ((), ())), preferred_element_type=f32)
        )
        totals.append(jnp.sum(feats.astype(f32), axis=0, keepdims=True))
    pad = jnp.zeros((ROW_TILE - share, feats_ref.shape[-1]), f32)
    shares = [
        jnp.concatenate(
            states[g * share : (g + 1) * share] + totals[g * share : (g + 1) * share] + [pad], axis=0
        )
        for g in range(GROUP)
    ]
    for m, ref in enumerate(share_refs):
        ref[...] = chosen(shares, where_ref[1] ^ m).astype(ref.dtype)


def chosen(values, index):
    result = values[0]
    for n, value in enumerate(values[1:]):
        result = jnp.where(index == n + 1, value, result)
    return result


def block_state(where, maps, keys, values, part, heads, dh, piece, after):
    feat = maps.shape[-1]
    rows = len(keys) * piece
    height = heads // GROUP * dh + ROW_TILE
    arrays, specs = operands(keys + values, piece, heads * dh)
    return pl.pallas_call(
        ordered(functools.partial(state_kernel, len(keys), heads, dh), len(after), 1),
        out_shape=[
            jax.ShapeDtypeStruct((heads, rows, feat), bf16),
            jax.ShapeDtypeStruct((height, feat), f32),
        ]
        + [jax.ShapeDtypeStruct((height, feat), bf16)] * (GROUP - 1),
        grid_spec=pltpu.PrefetchScalarGridSpec(
            num_scalar_prefetch=1,
            grid=(1,),
            in_specs=waits(after)
            + [
                pl.BlockSpec((heads, 2 * dh, feat), lambda *_: (part, 0, 0)),
            ]
            + specs,
            out_specs=[full(heads, rows, feat)] + [full(height, feat)] * GROUP,
        ),
        compiler_params=params(),
        cost_estimate=busy(0),
        name="block_state",
    )(where, *after, maps, *arrays)


def step_kernel(levels, where_ref, *refs):
    ins = refs[: len(refs) - (1 if len(refs) < 2 * GROUP + levels else GROUP)]
    outs = refs[len(ins) :]
    values = [ref[...].astype(f32) for ref in ins[:GROUP]]
    got = [ref[...].astype(f32) for ref in ins[GROUP:]]
    if len(outs) == 1:
        total = values[0]
        for value in values[1:] + got:
            total = total + value
        outs[0][...] = total.astype(bf16)
        return
    prior = jnp.zeros_like(values[0])
    for level, value in enumerate(got):
        prior = prior + jnp.where(where_ref[2 + level] == 1, value, 0.0)
    mine = where_ref[1]
    for m, out in enumerate(outs):
        result = prior
        for other, value in enumerate(values):
            if other != m:
                result = result + jnp.where((mine ^ other) < (mine ^ m), value, 0.0)
        out[...] = result.astype(bf16)


def chain_step(where, levels, values, after):
    shape = values[0].shape
    count = GROUP if len(values) == GROUP + levels else 1
    return pl.pallas_call(
        ordered(functools.partial(step_kernel, levels), len(after), 0),
        grid=(1,),
        out_shape=[jax.ShapeDtypeStruct(shape, bf16)] * count,
        in_specs=waits(after)
        + [pl.BlockSpec(memory_space=pltpu.SMEM)]
        + [full(*shape)] * len(values),
        out_specs=[full(*shape)] * count,
        compiler_params=params(),
        cost_estimate=busy(0),
        name="chain_step",
    )(*after, where, *values)


def local_kernel(partners, heads, dh, where_ref, maps_ref, feats_ref, *refs):
    q_refs, v_refs = refs[:partners], refs[partners : 2 * partners]
    query_feats_ref, local_ref = refs[2 * partners :]
    piece = q_refs[0].shape[2]
    rows = partners * piece
    me = where_ref[0]

    def places(shape, dim):
        ids = lax.broadcasted_iota(jnp.int32, shape, dim)
        result = ids + (me ^ 0) * piece
        for k in range(1, partners):
            result = jnp.where(ids >= k * piece, ids + ((me ^ k) - k) * piece, result)
        return result

    causal = places((rows, 1), 0) >= places((1, rows), 1)
    ones = jnp.ones((rows, dh), bf16)
    for i in range(heads):
        cut = slice(i * dh, (i + 1) * dh)
        queries, values = joined(q_refs, cut), joined(v_refs, cut)
        query_feats = features(queries, maps_ref[i])
        query_feats_ref[i] = query_feats
        scores = lax.dot_general(
            query_feats, feats_ref[i], (((1,), (1,)), ((), ())), preferred_element_type=f32
        )
        weights = jnp.where(causal, scores, 0.0).astype(bf16)
        local_ref[i] = jnp.dot(
            weights, jnp.concatenate([values, ones], axis=1), preferred_element_type=f32
        )


def attend_local(where, maps, feats, queries, values, part, heads, dh, piece, after):
    partners = len(queries)
    feat = maps.shape[-1]
    rows = partners * piece
    arrays, specs = operands(queries + values, piece, heads * dh)
    return pl.pallas_call(
        ordered(functools.partial(local_kernel, partners, heads, dh), len(after), 1),
        out_shape=[
            jax.ShapeDtypeStruct((heads, rows, feat), bf16),
            jax.ShapeDtypeStruct((heads, rows, 2 * dh), f32),
        ],
        grid_spec=pltpu.PrefetchScalarGridSpec(
            num_scalar_prefetch=1,
            grid=(1,),
            in_specs=waits(after)
            + [
                pl.BlockSpec((heads, 2 * dh, feat), lambda *_: (part, 0, 0)),
                full(*feats.shape),
            ]
            + specs,
            out_specs=[full(heads, rows, feat), full(heads, rows, 2 * dh)],
        ),
        compiler_params=params(),
        cost_estimate=busy(0),
        name="attend_local",
    )(where, *after, maps, feats, *arrays)


def prior_kernel(partners, heads, dh, where_ref, query_feats_ref, local_ref, *refs):
    share_refs, (stay_ref, leave_ref) = refs[:GROUP], refs[GROUP:]
    piece = query_feats_ref.shape[1] // partners
    share = heads // GROUP
    for i in range(heads):
        j = i % share
        state, total = slice(j * dh, (j + 1) * dh), slice(share * dh, share * dh + ROW_TILE)
        source = where_ref[1] ^ (i // share)
        prior = chosen([ref[state, :] for ref in share_refs], source)
        tail = chosen([ref[total, :] for ref in share_refs], source)
        tail = jnp.broadcast_to(tail[j : j + 1, :], prior.shape)
        both = local_ref[i] + lax.dot_general(
            query_feats_ref[i],
            jnp.concatenate([prior, tail], axis=0),
            (((1,), (1,)), ((), ())),
            preferred_element_type=f32,
        )
        attended = (both[:, :dh] / both[:, dh:]).astype(bf16)
        for k in range(partners):
            out = leave_ref if k & 1 else stay_ref
            out[k // 2, :, i * dh : (i + 1) * dh] = attended[k * piece : (k + 1) * piece]


def attend_prior(where, query_feats, local, shares, partners, dh, after):
    heads, rows, feat = query_feats.shape
    out = jax.ShapeDtypeStruct((partners // 2, rows // partners, heads * dh), bf16)
    return pl.pallas_call(
        ordered(functools.partial(prior_kernel, partners, heads, dh), len(after), 0),
        grid=(1,),
        out_shape=[out, out],
        in_specs=waits(after)
        + [pl.BlockSpec(memory_space=pltpu.SMEM)]
        + [full(*value.shape) for value in (query_feats, local, *shares)],
        out_specs=[full(*out.shape)] * 2,
        compiler_params=params(),
        cost_estimate=busy(0),
        name="attend_prior",
    )(*after, where, query_feats, local, *shares)


def project_kernel(parts, *refs):
    own_refs, other_refs = refs[:parts], refs[parts : 2 * parts]
    own_w, other_w, stay_ref, *leave_refs = refs[2 * parts :]
    groups, piece, width = own_refs[0].shape
    acc = None
    for lhs_refs, w_ref in ((own_refs, own_w), (other_refs, other_w)):
        for p, ref in enumerate(lhs_refs):
            lhs = ref[...].reshape(groups * piece, width)
            term = jnp.dot(
                lhs, w_ref[p * width : (p + 1) * width, :], preferred_element_type=f32
            )
            acc = term if acc is None else acc + term
    stay_ref[...] = acc[:piece]
    for g, ref in enumerate(leave_refs):
        ref[...] = acc[(g + 1) * piece : (g + 2) * piece].astype(bf16)


def project(own, other, own_w, other_w, slabs, slab, after):
    parts, (groups, piece, width) = len(own), own[0].shape
    depth, cols = own_w.shape
    unit = cols // sum(slabs)
    tile = math.gcd(unit, 512)
    first, cols = sum(slabs[:slab]) * unit // tile, slabs[slab] * unit
    lhs = pl.BlockSpec((groups, piece, width), lambda n: (0, 0, 0))
    weight = pl.BlockSpec((depth, tile), lambda n: (0, first + n))
    out = pl.BlockSpec((piece, tile), lambda n: (0, n))
    return pl.pallas_call(
        ordered(functools.partial(project_kernel, parts), len(after), 0),
        grid=(cols // tile,),
        out_shape=[jax.ShapeDtypeStruct((piece, cols), f32)]
        + [jax.ShapeDtypeStruct((piece, cols), bf16)] * (groups - 1),
        in_specs=waits(after) + [lhs] * (2 * parts) + [weight, weight],
        out_specs=[out] * groups,
        compiler_params=params(),
        cost_estimate=busy(0),
        name="project",
    )(*after, *own, *other, own_w, other_w)


def finish_kernel(counts, *refs):
    refs = list(refs)
    out_ref = refs.pop()
    for s, slabs in enumerate(counts):
        at = 0
        for shares in slabs:
            total = refs.pop(0)[...]
            for _ in range(shares):
                total = total + refs.pop(0)[...].astype(f32)
            width = total.shape[1]
            out_ref[s, :, at : at + width] = total.astype(bf16)
            at += width


def finish(sums, piece):
    counts = [[len(shares) for _, shares in slabs] for slabs in sums]
    values = [value for slabs in sums for total, shares in slabs for value in (total, *shares)]
    out = (len(sums), piece, sum(total.shape[1] for total, _ in sums[0]))
    return pl.pallas_call(
        functools.partial(finish_kernel, counts),
        grid=(1,),
        out_shape=jax.ShapeDtypeStruct(out, bf16),
        in_specs=[full(*value.shape) for value in values],
        out_specs=full(*out),
        compiler_params=params(),
        cost_estimate=busy(0),
        name="finish",
    )(*values)


def nothing(*refs):
    pass


def later_than(value, after):
    anywhere = pl.BlockSpec(memory_space=pl.ANY)
    return pl.pallas_call(
        nothing,
        out_shape=jax.ShapeDtypeStruct(value.shape, value.dtype),
        in_specs=[anywhere] * (1 + len(after)),
        out_specs=anywhere,
        input_output_aliases={0: 0},
        compiler_params=params(1),
        cost_estimate=busy(0),
        name="later_than",
    )(value, *after)


def body(qkv_tokens, sign_bits, out_weight):
    partners, blocks = lax.axis_size("head"), lax.axis_size("seq")
    me, index = lax.axis_index("head"), lax.axis_index("seq")
    seqs = qkv_tokens.shape[0]
    all_heads, dh = sign_bits.shape[0], sign_bits.shape[-1]
    parts = CHUNKS
    heads = all_heads // parts
    levels = (blocks // GROUP).bit_length() - 1
    x = qkv_tokens.transpose(0, 2, 1, 3)
    piece = x.shape[2]
    where = jnp.stack(
        [me, index % GROUP] + [(index // GROUP >> l) & 1 for l in range(levels)]
    ).astype(jnp.int32)
    work = [(s, c) for s in range(seqs) for c in range(parts)]

    messages = [(s, c, (1, 2), parts) for s, c in work if s > 0]
    messages += [(s, 0, (0,), 1) for s in range(seqs)]
    outer, shape = range(2, partners, 2), (piece, x.shape[3] // partners)
    lead = [(x, s, k + 1) for s in range(seqs) for k in range(0, partners, 2)]
    wanted = [([(x, 0, k), (x, 0, k + 1)], (1, 2), 0, 1) for k in outer]
    *first, near = pack(where, partners, wanted + [(lead, (0, 1, 2), 0, 1)], shape, 60)
    first = [swap(value, "head", k) for value, k in zip(first, outer)]
    near = swap(near, "head", 1)
    wanted = [
        ([(x, s, k), (near, s * (partners // 2) + k // 2, None)], kinds, c, cuts)
        for s, c, kinds, cuts in messages
        for k in outer
    ]
    wanted.append(([(x, s, 0) for s in range(seqs)], (0, 1, 2), 0, 1))
    *packed, own_rows = pack(where, partners, wanted, shape, 20)
    hops = [swap(second_half(value, [own_rows]), "head", 1) for value in first]
    later = [swap(value, "head", k) for value, k in zip(packed, list(outer) * len(messages))]

    def pieces(n, kind):
        s, c = work[n]
        found = [(own_rows, s, kind, c), (near, s * (partners // 2), kind, c)]
        for t in range(len(outer)):
            if kind > 0 and s == 0:
                found += [(first[t], 0, kind - 1, c), (hops[t], 0, kind - 1, c)]
            else:
                message = n - parts if kind > 0 else len(work) - parts + s
                both = later[message * len(outer) + t]
                at, col = (kind - 1, 0) if kind > 0 else (0, c)
                found += [(both, 0, at, col), (both, 1, at, col)]
        return found

    maps = integer_maps(sign_bits)

    last = [own_rows]
    feats, chains, ends, locals_, own, other, totals = {}, {}, {}, {}, {}, {}, {}

    def state(n):
        feats[n], mine, *others = block_state(
            where, maps, pieces(n, 1), pieces(n, 2), work[n][1], heads, dh, piece, last
        )
        chains[n] = [mine] + [swap(value, "seq", m + 1) for m, value in enumerate(others)]
        last[:] = [mine]

    def step(n):
        first_out, *others = chain_step(where, levels, chains[n], last)
        last[:] = [first_out]
        if others:
            ends[n] = [first_out] + [swap(value, "seq", m + 1) for m, value in enumerate(others)]
        else:
            chains[n] = chains[n] + [swap(first_out, "seq", GROUP << (len(chains[n]) - GROUP))]

    def local(n):
        locals_[n] = attend_local(
            where, maps, feats[n], pieces(n, 0), pieces(n, 2), work[n][1], heads, dh, piece, last
        )
        last[:] = [locals_[n][0]]

    def attend(n):
        stay, leave = attend_prior(where, *locals_[n], ends[n], partners, dh, last)
        own.setdefault(work[n][0], []).append(stay)
        other.setdefault(work[n][0], []).append(swap(leave, "head", 1))
        last[:] = [stay]

    def multiply(s, slab):
        for key in ((s, slab - 1),) if s < seqs - 1 else ((s - 1, slab),) if slab > 0 else ():
            if key in totals:
                last.extend(totals[key][1])
        total, *shares = project(own[s], other[s], out_weight, other_weight, slabs[s], slab, last)
        totals[s, slab] = total, [swap(v, "head", 2 * (g + 1)) for g, v in enumerate(shares)]
        last[:] = [total]

    slabs = [SLABS[0]] * (seqs - 1) + [SLABS[1]]
    plan = []
    for n, (s, c) in enumerate(work):
        came = 22 * s + 8 * c / parts
        end = came + 22 + 9 * levels
        plan.append((came, state, n))
        plan += [(came + 12 + 9 * j, step, n) for j in range(levels + 1)]
        plan.append((end - 7, local, n))
        plan.append((end + 4, attend, n))
        if c == parts - 1:
            plan += [(end + (7.5 if j == 0 or s > 0 else 13) + 3.5 * j, multiply, s, j) for j in range(len(slabs[s]))]
    plan = sorted(plan, key=lambda entry: entry[0])
    state(0)
    other_weight = swap(later_than(out_weight, last), "head", 1)
    for _, act, *which in plan:
        if (act, which) != (state, [0]):
            act(*which)

    return finish([[totals[s, n] for n in range(len(slabs[s]))] for s in range(seqs)], piece)


def solution(mesh):
    return jax.shard_map(
        body,
        mesh=mesh,
        in_specs=(
            P(None, ("seq", "head"), None, None),
            P("head", None, None, None),
            P("head", None),
        ),
        out_specs=P(None, ("seq", "head"), None),
        check_vma=False,
    )
```

```python
import functools
import math

import jax
import jax.numpy as jnp
import numpy as np
from jax import lax
from jax.experimental import pallas as pl
from jax.experimental.pallas import tpu as pltpu
from jax.sharding import PartitionSpec as P

logit_divisor = 1.3
norm_epsilon = 1e-06
CHUNKS = 1

SLABS = (8,), (4, 3, 1)

bf16, f32 = jnp.bfloat16, jnp.float32
ROW_TILE = 16
GROUP = 4


def params(mebibytes=20):
    return pltpu.CompilerParams(vmem_limit_bytes=mebibytes * 1024 * 1024)


def full(*shape):
    return pl.BlockSpec(shape, lambda *_: (0,) * len(shape))


def ordered(kernel, count, skip):
    return lambda *refs: kernel(*refs[:skip], *refs[skip + count :])


def busy(microseconds):
    return pl.CostEstimate(flops=int(microseconds * 1e9), bytes_accessed=0, transcendentals=0)


def waits(after):
    return [pl.BlockSpec(memory_space=pl.ANY)] * len(after)


def swap(value, axis, bit):
    return lax.ppermute(value, axis, [(j, j ^ bit) for j in range(lax.axis_size(axis))])


def sign_matrix(order):
    ids = np.arange(order)
    common = ids[:, None] & ids[None, :]
    parity = np.zeros_like(common)
    while common.any():
        parity ^= common & 1
        common = common >> 1
    return (1 - 2 * parity).astype(np.float32)


def integer_maps(sign_bits):
    heads, blocks, _, dh = sign_bits.shape
    had = jnp.asarray(sign_matrix(dh), bf16)
    signed = (2 * sign_bits - 1).astype(bf16)
    inner = jnp.einsum("hbij,jk->hbik", had * signed[:, :, 1, None, :], had, preferred_element_type=f32)
    outer = inner.astype(bf16) * signed[:, :, 2, None, :]
    whole = jnp.einsum("hbij,jk->hbik", outer, had, preferred_element_type=f32)
    whole = whole * signed[:, :, 0, :, None].astype(f32)
    whole = whole.transpose(0, 2, 1, 3).reshape(heads, dh, blocks * dh)
    near = lax.reduce_precision(whole, 8, 7)
    return jnp.concatenate([near, whole - near], axis=1).astype(bf16)


def features(rows, maps):
    dh = rows.shape[-1]
    wide = rows.astype(f32)
    mean = jnp.sum(wide * wide, axis=-1, keepdims=True) * (1.0 / dh)
    scale = lax.rsqrt(mean + norm_epsilon) * (logit_divisor / dh**0.25 / dh)
    twice = jnp.concatenate([rows, rows], axis=1)
    return jnp.exp(jnp.dot(twice, maps, preferred_element_type=f32) * scale).astype(bf16)


def pack_kernel(places, arrays, where_ref, *refs):
    ins, outs, sems = refs[:arrays], refs[arrays:-1], refs[-1]
    copies = []
    for n, (which, first, kind, k, part, parts, out, index) in enumerate(places):
        width = outs[out].shape[-1]
        group = 0 if k is None else where_ref[0] ^ k
        start = pl.multiple_of((group * parts + part) * width, width)
        source = ins[which].at[first, kind, :, pl.ds(start, width)]
        copies.append(pltpu.make_async_copy(source, outs[out].at[index], sems.at[n]))
    for copy in copies:
        copy.start()
    for copy in copies:
        copy.wait()


def pack(where, partners, wanted, shape, mebibytes):
    rows, cols = shape
    arrays, places, shapes = [], [], []
    for out, (lead, kinds, part, parts) in enumerate(wanted):
        shapes.append((len(lead), len(kinds), rows, cols // parts))
        for i, (array, first, k) in enumerate(lead):
            if not any(array is known for known in arrays):
                arrays.append(array)
            which = [array is known for known in arrays].index(True)
            for j, kind in enumerate(kinds):
                places.append((which, first, kind, k, part, parts, out, (i, j)))
    return pl.pallas_call(
        functools.partial(pack_kernel, places, len(arrays)),
        out_shape=[jax.ShapeDtypeStruct(shape, bf16) for shape in shapes],
        in_specs=[pl.BlockSpec(memory_space=pltpu.SMEM)]
        + [pl.BlockSpec(memory_space=pl.ANY)] * len(arrays),
        out_specs=[pl.BlockSpec(memory_space=pltpu.VMEM)] * len(shapes),
        scratch_shapes=[pltpu.SemaphoreType.DMA((len(places),))],
        compiler_params=params(mebibytes),
        cost_estimate=busy(0),
        name="pack",
    )(where, *arrays)


def copy_kernel(in_ref, out_ref):
    out_ref[...] = in_ref[...]


def second_half(value, after):
    shape = (1, *value.shape[1:])
    return pl.pallas_call(
        ordered(copy_kernel, len(after), 0),
        grid=(1,),
        out_shape=jax.ShapeDtypeStruct(shape, value.dtype),
        in_specs=waits(after) + [pl.BlockSpec(shape, lambda _: (1, 0, 0, 0))],
        out_specs=full(*shape),
        compiler_params=params(),
        cost_estimate=busy(0),
        name="second_half",
    )(*after, value)


def operands(pieces, rows, width):
    specs = []
    for _, lead, kind, col in pieces:
        if callable(col):
            at = lambda _, where, lead=lead, kind=kind, col=col: (lead, kind, 0, col(where))
        else:
            at = lambda _, where, at=(lead, kind, 0, col): at
        specs.append(pl.BlockSpec((1, 1, rows, width), at))
    return [piece[0] for piece in pieces], specs


def joined(refs, cut):
    return jnp.concatenate([ref[0, 0, :, cut] for ref in refs], axis=0)


def state_kernel(partners, heads, dh, where_ref, maps_ref, *refs):
    k_refs, v_refs = refs[:partners], refs[partners : 2 * partners]
    feats_ref, *share_refs = refs[2 * partners :]
    share = heads // GROUP
    states, totals = [], []
    for i in range(heads):
        cut = slice(i * dh, (i + 1) * dh)
        keys, values = joined(k_refs, cut), joined(v_refs, cut)
        feats = features(keys, maps_ref[i])
        feats_ref[i] = feats
        states.append(
            lax.dot_general(values, feats, (((0,), (0,)), ((), ())), preferred_element_type=f32)
        )
        totals.append(jnp.sum(feats.astype(f32), axis=0, keepdims=True))
    pad = jnp.zeros((ROW_TILE - share, feats_ref.shape[-1]), f32)
    shares = [
        jnp.concatenate(
            states[g * share : (g + 1) * share] + totals[g * share : (g + 1) * share] + [pad], axis=0
        )
        for g in range(GROUP)
    ]
    for m, ref in enumerate(share_refs):
        ref[...] = chosen(shares, where_ref[1] ^ m).astype(ref.dtype)


def chosen(values, index):
    result = values[0]
    for n, value in enumerate(values[1:]):
        result = jnp.where(index == n + 1, value, result)
    return result


def block_state(where, maps, keys, values, part, heads, dh, piece, after, beside):
    feat = maps.shape[-1]
    rows = len(keys) * piece
    height = heads // GROUP * dh + ROW_TILE
    arrays, specs = operands(keys + values, piece, heads * dh)
    return pl.pallas_call(
        ordered(functools.partial(state_kernel, len(keys), heads, dh), len(after), 1),
        out_shape=[
            jax.ShapeDtypeStruct((heads, rows, feat), bf16),
            jax.ShapeDtypeStruct((height, feat), f32),
        ]
        + [jax.ShapeDtypeStruct((height, feat), bf16)] * (GROUP - 1),
        grid_spec=pltpu.PrefetchScalarGridSpec(
            num_scalar_prefetch=1,
            grid=(1,),
            in_specs=waits(after)
            + [
                pl.BlockSpec((heads, 2 * dh, feat), lambda *_: (part, 0, 0)),
            ]
            + specs,
            out_specs=[full(heads, rows, feat)] + [full(height, feat)] * GROUP,
        ),
        compiler_params=params(),
        cost_estimate=busy(beside),
        name="block_state",
    )(where, *after, maps, *arrays)


def step_kernel(levels, where_ref, *refs):
    ins = refs[: len(refs) - (1 if len(refs) < 2 * GROUP + levels else GROUP)]
    outs = refs[len(ins) :]
    values = [ref[...].astype(f32) for ref in ins[:GROUP]]
    got = [ref[...].astype(f32) for ref in ins[GROUP:]]
    if len(outs) == 1:
        total = values[0]
        for value in values[1:] + got:
            total = total + value
        outs[0][...] = total.astype(bf16)
        return
    prior = jnp.zeros_like(values[0])
    for level, value in enumerate(got):
        prior = prior + jnp.where(where_ref[2 + level] == 1, value, 0.0)
    mine = where_ref[1]
    for m, out in enumerate(outs):
        result = prior
        for other, value in enumerate(values):
            if other != m:
                result = result + jnp.where((mine ^ other) < (mine ^ m), value, 0.0)
        out[...] = result.astype(bf16)


def chain_step(where, levels, values, after):
    shape = values[0].shape
    count = GROUP if len(values) == GROUP + levels else 1
    return pl.pallas_call(
        ordered(functools.partial(step_kernel, levels), len(after), 0),
        grid=(1,),
        out_shape=[jax.ShapeDtypeStruct(shape, bf16)] * count,
        in_specs=waits(after)
        + [pl.BlockSpec(memory_space=pltpu.SMEM)]
        + [full(*shape)] * len(values),
        out_specs=[full(*shape)] * count,
        compiler_params=params(),
        cost_estimate=busy(0),
        name="chain_step",
    )(*after, where, *values)


def local_kernel(partners, heads, dh, where_ref, maps_ref, feats_ref, *refs):
    q_refs, v_refs = refs[:partners], refs[partners : 2 * partners]
    query_feats_ref, local_ref = refs[2 * partners :]
    piece = q_refs[0].shape[2]
    rows = partners * piece
    me = where_ref[0]

    def places(shape, dim):
        ids = lax.broadcasted_iota(jnp.int32, shape, dim)
        result = ids + (me ^ 0) * piece
        for k in range(1, partners):
            result = jnp.where(ids >= k * piece, ids + ((me ^ k) - k) * piece, result)
        return result

    causal = places((rows, 1), 0) >= places((1, rows), 1)
    ones = jnp.ones((rows, dh), bf16)
    for i in range(heads):
        cut = slice(i * dh, (i + 1) * dh)
        queries, values = joined(q_refs, cut), joined(v_refs, cut)
        query_feats = features(queries, maps_ref[i])
        query_feats_ref[i] = query_feats
        scores = lax.dot_general(
            query_feats, feats_ref[i], (((1,), (1,)), ((), ())), preferred_element_type=f32
        )
        weights = jnp.where(causal, scores, 0.0).astype(bf16)
        local_ref[i] = jnp.dot(
            weights, jnp.concatenate([values, ones], axis=1), preferred_element_type=f32
        )


def attend_local(where, maps, feats, queries, values, part, heads, dh, piece, after):
    partners = len(queries)
    feat = maps.shape[-1]
    rows = partners * piece
    arrays, specs = operands(queries + values, piece, heads * dh)
    return pl.pallas_call(
        ordered(functools.partial(local_kernel, partners, heads, dh), len(after), 1),
        out_shape=[
            jax.ShapeDtypeStruct((heads, rows, feat), bf16),
            jax.ShapeDtypeStruct((heads, rows, 2 * dh), f32),
        ],
        grid_spec=pltpu.PrefetchScalarGridSpec(
            num_scalar_prefetch=1,
            grid=(1,),
            in_specs=waits(after)
            + [
                pl.BlockSpec((heads, 2 * dh, feat), lambda *_: (part, 0, 0)),
                full(*feats.shape),
            ]
            + specs,
            out_specs=[full(heads, rows, feat), full(heads, rows, 2 * dh)],
        ),
        compiler_params=params(),
        cost_estimate=busy(3),
        name="attend_local",
    )(where, *after, maps, feats, *arrays)


def prior_kernel(partners, heads, dh, where_ref, query_feats_ref, local_ref, *refs):
    share_refs, (stay_ref, leave_ref) = refs[:GROUP], refs[GROUP:]
    piece = query_feats_ref.shape[1] // partners
    share = heads // GROUP
    for i in range(heads):
        j = i % share
        state, total = slice(j * dh, (j + 1) * dh), slice(share * dh, share * dh + ROW_TILE)
        source = where_ref[1] ^ (i // share)
        prior = chosen([ref[state, :] for ref in share_refs], source)
        tail = chosen([ref[total, :] for ref in share_refs], source)
        tail = jnp.broadcast_to(tail[j : j + 1, :], prior.shape)
        both = local_ref[i] + lax.dot_general(
            query_feats_ref[i],
            jnp.concatenate([prior, tail], axis=0),
            (((1,), (1,)), ((), ())),
            preferred_element_type=f32,
        )
        attended = (both[:, :dh] / both[:, dh:]).astype(bf16)
        for k in range(partners):
            out = leave_ref if k & 1 else stay_ref
            out[k // 2, :, i * dh : (i + 1) * dh] = attended[k * piece : (k + 1) * piece]


def attend_prior(where, query_feats, local, shares, partners, dh, after, beside):
    heads, rows, feat = query_feats.shape
    out = jax.ShapeDtypeStruct((partners // 2, rows // partners, heads * dh), bf16)
    return pl.pallas_call(
        ordered(functools.partial(prior_kernel, partners, heads, dh), len(after), 0),
        grid=(1,),
        out_shape=[out, out],
        in_specs=waits(after)
        + [pl.BlockSpec(memory_space=pltpu.SMEM)]
        + [full(*value.shape) for value in (query_feats, local, *shares)],
        out_specs=[full(*out.shape)] * 2,
        compiler_params=params(),
        cost_estimate=busy(beside),
        name="attend_prior",
    )(*after, where, query_feats, local, *shares)


def project_kernel(parts, *refs):
    own_refs, other_refs = refs[:parts], refs[parts : 2 * parts]
    own_w, other_w, stay_ref, *leave_refs = refs[2 * parts :]
    groups, piece, width = own_refs[0].shape
    acc = None
    for lhs_refs, w_ref in ((own_refs, own_w), (other_refs, other_w)):
        for p, ref in enumerate(lhs_refs):
            lhs = ref[...].reshape(groups * piece, width)
            term = jnp.dot(
                lhs, w_ref[p * width : (p + 1) * width, :], preferred_element_type=f32
            )
            acc = term if acc is None else acc + term
    stay_ref[...] = acc[:piece]
    for g, ref in enumerate(leave_refs):
        ref[...] = acc[(g + 1) * piece : (g + 2) * piece].astype(bf16)


def project(own, other, own_w, other_w, slabs, slab, after, beside):
    parts, (groups, piece, width) = len(own), own[0].shape
    depth, cols = own_w.shape
    unit = cols // sum(slabs)
    tile = math.gcd(unit, 512)
    first, cols = sum(slabs[:slab]) * unit // tile, slabs[slab] * unit
    lhs = pl.BlockSpec((groups, piece, width), lambda n: (0, 0, 0))
    weight = pl.BlockSpec((depth, tile), lambda n: (0, first + n))
    out = pl.BlockSpec((piece, tile), lambda n: (0, n))
    return pl.pallas_call(
        ordered(functools.partial(project_kernel, parts), len(after), 0),
        grid=(cols // tile,),
        out_shape=[jax.ShapeDtypeStruct((piece, cols), f32)]
        + [jax.ShapeDtypeStruct((piece, cols), bf16)] * (groups - 1),
        in_specs=waits(after) + [lhs] * (2 * parts) + [weight, weight],
        out_specs=[out] * groups,
        compiler_params=params(),
        cost_estimate=busy(beside),
        name="project",
    )(*after, *own, *other, own_w, other_w)


def finish_kernel(counts, *refs):
    refs = list(refs)
    out_ref = refs.pop()
    for s, slabs in enumerate(counts):
        at = 0
        for shares in slabs:
            total = refs.pop(0)[...]
            for _ in range(shares):
                total = total + refs.pop(0)[...].astype(f32)
            width = total.shape[1]
            out_ref[s, :, at : at + width] = total.astype(bf16)
            at += width


def finish(sums, piece):
    counts = [[len(shares) for _, shares in slabs] for slabs in sums]
    values = [value for slabs in sums for total, shares in slabs for value in (total, *shares)]
    out = (len(sums), piece, sum(total.shape[1] for total, _ in sums[0]))
    return pl.pallas_call(
        functools.partial(finish_kernel, counts),
        grid=(1,),
        out_shape=jax.ShapeDtypeStruct(out, bf16),
        in_specs=[full(*value.shape) for value in values],
        out_specs=full(*out),
        compiler_params=params(),
        cost_estimate=busy(0),
        name="finish",
    )(*values)


def nothing(*refs):
    pass


def later_than(value, after):
    anywhere = pl.BlockSpec(memory_space=pl.ANY)
    return pl.pallas_call(
        nothing,
        out_shape=jax.ShapeDtypeStruct(value.shape, value.dtype),
        in_specs=[anywhere] * (1 + len(after)),
        out_specs=anywhere,
        input_output_aliases={0: 0},
        compiler_params=params(1),
        cost_estimate=busy(0),
        name="later_than",
    )(value, *after)


def body(qkv_tokens, sign_bits, out_weight):
    partners, blocks = lax.axis_size("head"), lax.axis_size("seq")
    me, index = lax.axis_index("head"), lax.axis_index("seq")
    seqs = qkv_tokens.shape[0]
    all_heads, dh = sign_bits.shape[0], sign_bits.shape[-1]
    parts = CHUNKS
    heads = all_heads // parts
    levels = (blocks // GROUP).bit_length() - 1
    x = qkv_tokens.transpose(0, 2, 1, 3)
    piece = x.shape[2]
    where = jnp.stack(
        [me, index % GROUP] + [(index // GROUP >> l) & 1 for l in range(levels)]
    ).astype(jnp.int32)
    work = [(s, c) for s in range(seqs) for c in range(parts)]

    messages = [(s, c, (1, 2), parts) for s, c in work if s > 0]
    messages += [(s, 0, (0,), 1) for s in range(seqs)]
    outer, shape = range(2, partners, 2), (piece, x.shape[3] // partners)
    lead = [(x, s, k + 1) for s in range(seqs) for k in range(0, partners, 2)]
    wanted = [([(x, 0, k), (x, 0, k + 1)], (1, 2), 0, 1) for k in outer]
    *first, near = pack(where, partners, wanted + [(lead, (0, 1, 2), 0, 1)], shape, 60)
    first = [swap(value, "head", k) for value, k in zip(first, outer)]
    near = swap(near, "head", 1)
    wanted = [
        ([(x, s, k), (near, s * (partners // 2) + k // 2, None)], kinds, c, cuts)
        for s, c, kinds, cuts in messages
        for k in outer
    ]
    wanted.append(([(x, s, 0) for s in range(seqs)], (0, 1, 2), 0, 1))
    *packed, own_rows = pack(where, partners, wanted, shape, 20)
    hops = [swap(second_half(value, [own_rows]), "head", 1) for value in first]
    later = [swap(value, "head", k) for value, k in zip(packed, list(outer) * len(messages))]

    def pieces(n, kind):
        s, c = work[n]
        found = [(own_rows, s, kind, c), (near, s * (partners // 2), kind, c)]
        for t in range(len(outer)):
            if kind > 0 and s == 0:
                found += [(first[t], 0, kind - 1, c), (hops[t], 0, kind - 1, c)]
            else:
                message = n - parts if kind > 0 else len(work) - parts + s
                both = later[message * len(outer) + t]
                at, col = (kind - 1, 0) if kind > 0 else (0, c)
                found += [(both, 0, at, col), (both, 1, at, col)]
        return found

    maps = integer_maps(sign_bits)

    last = [own_rows]
    feats, chains, ends, locals_, own, other, totals = {}, {}, {}, {}, {}, {}, {}

    def state(n):
        feats[n], mine, *others = block_state(
            where, maps, pieces(n, 1), pieces(n, 2), work[n][1], heads, dh, piece, last, 3 if n else 0
        )
        chains[n] = [mine] + [swap(value, "seq", m + 1) for m, value in enumerate(others)]
        last[:] = [mine]

    def step(n):
        first_out, *others = chain_step(where, levels, chains[n], last)
        last[:] = [first_out]
        if others:
            ends[n] = [first_out] + [swap(value, "seq", m + 1) for m, value in enumerate(others)]
        else:
            chains[n] = chains[n] + [swap(first_out, "seq", GROUP << (len(chains[n]) - GROUP))]

    def local(n):
        locals_[n] = attend_local(
            where, maps, feats[n], pieces(n, 0), pieces(n, 2), work[n][1], heads, dh, piece, last
        )
        last[:] = [locals_[n][0]]

    def attend(n):
        stay, leave = attend_prior(
            where, *locals_[n], ends[n], partners, dh, last, 1 if n + 1 < len(work) else 0
        )
        own.setdefault(work[n][0], []).append(stay)
        other.setdefault(work[n][0], []).append(swap(leave, "head", 1))
        last[:] = [stay]

    def multiply(s, slab):
        if slab == 1:
            for key in totals:
                if key[0] < s:
                    last.extend(totals[key][1])
        total, *shares = project(
            own[s], other[s], out_weight, other_weight, slabs[s], slab, last, 0 if s == seqs - 1 else 6
        )
        totals[s, slab] = total, [swap(v, "head", 2 * (g + 1)) for g, v in enumerate(shares)]
        last[:] = [total]

    slabs = [SLABS[0]] * (seqs - 1) + [SLABS[1]]
    plan = []
    for n, (s, c) in enumerate(work):
        came = 22 * s + 8 * c / parts
        end = came + 22 + 9 * levels
        plan.append((came, state, n))
        plan += [(came + 12 + 9 * j, step, n) for j in range(levels + 1)]
        plan.append((end - 7, local, n))
        plan.append((end + 4, attend, n))
        if c == parts - 1:
            plan += [(end + 6 + 3.5 * j, multiply, s, j) for j in range(len(slabs[s]))]
    plan = sorted(plan, key=lambda entry: entry[0])
    state(0)
    other_weight = swap(later_than(out_weight, last), "head", 1)
    for _, act, *which in plan:
        if (act, which) != (state, [0]):
            act(*which)

    return finish([[totals[s, n] for n in range(len(slabs[s]))] for s in range(seqs)], piece)


def solution(mesh):
    return jax.shard_map(
        body,
        mesh=mesh,
        in_specs=(
            P(None, ("seq", "head"), None, None),
            P("head", None, None, None),
            P("head", None),
        ),
        out_specs=P(None, ("seq", "head"), None),
        check_vma=False,
    )
```

```python
import functools
import math

import jax
import jax.numpy as jnp
import numpy as np
from jax import lax
from jax.experimental import pallas as pl
from jax.experimental.pallas import tpu as pltpu
from jax.sharding import PartitionSpec as P

logit_divisor = 1.3
norm_epsilon = 1e-06
CHUNKS = 1

SLABS = (8,), (4, 3, 1)

bf16, f32 = jnp.bfloat16, jnp.float32
ROW_TILE = 16
GROUP = 4


def params(mebibytes=20):
    return pltpu.CompilerParams(vmem_limit_bytes=mebibytes * 1024 * 1024)


def full(*shape):
    return pl.BlockSpec(shape, lambda *_: (0,) * len(shape))


def ordered(kernel, count, skip):
    return lambda *refs: kernel(*refs[:skip], *refs[skip + count :])


def busy(microseconds):
    return pl.CostEstimate(flops=int(microseconds * 1e9), bytes_accessed=0, transcendentals=0)


def waits(after):
    return [pl.BlockSpec(memory_space=pl.ANY)] * len(after)


def swap(value, axis, bit):
    return lax.ppermute(value, axis, [(j, j ^ bit) for j in range(lax.axis_size(axis))])


def sign_matrix(order):
    ids = np.arange(order)
    common = ids[:, None] & ids[None, :]
    parity = np.zeros_like(common)
    while common.any():
        parity ^= common & 1
        common = common >> 1
    return (1 - 2 * parity).astype(np.float32)


def integer_maps(sign_bits):
    heads, blocks, _, dh = sign_bits.shape
    had = jnp.asarray(sign_matrix(dh), bf16)
    signed = (2 * sign_bits - 1).astype(bf16)
    inner = jnp.einsum("hbij,jk->hbik", had * signed[:, :, 1, None, :], had, preferred_element_type=f32)
    outer = inner.astype(bf16) * signed[:, :, 2, None, :]
    whole = jnp.einsum("hbij,jk->hbik", outer, had, preferred_element_type=f32)
    whole = whole * signed[:, :, 0, :, None].astype(f32)
    whole = whole.transpose(0, 2, 1, 3).reshape(heads, dh, blocks * dh)
    near = lax.reduce_precision(whole, 8, 7)
    return jnp.concatenate([near, whole - near], axis=1).astype(bf16)


def features(rows, maps):
    dh = rows.shape[-1]
    wide = rows.astype(f32)
    mean = jnp.sum(wide * wide, axis=-1, keepdims=True) * (1.0 / dh)
    scale = lax.rsqrt(mean + norm_epsilon) * (logit_divisor / dh**0.25 / dh)
    twice = jnp.concatenate([rows, rows], axis=1)
    return jnp.exp(jnp.dot(twice, maps, preferred_element_type=f32) * scale).astype(bf16)


def pack_kernel(places, arrays, where_ref, *refs):
    ins, outs, sems = refs[:arrays], refs[arrays:-1], refs[-1]
    copies = []
    for n, (which, first, second, k, out, index) in enumerate(places):
        width = outs[out].shape[-1]
        start = 0 if k is None else pl.multiple_of((where_ref[0] ^ k) * width, width)
        source = ins[which].at[first, second, :, pl.ds(start, width)]
        copies.append(pltpu.make_async_copy(source, outs[out].at[index], sems.at[n]))
    for copy in copies:
        copy.start()
    for copy in copies:
        copy.wait()


def pack(where, wanted, shape, mebibytes):
    arrays, places, shapes = [], [], []
    for out, table in enumerate(wanted):
        shapes.append((len(table), len(table[0]), *shape))
        for i, row in enumerate(table):
            for j, (array, first, second, k) in enumerate(row):
                if not any(array is known for known in arrays):
                    arrays.append(array)
                which = [array is known for known in arrays].index(True)
                places.append((which, first, second, k, out, (i, j)))
    return pl.pallas_call(
        functools.partial(pack_kernel, places, len(arrays)),
        out_shape=[jax.ShapeDtypeStruct(shape, bf16) for shape in shapes],
        in_specs=[pl.BlockSpec(memory_space=pltpu.SMEM)]
        + [pl.BlockSpec(memory_space=pl.ANY)] * len(arrays),
        out_specs=[pl.BlockSpec(memory_space=pltpu.VMEM)] * len(shapes),
        scratch_shapes=[pltpu.SemaphoreType.DMA((len(places),))],
        compiler_params=params(mebibytes),
        cost_estimate=busy(0),
        name="pack",
    )(where, *arrays)


def operands(pieces, rows, width):
    specs = []
    for _, lead, kind, col in pieces:
        if callable(col):
            at = lambda _, where, lead=lead, kind=kind, col=col: (lead, kind, 0, col(where))
        else:
            at = lambda _, where, at=(lead, kind, 0, col): at
        specs.append(pl.BlockSpec((1, 1, rows, width), at))
    return [piece[0] for piece in pieces], specs


def joined(refs, cut):
    return jnp.concatenate([ref[0, 0, :, cut] for ref in refs], axis=0)


def sums_kernel(pieces, heads, dh, maps_ref, *refs):
    k_refs, v_refs = refs[:pieces], refs[pieces : 2 * pieces]
    *before, feats_ref, sums_ref = refs[2 * pieces :]
    for i in range(heads):
        cut = slice(i * dh, (i + 1) * dh)
        keys, values = joined(k_refs, cut), joined(v_refs, cut)
        feats = features(keys, maps_ref[i])
        feats_ref[i] = feats
        state = lax.dot_general(
            values, feats, (((0,), (0,)), ((), ())), preferred_element_type=f32
        )
        total = jnp.sum(feats.astype(f32), axis=0, keepdims=True)
        total = jnp.broadcast_to(total, (sums_ref.shape[1] - dh, total.shape[1]))
        sums = jnp.concatenate([state, total], axis=0)
        sums_ref[i] = before[0][i] + sums if before else sums


def early_sums(where, maps, keys, values, part, heads, dh, piece, after):
    feat = maps.shape[-1]
    rows = len(keys) * piece
    arrays, specs = operands(keys + values, piece, heads * dh)
    return pl.pallas_call(
        ordered(functools.partial(sums_kernel, len(keys), heads, dh), 1 + len(after), 0),
        out_shape=[
            jax.ShapeDtypeStruct((heads, rows, feat), bf16),
            jax.ShapeDtypeStruct((heads, dh + 8, feat), f32),
        ],
        grid_spec=pltpu.PrefetchScalarGridSpec(
            num_scalar_prefetch=1,
            grid=(1,),
            in_specs=waits(after)
            + [pl.BlockSpec((heads, 2 * dh, feat), lambda *_: (part, 0, 0))]
            + specs,
            out_specs=[full(heads, rows, feat), full(heads, dh + 8, feat)],
        ),
        compiler_params=params(),
        cost_estimate=busy(0),
        name="early_sums",
    )(where, *after, maps, *arrays)


def state_kernel(pieces, heads, dh, where_ref, maps_ref, *refs):
    *ins, feats_ref, sums_ref = refs[: 2 * pieces + 2] + refs[-1:]
    share_refs = refs[2 * pieces + 2 : -1]
    sums_kernel(pieces, heads, dh, maps_ref, *ins, feats_ref, sums_ref)
    share = heads // GROUP
    pad = jnp.zeros((ROW_TILE - share, feats_ref.shape[-1]), f32)
    states = [sums_ref[i] for i in range(heads)]
    shares = []
    for g in range(GROUP):
        mine = states[g * share : (g + 1) * share]
        shares.append(
            jnp.concatenate([v[:dh] for v in mine] + [v[dh : dh + 1] for v in mine] + [pad], axis=0)
        )
    for m, ref in enumerate(share_refs):
        ref[...] = chosen(shares, where_ref[1] ^ m).astype(ref.dtype)


def chosen(values, index):
    result = values[0]
    for n, value in enumerate(values[1:]):
        result = jnp.where(index == n + 1, value, result)
    return result


def block_state(where, maps, keys, values, before, part, heads, dh, piece, after, beside):
    feat = maps.shape[-1]
    rows = len(keys) * piece
    height = heads // GROUP * dh + ROW_TILE
    arrays, specs = operands(keys + values, piece, heads * dh)
    return pl.pallas_call(
        ordered(functools.partial(state_kernel, len(keys), heads, dh), len(after), 1),
        out_shape=[
            jax.ShapeDtypeStruct((heads, rows, feat), bf16),
            jax.ShapeDtypeStruct((height, feat), f32),
        ]
        + [jax.ShapeDtypeStruct((height, feat), bf16)] * (GROUP - 1),
        grid_spec=pltpu.PrefetchScalarGridSpec(
            num_scalar_prefetch=1,
            scratch_shapes=[pltpu.VMEM(before.shape, f32)],
            grid=(1,),
            in_specs=waits(after)
            + [
                pl.BlockSpec((heads, 2 * dh, feat), lambda *_: (part, 0, 0)),
            ]
            + specs
            + [full(*before.shape)],
            out_specs=[full(heads, rows, feat)] + [full(height, feat)] * GROUP,
        ),
        compiler_params=params(),
        cost_estimate=busy(beside),
        name="block_state",
    )(where, *after, maps, *arrays, before)


def step_kernel(levels, where_ref, *refs):
    ins = refs[: len(refs) - (1 if len(refs) < 2 * GROUP + levels else GROUP)]
    outs = refs[len(ins) :]
    values = [ref[...].astype(f32) for ref in ins[:GROUP]]
    got = [ref[...].astype(f32) for ref in ins[GROUP:]]
    if len(outs) == 1:
        total = values[0]
        for value in values[1:] + got:
            total = total + value
        outs[0][...] = total.astype(bf16)
        return
    prior = jnp.zeros_like(values[0])
    for level, value in enumerate(got):
        prior = prior + jnp.where(where_ref[2 + level] == 1, value, 0.0)
    mine = where_ref[1]
    for m, out in enumerate(outs):
        result = prior
        for other, value in enumerate(values):
            if other != m:
                result = result + jnp.where((mine ^ other) < (mine ^ m), value, 0.0)
        out[...] = result.astype(bf16)


def chain_step(where, levels, values, after):
    shape = values[0].shape
    count = GROUP if len(values) == GROUP + levels else 1
    return pl.pallas_call(
        ordered(functools.partial(step_kernel, levels), len(after), 0),
        grid=(1,),
        out_shape=[jax.ShapeDtypeStruct(shape, bf16)] * count,
        in_specs=waits(after)
        + [pl.BlockSpec(memory_space=pltpu.SMEM)]
        + [full(*shape)] * len(values),
        out_specs=[full(*shape)] * count,
        compiler_params=params(),
        cost_estimate=busy(0),
        name="chain_step",
    )(*after, where, *values)


def local_kernel(partners, heads, dh, where_ref, maps_ref, early_ref, late_ref, *refs):
    q_refs, v_refs = refs[:partners], refs[partners : 2 * partners]
    query_feats_ref, local_ref = refs[2 * partners :]
    piece = q_refs[0].shape[2]
    rows = partners * piece
    me = where_ref[0]

    def places(shape, dim):
        ids = lax.broadcasted_iota(jnp.int32, shape, dim)
        result = ids + (me ^ 0) * piece
        for k in range(1, partners):
            result = jnp.where(ids >= k * piece, ids + ((me ^ k) - k) * piece, result)
        return result

    causal = places((rows, 1), 0) >= places((1, rows), 1)
    ones = jnp.ones((rows, dh), bf16)
    for i in range(heads):
        cut = slice(i * dh, (i + 1) * dh)
        queries, values = joined(q_refs, cut), joined(v_refs, cut)
        query_feats = features(queries, maps_ref[i])
        query_feats_ref[i] = query_feats
        scores = lax.dot_general(
            query_feats,
            jnp.concatenate([early_ref[i], late_ref[i]], axis=0),
            (((1,), (1,)), ((), ())),
            preferred_element_type=f32,
        )
        weights = jnp.where(causal, scores, 0.0).astype(bf16)
        local_ref[i] = jnp.dot(
            weights, jnp.concatenate([values, ones], axis=1), preferred_element_type=f32
        )


def attend_local(where, maps, feats, queries, values, part, heads, dh, piece, after):
    partners = len(queries)
    feat = maps.shape[-1]
    rows = partners * piece
    arrays, specs = operands(queries + values, piece, heads * dh)
    return pl.pallas_call(
        ordered(functools.partial(local_kernel, partners, heads, dh), len(after), 1),
        out_shape=[
            jax.ShapeDtypeStruct((heads, rows, feat), bf16),
            jax.ShapeDtypeStruct((heads, rows, 2 * dh), f32),
        ],
        grid_spec=pltpu.PrefetchScalarGridSpec(
            num_scalar_prefetch=1,
            grid=(1,),
            in_specs=waits(after)
            + [
                pl.BlockSpec((heads, 2 * dh, feat), lambda *_: (part, 0, 0)),
                *[full(*part_.shape) for part_ in feats],
            ]
            + specs,
            out_specs=[full(heads, rows, feat), full(heads, rows, 2 * dh)],
        ),
        compiler_params=params(),
        cost_estimate=busy(3),
        name="attend_local",
    )(where, *after, maps, *feats, *arrays)


def prior_kernel(partners, heads, dh, where_ref, query_feats_ref, local_ref, *refs):
    share_refs, (stay_ref, leave_ref) = refs[:GROUP], refs[GROUP:]
    piece = query_feats_ref.shape[1] // partners
    share = heads // GROUP
    for i in range(heads):
        j = i % share
        state, total = slice(j * dh, (j + 1) * dh), slice(share * dh, share * dh + ROW_TILE)
        source = where_ref[1] ^ (i // share)
        prior = chosen([ref[state, :] for ref in share_refs], source)
        tail = chosen([ref[total, :] for ref in share_refs], source)
        tail = jnp.broadcast_to(tail[j : j + 1, :], prior.shape)
        both = local_ref[i] + lax.dot_general(
            query_feats_ref[i],
            jnp.concatenate([prior, tail], axis=0),
            (((1,), (1,)), ((), ())),
            preferred_element_type=f32,
        )
        attended = (both[:, :dh] / both[:, dh:]).astype(bf16)
        for k in range(partners):
            out = leave_ref if k & 1 else stay_ref
            out[k // 2, :, i * dh : (i + 1) * dh] = attended[k * piece : (k + 1) * piece]


def attend_prior(where, query_feats, local, shares, partners, dh, after, beside):
    heads, rows, feat = query_feats.shape
    out = jax.ShapeDtypeStruct((partners // 2, rows // partners, heads * dh), bf16)
    return pl.pallas_call(
        ordered(functools.partial(prior_kernel, partners, heads, dh), len(after), 0),
        grid=(1,),
        out_shape=[out, out],
        in_specs=waits(after)
        + [pl.BlockSpec(memory_space=pltpu.SMEM)]
        + [full(*value.shape) for value in (query_feats, local, *shares)],
        out_specs=[full(*out.shape)] * 2,
        compiler_params=params(),
        cost_estimate=busy(beside),
        name="attend_prior",
    )(*after, where, query_feats, local, *shares)


def project_kernel(parts, *refs):
    own_refs, other_refs = refs[:parts], refs[parts : 2 * parts]
    own_w, other_w, stay_ref, *leave_refs = refs[2 * parts :]
    groups, piece, width = own_refs[0].shape
    acc = None
    for lhs_refs, w_ref in ((own_refs, own_w), (other_refs, other_w)):
        for p, ref in enumerate(lhs_refs):
            lhs = ref[...].reshape(groups * piece, width)
            term = jnp.dot(
                lhs, w_ref[p * width : (p + 1) * width, :], preferred_element_type=f32
            )
            acc = term if acc is None else acc + term
    stay_ref[...] = acc[:piece]
    for g, ref in enumerate(leave_refs):
        ref[...] = acc[(g + 1) * piece : (g + 2) * piece].astype(bf16)


def project(own, other, own_w, other_w, slabs, slab, after, beside):
    parts, (groups, piece, width) = len(own), own[0].shape
    depth, cols = own_w.shape
    unit = cols // sum(slabs)
    tile = math.gcd(unit, 512)
    first, cols = sum(slabs[:slab]) * unit // tile, slabs[slab] * unit
    lhs = pl.BlockSpec((groups, piece, width), lambda n: (0, 0, 0))
    weight = pl.BlockSpec((depth, tile), lambda n: (0, first + n))
    out = pl.BlockSpec((piece, tile), lambda n: (0, n))
    return pl.pallas_call(
        ordered(functools.partial(project_kernel, parts), len(after), 0),
        grid=(cols // tile,),
        out_shape=[jax.ShapeDtypeStruct((piece, cols), f32)]
        + [jax.ShapeDtypeStruct((piece, cols), bf16)] * (groups - 1),
        in_specs=waits(after) + [lhs] * (2 * parts) + [weight, weight],
        out_specs=[out] * groups,
        compiler_params=params(),
        cost_estimate=busy(beside),
        name="project",
    )(*after, *own, *other, own_w, other_w)


def finish_kernel(counts, *refs):
    refs = list(refs)
    out_ref = refs.pop()
    for s, slabs in enumerate(counts):
        at = 0
        for shares in slabs:
            total = refs.pop(0)[...]
            for _ in range(shares):
                total = total + refs.pop(0)[...].astype(f32)
            width = total.shape[1]
            out_ref[s, :, at : at + width] = total.astype(bf16)
            at += width


def finish(sums, piece):
    counts = [[len(shares) for _, shares in slabs] for slabs in sums]
    values = [value for slabs in sums for total, shares in slabs for value in (total, *shares)]
    out = (len(sums), piece, sum(total.shape[1] for total, _ in sums[0]))
    return pl.pallas_call(
        functools.partial(finish_kernel, counts),
        grid=(1,),
        out_shape=jax.ShapeDtypeStruct(out, bf16),
        in_specs=[full(*value.shape) for value in values],
        out_specs=full(*out),
        compiler_params=params(),
        cost_estimate=busy(0),
        name="finish",
    )(*values)


def nothing(*refs):
    pass


def later_than(value, after):
    anywhere = pl.BlockSpec(memory_space=pl.ANY)
    return pl.pallas_call(
        nothing,
        out_shape=jax.ShapeDtypeStruct(value.shape, value.dtype),
        in_specs=[anywhere] * (1 + len(after)),
        out_specs=anywhere,
        input_output_aliases={0: 0},
        compiler_params=params(1),
        cost_estimate=busy(0),
        name="later_than",
    )(value, *after)


def body(qkv_tokens, sign_bits, out_weight):
    partners, blocks = lax.axis_size("head"), lax.axis_size("seq")
    me, index = lax.axis_index("head"), lax.axis_index("seq")
    seqs = qkv_tokens.shape[0]
    all_heads, dh = sign_bits.shape[0], sign_bits.shape[-1]
    parts = CHUNKS
    heads = all_heads // parts
    levels = (blocks // GROUP).bit_length() - 1
    x = qkv_tokens.transpose(0, 2, 1, 3)
    piece = x.shape[2]
    where = jnp.stack(
        [me, index % GROUP] + [(index // GROUP >> l) & 1 for l in range(levels)]
    ).astype(jnp.int32)
    work = [(s, c) for s in range(seqs) for c in range(parts)]

    outer, shape = range(2, partners, 2), (piece, x.shape[3] // partners)
    beside = [(s, kind, 1) for s in range(seqs) for kind in (0, 1, 2)]
    beside += [
        (s, kind, k + 1)
        for s in range(seqs)
        for kind in (0, 1, 2)
        for k in outer
        if s > 0 or kind == 0
    ]
    straight = [[[(x, 0, kind, k) for kind in (1, 2)]] for k in range(2, partners)]
    *first, near = pack(where, [*straight, [[(x, *entry) for entry in beside]]], shape, 60)
    first = [swap(value, "head", k + 2) for k, value in enumerate(first)]
    near = swap(near, "head", 1)
    messages = [(s, (1, 2)) for s in range(1, seqs)] + [(s, (0,)) for s in range(seqs)]
    wanted = [
        [
            [(x, s, kind, k) for kind in kinds],
            [(near, 0, beside.index((s, kind, k + 1)), None) for kind in kinds],
        ]
        for s, kinds in messages
        for k in outer
    ]
    wanted.append([[(x, s, kind, 0) for kind in (0, 1, 2)] for s in range(seqs)])
    *packed, own_rows = pack(where, wanted, shape, 20)
    packed = [swap(value, "head", k) for value, k in zip(packed, list(outer) * len(messages))]
    packed = [packed[n * len(outer) : (n + 1) * len(outer)] for n in range(len(messages))]
    asked = packed[seqs - 1 :]

    def pieces(n, kind):
        s, c = work[n]
        found = [(own_rows, s, kind, c), (near, 0, beside.index((s, kind, 1)), c)]
        if s == 0 and kind > 0:
            return found + [(value, 0, kind - 1, c) for value in first]
        row, at = (packed[s - 1], kind - 1) if kind > 0 else (asked[s], 0)
        return found + [(value, half, at, c) for value in row for half in (0, 1)]

    maps = integer_maps(sign_bits)

    last = [own_rows]
    begun, chains, ends, locals_, own, other, totals = {}, {}, {}, {}, {}, {}, {}

    def early(n):
        begun[n] = early_sums(
            where, maps, pieces(n, 1)[:2], pieces(n, 2)[:2], work[n][1], heads, dh, piece, last
        )
        last[:] = [begun[n][0]]

    def state(n):
        feats, mine, *others = block_state(
            where,
            maps,
            pieces(n, 1)[2:],
            pieces(n, 2)[2:],
            begun[n][1],
            work[n][1],
            heads,
            dh,
            piece,
            last,
            3 if n else 0,
        )
        begun[n] = begun[n][0], feats
        chains[n] = [mine] + [swap(value, "seq", m + 1) for m, value in enumerate(others)]
        last[:] = [mine]

    def step(n):
        first_out, *others = chain_step(where, levels, chains[n], last)
        last[:] = [first_out]
        if others:
            ends[n] = [first_out] + [swap(value, "seq", m + 1) for m, value in enumerate(others)]
        else:
            chains[n] = chains[n] + [swap(first_out, "seq", GROUP << (len(chains[n]) - GROUP))]

    def local(n):
        locals_[n] = attend_local(
            where, maps, begun[n], pieces(n, 0), pieces(n, 2), work[n][1], heads, dh, piece, last
        )
        last[:] = [locals_[n][0]]

    def attend(n):
        stay, leave = attend_prior(
            where, *locals_[n], ends[n], partners, dh, last, 1 if n + 1 < len(work) else 0
        )
        own.setdefault(work[n][0], []).append(stay)
        other.setdefault(work[n][0], []).append(swap(leave, "head", 1))
        last[:] = [stay]

    def multiply(s, slab):
        if slab == 1:
            for key in totals:
                if key[0] < s:
                    last.extend(totals[key][1])
        total, *shares = project(
            own[s], other[s], out_weight, other_weight, slabs[s], slab, last, 0 if s == seqs - 1 else 6
        )
        totals[s, slab] = total, [swap(v, "head", 2 * (g + 1)) for g, v in enumerate(shares)]
        last[:] = [total]

    slabs = [SLABS[0]] * (seqs - 1) + [SLABS[1]]
    plan = []
    for n, (s, c) in enumerate(work):
        came = 22 * s + 8 * c / parts
        end = came + 22 + 9 * levels
        plan.append((came, state, n))
        if n > 0:
            plan.append((came - 21, early, n))
        plan += [(came + 12 + 9 * j, step, n) for j in range(levels + 1)]
        plan.append((end - 7, local, n))
        plan.append((end + 4, attend, n))
        if c == parts - 1:
            plan += [(end + 6 + 3.5 * j, multiply, s, j) for j in range(len(slabs[s]))]
    plan = sorted(plan, key=lambda entry: entry[0])
    early(0)
    state(0)
    other_weight = swap(later_than(out_weight, last), "head", 1)
    for _, act, *which in plan:
        if (act, which) != (state, [0]):
            act(*which)

    return finish([[totals[s, n] for n in range(len(slabs[s]))] for s in range(seqs)], piece)


def solution(mesh):
    return jax.shard_map(
        body,
        mesh=mesh,
        in_specs=(
            P(None, ("seq", "head"), None, None),
            P("head", None, None, None),
            P("head", None),
        ),
        out_specs=P(None, ("seq", "head"), None),
        check_vma=False,
    )
```

```python
import functools
import math

import jax
import jax.numpy as jnp
import numpy as np
from jax import lax
from jax.experimental import pallas as pl
from jax.experimental.pallas import tpu as pltpu
from jax.sharding import PartitionSpec as P

logit_divisor = 1.3
norm_epsilon = 1e-06
CHUNKS = 1

SLABS = (8,), (4, 3, 1)

bf16, f32 = jnp.bfloat16, jnp.float32
ROW_TILE = 16
STEP_US = 4
GROUP = 4


def params(mebibytes=20):
    return pltpu.CompilerParams(vmem_limit_bytes=mebibytes * 1024 * 1024)


def full(*shape):
    return pl.BlockSpec(shape, lambda *_: (0,) * len(shape))


def ordered(kernel, count, skip):
    return lambda *refs: kernel(*refs[:skip], *refs[skip + count :])


def busy(microseconds):
    return pl.CostEstimate(flops=int(microseconds * 1e9), bytes_accessed=0, transcendentals=0)


def waits(after):
    return [pl.BlockSpec(memory_space=pl.ANY)] * len(after)


def swap(value, axis, bit):
    return lax.ppermute(value, axis, [(j, j ^ bit) for j in range(lax.axis_size(axis))])


def sign_matrix(order):
    ids = np.arange(order)
    common = ids[:, None] & ids[None, :]
    parity = np.zeros_like(common)
    while common.any():
        parity ^= common & 1
        common = common >> 1
    return (1 - 2 * parity).astype(np.float32)


def maps_kernel(bits_ref, had_ref, maps_ref):
    had = had_ref[...]
    dh = had.shape[0]
    for h in range(bits_ref.shape[0]):
        for b in range(bits_ref.shape[1]):
            signs = (2 * bits_ref[h, b] - 1).astype(f32)
            inner = jnp.dot((had * signs[2:3]).astype(bf16), had, preferred_element_type=f32)
            outer = jnp.dot((inner * signs[1:2]).astype(bf16), had, preferred_element_type=f32)
            whole = outer * signs[0:1]
            near = whole.astype(bf16)
            rows = slice(b * dh, (b + 1) * dh)
            maps_ref[h, rows, :dh] = near
            maps_ref[h, rows, dh:] = (whole - near.astype(f32)).astype(bf16)


def integer_maps(sign_bits):
    heads, blocks, kinds, dh = sign_bits.shape
    return pl.pallas_call(
        maps_kernel,
        grid=(1,),
        out_shape=jax.ShapeDtypeStruct((heads, blocks * dh, 2 * dh), bf16),
        in_specs=[full(heads, blocks, kinds, dh), full(dh, dh)],
        out_specs=full(heads, blocks * dh, 2 * dh),
        compiler_params=params(),
        cost_estimate=busy(0),
        name="integer_maps",
    )(sign_bits, jnp.asarray(sign_matrix(dh), bf16))


def features(rows, maps):
    dh = rows.shape[-1]
    wide = rows.astype(f32)
    mean = jnp.sum(wide * wide, axis=-1, keepdims=True) * (1.0 / dh)
    scale = lax.rsqrt(mean + norm_epsilon) * (logit_divisor / dh**0.25 / dh)
    twice = jnp.concatenate([rows, rows], axis=1)
    product = lax.dot_general(twice, maps, (((1,), (1,)), ((), ())), preferred_element_type=f32)
    return jnp.exp(product * scale).astype(bf16)


def pack_kernel(places, arrays, where_ref, *refs):
    ins, outs, sems = refs[:arrays], refs[arrays:-1], refs[-1]
    copies = []
    for n, (which, first, second, k, out, index) in enumerate(places):
        width = outs[out].shape[-1]
        start = 0 if k is None else pl.multiple_of((where_ref[0] ^ k) * width, width)
        source = ins[which].at[first, second, :, pl.ds(start, width)]
        copies.append(pltpu.make_async_copy(source, outs[out].at[index], sems.at[n]))
    for copy in copies:
        copy.start()
    for copy in copies:
        copy.wait()


def pack(where, wanted, shape, mebibytes):
    arrays, places, shapes = [], [], []
    for out, table in enumerate(wanted):
        shapes.append((len(table), len(table[0]), *shape))
        for i, row in enumerate(table):
            for j, (array, first, second, k) in enumerate(row):
                if not any(array is known for known in arrays):
                    arrays.append(array)
                which = [array is known for known in arrays].index(True)
                places.append((which, first, second, k, out, (i, j)))
    return pl.pallas_call(
        functools.partial(pack_kernel, places, len(arrays)),
        out_shape=[jax.ShapeDtypeStruct(shape, bf16) for shape in shapes],
        in_specs=[pl.BlockSpec(memory_space=pltpu.SMEM)]
        + [pl.BlockSpec(memory_space=pl.ANY)] * len(arrays),
        out_specs=[pl.BlockSpec(memory_space=pltpu.VMEM)] * len(shapes),
        scratch_shapes=[pltpu.SemaphoreType.DMA((len(places),))],
        compiler_params=params(mebibytes),
        cost_estimate=busy(0),
        name="pack",
    )(where, *arrays)


def operands(pieces, rows, width):
    specs = []
    for _, lead, kind, col in pieces:
        if callable(col):
            at = lambda _, where, lead=lead, kind=kind, col=col: (lead, kind, 0, col(where))
        else:
            at = lambda _, where, at=(lead, kind, 0, col): at
        specs.append(pl.BlockSpec((1, 1, rows, width), at))
    return [piece[0] for piece in pieces], specs


def joined(refs, cut):
    return jnp.concatenate([ref[0, 0, :, cut] for ref in refs], axis=0)


def sums_kernel(pieces, heads, dh, maps_ref, *refs):
    k_refs, v_refs = refs[:pieces], refs[pieces : 2 * pieces]
    *before, feats_ref, sums_ref = refs[2 * pieces :]
    for i in range(heads):
        cut = slice(i * dh, (i + 1) * dh)
        keys, values = joined(k_refs, cut), joined(v_refs, cut)
        feats = features(keys, maps_ref[i])
        feats_ref[i] = feats
        state = lax.dot_general(
            values, feats, (((0,), (0,)), ((), ())), preferred_element_type=f32
        )
        total = jnp.sum(feats.astype(f32), axis=0, keepdims=True)
        total = jnp.broadcast_to(total, (sums_ref.shape[1] - dh, total.shape[1]))
        sums = jnp.concatenate([state, total], axis=0)
        sums_ref[i] = before[0][i] + sums if before else sums


def early_sums(where, maps, keys, values, part, heads, dh, piece, after):
    feat = maps.shape[1]
    rows = len(keys) * piece
    arrays, specs = operands(keys + values, piece, heads * dh)
    return pl.pallas_call(
        ordered(functools.partial(sums_kernel, len(keys), heads, dh), 1 + len(after), 0),
        out_shape=[
            jax.ShapeDtypeStruct((heads, rows, feat), bf16),
            jax.ShapeDtypeStruct((heads, dh + 8, feat), f32),
        ],
        grid_spec=pltpu.PrefetchScalarGridSpec(
            num_scalar_prefetch=1,
            grid=(1,),
            in_specs=waits(after)
            + [pl.BlockSpec((heads, feat, 2 * dh), lambda *_: (part, 0, 0))]
            + specs,
            out_specs=[full(heads, rows, feat), full(heads, dh + 8, feat)],
        ),
        compiler_params=params(),
        cost_estimate=busy(0),
        name="early_sums",
    )(where, *after, maps, *arrays)


def state_kernel(pieces, heads, dh, where_ref, maps_ref, *refs):
    *ins, feats_ref, sums_ref = refs[: 2 * pieces + 2] + refs[-1:]
    share_refs = refs[2 * pieces + 2 : -1]
    sums_kernel(pieces, heads, dh, maps_ref, *ins, feats_ref, sums_ref)
    share = heads // GROUP
    pad = jnp.zeros((ROW_TILE - share, feats_ref.shape[-1]), f32)
    states = [sums_ref[i] for i in range(heads)]
    shares = []
    for g in range(GROUP):
        mine = states[g * share : (g + 1) * share]
        shares.append(
            jnp.concatenate([v[:dh] for v in mine] + [v[dh : dh + 1] for v in mine] + [pad], axis=0)
        )
    for m, ref in enumerate(share_refs):
        ref[...] = chosen(shares, where_ref[1] ^ m).astype(ref.dtype)


def chosen(values, index):
    result = values[0]
    for n, value in enumerate(values[1:]):
        result = jnp.where(index == n + 1, value, result)
    return result


def block_state(where, maps, keys, values, before, part, heads, dh, piece, after, beside):
    feat = maps.shape[1]
    rows = len(keys) * piece
    height = heads // GROUP * dh + ROW_TILE
    arrays, specs = operands(keys + values, piece, heads * dh)
    return pl.pallas_call(
        ordered(functools.partial(state_kernel, len(keys), heads, dh), len(after), 1),
        out_shape=[
            jax.ShapeDtypeStruct((heads, rows, feat), bf16),
            jax.ShapeDtypeStruct((height, feat), f32),
        ]
        + [jax.ShapeDtypeStruct((height, feat), bf16)] * (GROUP - 1),
        grid_spec=pltpu.PrefetchScalarGridSpec(
            num_scalar_prefetch=1,
            scratch_shapes=[pltpu.VMEM(before.shape, f32)],
            grid=(1,),
            in_specs=waits(after)
            + [
                pl.BlockSpec((heads, feat, 2 * dh), lambda *_: (part, 0, 0)),
            ]
            + specs
            + [full(*before.shape)],
            out_specs=[full(heads, rows, feat)] + [full(height, feat)] * GROUP,
        ),
        compiler_params=params(),
        cost_estimate=busy(beside),
        name="block_state",
    )(where, *after, maps, *arrays, before)


def step_kernel(levels, where_ref, *refs):
    ins = refs[: len(refs) - (1 if len(refs) < 2 * GROUP + levels else GROUP)]
    outs = refs[len(ins) :]
    values = [ref[...].astype(f32) for ref in ins[:GROUP]]
    got = [ref[...].astype(f32) for ref in ins[GROUP:]]
    if len(outs) == 1:
        total = values[0]
        for value in values[1:] + got:
            total = total + value
        outs[0][...] = total.astype(bf16)
        return
    prior = jnp.zeros_like(values[0])
    for level, value in enumerate(got):
        prior = prior + jnp.where(where_ref[2 + level] == 1, value, 0.0)
    mine = where_ref[1]
    for m, out in enumerate(outs):
        result = prior
        for other, value in enumerate(values):
            if other != m:
                result = result + jnp.where((mine ^ other) < (mine ^ m), value, 0.0)
        out[...] = result.astype(bf16)


def chain_step(where, levels, values, after, beside):
    shape = values[0].shape
    count = GROUP if len(values) == GROUP + levels else 1
    return pl.pallas_call(
        ordered(functools.partial(step_kernel, levels), len(after), 0),
        grid=(1,),
        out_shape=[jax.ShapeDtypeStruct(shape, bf16)] * count,
        in_specs=waits(after)
        + [pl.BlockSpec(memory_space=pltpu.SMEM)]
        + [full(*shape)] * len(values),
        out_specs=[full(*shape)] * count,
        compiler_params=params(),
        cost_estimate=busy(beside),
        name="chain_step",
    )(*after, where, *values)


def local_kernel(partners, heads, dh, where_ref, maps_ref, early_ref, late_ref, *refs):
    q_refs, v_refs = refs[:partners], refs[partners : 2 * partners]
    query_feats_ref, local_ref = refs[2 * partners :]
    piece = q_refs[0].shape[2]
    rows = partners * piece
    me = where_ref[0]

    def places(shape, dim):
        ids = lax.broadcasted_iota(jnp.int32, shape, dim)
        result = ids + (me ^ 0) * piece
        for k in range(1, partners):
            result = jnp.where(ids >= k * piece, ids + ((me ^ k) - k) * piece, result)
        return result

    causal = places((rows, 1), 0) >= places((1, rows), 1)
    ones = jnp.ones((rows, dh), bf16)
    for i in range(heads):
        cut = slice(i * dh, (i + 1) * dh)
        queries, values = joined(q_refs, cut), joined(v_refs, cut)
        query_feats = features(queries, maps_ref[i])
        query_feats_ref[i] = query_feats
        scores = lax.dot_general(
            query_feats,
            jnp.concatenate([early_ref[i], late_ref[i]], axis=0),
            (((1,), (1,)), ((), ())),
            preferred_element_type=f32,
        )
        weights = jnp.where(causal, scores, 0.0).astype(bf16)
        local_ref[i] = jnp.dot(
            weights, jnp.concatenate([values, ones], axis=1), preferred_element_type=f32
        )


def attend_local(where, maps, feats, queries, values, part, heads, dh, piece, after):
    partners = len(queries)
    feat = maps.shape[1]
    rows = partners * piece
    arrays, specs = operands(queries + values, piece, heads * dh)
    return pl.pallas_call(
        ordered(functools.partial(local_kernel, partners, heads, dh), len(after), 1),
        out_shape=[
            jax.ShapeDtypeStruct((heads, rows, feat), bf16),
            jax.ShapeDtypeStruct((heads, rows, 2 * dh), f32),
        ],
        grid_spec=pltpu.PrefetchScalarGridSpec(
            num_scalar_prefetch=1,
            grid=(1,),
            in_specs=waits(after)
            + [
                pl.BlockSpec((heads, feat, 2 * dh), lambda *_: (part, 0, 0)),
                *[full(*part_.shape) for part_ in feats],
            ]
            + specs,
            out_specs=[full(heads, rows, feat), full(heads, rows, 2 * dh)],
        ),
        compiler_params=params(),
        cost_estimate=busy(3),
        name="attend_local",
    )(where, *after, maps, *feats, *arrays)


def prior_kernel(partners, heads, dh, where_ref, query_feats_ref, local_ref, *refs):
    share_refs, (stay_ref, leave_ref) = refs[:GROUP], refs[GROUP:]
    piece = query_feats_ref.shape[1] // partners
    share = heads // GROUP
    for i in range(heads):
        j = i % share
        state, total = slice(j * dh, (j + 1) * dh), slice(share * dh, share * dh + ROW_TILE)
        source = where_ref[1] ^ (i // share)
        prior = chosen([ref[state, :] for ref in share_refs], source)
        tail = chosen([ref[total, :] for ref in share_refs], source)
        tail = jnp.broadcast_to(tail[j : j + 1, :], prior.shape)
        both = local_ref[i] + lax.dot_general(
            query_feats_ref[i],
            jnp.concatenate([prior, tail], axis=0),
            (((1,), (1,)), ((), ())),
            preferred_element_type=f32,
        )
        attended = (both[:, :dh] / both[:, dh:]).astype(bf16)
        for k in range(partners):
            out = leave_ref if k & 1 else stay_ref
            out[k // 2, :, i * dh : (i + 1) * dh] = attended[k * piece : (k + 1) * piece]


def attend_prior(where, query_feats, local, shares, partners, dh, after, beside):
    heads, rows, feat = query_feats.shape
    out = jax.ShapeDtypeStruct((partners // 2, rows // partners, heads * dh), bf16)
    return pl.pallas_call(
        ordered(functools.partial(prior_kernel, partners, heads, dh), len(after), 0),
        grid=(1,),
        out_shape=[out, out],
        in_specs=waits(after)
        + [pl.BlockSpec(memory_space=pltpu.SMEM)]
        + [full(*value.shape) for value in (query_feats, local, *shares)],
        out_specs=[full(*out.shape)] * 2,
        compiler_params=params(),
        cost_estimate=busy(beside),
        name="attend_prior",
    )(*after, where, query_feats, local, *shares)


def project_kernel(parts, *refs):
    own_refs, other_refs = refs[:parts], refs[parts : 2 * parts]
    own_w, other_w, stay_ref, *leave_refs = refs[2 * parts :]
    groups, piece, width = own_refs[0].shape
    acc = None
    for lhs_refs, w_ref in ((own_refs, own_w), (other_refs, other_w)):
        for p, ref in enumerate(lhs_refs):
            lhs = ref[...].reshape(groups * piece, width)
            term = jnp.dot(
                lhs, w_ref[p * width : (p + 1) * width, :], preferred_element_type=f32
            )
            acc = term if acc is None else acc + term
    stay_ref[...] = acc[:piece]
    for g, ref in enumerate(leave_refs):
        ref[...] = acc[(g + 1) * piece : (g + 2) * piece].astype(bf16)


def project(own, other, own_w, other_w, slabs, slab, after, beside):
    parts, (groups, piece, width) = len(own), own[0].shape
    depth, cols = own_w.shape
    unit = cols // sum(slabs)
    tile = math.gcd(cols * slabs[slab] // sum(slabs), 1024)
    tile = math.gcd(tile, sum(slabs[:slab]) * unit) if slab else tile
    first, cols = sum(slabs[:slab]) * unit // tile, slabs[slab] * unit
    lhs = pl.BlockSpec((groups, piece, width), lambda n: (0, 0, 0))
    weight = pl.BlockSpec((depth, tile), lambda n: (0, first + n))
    out = pl.BlockSpec((piece, tile), lambda n: (0, n))
    return pl.pallas_call(
        ordered(functools.partial(project_kernel, parts), len(after), 0),
        grid=(cols // tile,),
        out_shape=[jax.ShapeDtypeStruct((piece, cols), f32)]
        + [jax.ShapeDtypeStruct((piece, cols), bf16)] * (groups - 1),
        in_specs=waits(after) + [lhs] * (2 * parts) + [weight, weight],
        out_specs=[out] * groups,
        compiler_params=params(),
        cost_estimate=busy(beside),
        name="project",
    )(*after, *own, *other, own_w, other_w)


def finish_kernel(counts, *refs):
    refs = list(refs)
    out_ref = refs.pop()
    for s, slabs in enumerate(counts):
        at = 0
        for shares in slabs:
            total = refs.pop(0)[...]
            for _ in range(shares):
                total = total + refs.pop(0)[...].astype(f32)
            width = total.shape[1]
            out_ref[s, :, at : at + width] = total.astype(bf16)
            at += width


def finish(sums, piece):
    counts = [[len(shares) for _, shares in slabs] for slabs in sums]
    values = [value for slabs in sums for total, shares in slabs for value in (total, *shares)]
    out = (len(sums), piece, sum(total.shape[1] for total, _ in sums[0]))
    return pl.pallas_call(
        functools.partial(finish_kernel, counts),
        grid=(1,),
        out_shape=jax.ShapeDtypeStruct(out, bf16),
        in_specs=[full(*value.shape) for value in values],
        out_specs=full(*out),
        compiler_params=params(),
        cost_estimate=busy(0),
        name="finish",
    )(*values)


def nothing(*refs):
    pass


def later_than(value, after):
    anywhere = pl.BlockSpec(memory_space=pl.ANY)
    return pl.pallas_call(
        nothing,
        out_shape=jax.ShapeDtypeStruct(value.shape, value.dtype),
        in_specs=[anywhere] * (1 + len(after)),
        out_specs=anywhere,
        input_output_aliases={0: 0},
        compiler_params=params(1),
        cost_estimate=busy(0),
        name="later_than",
    )(value, *after)


def body(qkv_tokens, sign_bits, out_weight):
    partners, blocks = lax.axis_size("head"), lax.axis_size("seq")
    me, index = lax.axis_index("head"), lax.axis_index("seq")
    seqs = qkv_tokens.shape[0]
    all_heads, dh = sign_bits.shape[0], sign_bits.shape[-1]
    parts = CHUNKS
    heads = all_heads // parts
    levels = (blocks // GROUP).bit_length() - 1
    x = qkv_tokens.transpose(0, 2, 1, 3)
    piece = x.shape[2]
    where = jnp.stack(
        [me, index % GROUP] + [(index // GROUP >> l) & 1 for l in range(levels)]
    ).astype(jnp.int32)
    work = [(s, c) for s in range(seqs) for c in range(parts)]

    outer, shape = range(2, partners, 2), (piece, x.shape[3] // partners)
    beside = [(s, kind, 1) for s in range(seqs) for kind in (0, 1, 2)]
    beside += [
        (s, kind, k + 1)
        for s in range(seqs)
        for kind in (0, 1, 2)
        for k in outer
        if s > 0 or kind == 0
    ]
    straight = [[[(x, 0, kind, k) for kind in (1, 2)]] for k in range(2, partners)]
    *first, near = pack(where, [*straight, [[(x, *entry) for entry in beside]]], shape, 60)
    first = [swap(value, "head", k + 2) for k, value in enumerate(first)]
    near = swap(near, "head", 1)
    messages = [(s, (1, 2)) for s in range(1, seqs)] + [(s, (0,)) for s in range(seqs)]
    wanted = [
        [
            [(x, s, kind, k) for kind in kinds],
            [(near, 0, beside.index((s, kind, k + 1)), None) for kind in kinds],
        ]
        for s, kinds in messages
        for k in outer
    ]
    wanted.append([[(x, s, kind, 0) for kind in (0, 1, 2)] for s in range(seqs)])
    *packed, own_rows = pack(where, wanted, shape, 20)
    packed = [swap(value, "head", k) for value, k in zip(packed, list(outer) * len(messages))]
    packed = [packed[n * len(outer) : (n + 1) * len(outer)] for n in range(len(messages))]
    asked = packed[seqs - 1 :]

    def pieces(n, kind):
        s, c = work[n]
        found = [(own_rows, s, kind, c), (near, 0, beside.index((s, kind, 1)), c)]
        if s == 0 and kind > 0:
            return found + [(value, 0, kind - 1, c) for value in first]
        row, at = (packed[s - 1], kind - 1) if kind > 0 else (asked[s], 0)
        return found + [(value, half, at, c) for value in row for half in (0, 1)]

    maps = integer_maps(sign_bits)

    last = [own_rows]
    begun, chains, ends, locals_, own, other, totals = {}, {}, {}, {}, {}, {}, {}

    def early(n):
        begun[n] = early_sums(
            where, maps, pieces(n, 1)[:2], pieces(n, 2)[:2], work[n][1], heads, dh, piece, last
        )
        last[:] = [begun[n][0]]

    def state(n):
        feats, mine, *others = block_state(
            where,
            maps,
            pieces(n, 1)[2:],
            pieces(n, 2)[2:],
            begun[n][1],
            work[n][1],
            heads,
            dh,
            piece,
            last,
            3 if n else 0,
        )
        begun[n] = begun[n][0], feats
        chains[n] = [mine] + [swap(value, "seq", m + 1) for m, value in enumerate(others)]
        last[:] = [mine]

    def step(n):
        first_out, *others = chain_step(where, levels, chains[n], last, STEP_US if n and len(chains[n]) == GROUP else 0)
        last[:] = [first_out]
        if others:
            ends[n] = [first_out] + [swap(value, "seq", m + 1) for m, value in enumerate(others)]
        else:
            chains[n] = chains[n] + [swap(first_out, "seq", GROUP << (len(chains[n]) - GROUP))]

    def local(n):
        locals_[n] = attend_local(
            where, maps, begun[n], pieces(n, 0), pieces(n, 2), work[n][1], heads, dh, piece, last
        )
        last[:] = [locals_[n][0]]

    def attend(n):
        stay, leave = attend_prior(
            where, *locals_[n], ends[n], partners, dh, last, 1 if n + 1 < len(work) else 0
        )
        own.setdefault(work[n][0], []).append(stay)
        other.setdefault(work[n][0], []).append(swap(leave, "head", 1))
        last[:] = [stay]

    def multiply(s, slab):
        if slab == 1:
            for key in totals:
                if key[0] < s:
                    last.extend(totals[key][1])
        total, *shares = project(
            own[s], other[s], out_weight, other_weight, slabs[s], slab, last, 0 if s == seqs - 1 else 6
        )
        totals[s, slab] = total, [swap(v, "head", 2 * (g + 1)) for g, v in enumerate(shares)]
        last[:] = [total]

    slabs = [SLABS[0]] * (seqs - 1) + [SLABS[1]]
    plan = []
    for n, (s, c) in enumerate(work):
        came = 22 * s + 8 * c / parts
        end = came + 22 + 9 * levels
        plan.append((came, state, n))
        if n > 0:
            plan.append((came - 21, early, n))
        plan += [(came + 12 + 9 * j, step, n) for j in range(levels + 1)]
        plan.append((end - 7, local, n))
        plan.append((end, attend, n))
        if c == parts - 1:
            plan += [(end + 6 + 3.5 * j, multiply, s, j) for j in range(len(slabs[s]))]
    plan = sorted(plan, key=lambda entry: entry[0])
    early(0)
    state(0)
    other_weight = swap(later_than(out_weight, last), "head", 1)
    for _, act, *which in plan:
        if (act, which) != (state, [0]):
            act(*which)

    return finish([[totals[s, n] for n in range(len(slabs[s]))] for s in range(seqs)], piece)


def solution(mesh):
    return jax.shard_map(
        body,
        mesh=mesh,
        in_specs=(
            P(None, ("seq", "head"), None, None),
            P("head", None, None, None),
            P("head", None),
        ),
        out_specs=P(None, ("seq", "head"), None),
        check_vma=False,
    )
```

```python
import functools
import math

import jax
import jax.numpy as jnp
import numpy as np
from jax import lax
from jax.experimental import pallas as pl
from jax.experimental.pallas import tpu as pltpu
from jax.sharding import PartitionSpec as P

logit_divisor = 1.3
norm_epsilon = 1e-06
SLABS = (8,), (4, 3, 1)

bf16, f32 = jnp.bfloat16, jnp.float32
ROW_TILE = 16
STEP_US = 4
GROUP = 4


def params(mebibytes=20):
    return pltpu.CompilerParams(vmem_limit_bytes=mebibytes * 1024 * 1024)


def vmem(count):
    return [pl.BlockSpec(memory_space=pltpu.VMEM)] * count


def smem():
    return pl.BlockSpec(memory_space=pltpu.SMEM)


def ordered(kernel, count, skip):
    return lambda *refs: kernel(*refs[:skip], *refs[skip + count :])


def busy(microseconds):
    return pl.CostEstimate(flops=int(microseconds * 1e9), bytes_accessed=0, transcendentals=0)


def waits(after):
    return [pl.BlockSpec(memory_space=pl.ANY)] * len(after)


def swap(value, axis, bit):
    return lax.ppermute(value, axis, [(j, j ^ bit) for j in range(lax.axis_size(axis))])


def sign_matrix(order):
    ids = np.arange(order)
    common = ids[:, None] & ids[None, :]
    parity = np.zeros_like(common)
    while common.any():
        parity ^= common & 1
        common = common >> 1
    return (1 - 2 * parity).astype(np.float32)


def maps_kernel(bits_ref, had_ref, maps_ref):
    had = had_ref[...]
    dh = had.shape[0]
    for h in range(bits_ref.shape[0]):
        for b in range(bits_ref.shape[1]):
            signs = (2 * bits_ref[h, b] - 1).astype(f32)
            inner = jnp.dot((had * signs[2:3]).astype(bf16), had, preferred_element_type=f32)
            outer = jnp.dot((inner * signs[1:2]).astype(bf16), had, preferred_element_type=f32)
            whole = outer * signs[0:1]
            near = whole.astype(bf16)
            rows = slice(b * dh, (b + 1) * dh)
            maps_ref[h, rows, :dh] = near
            maps_ref[h, rows, dh:] = (whole - near.astype(f32)).astype(bf16)


def integer_maps(sign_bits):
    heads, blocks, _, dh = sign_bits.shape
    return pl.pallas_call(
        maps_kernel,
        out_shape=jax.ShapeDtypeStruct((heads, blocks * dh, 2 * dh), bf16),
        in_specs=vmem(2),
        out_specs=vmem(1)[0],
        compiler_params=params(),
        cost_estimate=busy(0),
        name="integer_maps",
    )(sign_bits, jnp.asarray(sign_matrix(dh), bf16))


def features(rows, maps):
    dh = rows.shape[-1]
    wide = rows.astype(f32)
    mean = jnp.sum(wide * wide, axis=-1, keepdims=True) * (1.0 / dh)
    scale = lax.rsqrt(mean + norm_epsilon) * (logit_divisor / dh**0.25 / dh)
    twice = jnp.concatenate([rows, rows], axis=1)
    product = lax.dot_general(twice, maps, (((1,), (1,)), ((), ())), preferred_element_type=f32)
    return jnp.exp(product * scale).astype(bf16)


def pack_kernel(places, arrays, where_ref, *refs):
    ins, outs, sems = refs[:arrays], refs[arrays:-1], refs[-1]
    copies = []
    for n, (which, first, second, k, out, i, j, count) in enumerate(places):
        width = outs[out].shape[-1]
        start = 0 if k is None else pl.multiple_of((where_ref[0] ^ k) * width, width)
        source = ins[which].at[first, pl.ds(second, count), :, pl.ds(start, width)]
        copies.append(pltpu.make_async_copy(source, outs[out].at[i, pl.ds(j, count)], sems.at[n]))
    for copy in copies:
        copy.start()
    for copy in copies:
        copy.wait()


def pack(where, wanted, shape, mebibytes):
    arrays, places, shapes = [], [], []
    for out, table in enumerate(wanted):
        shapes.append((len(table), len(table[0]), *shape))
        for i, row in enumerate(table):
            for j, (array, first, second, k) in enumerate(row):
                if not any(array is known for known in arrays):
                    arrays.append(array)
                which = [array is known for known in arrays].index(True)
                before = places[-1] if places else None
                if before and before[:6] == (which, first, second - before[7], k, out, i):
                    places[-1] = (*before[:7], before[7] + 1)
                else:
                    places.append((which, first, second, k, out, i, j, 1))
    return pl.pallas_call(
        functools.partial(pack_kernel, places, len(arrays)),
        out_shape=[jax.ShapeDtypeStruct(shape, bf16) for shape in shapes],
        in_specs=[pl.BlockSpec(memory_space=pltpu.SMEM)]
        + [pl.BlockSpec(memory_space=pl.ANY)] * len(arrays),
        out_specs=[pl.BlockSpec(memory_space=pltpu.VMEM)] * len(shapes),
        scratch_shapes=[pltpu.SemaphoreType.DMA((len(places),))],
        compiler_params=params(mebibytes),
        cost_estimate=busy(0),
        name="pack",
    )(where, *arrays)


def joined(refs, places, cut):
    return jnp.concatenate(
        [ref[lead, kind, :, cut] for ref, (lead, kind) in zip(refs, places)], axis=0
    )


def sums_kernel(k_at, v_at, heads, dh, maps_ref, *refs):
    pieces = len(k_at)
    k_refs, v_refs = refs[:pieces], refs[pieces : 2 * pieces]
    *before, feats_ref, sums_ref = refs[2 * pieces :]
    for i in range(heads):
        cut = slice(i * dh, (i + 1) * dh)
        keys, values = joined(k_refs, k_at, cut), joined(v_refs, v_at, cut)
        feats = features(keys, maps_ref[i])
        feats_ref[i] = feats
        state = lax.dot_general(
            values, feats, (((0,), (0,)), ((), ())), preferred_element_type=f32
        )
        total = jnp.sum(feats.astype(f32), axis=0, keepdims=True)
        total = jnp.broadcast_to(total, (sums_ref.shape[1] - dh, total.shape[1]))
        sums = jnp.concatenate([state, total], axis=0)
        sums_ref[i] = before[0][i] + sums if before else sums


def early_sums(maps, keys, values, heads, dh, piece, after):
    feat = maps.shape[1]
    rows = len(keys) * piece
    (arrays, k_at), (others, v_at) = split(keys), split(values)
    return pl.pallas_call(
        ordered(functools.partial(sums_kernel, k_at, v_at, heads, dh), len(after), 0),
        out_shape=[
            jax.ShapeDtypeStruct((heads, rows, feat), bf16),
            jax.ShapeDtypeStruct((heads, dh + 8, feat), f32),
        ],
        in_specs=waits(after) + vmem(1 + 2 * len(keys)),
        out_specs=vmem(2),
        compiler_params=params(),
        cost_estimate=busy(0),
        name="early_sums",
    )(*after, maps, *arrays, *others)


def split(pieces):
    return [piece[0] for piece in pieces], [piece[1:] for piece in pieces]


def state_kernel(k_at, v_at, heads, dh, where_ref, maps_ref, *refs):
    count = 2 * len(k_at) + 2
    *ins, feats_ref, sums_ref = refs[:count] + refs[-1:]
    share_refs = refs[count:-1]
    sums_kernel(k_at, v_at, heads, dh, maps_ref, *ins, feats_ref, sums_ref)
    share = heads // GROUP
    pad = jnp.zeros((ROW_TILE - share, feats_ref.shape[-1]), f32)
    states = [sums_ref[i] for i in range(heads)]
    shares = []
    for g in range(GROUP):
        mine = states[g * share : (g + 1) * share]
        shares.append(
            jnp.concatenate([v[:dh] for v in mine] + [v[dh : dh + 1] for v in mine] + [pad], axis=0)
        )
    for m, ref in enumerate(share_refs):
        ref[...] = chosen(shares, where_ref[1] ^ m).astype(ref.dtype)


def chosen(values, index):
    result = values[0]
    for n, value in enumerate(values[1:]):
        result = jnp.where(index == n + 1, value, result)
    return result


def block_state(where, maps, keys, values, before, heads, dh, piece, after, beside):
    feat = maps.shape[1]
    rows = len(keys) * piece
    height = heads // GROUP * dh + ROW_TILE
    (arrays, k_at), (others, v_at) = split(keys), split(values)
    return pl.pallas_call(
        ordered(functools.partial(state_kernel, k_at, v_at, heads, dh), len(after), 0),
        out_shape=[
            jax.ShapeDtypeStruct((heads, rows, feat), bf16),
            jax.ShapeDtypeStruct((height, feat), f32),
        ]
        + [jax.ShapeDtypeStruct((height, feat), bf16)] * (GROUP - 1),
        in_specs=waits(after) + [smem()] + vmem(2 + 2 * len(keys)),
        out_specs=vmem(1 + GROUP),
        scratch_shapes=[pltpu.VMEM(before.shape, f32)],
        compiler_params=params(),
        cost_estimate=busy(beside),
        name="block_state",
    )(*after, where, maps, *arrays, *others, before)


def step_kernel(levels, where_ref, *refs):
    ins = refs[: len(refs) - (1 if len(refs) < 2 * GROUP + levels else GROUP)]
    outs = refs[len(ins) :]
    values = [ref[...].astype(f32) for ref in ins[:GROUP]]
    got = [ref[...].astype(f32) for ref in ins[GROUP:]]
    if len(outs) == 1:
        total = values[0]
        for value in values[1:] + got:
            total = total + value
        outs[0][...] = total.astype(bf16)
        return
    prior = jnp.zeros_like(values[0])
    for level, value in enumerate(got):
        prior = prior + jnp.where(where_ref[2 + level] == 1, value, 0.0)
    mine = where_ref[1]
    for m, out in enumerate(outs):
        result = prior
        for other, value in enumerate(values):
            if other != m:
                result = result + jnp.where((mine ^ other) < (mine ^ m), value, 0.0)
        out[...] = result.astype(bf16)


def chain_step(where, levels, values, after, beside):
    shape = values[0].shape
    count = GROUP if len(values) == GROUP + levels else 1
    return pl.pallas_call(
        ordered(functools.partial(step_kernel, levels), len(after), 0),
        out_shape=[jax.ShapeDtypeStruct(shape, bf16)] * count,
        in_specs=waits(after) + [smem()] + vmem(len(values)),
        out_specs=vmem(count),
        compiler_params=params(),
        cost_estimate=busy(beside),
        name="chain_step",
    )(*after, where, *values)


def local_kernel(q_at, v_at, heads, dh, where_ref, maps_ref, early_ref, late_ref, *refs):
    partners = len(q_at)
    q_refs, v_refs = refs[:partners], refs[partners : 2 * partners]
    query_feats_ref, local_ref = refs[2 * partners :]
    piece = q_refs[0].shape[2]
    rows = partners * piece
    me = where_ref[0]

    def places(shape, dim):
        ids = lax.broadcasted_iota(jnp.int32, shape, dim)
        result = ids + (me ^ 0) * piece
        for k in range(1, partners):
            result = jnp.where(ids >= k * piece, ids + ((me ^ k) - k) * piece, result)
        return result

    causal = places((rows, 1), 0) >= places((1, rows), 1)
    ones = jnp.ones((rows, dh), bf16)
    for i in range(heads):
        cut = slice(i * dh, (i + 1) * dh)
        queries, values = joined(q_refs, q_at, cut), joined(v_refs, v_at, cut)
        query_feats = features(queries, maps_ref[i])
        query_feats_ref[i] = query_feats
        scores = lax.dot_general(
            query_feats,
            jnp.concatenate([early_ref[i], late_ref[i]], axis=0),
            (((1,), (1,)), ((), ())),
            preferred_element_type=f32,
        )
        weights = jnp.where(causal, scores, 0.0).astype(bf16)
        local_ref[i] = jnp.dot(
            weights, jnp.concatenate([values, ones], axis=1), preferred_element_type=f32
        )


def attend_local(where, maps, feats, queries, values, heads, dh, piece, after):
    feat = maps.shape[1]
    rows = len(queries) * piece
    (arrays, q_at), (others, v_at) = split(queries), split(values)
    return pl.pallas_call(
        ordered(functools.partial(local_kernel, q_at, v_at, heads, dh), len(after), 0),
        out_shape=[
            jax.ShapeDtypeStruct((heads, rows, feat), bf16),
            jax.ShapeDtypeStruct((heads, rows, 2 * dh), f32),
        ],
        in_specs=waits(after) + [smem()] + vmem(1 + len(feats) + 2 * len(queries)),
        out_specs=vmem(2),
        compiler_params=params(),
        cost_estimate=busy(3),
        name="attend_local",
    )(*after, where, maps, *feats, *arrays, *others)


def prior_kernel(partners, heads, dh, where_ref, query_feats_ref, local_ref, *refs):
    share_refs, (stay_ref, leave_ref) = refs[:GROUP], refs[GROUP:]
    piece = query_feats_ref.shape[1] // partners
    share = heads // GROUP
    for i in range(heads):
        j = i % share
        state, total = slice(j * dh, (j + 1) * dh), slice(share * dh, share * dh + ROW_TILE)
        source = where_ref[1] ^ (i // share)
        prior = chosen([ref[state, :] for ref in share_refs], source)
        tail = chosen([ref[total, :] for ref in share_refs], source)
        tail = jnp.broadcast_to(tail[j : j + 1, :], prior.shape)
        both = local_ref[i] + lax.dot_general(
            query_feats_ref[i],
            jnp.concatenate([prior, tail], axis=0),
            (((1,), (1,)), ((), ())),
            preferred_element_type=f32,
        )
        attended = (both[:, :dh] / both[:, dh:]).astype(bf16)
        for k in range(partners):
            out = leave_ref if k & 1 else stay_ref
            out[k // 2, :, i * dh : (i + 1) * dh] = attended[k * piece : (k + 1) * piece]


def attend_prior(where, query_feats, local, shares, partners, dh, after, beside):
    heads, rows, feat = query_feats.shape
    out = jax.ShapeDtypeStruct((partners // 2, rows // partners, heads * dh), bf16)
    return pl.pallas_call(
        ordered(functools.partial(prior_kernel, partners, heads, dh), len(after), 0),
        out_shape=[out, out],
        in_specs=waits(after) + [smem()] + vmem(2 + len(shares)),
        out_specs=vmem(2),
        compiler_params=params(),
        cost_estimate=busy(beside),
        name="attend_prior",
    )(*after, where, query_feats, local, *shares)


def project_kernel(parts, *refs):
    own_refs, other_refs = refs[:parts], refs[parts : 2 * parts]
    own_w, other_w, stay_ref, *leave_refs = refs[2 * parts :]
    groups, piece, width = own_refs[0].shape
    acc = None
    for lhs_refs, w_ref in ((own_refs, own_w), (other_refs, other_w)):
        for p, ref in enumerate(lhs_refs):
            lhs = ref[...].reshape(groups * piece, width)
            term = jnp.dot(
                lhs, w_ref[p * width : (p + 1) * width, :], preferred_element_type=f32
            )
            acc = term if acc is None else acc + term
    stay_ref[...] = acc[:piece]
    for g, ref in enumerate(leave_refs):
        ref[...] = acc[(g + 1) * piece : (g + 2) * piece].astype(bf16)


def project(own, other, own_w, other_w, slabs, slab, after, beside):
    parts, (groups, piece, width) = len(own), own[0].shape
    depth, cols = own_w.shape
    unit = cols // sum(slabs)
    tile = math.gcd(cols * slabs[slab] // sum(slabs), 1024)
    tile = math.gcd(tile, sum(slabs[:slab]) * unit) if slab else tile
    first, cols = sum(slabs[:slab]) * unit // tile, slabs[slab] * unit
    lhs = pl.BlockSpec((groups, piece, width), lambda n: (0, 0, 0))
    weight = pl.BlockSpec((depth, tile), lambda n: (0, first + n))
    out = pl.BlockSpec((piece, tile), lambda n: (0, n))
    return pl.pallas_call(
        ordered(functools.partial(project_kernel, parts), len(after), 0),
        grid=(cols // tile,),
        out_shape=[jax.ShapeDtypeStruct((piece, cols), f32)]
        + [jax.ShapeDtypeStruct((piece, cols), bf16)] * (groups - 1),
        in_specs=waits(after) + [lhs] * (2 * parts) + [weight, weight],
        out_specs=[out] * groups,
        compiler_params=params(),
        cost_estimate=busy(beside),
        name="project",
    )(*after, *own, *other, own_w, other_w)


def finish_kernel(counts, *refs):
    refs = list(refs)
    out_ref = refs.pop()
    for s, slabs in enumerate(counts):
        at = 0
        for shares in slabs:
            total = refs.pop(0)[...]
            for _ in range(shares):
                total = total + refs.pop(0)[...].astype(f32)
            width = total.shape[1]
            out_ref[s, :, at : at + width] = total.astype(bf16)
            at += width


def finish(sums, piece):
    counts = [[len(shares) for _, shares in slabs] for slabs in sums]
    values = [value for slabs in sums for total, shares in slabs for value in (total, *shares)]
    out = (len(sums), piece, sum(total.shape[1] for total, _ in sums[0]))
    return pl.pallas_call(
        functools.partial(finish_kernel, counts),
        grid=(1,),
        out_shape=jax.ShapeDtypeStruct(out, bf16),
        in_specs=[pl.BlockSpec(value.shape, lambda _: (0, 0)) for value in values],
        out_specs=pl.BlockSpec(out, lambda _: (0, 0, 0)),
        compiler_params=params(),
        cost_estimate=busy(0),
        name="finish",
    )(*values)


def nothing(*refs):
    pass


def later_than(value, after):
    anywhere = pl.BlockSpec(memory_space=pl.ANY)
    return pl.pallas_call(
        nothing,
        out_shape=jax.ShapeDtypeStruct(value.shape, value.dtype),
        in_specs=[anywhere] * (1 + len(after)),
        out_specs=anywhere,
        input_output_aliases={0: 0},
        compiler_params=params(1),
        cost_estimate=busy(0),
        name="later_than",
    )(value, *after)


def body(qkv_tokens, sign_bits, out_weight):
    partners, blocks = lax.axis_size("head"), lax.axis_size("seq")
    me, index = lax.axis_index("head"), lax.axis_index("seq")
    seqs = qkv_tokens.shape[0]
    heads, dh = sign_bits.shape[0], sign_bits.shape[-1]
    levels = (blocks // GROUP).bit_length() - 1
    x = qkv_tokens.transpose(0, 2, 1, 3)
    piece = x.shape[2]
    where = jnp.stack(
        [me, index % GROUP] + [(index // GROUP >> l) & 1 for l in range(levels)]
    ).astype(jnp.int32)

    outer, shape = range(2, partners, 2), (piece, x.shape[3] // partners)
    beside = [(s, kind, 1) for s in range(seqs) for kind in (0, 1, 2)]
    beside += [
        (s, kind, k + 1)
        for s in range(seqs)
        for kind in (0, 1, 2)
        for k in outer
        if s > 0 or kind == 0
    ]
    straight = [[[(x, 0, kind, k) for kind in (1, 2)]] for k in range(2, partners)]
    *first, near = pack(where, [*straight, [[(x, *entry) for entry in beside]]], shape, 60)
    first = [swap(value, "head", k + 2) for k, value in enumerate(first)]
    near = swap(near, "head", 1)
    messages = [(s, (1, 2)) for s in range(1, seqs)] + [(s, (0,)) for s in range(seqs)]
    wanted = [
        [
            [(x, s, kind, k) for kind in kinds],
            [(near, 0, beside.index((s, kind, k + 1)), None) for kind in kinds],
        ]
        for s, kinds in messages
        for k in outer
    ]
    wanted.append([[(x, s, kind, 0) for kind in (0, 1, 2)] for s in range(seqs)])
    *packed, own_rows = pack(where, wanted, shape, 20)
    packed = [swap(value, "head", k) for value, k in zip(packed, list(outer) * len(messages))]
    packed = [packed[n * len(outer) : (n + 1) * len(outer)] for n in range(len(messages))]
    asked = packed[seqs - 1 :]

    def pieces(s, kind):
        found = [(own_rows, s, kind), (near, 0, beside.index((s, kind, 1)))]
        if s == 0 and kind > 0:
            return found + [(value, 0, kind - 1) for value in first]
        row, at = (packed[s - 1], kind - 1) if kind > 0 else (asked[s], 0)
        return found + [(value, half, at) for value in row for half in (0, 1)]

    maps = integer_maps(sign_bits)

    last = [own_rows]
    begun, chains, ends, locals_, own, other, totals = {}, {}, {}, {}, {}, {}, {}

    def early(n):
        begun[n] = early_sums(
            maps, pieces(n, 1)[:2], pieces(n, 2)[:2], heads, dh, piece, last
        )
        last[:] = [begun[n][0]]

    def state(n):
        feats, mine, *others = block_state(
            where,
            maps,
            pieces(n, 1)[2:],
            pieces(n, 2)[2:],
            begun[n][1],
            heads,
            dh,
            piece,
            last,
            3 if n else 0,
        )
        begun[n] = begun[n][0], feats
        chains[n] = [mine] + [swap(value, "seq", m + 1) for m, value in enumerate(others)]
        last[:] = [mine]

    def step(n):
        first_out, *others = chain_step(where, levels, chains[n], last, STEP_US if n and len(chains[n]) == GROUP else 0)
        last[:] = [first_out]
        if others:
            ends[n] = [first_out] + [swap(value, "seq", m + 1) for m, value in enumerate(others)]
        else:
            chains[n] = chains[n] + [swap(first_out, "seq", GROUP << (len(chains[n]) - GROUP))]

    def local(n):
        locals_[n] = attend_local(
            where, maps, begun[n], pieces(n, 0), pieces(n, 2), heads, dh, piece, last
        )
        last[:] = [locals_[n][0]]

    def attend(n):
        stay, leave = attend_prior(
            where, *locals_[n], ends[n], partners, dh, last, 1 if n + 1 < seqs else 0
        )
        own[n], other[n] = [stay], [swap(leave, "head", 1)]
        last[:] = [stay]

    def multiply(s, slab):
        if slab == 1:
            for key in totals:
                if key[0] < s:
                    last.extend(totals[key][1])
        total, *shares = project(
            own[s], other[s], out_weight, other_weight, slabs[s], slab, last, 0 if s == seqs - 1 else 6
        )
        totals[s, slab] = total, [swap(v, "head", 2 * (g + 1)) for g, v in enumerate(shares)]
        last[:] = [total]

    slabs = [SLABS[0]] * (seqs - 1) + [SLABS[1]]
    plan = []
    for n in range(seqs):
        came = 22 * n
        end = came + 22 + 9 * levels
        plan.append((came, state, n))
        if n > 0:
            plan.append((came - 21, early, n))
        plan += [(came + 12 + 9 * j, step, n) for j in range(levels + 1)]
        plan.append((end - 7, local, n))
        plan.append((end, attend, n))
        plan += [(end + 6 + 3.5 * j, multiply, n, j) for j in range(len(slabs[n]))]
    plan = sorted(plan, key=lambda entry: entry[0])
    early(0)
    state(0)
    other_weight = swap(later_than(out_weight, last), "head", 1)
    for _, act, *which in plan:
        if (act, which) != (state, [0]):
            act(*which)

    return finish([[totals[s, n] for n in range(len(slabs[s]))] for s in range(seqs)], piece)


def solution(mesh):
    return jax.shard_map(
        body,
        mesh=mesh,
        in_specs=(
            P(None, ("seq", "head"), None, None),
            P("head", None, None, None),
            P("head", None),
        ),
        out_specs=P(None, ("seq", "head"), None),
        check_vma=False,
    )
```

```python
import functools
import math

import jax
import jax.numpy as jnp
import numpy as np
from jax import lax
from jax.experimental import pallas as pl
from jax.experimental.pallas import tpu as pltpu
from jax.sharding import PartitionSpec as P

logit_divisor = 1.3
norm_epsilon = 1e-06
SLABS = (8,), (4, 3, 1)

bf16, f32 = jnp.bfloat16, jnp.float32
ROW_TILE = 16
STEP_US = 4
GROUP = 4


def params(mebibytes=20):
    return pltpu.CompilerParams(vmem_limit_bytes=mebibytes * 1024 * 1024)


def vmem(count):
    return [pl.BlockSpec(memory_space=pltpu.VMEM)] * count


def smem():
    return pl.BlockSpec(memory_space=pltpu.SMEM)


def ordered(kernel, count, skip):
    return lambda *refs: kernel(*refs[:skip], *refs[skip + count :])


def busy(microseconds):
    return pl.CostEstimate(flops=int(microseconds * 1e9), bytes_accessed=0, transcendentals=0)


def waits(after):
    return [pl.BlockSpec(memory_space=pl.ANY)] * len(after)


def swap(value, axis, bit):
    return lax.ppermute(value, axis, [(j, j ^ bit) for j in range(lax.axis_size(axis))])


def sign_matrix(order):
    ids = np.arange(order)
    common = ids[:, None] & ids[None, :]
    parity = np.zeros_like(common)
    while common.any():
        parity ^= common & 1
        common = common >> 1
    return (1 - 2 * parity).astype(np.float32)


def maps_kernel(bits_ref, had_ref, maps_ref):
    had = had_ref[...]
    dh = had.shape[0]
    for h in range(bits_ref.shape[0]):
        for b in range(bits_ref.shape[1]):
            signs = (2 * bits_ref[h, b] - 1).astype(f32)
            inner = jnp.dot((had * signs[2:3]).astype(bf16), had, preferred_element_type=f32)
            outer = jnp.dot((inner * signs[1:2]).astype(bf16), had, preferred_element_type=f32)
            whole = outer * signs[0:1]
            near = whole.astype(bf16)
            rows = slice(b * dh, (b + 1) * dh)
            maps_ref[h, rows, :dh] = near
            maps_ref[h, rows, dh:] = (whole - near.astype(f32)).astype(bf16)


def integer_maps(sign_bits):
    heads, blocks, _, dh = sign_bits.shape
    return pl.pallas_call(
        maps_kernel,
        out_shape=jax.ShapeDtypeStruct((heads, blocks * dh, 2 * dh), bf16),
        in_specs=vmem(2),
        out_specs=vmem(1)[0],
        compiler_params=params(),
        cost_estimate=busy(0),
        name="integer_maps",
    )(sign_bits, jnp.asarray(sign_matrix(dh), bf16))


def features(rows, maps):
    dh = rows.shape[-1]
    wide = rows.astype(f32)
    mean = jnp.sum(wide * wide, axis=-1, keepdims=True) * (1.0 / dh)
    scale = lax.rsqrt(mean + norm_epsilon) * (logit_divisor / dh**0.25 / dh)
    twice = jnp.concatenate([rows, rows], axis=1)
    product = lax.dot_general(twice, maps, (((1,), (1,)), ((), ())), preferred_element_type=f32)
    return jnp.exp(product * scale).astype(bf16)


def pack_kernel(places, arrays, where_ref, *refs):
    ins, outs, sems = refs[:arrays], refs[arrays:-1], refs[-1]
    copies = []
    for n, (which, first, second, k, out, i, j, count) in enumerate(places):
        width = outs[out].shape[-1]
        start = 0 if k is None else pl.multiple_of((where_ref[0] ^ k) * width, width)
        source = ins[which].at[first, pl.ds(second, count), :, pl.ds(start, width)]
        copies.append(pltpu.make_async_copy(source, outs[out].at[i, pl.ds(j, count)], sems.at[n]))
    for copy in copies:
        copy.start()
    for copy in copies:
        copy.wait()


def pack(where, wanted, shape, mebibytes):
    arrays, places, shapes = [], [], []
    for out, table in enumerate(wanted):
        shapes.append((len(table), len(table[0]), *shape))
        for i, row in enumerate(table):
            for j, (array, first, second, k) in enumerate(row):
                if not any(array is known for known in arrays):
                    arrays.append(array)
                which = [array is known for known in arrays].index(True)
                before = places[-1] if places else None
                if before and before[:6] == (which, first, second - before[7], k, out, i):
                    places[-1] = (*before[:7], before[7] + 1)
                else:
                    places.append((which, first, second, k, out, i, j, 1))
    return pl.pallas_call(
        functools.partial(pack_kernel, places, len(arrays)),
        out_shape=[jax.ShapeDtypeStruct(shape, bf16) for shape in shapes],
        in_specs=[pl.BlockSpec(memory_space=pltpu.SMEM)]
        + [pl.BlockSpec(memory_space=pl.ANY)] * len(arrays),
        out_specs=[pl.BlockSpec(memory_space=pltpu.VMEM)] * len(shapes),
        scratch_shapes=[pltpu.SemaphoreType.DMA((len(places),))],
        compiler_params=params(mebibytes),
        cost_estimate=busy(0),
        name="pack",
    )(where, *arrays)


def joined(refs, places, cut):
    return jnp.concatenate(
        [ref[lead, kind, :, cut] for ref, (lead, kind) in zip(refs, places)], axis=0
    )


def sums_kernel(k_at, v_at, heads, dh, maps_ref, *refs):
    pieces = len(k_at)
    k_refs, v_refs = refs[:pieces], refs[pieces : 2 * pieces]
    *before, feats_ref, sums_ref = refs[2 * pieces :]
    for i in range(heads):
        cut = slice(i * dh, (i + 1) * dh)
        keys, values = joined(k_refs, k_at, cut), joined(v_refs, v_at, cut)
        feats = features(keys, maps_ref[i])
        feats_ref[i] = feats
        state = lax.dot_general(
            values, feats, (((0,), (0,)), ((), ())), preferred_element_type=f32
        )
        total = jnp.sum(feats.astype(f32), axis=0, keepdims=True)
        total = jnp.broadcast_to(total, (sums_ref.shape[1] - dh, total.shape[1]))
        sums = jnp.concatenate([state, total], axis=0)
        sums_ref[i] = before[0][i] + sums if before else sums


def early_sums(maps, keys, values, heads, dh, piece, after):
    feat = maps.shape[1]
    rows = len(keys) * piece
    (arrays, k_at), (others, v_at) = split(keys), split(values)
    return pl.pallas_call(
        ordered(functools.partial(sums_kernel, k_at, v_at, heads, dh), len(after), 0),
        out_shape=[
            jax.ShapeDtypeStruct((heads, rows, feat), bf16),
            jax.ShapeDtypeStruct((heads, dh + 8, feat), f32),
        ],
        in_specs=waits(after) + vmem(1 + 2 * len(keys)),
        out_specs=vmem(2),
        compiler_params=params(),
        cost_estimate=busy(0),
        name="early_sums",
    )(*after, maps, *arrays, *others)


def split(pieces):
    return [piece[0] for piece in pieces], [piece[1:] for piece in pieces]


def state_kernel(k_at, v_at, heads, dh, where_ref, maps_ref, *refs):
    count = 2 * len(k_at) + 2
    *ins, feats_ref, sums_ref = refs[:count] + refs[-1:]
    share_refs = refs[count:-1]
    sums_kernel(k_at, v_at, heads, dh, maps_ref, *ins, feats_ref, sums_ref)
    share = heads // GROUP
    pad = jnp.zeros((ROW_TILE - share, feats_ref.shape[-1]), f32)
    states = [sums_ref[i] for i in range(heads)]
    shares = []
    for g in range(GROUP):
        mine = states[g * share : (g + 1) * share]
        shares.append(
            jnp.concatenate([v[:dh] for v in mine] + [v[dh : dh + 1] for v in mine] + [pad], axis=0)
        )
    for m, ref in enumerate(share_refs):
        ref[...] = chosen(shares, where_ref[1] ^ m).astype(ref.dtype)


def chosen(values, index):
    result = values[0]
    for n, value in enumerate(values[1:]):
        result = jnp.where(index == n + 1, value, result)
    return result


def block_state(where, maps, keys, values, before, heads, dh, piece, after, beside):
    feat = maps.shape[1]
    rows = len(keys) * piece
    height = heads // GROUP * dh + ROW_TILE
    (arrays, k_at), (others, v_at) = split(keys), split(values)
    return pl.pallas_call(
        ordered(functools.partial(state_kernel, k_at, v_at, heads, dh), len(after), 0),
        out_shape=[
            jax.ShapeDtypeStruct((heads, rows, feat), bf16),
            jax.ShapeDtypeStruct((height, feat), f32),
        ]
        + [jax.ShapeDtypeStruct((height, feat), bf16)] * (GROUP - 1),
        in_specs=waits(after) + [smem()] + vmem(2 + 2 * len(keys)),
        out_specs=vmem(1 + GROUP),
        scratch_shapes=[pltpu.VMEM(before.shape, f32)],
        compiler_params=params(),
        cost_estimate=busy(beside),
        name="block_state",
    )(*after, where, maps, *arrays, *others, before)


def step_kernel(levels, where_ref, *refs):
    ins = refs[: len(refs) - (1 if len(refs) < 2 * GROUP + levels else GROUP)]
    outs = refs[len(ins) :]
    values = [ref[...].astype(f32) for ref in ins[:GROUP]]
    got = [ref[...].astype(f32) for ref in ins[GROUP:]]
    if len(outs) == 1:
        total = values[0]
        for value in values[1:] + got:
            total = total + value
        outs[0][...] = total.astype(bf16)
        return
    prior = jnp.zeros_like(values[0])
    for level, value in enumerate(got):
        prior = prior + jnp.where(where_ref[2 + level] == 1, value, 0.0)
    mine = where_ref[1]
    for m, out in enumerate(outs):
        result = prior
        for other, value in enumerate(values):
            if other != m:
                result = result + jnp.where((mine ^ other) < (mine ^ m), value, 0.0)
        out[...] = result.astype(bf16)


def chain_step(where, levels, values, after, beside):
    shape = values[0].shape
    count = GROUP if len(values) == GROUP + levels else 1
    return pl.pallas_call(
        ordered(functools.partial(step_kernel, levels), len(after), 0),
        out_shape=[jax.ShapeDtypeStruct(shape, bf16)] * count,
        in_specs=waits(after) + [smem()] + vmem(len(values)),
        out_specs=vmem(count),
        compiler_params=params(),
        cost_estimate=busy(beside),
        name="chain_step",
    )(*after, where, *values)


def local_kernel(first, q_at, v_at, heads, dh, where_ref, maps_ref, early_ref, late_ref, *refs):
    asking, partners = len(q_at), len(v_at)
    q_refs, v_refs = refs[:asking], refs[asking : asking + partners]
    query_feats_ref, local_ref = refs[asking + partners :]
    piece = q_refs[0].shape[2]
    rows = partners * piece
    me = where_ref[0]

    def places(first, count, shape, dim):
        ids = lax.broadcasted_iota(jnp.int32, shape, dim)
        result = ids + (me ^ first) * piece
        for j in range(1, count):
            result = jnp.where(ids >= j * piece, ids + ((me ^ (first + j)) - j) * piece, result)
        return result

    here = places(first, asking, (asking * piece, 1), 0)
    causal = here >= places(0, partners, (1, rows), 1)
    ones = jnp.ones((rows, dh), bf16)
    for i in range(heads):
        cut = slice(i * dh, (i + 1) * dh)
        queries, values = joined(q_refs, q_at, cut), joined(v_refs, v_at, cut)
        query_feats = features(queries, maps_ref[i])
        query_feats_ref[i] = query_feats
        scores = lax.dot_general(
            query_feats,
            jnp.concatenate([early_ref[i], late_ref[i]], axis=0),
            (((1,), (1,)), ((), ())),
            preferred_element_type=f32,
        )
        weights = jnp.where(causal, scores, 0.0).astype(bf16)
        local_ref[i] = jnp.dot(
            weights, jnp.concatenate([values, ones], axis=1), preferred_element_type=f32
        )


def attend_local(where, maps, feats, queries, values, first, heads, dh, piece, after, beside):
    feat = maps.shape[1]
    rows = len(queries) * piece
    (arrays, q_at), (others, v_at) = split(queries), split(values)
    return pl.pallas_call(
        ordered(functools.partial(local_kernel, first, q_at, v_at, heads, dh), len(after), 0),
        out_shape=[
            jax.ShapeDtypeStruct((heads, rows, feat), bf16),
            jax.ShapeDtypeStruct((heads, rows, 2 * dh), f32),
        ],
        in_specs=waits(after) + [smem()] + vmem(1 + len(feats) + len(queries) + len(values)),
        out_specs=vmem(2),
        compiler_params=params(),
        cost_estimate=busy(beside),
        name="attend_local",
    )(*after, where, maps, *feats, *arrays, *others)


def prior_kernel(pieces, heads, dh, where_ref, *refs):
    parts = len(pieces)
    asked = [(refs[2 * p], refs[2 * p + 1]) for p in range(parts)]
    share_refs, (stay_ref, leave_ref) = refs[2 * parts : 2 * parts + GROUP], refs[-2:]
    piece = stay_ref.shape[1]
    share = heads // GROUP
    for i in range(heads):
        j = i % share
        state, total = slice(j * dh, (j + 1) * dh), slice(share * dh, share * dh + ROW_TILE)
        source = where_ref[1] ^ (i // share)
        prior = chosen([ref[state, :] for ref in share_refs], source)
        tail = chosen([ref[total, :] for ref in share_refs], source)
        tail = jnp.broadcast_to(tail[j : j + 1, :], prior.shape)
        prior = jnp.concatenate([prior, tail], axis=0)
        first = 0
        for count, (query_feats_ref, local_ref) in zip(pieces, asked):
            both = local_ref[i] + lax.dot_general(
                query_feats_ref[i], prior, (((1,), (1,)), ((), ())), preferred_element_type=f32
            )
            attended = (both[:, :dh] / both[:, dh:]).astype(bf16)
            for n in range(count):
                out = leave_ref if (first + n) & 1 else stay_ref
                out[(first + n) // 2, :, i * dh : (i + 1) * dh] = attended[n * piece : (n + 1) * piece]
            first += count


def attend_prior(where, asked, shares, piece, dh, after, beside):
    heads = asked[0][0].shape[0]
    pieces = [query_feats.shape[1] // piece for query_feats, _ in asked]
    out = jax.ShapeDtypeStruct((sum(pieces) // 2, piece, heads * dh), bf16)
    values = [value for pair in asked for value in pair]
    return pl.pallas_call(
        ordered(functools.partial(prior_kernel, pieces, heads, dh), len(after), 0),
        out_shape=[out, out],
        in_specs=waits(after) + [smem()] + vmem(len(values) + len(shares)),
        out_specs=vmem(2),
        compiler_params=params(),
        cost_estimate=busy(beside),
        name="attend_prior",
    )(*after, where, *values, *shares)


def project_kernel(parts, *refs):
    own_refs, other_refs = refs[:parts], refs[parts : 2 * parts]
    own_w, other_w, stay_ref, *leave_refs = refs[2 * parts :]
    groups, piece, width = own_refs[0].shape
    acc = None
    for lhs_refs, w_ref in ((own_refs, own_w), (other_refs, other_w)):
        for p, ref in enumerate(lhs_refs):
            lhs = ref[...].reshape(groups * piece, width)
            term = jnp.dot(
                lhs, w_ref[p * width : (p + 1) * width, :], preferred_element_type=f32
            )
            acc = term if acc is None else acc + term
    stay_ref[...] = acc[:piece]
    for g, ref in enumerate(leave_refs):
        ref[...] = acc[(g + 1) * piece : (g + 2) * piece].astype(bf16)


def project(own, other, own_w, other_w, slabs, slab, after, beside):
    parts, (groups, piece, width) = len(own), own[0].shape
    depth, cols = own_w.shape
    unit = cols // sum(slabs)
    tile = math.gcd(cols * slabs[slab] // sum(slabs), 1024)
    tile = math.gcd(tile, sum(slabs[:slab]) * unit) if slab else tile
    first, cols = sum(slabs[:slab]) * unit // tile, slabs[slab] * unit
    lhs = pl.BlockSpec((groups, piece, width), lambda n: (0, 0, 0))
    weight = pl.BlockSpec((depth, tile), lambda n: (0, first + n))
    out = pl.BlockSpec((piece, tile), lambda n: (0, n))
    return pl.pallas_call(
        ordered(functools.partial(project_kernel, parts), len(after), 0),
        grid=(cols // tile,),
        out_shape=[jax.ShapeDtypeStruct((piece, cols), f32)]
        + [jax.ShapeDtypeStruct((piece, cols), bf16)] * (groups - 1),
        in_specs=waits(after) + [lhs] * (2 * parts) + [weight, weight],
        out_specs=[out] * groups,
        compiler_params=params(),
        cost_estimate=busy(beside),
        name="project",
    )(*after, *own, *other, own_w, other_w)


def finish_kernel(counts, *refs):
    refs = list(refs)
    out_ref = refs.pop()
    for s, slabs in enumerate(counts):
        at = 0
        for shares in slabs:
            total = refs.pop(0)[...]
            for _ in range(shares):
                total = total + refs.pop(0)[...].astype(f32)
            width = total.shape[1]
            out_ref[s, :, at : at + width] = total.astype(bf16)
            at += width


def finish(sums, piece):
    *slabs, (total, shares) = sums[-1]
    most = [*sums[:-1], slabs]
    counts = [[len(given) for _, given in row] for row in most]
    values = [value for row in most for own, given in row for value in (own, *given)]
    out = jax.ShapeDtypeStruct(
        (len(sums), piece, sum(own.shape[1] for own, _ in sums[-1])), bf16
    )
    begun = pl.pallas_call(
        functools.partial(finish_kernel, counts),
        grid=(1,),
        out_shape=out,
        in_specs=[pl.BlockSpec(value.shape, lambda _: (0, 0)) for value in values],
        out_specs=pl.BlockSpec(out.shape, lambda _: (0, 0, 0)),
        compiler_params=params(),
        cost_estimate=busy(3),
        name="finish",
    )(*values)
    width = total.shape[1]
    place = (len(sums) - 1, 0, out.shape[2] // width - 1)
    return pl.pallas_call(
        ordered(functools.partial(finish_kernel, [[len(shares)]]), 1, 0),
        grid=(1,),
        out_shape=out,
        in_specs=waits([begun])
        + [pl.BlockSpec(value.shape, lambda _: (0, 0)) for value in (total, *shares)],
        out_specs=pl.BlockSpec((1, piece, width), lambda _: place),
        input_output_aliases={0: 0},
        compiler_params=params(),
        cost_estimate=busy(0),
        name="finish_last",
    )(begun, total, *shares)


def nothing(*refs):
    pass


def later_than(value, after):
    anywhere = pl.BlockSpec(memory_space=pl.ANY)
    return pl.pallas_call(
        nothing,
        out_shape=jax.ShapeDtypeStruct(value.shape, value.dtype),
        in_specs=[anywhere] * (1 + len(after)),
        out_specs=anywhere,
        input_output_aliases={0: 0},
        compiler_params=params(1),
        cost_estimate=busy(0),
        name="later_than",
    )(value, *after)


def body(qkv_tokens, sign_bits, out_weight):
    partners, blocks = lax.axis_size("head"), lax.axis_size("seq")
    me, index = lax.axis_index("head"), lax.axis_index("seq")
    seqs = qkv_tokens.shape[0]
    heads, dh = sign_bits.shape[0], sign_bits.shape[-1]
    levels = (blocks // GROUP).bit_length() - 1
    x = qkv_tokens.transpose(0, 2, 1, 3)
    piece = x.shape[2]
    where = jnp.stack(
        [me, index % GROUP] + [(index // GROUP >> l) & 1 for l in range(levels)]
    ).astype(jnp.int32)

    outer, shape = range(2, partners, 2), (piece, x.shape[3] // partners)
    beside = [(s, kind, 1) for s in range(seqs) for kind in (0, 1, 2)]
    beside += [
        (s, kind, k + 1)
        for s in range(seqs)
        for kind in (0, 1, 2)
        for k in outer
        if s > 0 or kind == 0
    ]
    straight = [[[(x, 0, kind, k) for kind in (1, 2)]] for k in range(2, partners)]
    *first, near = pack(where, [*straight, [[(x, *entry) for entry in beside]]], shape, 60)
    first = [swap(value, "head", k + 2) for k, value in enumerate(first)]
    near = swap(near, "head", 1)
    messages = [(s, (1, 2)) for s in range(1, seqs)] + [(s, (0,)) for s in range(seqs)]
    wanted = [
        [
            [(x, s, kind, k) for kind in kinds],
            [(near, 0, beside.index((s, kind, k + 1)), None) for kind in kinds],
        ]
        for s, kinds in messages
        for k in outer
    ]
    wanted.append([[(x, s, kind, 0) for kind in (0, 1, 2)] for s in range(seqs)])
    *packed, own_rows = pack(where, wanted, shape, 20)
    packed = [swap(value, "head", k) for value, k in zip(packed, list(outer) * len(messages))]
    packed = [packed[n * len(outer) : (n + 1) * len(outer)] for n in range(len(messages))]
    asked = packed[seqs - 1 :]

    def pieces(s, kind):
        found = [(own_rows, s, kind), (near, 0, beside.index((s, kind, 1)))]
        if s == 0 and kind > 0:
            return found + [(value, 0, kind - 1) for value in first]
        row, at = (packed[s - 1], kind - 1) if kind > 0 else (asked[s], 0)
        return found + [(value, half, at) for value in row for half in (0, 1)]

    maps = integer_maps(sign_bits)

    last = [own_rows]
    begun, chains, ends, locals_, own, other, totals = {}, {}, {}, {}, {}, {}, {}

    def early(n):
        begun[n] = early_sums(
            maps, pieces(n, 1)[:2], pieces(n, 2)[:2], heads, dh, piece, last
        )
        last[:] = [begun[n][0]]

    def state(n):
        feats, mine, *others = block_state(
            where,
            maps,
            pieces(n, 1)[2:],
            pieces(n, 2)[2:],
            begun[n][1],
            heads,
            dh,
            piece,
            last,
            3 if n else 0,
        )
        begun[n] = begun[n][0], feats
        chains[n] = [mine] + [swap(value, "seq", m + 1) for m, value in enumerate(others)]
        last[:] = [mine]

    def step(n):
        first_out, *others = chain_step(where, levels, chains[n], last, STEP_US if n and len(chains[n]) == GROUP else 0)
        last[:] = [first_out]
        if others:
            ends[n] = [first_out] + [swap(value, "seq", m + 1) for m, value in enumerate(others)]
        else:
            chains[n] = chains[n] + [swap(first_out, "seq", GROUP << (len(chains[n]) - GROUP))]

    def local(n, first, last_row):
        part = attend_local(
            where,
            maps,
            begun[n],
            pieces(n, 0)[first:last_row],
            pieces(n, 2),
            first,
            heads,
            dh,
            piece,
            last,
            3 if n == 0 or first > 0 else 0,
        )
        locals_.setdefault(n, []).append(part)
        last[:] = [part[0]]

    def attend(n):
        stay, leave = attend_prior(
            where, locals_[n], ends[n], piece, dh, last, 1 if n + 1 < seqs else 0
        )
        own[n], other[n] = [stay], [swap(leave, "head", 1)]
        last[:] = [stay]

    def multiply(s, slab):
        if slab == 1:
            for key in totals:
                if key[0] < s:
                    last.extend(totals[key][1])
        total, *shares = project(
            own[s], other[s], out_weight, other_weight, slabs[s], slab, last, 0 if s == seqs - 1 else 6
        )
        totals[s, slab] = total, [swap(v, "head", 2 * (g + 1)) for g, v in enumerate(shares)]
        last[:] = [total]

    slabs = [SLABS[0]] * (seqs - 1) + [SLABS[1]]
    plan = []
    for n in range(seqs):
        came = 22 * n
        end = came + 22 + 9 * levels
        plan.append((came, state, n))
        if n > 0:
            plan.append((came - 21, early, n))
        plan += [(came + 12 + 9 * j, step, n) for j in range(levels + 1)]
        plan.append((came + 12.5 if n == 0 else end - 7.1, local, n, 0, 2))
        plan.append((end - 7, local, n, 2, partners))
        plan.append((end, attend, n))
        plan += [(end + 6 + 3.5 * j, multiply, n, j) for j in range(len(slabs[n]))]
    plan = sorted(plan, key=lambda entry: entry[0])
    early(0)
    state(0)
    other_weight = swap(later_than(out_weight, last), "head", 1)
    for _, act, *which in plan:
        if (act, which) != (state, [0]):
            act(*which)

    return finish([[totals[s, n] for n in range(len(slabs[s]))] for s in range(seqs)], piece)


def solution(mesh):
    return jax.shard_map(
        body,
        mesh=mesh,
        in_specs=(
            P(None, ("seq", "head"), None, None),
            P("head", None, None, None),
            P("head", None),
        ),
        out_specs=P(None, ("seq", "head"), None),
        check_vma=False,
    )
```

```python
import functools
import math

import jax
import jax.numpy as jnp
import numpy as np
from jax import lax
from jax.experimental import pallas as pl
from jax.experimental.pallas import tpu as pltpu
from jax.sharding import PartitionSpec as P

logit_divisor = 1.3
norm_epsilon = 1e-06
SLABS = (8,), (4, 3, 1)

bf16, f32 = jnp.bfloat16, jnp.float32
ROW_TILE = 16
STEP_US = 4
GROUP = 4


def params(mebibytes=20):
    return pltpu.CompilerParams(vmem_limit_bytes=mebibytes * 1024 * 1024)


def vmem(count):
    return [pl.BlockSpec(memory_space=pltpu.VMEM)] * count


def smem():
    return pl.BlockSpec(memory_space=pltpu.SMEM)


def ordered(kernel, count, skip):
    return lambda *refs: kernel(*refs[:skip], *refs[skip + count :])


def busy(microseconds):
    return pl.CostEstimate(flops=int(microseconds * 1e9), bytes_accessed=0, transcendentals=0)


def waits(after):
    return [pl.BlockSpec(memory_space=pl.ANY)] * len(after)


def swap(value, axis, bit):
    return lax.ppermute(value, axis, [(j, j ^ bit) for j in range(lax.axis_size(axis))])


def sign_matrix(order):
    ids = np.arange(order)
    common = ids[:, None] & ids[None, :]
    parity = np.zeros_like(common)
    while common.any():
        parity ^= common & 1
        common = common >> 1
    return (1 - 2 * parity).astype(np.float32)


def maps_kernel(bits_ref, had_ref, maps_ref):
    had = had_ref[...]
    dh = had.shape[0]
    for h in range(bits_ref.shape[0]):
        for b in range(bits_ref.shape[1]):
            signs = (2 * bits_ref[h, b] - 1).astype(f32)
            inner = jnp.dot((had * signs[2:3]).astype(bf16), had, preferred_element_type=f32)
            outer = jnp.dot((inner * signs[1:2]).astype(bf16), had, preferred_element_type=f32)
            whole = outer * signs[0:1]
            near = whole.astype(bf16)
            rows = slice(b * dh, (b + 1) * dh)
            maps_ref[h, rows, :dh] = near
            maps_ref[h, rows, dh:] = (whole - near.astype(f32)).astype(bf16)


def integer_maps(sign_bits):
    heads, blocks, _, dh = sign_bits.shape
    return pl.pallas_call(
        maps_kernel,
        out_shape=jax.ShapeDtypeStruct((heads, blocks * dh, 2 * dh), bf16),
        in_specs=vmem(2),
        out_specs=vmem(1)[0],
        compiler_params=params(),
        cost_estimate=busy(0),
        name="integer_maps",
    )(sign_bits, jnp.asarray(sign_matrix(dh), bf16))


def features(rows_of, maps_ref, out_ref):
    heads, _, twice = maps_ref.shape
    dh = twice // 2
    rows = [rows_of(i) for i in range(heads)]
    scales = []
    for i in range(heads):
        wide = rows[i].astype(f32)
        mean = jnp.sum(wide * wide, axis=-1, keepdims=True) * (1.0 / dh)
        scales.append(lax.rsqrt(mean + norm_epsilon) * (logit_divisor / dh**0.25 / dh))
    for i in range(heads):
        product = lax.dot_general(
            jnp.concatenate([rows[i], rows[i]], axis=1),
            maps_ref[i],
            (((1,), (1,)), ((), ())),
            preferred_element_type=f32,
        )
        out_ref[i] = jnp.exp(product * scales[i]).astype(bf16)


def pack_kernel(places, arrays, where_ref, *refs):
    ins, outs, sems = refs[:arrays], refs[arrays:-1], refs[-1]
    copies = []
    for n, (which, first, second, k, out, i, j, count) in enumerate(places):
        width = outs[out].shape[-1]
        start = 0 if k is None else pl.multiple_of((where_ref[0] ^ k) * width, width)
        source = ins[which].at[first, pl.ds(second, count), :, pl.ds(start, width)]
        copies.append(pltpu.make_async_copy(source, outs[out].at[i, pl.ds(j, count)], sems.at[n]))
    for copy in copies:
        copy.start()
    for copy in copies:
        copy.wait()


def pack(where, wanted, shape, mebibytes):
    arrays, places, shapes = [], [], []
    for out, table in enumerate(wanted):
        shapes.append((len(table), len(table[0]), *shape))
        for i, row in enumerate(table):
            for j, (array, first, second, k) in enumerate(row):
                if not any(array is known for known in arrays):
                    arrays.append(array)
                which = [array is known for known in arrays].index(True)
                before = places[-1] if places else None
                if before and before[:6] == (which, first, second - before[7], k, out, i):
                    places[-1] = (*before[:7], before[7] + 1)
                else:
                    places.append((which, first, second, k, out, i, j, 1))
    return pl.pallas_call(
        functools.partial(pack_kernel, places, len(arrays)),
        out_shape=[jax.ShapeDtypeStruct(shape, bf16) for shape in shapes],
        in_specs=[pl.BlockSpec(memory_space=pltpu.SMEM)]
        + [pl.BlockSpec(memory_space=pl.ANY)] * len(arrays),
        out_specs=[pl.BlockSpec(memory_space=pltpu.VMEM)] * len(shapes),
        scratch_shapes=[pltpu.SemaphoreType.DMA((len(places),))],
        compiler_params=params(mebibytes),
        cost_estimate=busy(0),
        name="pack",
    )(where, *arrays)


def joined(refs, places, cut):
    return jnp.concatenate(
        [ref[lead, kind, :, cut] for ref, (lead, kind) in zip(refs, places)], axis=0
    )


def sums_kernel(k_at, v_at, heads, dh, maps_ref, *refs):
    pieces = len(k_at)
    k_refs, v_refs = refs[:pieces], refs[pieces : 2 * pieces]
    *before, feats_ref, sums_ref = refs[2 * pieces :]
    cuts = [slice(i * dh, (i + 1) * dh) for i in range(heads)]
    features(lambda i: joined(k_refs, k_at, cuts[i]), maps_ref, feats_ref)
    for i in range(heads):
        feats = feats_ref[i]
        state = lax.dot_general(
            joined(v_refs, v_at, cuts[i]),
            feats,
            (((0,), (0,)), ((), ())),
            preferred_element_type=f32,
        )
        sums_ref[i, :dh] = before[0][i, :dh] + state if before else state
    for i in range(heads):
        total = jnp.sum(feats_ref[i].astype(f32), axis=0, keepdims=True)
        total = jnp.broadcast_to(total, (sums_ref.shape[1] - dh, total.shape[1]))
        sums_ref[i, dh:] = before[0][i, dh:] + total if before else total


def early_sums(maps, keys, values, heads, dh, piece, after):
    feat = maps.shape[1]
    rows = len(keys) * piece
    (arrays, k_at), (others, v_at) = split(keys), split(values)
    return pl.pallas_call(
        ordered(functools.partial(sums_kernel, k_at, v_at, heads, dh), len(after), 0),
        out_shape=[
            jax.ShapeDtypeStruct((heads, rows, feat), bf16),
            jax.ShapeDtypeStruct((heads, dh + 8, feat), f32),
        ],
        in_specs=waits(after) + vmem(1 + 2 * len(keys)),
        out_specs=vmem(2),
        compiler_params=params(),
        cost_estimate=busy(0),
        name="early_sums",
    )(*after, maps, *arrays, *others)


def split(pieces):
    return [piece[0] for piece in pieces], [piece[1:] for piece in pieces]


def state_kernel(k_at, v_at, heads, dh, where_ref, maps_ref, *refs):
    count = 2 * len(k_at) + 2
    *ins, feats_ref, sums_ref = refs[:count] + refs[-1:]
    share_refs = refs[count:-1]
    sums_kernel(k_at, v_at, heads, dh, maps_ref, *ins, feats_ref, sums_ref)
    share = heads // GROUP
    pad = jnp.zeros((ROW_TILE - share, feats_ref.shape[-1]), f32)
    states = [sums_ref[i] for i in range(heads)]
    shares = []
    for g in range(GROUP):
        mine = states[g * share : (g + 1) * share]
        shares.append(
            jnp.concatenate([v[:dh] for v in mine] + [v[dh : dh + 1] for v in mine] + [pad], axis=0)
        )
    for m, ref in enumerate(share_refs):
        ref[...] = chosen(shares, where_ref[1] ^ m).astype(ref.dtype)


def chosen(values, index):
    result = values[0]
    for n, value in enumerate(values[1:]):
        result = jnp.where(index == n + 1, value, result)
    return result


def block_state(where, maps, keys, values, before, heads, dh, piece, after, beside):
    feat = maps.shape[1]
    rows = len(keys) * piece
    height = heads // GROUP * dh + ROW_TILE
    (arrays, k_at), (others, v_at) = split(keys), split(values)
    return pl.pallas_call(
        ordered(functools.partial(state_kernel, k_at, v_at, heads, dh), len(after), 0),
        out_shape=[
            jax.ShapeDtypeStruct((heads, rows, feat), bf16),
            jax.ShapeDtypeStruct((height, feat), f32),
        ]
        + [jax.ShapeDtypeStruct((height, feat), bf16)] * (GROUP - 1),
        in_specs=waits(after) + [smem()] + vmem(2 + 2 * len(keys)),
        out_specs=vmem(1 + GROUP),
        scratch_shapes=[pltpu.VMEM(before.shape, f32)],
        compiler_params=params(),
        cost_estimate=busy(beside),
        name="block_state",
    )(*after, where, maps, *arrays, *others, before)


def step_kernel(levels, where_ref, *refs):
    ins = refs[: len(refs) - (1 if len(refs) < 2 * GROUP + levels else GROUP)]
    outs = refs[len(ins) :]
    values = [ref[...].astype(f32) for ref in ins[:GROUP]]
    got = [ref[...].astype(f32) for ref in ins[GROUP:]]
    if len(outs) == 1:
        total = values[0]
        for value in values[1:] + got:
            total = total + value
        outs[0][...] = total.astype(bf16)
        return
    prior = jnp.zeros_like(values[0])
    for level, value in enumerate(got):
        prior = prior + jnp.where(where_ref[2 + level] == 1, value, 0.0)
    mine = where_ref[1]
    for m, out in enumerate(outs):
        result = prior
        for other, value in enumerate(values):
            if other != m:
                result = result + jnp.where((mine ^ other) < (mine ^ m), value, 0.0)
        out[...] = result.astype(bf16)


def chain_step(where, levels, values, after, beside):
    shape = values[0].shape
    count = GROUP if len(values) == GROUP + levels else 1
    return pl.pallas_call(
        ordered(functools.partial(step_kernel, levels), len(after), 0),
        out_shape=[jax.ShapeDtypeStruct(shape, bf16)] * count,
        in_specs=waits(after) + [smem()] + vmem(len(values)),
        out_specs=vmem(count),
        compiler_params=params(),
        cost_estimate=busy(beside),
        name="chain_step",
    )(*after, where, *values)


def local_kernel(first, q_at, v_at, heads, dh, where_ref, maps_ref, early_ref, late_ref, *refs):
    asking, partners = len(q_at), len(v_at)
    q_refs, v_refs = refs[:asking], refs[asking : asking + partners]
    query_feats_ref, local_ref, weights_ref = refs[asking + partners :]
    piece = q_refs[0].shape[2]
    rows = partners * piece
    me = where_ref[0]

    def places(first, count, shape, dim):
        ids = lax.broadcasted_iota(jnp.int32, shape, dim)
        result = ids + (me ^ first) * piece
        for j in range(1, count):
            result = jnp.where(ids >= j * piece, ids + ((me ^ (first + j)) - j) * piece, result)
        return result

    here = places(first, asking, (asking * piece, 1), 0)
    causal = here >= places(0, partners, (1, rows), 1)
    ones = jnp.ones((rows, dh), bf16)
    cuts = [slice(i * dh, (i + 1) * dh) for i in range(heads)]
    features(lambda i: joined(q_refs, q_at, cuts[i]), maps_ref, query_feats_ref)
    for i in range(heads):
        scores = lax.dot_general(
            query_feats_ref[i],
            jnp.concatenate([early_ref[i], late_ref[i]], axis=0),
            (((1,), (1,)), ((), ())),
            preferred_element_type=f32,
        )
        weights_ref[i] = jnp.where(causal, scores, 0.0).astype(bf16)
    for i in range(heads):
        local_ref[i] = jnp.dot(
            weights_ref[i],
            jnp.concatenate([joined(v_refs, v_at, cuts[i]), ones], axis=1),
            preferred_element_type=f32,
        )


def attend_local(where, maps, feats, queries, values, first, heads, dh, piece, after, beside):
    feat = maps.shape[1]
    rows = len(queries) * piece
    (arrays, q_at), (others, v_at) = split(queries), split(values)
    return pl.pallas_call(
        ordered(functools.partial(local_kernel, first, q_at, v_at, heads, dh), len(after), 0),
        out_shape=[
            jax.ShapeDtypeStruct((heads, rows, feat), bf16),
            jax.ShapeDtypeStruct((heads, rows, 2 * dh), f32),
        ],
        in_specs=waits(after) + [smem()] + vmem(1 + len(feats) + len(queries) + len(values)),
        out_specs=vmem(2),
        scratch_shapes=[pltpu.VMEM((heads, rows, len(values) * piece), bf16)],
        compiler_params=params(),
        cost_estimate=busy(beside),
        name="attend_local",
    )(*after, where, maps, *feats, *arrays, *others)


def prior_kernel(pieces, heads, dh, where_ref, *refs):
    parts = len(pieces)
    asked = [(refs[2 * p], refs[2 * p + 1]) for p in range(parts)]
    share_refs, (stay_ref, leave_ref) = refs[2 * parts : 2 * parts + GROUP], refs[-2:]
    piece = stay_ref.shape[1]
    share = heads // GROUP
    priors = []
    for i in range(heads):
        j = i % share
        state, total = slice(j * dh, (j + 1) * dh), slice(share * dh, share * dh + ROW_TILE)
        source = where_ref[1] ^ (i // share)
        prior = chosen([ref[state, :] for ref in share_refs], source)
        tail = chosen([ref[total, :] for ref in share_refs], source)
        tail = jnp.broadcast_to(tail[j : j + 1, :], prior.shape)
        priors.append(jnp.concatenate([prior, tail], axis=0))
    first = 0
    for count, (query_feats_ref, local_ref) in zip(pieces, asked):
        sums = [
            local_ref[i]
            + lax.dot_general(
                query_feats_ref[i], priors[i], (((1,), (1,)), ((), ())), preferred_element_type=f32
            )
            for i in range(heads)
        ]
        for i in range(heads):
            attended = (sums[i][:, :dh] / sums[i][:, dh:]).astype(bf16)
            for n in range(count):
                out = leave_ref if (first + n) & 1 else stay_ref
                out[(first + n) // 2, :, i * dh : (i + 1) * dh] = attended[n * piece : (n + 1) * piece]
        first += count


def attend_prior(where, asked, shares, piece, dh, after, beside):
    heads = asked[0][0].shape[0]
    pieces = [query_feats.shape[1] // piece for query_feats, _ in asked]
    out = jax.ShapeDtypeStruct((sum(pieces) // 2, piece, heads * dh), bf16)
    values = [value for pair in asked for value in pair]
    return pl.pallas_call(
        ordered(functools.partial(prior_kernel, pieces, heads, dh), len(after), 0),
        out_shape=[out, out],
        in_specs=waits(after) + [smem()] + vmem(len(values) + len(shares)),
        out_specs=vmem(2),
        compiler_params=params(),
        cost_estimate=busy(beside),
        name="attend_prior",
    )(*after, where, *values, *shares)


def project_kernel(parts, *refs):
    own_refs, other_refs = refs[:parts], refs[parts : 2 * parts]
    own_w, other_w, stay_ref, *leave_refs = refs[2 * parts :]
    groups, piece, width = own_refs[0].shape
    acc = None
    for lhs_refs, w_ref in ((own_refs, own_w), (other_refs, other_w)):
        for p, ref in enumerate(lhs_refs):
            lhs = ref[...].reshape(groups * piece, width)
            term = jnp.dot(
                lhs, w_ref[p * width : (p + 1) * width, :], preferred_element_type=f32
            )
            acc = term if acc is None else acc + term
    stay_ref[...] = acc[:piece]
    for g, ref in enumerate(leave_refs):
        ref[...] = acc[(g + 1) * piece : (g + 2) * piece].astype(bf16)


def project(own, other, own_w, other_w, slabs, slab, after, beside):
    parts, (groups, piece, width) = len(own), own[0].shape
    depth, cols = own_w.shape
    unit = cols // sum(slabs)
    tile = math.gcd(cols * slabs[slab] // sum(slabs), 1024)
    tile = math.gcd(tile, sum(slabs[:slab]) * unit) if slab else tile
    first, cols = sum(slabs[:slab]) * unit // tile, slabs[slab] * unit
    lhs = pl.BlockSpec((groups, piece, width), lambda n: (0, 0, 0))
    weight = pl.BlockSpec((depth, tile), lambda n: (0, first + n))
    out = pl.BlockSpec((piece, tile), lambda n: (0, n))
    return pl.pallas_call(
        ordered(functools.partial(project_kernel, parts), len(after), 0),
        grid=(cols // tile,),
        out_shape=[jax.ShapeDtypeStruct((piece, cols), f32)]
        + [jax.ShapeDtypeStruct((piece, cols), bf16)] * (groups - 1),
        in_specs=waits(after) + [lhs] * (2 * parts) + [weight, weight],
        out_specs=[out] * groups,
        compiler_params=params(),
        cost_estimate=busy(beside),
        name="project",
    )(*after, *own, *other, own_w, other_w)


def finish_kernel(counts, *refs):
    refs = list(refs)
    out_ref = refs.pop()
    for s, slabs in enumerate(counts):
        at = 0
        for shares in slabs:
            total = refs.pop(0)[...]
            for _ in range(shares):
                total = total + refs.pop(0)[...].astype(f32)
            width = total.shape[1]
            out_ref[s, :, at : at + width] = total.astype(bf16)
            at += width


def finish(sums, piece):
    *slabs, (total, shares) = sums[-1]
    most = [*sums[:-1], slabs]
    counts = [[len(given) for _, given in row] for row in most]
    values = [value for row in most for own, given in row for value in (own, *given)]
    out = jax.ShapeDtypeStruct(
        (len(sums), piece, sum(own.shape[1] for own, _ in sums[-1])), bf16
    )
    begun = pl.pallas_call(
        functools.partial(finish_kernel, counts),
        grid=(1,),
        out_shape=out,
        in_specs=[pl.BlockSpec(value.shape, lambda _: (0, 0)) for value in values],
        out_specs=pl.BlockSpec(out.shape, lambda _: (0, 0, 0)),
        compiler_params=params(),
        cost_estimate=busy(3),
        name="finish",
    )(*values)
    width = total.shape[1]
    place = (len(sums) - 1, 0, out.shape[2] // width - 1)
    return pl.pallas_call(
        ordered(functools.partial(finish_kernel, [[len(shares)]]), 1, 0),
        grid=(1,),
        out_shape=out,
        in_specs=waits([begun])
        + [pl.BlockSpec(value.shape, lambda _: (0, 0)) for value in (total, *shares)],
        out_specs=pl.BlockSpec((1, piece, width), lambda _: place),
        input_output_aliases={0: 0},
        compiler_params=params(),
        cost_estimate=busy(0),
        name="finish_last",
    )(begun, total, *shares)


def nothing(*refs):
    pass


def later_than(value, after):
    anywhere = pl.BlockSpec(memory_space=pl.ANY)
    return pl.pallas_call(
        nothing,
        out_shape=jax.ShapeDtypeStruct(value.shape, value.dtype),
        in_specs=[anywhere] * (1 + len(after)),
        out_specs=anywhere,
        input_output_aliases={0: 0},
        compiler_params=params(1),
        cost_estimate=busy(0),
        name="later_than",
    )(value, *after)


def body(qkv_tokens, sign_bits, out_weight):
    partners, blocks = lax.axis_size("head"), lax.axis_size("seq")
    me, index = lax.axis_index("head"), lax.axis_index("seq")
    seqs = qkv_tokens.shape[0]
    heads, dh = sign_bits.shape[0], sign_bits.shape[-1]
    levels = (blocks // GROUP).bit_length() - 1
    x = qkv_tokens.transpose(0, 2, 1, 3)
    piece = x.shape[2]
    where = jnp.stack(
        [me, index % GROUP] + [(index // GROUP >> l) & 1 for l in range(levels)]
    ).astype(jnp.int32)

    outer, shape = range(2, partners, 2), (piece, x.shape[3] // partners)
    beside = [(s, kind, 1) for s in range(seqs) for kind in (0, 1, 2)]
    beside += [
        (s, kind, k + 1)
        for s in range(seqs)
        for kind in (0, 1, 2)
        for k in outer
        if s > 0 or kind == 0
    ]
    straight = [[[(x, 0, kind, k) for kind in (1, 2)]] for k in range(2, partners)]
    *first, near = pack(where, [*straight, [[(x, *entry) for entry in beside]]], shape, 60)
    first = [swap(value, "head", k + 2) for k, value in enumerate(first)]
    near = swap(near, "head", 1)
    messages = [(s, (1, 2)) for s in range(1, seqs)] + [(s, (0,)) for s in range(seqs)]
    wanted = [
        [
            [(x, s, kind, k) for kind in kinds],
            [(near, 0, beside.index((s, kind, k + 1)), None) for kind in kinds],
        ]
        for s, kinds in messages
        for k in outer
    ]
    wanted.append([[(x, s, kind, 0) for kind in (0, 1, 2)] for s in range(seqs)])
    *packed, own_rows = pack(where, wanted, shape, 20)
    packed = [swap(value, "head", k) for value, k in zip(packed, list(outer) * len(messages))]
    packed = [packed[n * len(outer) : (n + 1) * len(outer)] for n in range(len(messages))]
    asked = packed[seqs - 1 :]

    def pieces(s, kind):
        found = [(own_rows, s, kind), (near, 0, beside.index((s, kind, 1)))]
        if s == 0 and kind > 0:
            return found + [(value, 0, kind - 1) for value in first]
        row, at = (packed[s - 1], kind - 1) if kind > 0 else (asked[s], 0)
        return found + [(value, half, at) for value in row for half in (0, 1)]

    maps = integer_maps(sign_bits)

    last = [own_rows]
    begun, chains, ends, locals_, own, other, totals = {}, {}, {}, {}, {}, {}, {}

    def early(n):
        begun[n] = early_sums(
            maps, pieces(n, 1)[:2], pieces(n, 2)[:2], heads, dh, piece, last
        )
        last[:] = [begun[n][0]]

    def state(n):
        feats, mine, *others = block_state(
            where,
            maps,
            pieces(n, 1)[2:],
            pieces(n, 2)[2:],
            begun[n][1],
            heads,
            dh,
            piece,
            last,
            3 if n else 0,
        )
        begun[n] = begun[n][0], feats
        chains[n] = [mine] + [swap(value, "seq", m + 1) for m, value in enumerate(others)]
        last[:] = [mine]

    def step(n):
        first_out, *others = chain_step(where, levels, chains[n], last, STEP_US if n and len(chains[n]) == GROUP else 0)
        last[:] = [first_out]
        if others:
            ends[n] = [first_out] + [swap(value, "seq", m + 1) for m, value in enumerate(others)]
        else:
            chains[n] = chains[n] + [swap(first_out, "seq", GROUP << (len(chains[n]) - GROUP))]

    def local(n, first, last_row):
        part = attend_local(
            where,
            maps,
            begun[n],
            pieces(n, 0)[first:last_row],
            pieces(n, 2),
            first,
            heads,
            dh,
            piece,
            last,
            3,
        )
        locals_.setdefault(n, []).append(part)
        last[:] = [part[0]]

    def attend(n):
        stay, leave = attend_prior(
            where, locals_[n], ends[n], piece, dh, last, 1 if n + 1 < seqs else 0
        )
        own[n], other[n] = [stay], [swap(leave, "head", 1)]
        last[:] = [stay]

    def multiply(s, slab):
        if slab == 1:
            for key in totals:
                if key[0] < s:
                    last.extend(totals[key][1])
        total, *shares = project(
            own[s], other[s], out_weight, other_weight, slabs[s], slab, last, 0 if s == seqs - 1 else 6
        )
        totals[s, slab] = total, [swap(v, "head", 2 * (g + 1)) for g, v in enumerate(shares)]
        last[:] = [total]

    slabs = [SLABS[0]] * (seqs - 1) + [SLABS[1]]
    plan = []
    for n in range(seqs):
        came = 22 * n
        end = came + 22 + 9 * levels
        plan.append((came, state, n))
        if n > 0:
            plan.append((came - 21, early, n))
        plan += [(came + 12 + 9 * j, step, n) for j in range(levels + 1)]
        if n == 0:
            plan += [(came + 12.5, local, n, 0, 2), (end - 7, local, n, 2, partners)]
        else:
            plan.append((end - 7, local, n, 0, partners))
        plan.append((end, attend, n))
        plan += [(end + 6 + 3.5 * j, multiply, n, j) for j in range(len(slabs[n]))]
    plan = sorted(plan, key=lambda entry: entry[0])
    early(0)
    state(0)
    other_weight = swap(later_than(out_weight, last), "head", 1)
    for _, act, *which in plan:
        if (act, which) != (state, [0]):
            act(*which)

    return finish([[totals[s, n] for n in range(len(slabs[s]))] for s in range(seqs)], piece)


def solution(mesh):
    return jax.shard_map(
        body,
        mesh=mesh,
        in_specs=(
            P(None, ("seq", "head"), None, None),
            P("head", None, None, None),
            P("head", None),
        ),
        out_specs=P(None, ("seq", "head"), None),
        check_vma=False,
    )
```

```python
import functools
import math

import jax
import jax.numpy as jnp
import numpy as np
from jax import lax
from jax.experimental import pallas as pl
from jax.experimental.pallas import tpu as pltpu
from jax.sharding import PartitionSpec as P

logit_divisor = 1.3
norm_epsilon = 1e-06
SLABS = (8,), (4, 3, 1)

bf16, f32 = jnp.bfloat16, jnp.float32
ROW_TILE = 16
STEP_US = 4
GROUP = 4


def params(mebibytes=20):
    return pltpu.CompilerParams(vmem_limit_bytes=mebibytes * 1024 * 1024)


def vmem(count):
    return [pl.BlockSpec(memory_space=pltpu.VMEM)] * count


def smem():
    return pl.BlockSpec(memory_space=pltpu.SMEM)


def ordered(kernel, count, skip):
    return lambda *refs: kernel(*refs[:skip], *refs[skip + count :])


def busy(microseconds):
    return pl.CostEstimate(flops=int(microseconds * 1e9), bytes_accessed=0, transcendentals=0)


def waits(after):
    return [pl.BlockSpec(memory_space=pl.ANY)] * len(after)


def swap(value, axis, bit):
    return lax.ppermute(value, axis, [(j, j ^ bit) for j in range(lax.axis_size(axis))])


def sign_matrix(order):
    ids = np.arange(order)
    common = ids[:, None] & ids[None, :]
    parity = np.zeros_like(common)
    while common.any():
        parity ^= common & 1
        common = common >> 1
    return (1 - 2 * parity).astype(np.float32)


def maps_kernel(bits_ref, had_ref, maps_ref):
    had = had_ref[...]
    dh = had.shape[0]
    for h in range(bits_ref.shape[0]):
        for b in range(bits_ref.shape[1]):
            signs = (2 * bits_ref[h, b] - 1).astype(f32)
            inner = jnp.dot((had * signs[2:3]).astype(bf16), had, preferred_element_type=f32)
            outer = jnp.dot((inner * signs[1:2]).astype(bf16), had, preferred_element_type=f32)
            whole = outer * signs[0:1]
            near = whole.astype(bf16)
            rows = slice(b * dh, (b + 1) * dh)
            maps_ref[h, rows, :dh] = near
            maps_ref[h, rows, dh:] = (whole - near.astype(f32)).astype(bf16)


def integer_maps(sign_bits):
    heads, blocks, _, dh = sign_bits.shape
    return pl.pallas_call(
        maps_kernel,
        out_shape=jax.ShapeDtypeStruct((heads, blocks * dh, 2 * dh), bf16),
        in_specs=vmem(2),
        out_specs=vmem(1)[0],
        compiler_params=params(),
        cost_estimate=busy(0),
        name="integer_maps",
    )(sign_bits, jnp.asarray(sign_matrix(dh), bf16))


def features(rows_of, maps_ref, out_ref):
    heads, _, twice = maps_ref.shape
    dh = twice // 2
    rows = [rows_of(i) for i in range(heads)]
    scales = []
    for i in range(heads):
        wide = rows[i].astype(f32)
        mean = jnp.sum(wide * wide, axis=-1, keepdims=True) * (1.0 / dh)
        scales.append(lax.rsqrt(mean + norm_epsilon) * (logit_divisor / dh**0.25 / dh))
    for i in range(heads):
        product = lax.dot_general(
            jnp.concatenate([rows[i], rows[i]], axis=1),
            maps_ref[i],
            (((1,), (1,)), ((), ())),
            preferred_element_type=f32,
        )
        out_ref[i] = jnp.exp(product * scales[i]).astype(bf16)


def pack_kernel(places, arrays, where_ref, *refs):
    ins, outs, sems = refs[:arrays], refs[arrays:-1], refs[-1]
    copies = []
    for n, (which, first, second, k, out, i, j, count) in enumerate(places):
        width = outs[out].shape[-1]
        start = 0 if k is None else pl.multiple_of((where_ref[0] ^ k) * width, width)
        source = ins[which].at[first, pl.ds(second, count), :, pl.ds(start, width)]
        copies.append(pltpu.make_async_copy(source, outs[out].at[i, pl.ds(j, count)], sems.at[n]))
    for copy in copies:
        copy.start()
    for copy in copies:
        copy.wait()


def pack(where, wanted, shape, mebibytes):
    arrays, places, shapes = [], [], []
    for out, table in enumerate(wanted):
        shapes.append((len(table), len(table[0]), *shape))
        for i, row in enumerate(table):
            for j, (array, first, second, k) in enumerate(row):
                if not any(array is known for known in arrays):
                    arrays.append(array)
                which = [array is known for known in arrays].index(True)
                before = places[-1] if places else None
                if before and before[:6] == (which, first, second - before[7], k, out, i):
                    places[-1] = (*before[:7], before[7] + 1)
                else:
                    places.append((which, first, second, k, out, i, j, 1))
    return pl.pallas_call(
        functools.partial(pack_kernel, places, len(arrays)),
        out_shape=[jax.ShapeDtypeStruct(shape, bf16) for shape in shapes],
        in_specs=[pl.BlockSpec(memory_space=pltpu.SMEM)]
        + [pl.BlockSpec(memory_space=pl.ANY)] * len(arrays),
        out_specs=[pl.BlockSpec(memory_space=pltpu.VMEM)] * len(shapes),
        scratch_shapes=[pltpu.SemaphoreType.DMA((len(places),))],
        compiler_params=params(mebibytes),
        cost_estimate=busy(0),
        name="pack",
    )(where, *arrays)


def joined(refs, places, cut):
    return jnp.concatenate(
        [ref[lead, kind, :, cut] for ref, (lead, kind) in zip(refs, places)], axis=0
    )


def sums_kernel(k_at, v_at, heads, dh, maps_ref, *refs):
    pieces = len(k_at)
    k_refs, v_refs = refs[:pieces], refs[pieces : 2 * pieces]
    *before, feats_ref, sums_ref = refs[2 * pieces :]
    cuts = [slice(i * dh, (i + 1) * dh) for i in range(heads)]
    features(lambda i: joined(k_refs, k_at, cuts[i]), maps_ref, feats_ref)
    for i in range(heads):
        feats = feats_ref[i]
        state = lax.dot_general(
            joined(v_refs, v_at, cuts[i]),
            feats,
            (((0,), (0,)), ((), ())),
            preferred_element_type=f32,
        )
        sums_ref[i, :dh] = before[0][i, :dh] + state if before else state
    for i in range(heads):
        total = jnp.sum(feats_ref[i].astype(f32), axis=0, keepdims=True)
        total = jnp.broadcast_to(total, (sums_ref.shape[1] - dh, total.shape[1]))
        sums_ref[i, dh:] = before[0][i, dh:] + total if before else total


def early_sums(maps, keys, values, heads, dh, piece, after):
    feat = maps.shape[1]
    rows = len(keys) * piece
    (arrays, k_at), (others, v_at) = split(keys), split(values)
    return pl.pallas_call(
        ordered(functools.partial(sums_kernel, k_at, v_at, heads, dh), len(after), 0),
        out_shape=[
            jax.ShapeDtypeStruct((heads, rows, feat), bf16),
            jax.ShapeDtypeStruct((heads, dh + 8, feat), f32),
        ],
        in_specs=waits(after) + vmem(1 + 2 * len(keys)),
        out_specs=vmem(2),
        compiler_params=params(),
        cost_estimate=busy(0),
        name="early_sums",
    )(*after, maps, *arrays, *others)


def split(pieces):
    return [piece[0] for piece in pieces], [piece[1:] for piece in pieces]


def state_kernel(k_at, v_at, heads, dh, where_ref, maps_ref, *refs):
    count = 2 * len(k_at) + 2
    *ins, feats_ref, sums_ref = refs[:count] + refs[-1:]
    share_refs = refs[count:-1]
    sums_kernel(k_at, v_at, heads, dh, maps_ref, *ins, feats_ref, sums_ref)
    share = heads // GROUP
    pad = jnp.zeros((ROW_TILE - share, feats_ref.shape[-1]), f32)
    states = [sums_ref[i] for i in range(heads)]
    shares = []
    for g in range(GROUP):
        mine = states[g * share : (g + 1) * share]
        shares.append(
            jnp.concatenate([v[:dh] for v in mine] + [v[dh : dh + 1] for v in mine] + [pad], axis=0)
        )
    for m, ref in enumerate(share_refs):
        ref[...] = chosen(shares, where_ref[1] ^ m).astype(ref.dtype)


def chosen(values, index):
    result = values[0]
    for n, value in enumerate(values[1:]):
        result = jnp.where(index == n + 1, value, result)
    return result


def block_state(where, maps, keys, values, before, heads, dh, piece, after, beside):
    feat = maps.shape[1]
    rows = len(keys) * piece
    height = heads // GROUP * dh + ROW_TILE
    (arrays, k_at), (others, v_at) = split(keys), split(values)
    return pl.pallas_call(
        ordered(functools.partial(state_kernel, k_at, v_at, heads, dh), len(after), 0),
        out_shape=[
            jax.ShapeDtypeStruct((heads, rows, feat), bf16),
            jax.ShapeDtypeStruct((height, feat), f32),
        ]
        + [jax.ShapeDtypeStruct((height, feat), bf16)] * (GROUP - 1),
        in_specs=waits(after) + [smem()] + vmem(2 + 2 * len(keys)),
        out_specs=vmem(1 + GROUP),
        scratch_shapes=[pltpu.VMEM(before.shape, f32)],
        compiler_params=params(),
        cost_estimate=busy(beside),
        name="block_state",
    )(*after, where, maps, *arrays, *others, before)


def step_kernel(levels, starts, height, riders, where_ref, *refs):
    count = len(starts)
    ins, extra, outs = refs[:count], refs[count : count + riders], refs[count + riders :]
    held = [ref[at : at + height, :].astype(f32) for ref, at in zip(ins, starts)]
    values, got = held[:GROUP], held[GROUP:]
    if len(outs) == 1:
        total = values[0]
        for value in values[1:] + got:
            total = total + value
        outs[0][...] = total.astype(bf16)
        return
    prior = jnp.zeros_like(values[0])
    for level, value in enumerate(got):
        prior = prior + jnp.where(where_ref[2 + level] == 1, value, 0.0)
    mine = where_ref[1]
    for m, out in enumerate(outs):
        result = prior
        for other, value in enumerate(values):
            if other != m:
                result = result + jnp.where((mine ^ other) < (mine ^ m), value, 0.0)
        out[:height, :] = result.astype(bf16)
    for out, ref in zip(outs[1:], extra):
        out[height:, :] = ref[...]


def chain_step(where, levels, values, riders, after, beside):
    arrays, starts = [value for value, _ in values], [at for _, at in values]
    height, feat = arrays[0].shape
    last = len(values) == GROUP + levels
    shapes = [(height, feat)] + [(height * (2 if riders else 1), feat)] * (GROUP - 1 if last else 0)
    return pl.pallas_call(
        ordered(
            functools.partial(step_kernel, levels, starts, height, len(riders)), len(after), 0
        ),
        out_shape=[jax.ShapeDtypeStruct(shape, bf16) for shape in shapes],
        in_specs=waits(after) + [smem()] + vmem(len(values) + len(riders)),
        out_specs=vmem(len(shapes)),
        compiler_params=params(),
        cost_estimate=busy(beside),
        name="chain_step",
    )(*after, where, *arrays, *riders)


def local_kernel(first, q_at, v_at, heads, dh, where_ref, maps_ref, early_ref, late_ref, *refs):
    asking, partners = len(q_at), len(v_at)
    q_refs, v_refs = refs[:asking], refs[asking : asking + partners]
    query_feats_ref, local_ref, weights_ref = refs[asking + partners :]
    piece = q_refs[0].shape[2]
    rows = partners * piece
    me = where_ref[0]

    def places(first, count, shape, dim):
        ids = lax.broadcasted_iota(jnp.int32, shape, dim)
        result = ids + (me ^ first) * piece
        for j in range(1, count):
            result = jnp.where(ids >= j * piece, ids + ((me ^ (first + j)) - j) * piece, result)
        return result

    here = places(first, asking, (asking * piece, 1), 0)
    causal = here >= places(0, partners, (1, rows), 1)
    ones = jnp.ones((rows, dh), bf16)
    cuts = [slice(i * dh, (i + 1) * dh) for i in range(heads)]
    features(lambda i: joined(q_refs, q_at, cuts[i]), maps_ref, query_feats_ref)
    for i in range(heads):
        scores = lax.dot_general(
            query_feats_ref[i],
            jnp.concatenate([early_ref[i], late_ref[i]], axis=0),
            (((1,), (1,)), ((), ())),
            preferred_element_type=f32,
        )
        weights_ref[i] = jnp.where(causal, scores, 0.0).astype(bf16)
    for i in range(heads):
        local_ref[i] = jnp.dot(
            weights_ref[i],
            jnp.concatenate([joined(v_refs, v_at, cuts[i]), ones], axis=1),
            preferred_element_type=f32,
        )


def attend_local(where, maps, feats, queries, values, first, heads, dh, piece, after, beside):
    feat = maps.shape[1]
    rows = len(queries) * piece
    (arrays, q_at), (others, v_at) = split(queries), split(values)
    return pl.pallas_call(
        ordered(functools.partial(local_kernel, first, q_at, v_at, heads, dh), len(after), 0),
        out_shape=[
            jax.ShapeDtypeStruct((heads, rows, feat), bf16),
            jax.ShapeDtypeStruct((heads, rows, 2 * dh), f32),
        ],
        in_specs=waits(after) + [smem()] + vmem(1 + len(feats) + len(queries) + len(values)),
        out_specs=vmem(2),
        scratch_shapes=[pltpu.VMEM((heads, rows, len(values) * piece), bf16)],
        compiler_params=params(),
        cost_estimate=busy(beside),
        name="attend_local",
    )(*after, where, maps, *feats, *arrays, *others)


def prior_kernel(pieces, starts, heads, dh, where_ref, *refs):
    parts = len(pieces)
    asked = [(refs[2 * p], refs[2 * p + 1]) for p in range(parts)]
    share_refs, (stay_ref, leave_ref) = refs[2 * parts : 2 * parts + GROUP], refs[-2:]
    piece = stay_ref.shape[1]
    share = heads // GROUP

    def rows(p, part):
        return share_refs[p][starts[p] + part.start : starts[p] + part.stop, :]

    priors = []
    for i in range(heads):
        j = i % share
        state, total = slice(j * dh, (j + 1) * dh), slice(share * dh, share * dh + ROW_TILE)
        source = where_ref[1] ^ (i // share)
        prior = chosen([rows(p, state) for p in range(GROUP)], source)
        tail = chosen([rows(p, total) for p in range(GROUP)], source)
        tail = jnp.broadcast_to(tail[j : j + 1, :], prior.shape)
        priors.append(jnp.concatenate([prior, tail], axis=0))
    first = 0
    for count, (query_feats_ref, local_ref) in zip(pieces, asked):
        sums = [
            local_ref[i]
            + lax.dot_general(
                query_feats_ref[i], priors[i], (((1,), (1,)), ((), ())), preferred_element_type=f32
            )
            for i in range(heads)
        ]
        for i in range(heads):
            attended = (sums[i][:, :dh] / sums[i][:, dh:]).astype(bf16)
            for n in range(count):
                out = leave_ref if (first + n) & 1 else stay_ref
                out[(first + n) // 2, :, i * dh : (i + 1) * dh] = attended[n * piece : (n + 1) * piece]
        first += count


def attend_prior(where, asked, shares, piece, dh, after, beside):
    heads = asked[0][0].shape[0]
    pieces = [query_feats.shape[1] // piece for query_feats, _ in asked]
    out = jax.ShapeDtypeStruct((sum(pieces) // 2, piece, heads * dh), bf16)
    values = [value for pair in asked for value in pair]
    arrays, starts = [value for value, _ in shares], [at for _, at in shares]
    return pl.pallas_call(
        ordered(functools.partial(prior_kernel, pieces, starts, heads, dh), len(after), 0),
        out_shape=[out, out],
        in_specs=waits(after) + [smem()] + vmem(len(values) + len(shares)),
        out_specs=vmem(2),
        compiler_params=params(),
        cost_estimate=busy(beside),
        name="attend_prior",
    )(*after, where, *values, *arrays)


def project_kernel(parts, *refs):
    own_refs, other_refs = refs[:parts], refs[parts : 2 * parts]
    own_w, other_w, stay_ref, *leave_refs = refs[2 * parts :]
    groups, piece, width = own_refs[0].shape
    acc = None
    for lhs_refs, w_ref in ((own_refs, own_w), (other_refs, other_w)):
        for p, ref in enumerate(lhs_refs):
            lhs = ref[...].reshape(groups * piece, width)
            term = jnp.dot(
                lhs, w_ref[p * width : (p + 1) * width, :], preferred_element_type=f32
            )
            acc = term if acc is None else acc + term
    stay_ref[...] = acc[:piece]
    for g, ref in enumerate(leave_refs):
        ref[...] = acc[(g + 1) * piece : (g + 2) * piece].astype(bf16)


def project(own, other, own_w, other_w, slabs, slab, after, beside):
    parts, (groups, piece, width) = len(own), own[0].shape
    depth, cols = own_w.shape
    unit = cols // sum(slabs)
    tile = math.gcd(cols * slabs[slab] // sum(slabs), 1024)
    tile = math.gcd(tile, sum(slabs[:slab]) * unit) if slab else tile
    first, cols = sum(slabs[:slab]) * unit // tile, slabs[slab] * unit
    lhs = pl.BlockSpec((groups, piece, width), lambda n: (0, 0, 0))
    weight = pl.BlockSpec((depth, tile), lambda n: (0, first + n))
    out = pl.BlockSpec((piece, tile), lambda n: (0, n))
    return pl.pallas_call(
        ordered(functools.partial(project_kernel, parts), len(after), 0),
        grid=(cols // tile,),
        out_shape=[jax.ShapeDtypeStruct((piece, cols), f32)]
        + [jax.ShapeDtypeStruct((piece, cols), bf16)] * (groups - 1),
        in_specs=waits(after) + [lhs] * (2 * parts) + [weight, weight],
        out_specs=[out] * groups,
        compiler_params=params(),
        cost_estimate=busy(beside),
        name="project",
    )(*after, *own, *other, own_w, other_w)


def finish_kernel(counts, *refs):
    refs = list(refs)
    out_ref = refs.pop()
    for s, slabs in enumerate(counts):
        at = 0
        for shares in slabs:
            total = refs.pop(0)[...]
            for _ in range(shares):
                total = total + refs.pop(0)[...].astype(f32)
            width = total.shape[1]
            out_ref[s, :, at : at + width] = total.astype(bf16)
            at += width


def finish(sums, piece):
    *slabs, (total, shares) = sums[-1]
    most = [*sums[:-1], slabs]
    counts = [[len(given) for _, given in row] for row in most]
    values = [value for row in most for own, given in row for value in (own, *given)]
    out = jax.ShapeDtypeStruct(
        (len(sums), piece, sum(own.shape[1] for own, _ in sums[-1])), bf16
    )
    begun = pl.pallas_call(
        functools.partial(finish_kernel, counts),
        grid=(1,),
        out_shape=out,
        in_specs=[pl.BlockSpec(value.shape, lambda _: (0, 0)) for value in values],
        out_specs=pl.BlockSpec(out.shape, lambda _: (0, 0, 0)),
        compiler_params=params(),
        cost_estimate=busy(3),
        name="finish",
    )(*values)
    width = total.shape[1]
    place = (len(sums) - 1, 0, out.shape[2] // width - 1)
    return pl.pallas_call(
        ordered(functools.partial(finish_kernel, [[len(shares)]]), 1, 0),
        grid=(1,),
        out_shape=out,
        in_specs=waits([begun])
        + [pl.BlockSpec(value.shape, lambda _: (0, 0)) for value in (total, *shares)],
        out_specs=pl.BlockSpec((1, piece, width), lambda _: place),
        input_output_aliases={0: 0},
        compiler_params=params(),
        cost_estimate=busy(0),
        name="finish_last",
    )(begun, total, *shares)


def nothing(*refs):
    pass


def later_than(value, after):
    anywhere = pl.BlockSpec(memory_space=pl.ANY)
    return pl.pallas_call(
        nothing,
        out_shape=jax.ShapeDtypeStruct(value.shape, value.dtype),
        in_specs=[anywhere] * (1 + len(after)),
        out_specs=anywhere,
        input_output_aliases={0: 0},
        compiler_params=params(1),
        cost_estimate=busy(0),
        name="later_than",
    )(value, *after)


def body(qkv_tokens, sign_bits, out_weight):
    partners, blocks = lax.axis_size("head"), lax.axis_size("seq")
    me, index = lax.axis_index("head"), lax.axis_index("seq")
    seqs = qkv_tokens.shape[0]
    heads, dh = sign_bits.shape[0], sign_bits.shape[-1]
    levels = (blocks // GROUP).bit_length() - 1
    x = qkv_tokens.transpose(0, 2, 1, 3)
    piece = x.shape[2]
    where = jnp.stack(
        [me, index % GROUP] + [(index // GROUP >> l) & 1 for l in range(levels)]
    ).astype(jnp.int32)

    outer, shape = range(2, partners, 2), (piece, x.shape[3] // partners)
    beside = [(s, kind, 1) for s in range(seqs) for kind in (0, 1, 2)]
    beside += [
        (s, kind, k + 1)
        for s in range(seqs)
        for kind in (0, 1, 2)
        for k in outer
        if s > 0 or kind == 0
    ]
    straight = [[[(x, 0, kind, k) for kind in (1, 2)]] for k in range(2, partners)]
    *first, near = pack(where, [*straight, [[(x, *entry) for entry in beside]]], shape, 60)
    first = [swap(value, "head", k + 2) for k, value in enumerate(first)]
    near = swap(near, "head", 1)
    messages = [(s, (1, 2)) for s in range(1, seqs)] + [(s, (0,)) for s in range(seqs)]
    wanted = [
        [
            [(x, s, kind, k) for kind in kinds],
            [(near, 0, beside.index((s, kind, k + 1)), None) for kind in kinds],
        ]
        for s, kinds in messages
        for k in outer
    ]
    wanted.append([[(x, s, kind, 0) for kind in (0, 1, 2)] for s in range(seqs)])
    *packed, own_rows = pack(where, wanted, shape, 20)
    packed = [swap(value, "head", k) for value, k in zip(packed, list(outer) * len(messages))]
    packed = [packed[n * len(outer) : (n + 1) * len(outer)] for n in range(len(messages))]
    asked = packed[seqs - 1 :]

    def pieces(s, kind):
        found = [(own_rows, s, kind), (near, 0, beside.index((s, kind, 1)))]
        if s == 0 and kind > 0:
            return found + [(value, 0, kind - 1) for value in first]
        row, at = (packed[s - 1], kind - 1) if kind > 0 else (asked[s], 0)
        return found + [(value, half, at) for value in row for half in (0, 1)]

    maps = integer_maps(sign_bits)

    last = [own_rows]
    begun, chains, riders, ends, locals_, own, other, totals = {}, {}, {}, {}, {}, {}, {}, {}

    def early(n):
        begun[n] = early_sums(
            maps, pieces(n, 1)[:2], pieces(n, 2)[:2], heads, dh, piece, last
        )
        last[:] = [begun[n][0]]

    def state(n):
        feats, mine, *others = block_state(
            where,
            maps,
            pieces(n, 1)[2:],
            pieces(n, 2)[2:],
            begun[n][1],
            heads,
            dh,
            piece,
            last,
            3 if n else 0,
        )
        begun[n] = begun[n][0], feats
        chains[n], riders[n] = [(mine, 0)], others
        if n == 0:
            chains[n] += [(swap(value, "seq", m + 1), 0) for m, value in enumerate(others)]
        last[:] = [mine]

    def step(n):
        ending = len(chains[n]) == GROUP + levels
        riding = riders[n + 1] if ending and n + 1 < seqs else []
        first_out, *others = chain_step(
            where,
            levels,
            chains[n],
            riding,
            last,
            STEP_US if n and len(chains[n]) == GROUP else 0,
        )
        last[:] = [first_out]
        if ending:
            came_back = [swap(value, "seq", m + 1) for m, value in enumerate(others)]
            ends[n] = [(first_out, 0)] + [(value, 0) for value in came_back]
            if riding:
                chains[n + 1] += [(value, riding[0].shape[0]) for value in came_back]
        else:
            bit = GROUP << (len(chains[n]) - GROUP)
            chains[n] = chains[n] + [(swap(first_out, "seq", bit), 0)]

    def local(n, first, last_row):
        part = attend_local(
            where,
            maps,
            begun[n],
            pieces(n, 0)[first:last_row],
            pieces(n, 2),
            first,
            heads,
            dh,
            piece,
            last,
            3,
        )
        locals_.setdefault(n, []).append(part)
        last[:] = [part[0]]

    def attend(n):
        stay, leave = attend_prior(
            where, locals_[n], ends[n], piece, dh, last, 1 if n + 1 < seqs else 0
        )
        own[n], other[n] = [stay], [swap(leave, "head", 1)]
        last[:] = [stay]

    def multiply(s, slab):
        if slab == 1:
            for key in totals:
                if key[0] < s:
                    last.extend(totals[key][1])
        total, *shares = project(
            own[s], other[s], out_weight, other_weight, slabs[s], slab, last, 0 if s == seqs - 1 else 6
        )
        totals[s, slab] = total, [swap(v, "head", 2 * (g + 1)) for g, v in enumerate(shares)]
        last[:] = [total]

    slabs = [SLABS[0]] * (seqs - 1) + [SLABS[1]]
    plan = []
    for n in range(seqs):
        came = (11.9 + 9 * levels) * n
        end = came + 22 + 9 * levels
        plan.append((came, state, n))
        if n > 0:
            plan.append((came - 21, early, n))
        plan += [(came + 12 + 9 * j, step, n) for j in range(levels + 1)]
        if n == 0:
            plan += [(came + 12.5, local, n, 0, 2), (end - 7, local, n, 2, partners)]
        else:
            plan.append((end - 7, local, n, 0, partners))
        plan.append((end, attend, n))
        plan += [(end + 6 + 3.5 * j, multiply, n, j) for j in range(len(slabs[n]))]
    plan = sorted(plan, key=lambda entry: entry[0])
    early(0)
    state(0)
    other_weight = swap(later_than(out_weight, last), "head", 1)
    for _, act, *which in plan:
        if (act, which) != (state, [0]):
            act(*which)

    return finish([[totals[s, n] for n in range(len(slabs[s]))] for s in range(seqs)], piece)


def solution(mesh):
    return jax.shard_map(
        body,
        mesh=mesh,
        in_specs=(
            P(None, ("seq", "head"), None, None),
            P("head", None, None, None),
            P("head", None),
        ),
        out_specs=P(None, ("seq", "head"), None),
        check_vma=False,
    )
```

```python
import functools
import math

import jax
import jax.numpy as jnp
import numpy as np
from jax import lax
from jax.experimental import pallas as pl
from jax.experimental.pallas import tpu as pltpu
from jax.sharding import PartitionSpec as P

logit_divisor = 1.3
norm_epsilon = 1e-06
SLABS = (8,), (4, 3, 1)

bf16, f32 = jnp.bfloat16, jnp.float32
ROW_TILE = 16
STEP_US = 4
GROUP = 4


def params(mebibytes=20):
    return pltpu.CompilerParams(vmem_limit_bytes=mebibytes * 1024 * 1024)


def vmem(count):
    return [pl.BlockSpec(memory_space=pltpu.VMEM)] * count


def smem():
    return pl.BlockSpec(memory_space=pltpu.SMEM)


def ordered(kernel, count, skip):
    return lambda *refs: kernel(*refs[:skip], *refs[skip + count :])


def busy(microseconds):
    return pl.CostEstimate(flops=int(microseconds * 1e9), bytes_accessed=0, transcendentals=0)


def waits(after):
    return [pl.BlockSpec(memory_space=pl.ANY)] * len(after)


def swap(value, axis, bit):
    return lax.ppermute(value, axis, [(j, j ^ bit) for j in range(lax.axis_size(axis))])


def sign_matrix(order):
    ids = np.arange(order)
    common = ids[:, None] & ids[None, :]
    parity = np.zeros_like(common)
    while common.any():
        parity ^= common & 1
        common = common >> 1
    return (1 - 2 * parity).astype(np.float32)


def maps_kernel(bits_ref, had_ref, maps_ref):
    had = had_ref[...]
    dh = had.shape[0]
    for h in range(bits_ref.shape[0]):
        for b in range(bits_ref.shape[1]):
            signs = (2 * bits_ref[h, b] - 1).astype(f32)
            inner = jnp.dot((had * signs[2:3]).astype(bf16), had, preferred_element_type=f32)
            outer = jnp.dot((inner * signs[1:2]).astype(bf16), had, preferred_element_type=f32)
            whole = jnp.transpose(outer * signs[0:1])
            near = whole.astype(bf16)
            columns = slice(b * dh, (b + 1) * dh)
            maps_ref[h, :dh, columns] = near
            maps_ref[h, dh:, columns] = (whole - near.astype(f32)).astype(bf16)


def integer_maps(sign_bits):
    heads, blocks, _, dh = sign_bits.shape
    return pl.pallas_call(
        maps_kernel,
        out_shape=jax.ShapeDtypeStruct((heads, 2 * dh, blocks * dh), bf16),
        in_specs=vmem(2),
        out_specs=vmem(1)[0],
        compiler_params=params(),
        cost_estimate=busy(0),
        name="integer_maps",
    )(sign_bits, jnp.asarray(sign_matrix(dh), bf16))


def features(rows_of, maps_ref, out_ref):
    heads, twice, _ = maps_ref.shape
    dh = twice // 2
    rows = [rows_of(i) for i in range(heads)]
    scales = []
    for i in range(heads):
        wide = rows[i].astype(f32)
        mean = jnp.sum(wide * wide, axis=-1, keepdims=True) * (1.0 / dh)
        scales.append(lax.rsqrt(mean + norm_epsilon) * (logit_divisor / dh**0.25 / dh))
    for i in range(heads):
        product = jnp.dot(
            jnp.concatenate([rows[i], rows[i]], axis=1), maps_ref[i], preferred_element_type=f32
        )
        out_ref[i] = jnp.exp(product * scales[i]).astype(bf16)


def pack_kernel(places, arrays, where_ref, *refs):
    ins, outs, sems = refs[:arrays], refs[arrays:-1], refs[-1]
    copies = []
    for n, (which, first, second, k, out, i, j, count) in enumerate(places):
        width = outs[out].shape[-1]
        start = 0 if k is None else pl.multiple_of((where_ref[0] ^ k) * width, width)
        source = ins[which].at[first, pl.ds(second, count), :, pl.ds(start, width)]
        copies.append(pltpu.make_async_copy(source, outs[out].at[i, pl.ds(j, count)], sems.at[n]))
    for copy in copies:
        copy.start()
    for copy in copies:
        copy.wait()


def first_pack_kernel(places, where_ref, x_ref, *refs):
    *outs, stage, loaded, packed = refs
    entries = sorted({place[:2] for place in places}, key=lambda entry: (entry[0], -entry[1]))
    loads = [
        pltpu.make_async_copy(x_ref.at[entry], stage.at[entry], loaded.at[n])
        for n, entry in enumerate(entries)
    ]
    for load in loads:
        load.start()
    copies = []
    for entry, load in zip(entries, loads):
        load.wait()
        for n, (first, second, k, out, i, j) in enumerate(places):
            if (first, second) == entry:
                width = outs[out].shape[-1]
                start = pl.multiple_of((where_ref[0] ^ k) * width, width)
                source = stage.at[first, second, :, pl.ds(start, width)]
                copies.append(pltpu.make_async_copy(source, outs[out].at[i, j], packed.at[n]))
                copies[-1].start()
    for copy in copies:
        copy.wait()


def first_pack(where, x, wanted, shape):
    places = [
        (first, second, k, out, i, j)
        for out, table in enumerate(wanted)
        for i, row in enumerate(table)
        for j, (first, second, k) in enumerate(row)
    ]
    shapes = [(len(table), len(table[0]), *shape) for table in wanted]
    return pl.pallas_call(
        functools.partial(first_pack_kernel, places),
        out_shape=[jax.ShapeDtypeStruct(shape, bf16) for shape in shapes],
        in_specs=[smem(), pl.BlockSpec(memory_space=pl.ANY)],
        out_specs=vmem(len(shapes)),
        scratch_shapes=[
            pltpu.VMEM(x.shape, bf16),
            pltpu.SemaphoreType.DMA((x.shape[0] * x.shape[1],)),
            pltpu.SemaphoreType.DMA((len(places),)),
        ],
        compiler_params=params(60),
        cost_estimate=busy(0),
        name="first_pack",
    )(where, x)


def pack(where, wanted, shape, mebibytes):
    arrays, places, shapes = [], [], []
    for out, table in enumerate(wanted):
        shapes.append((len(table), len(table[0]), *shape))
        for i, row in enumerate(table):
            for j, (array, first, second, k) in enumerate(row):
                if not any(array is known for known in arrays):
                    arrays.append(array)
                which = [array is known for known in arrays].index(True)
                before = places[-1] if places else None
                if before and before[:6] == (which, first, second - before[7], k, out, i):
                    places[-1] = (*before[:7], before[7] + 1)
                else:
                    places.append((which, first, second, k, out, i, j, 1))
    return pl.pallas_call(
        functools.partial(pack_kernel, places, len(arrays)),
        out_shape=[jax.ShapeDtypeStruct(shape, bf16) for shape in shapes],
        in_specs=[pl.BlockSpec(memory_space=pltpu.SMEM)]
        + [pl.BlockSpec(memory_space=pl.ANY)] * len(arrays),
        out_specs=[pl.BlockSpec(memory_space=pltpu.VMEM)] * len(shapes),
        scratch_shapes=[pltpu.SemaphoreType.DMA((len(places),))],
        compiler_params=params(mebibytes),
        cost_estimate=busy(0),
        name="pack",
    )(where, *arrays)


def joined(refs, places, cut):
    return jnp.concatenate(
        [ref[lead, kind, :, cut] for ref, (lead, kind) in zip(refs, places)], axis=0
    )


def sums_kernel(k_at, v_at, heads, dh, maps_ref, *refs):
    pieces = len(k_at)
    k_refs, v_refs = refs[:pieces], refs[pieces : 2 * pieces]
    *before, feats_ref, sums_ref = refs[2 * pieces :]
    cuts = [slice(i * dh, (i + 1) * dh) for i in range(heads)]
    features(lambda i: joined(k_refs, k_at, cuts[i]), maps_ref, feats_ref)
    for i in range(heads):
        feats = feats_ref[i]
        state = lax.dot_general(
            joined(v_refs, v_at, cuts[i]),
            feats,
            (((0,), (0,)), ((), ())),
            preferred_element_type=f32,
        )
        sums_ref[i, :dh] = before[0][i, :dh] + state if before else state
    for i in range(heads):
        total = jnp.sum(feats_ref[i].astype(f32), axis=0, keepdims=True)
        total = jnp.broadcast_to(total, (sums_ref.shape[1] - dh, total.shape[1]))
        sums_ref[i, dh:] = before[0][i, dh:] + total if before else total


def early_sums(maps, keys, values, heads, dh, piece, after):
    feat = maps.shape[2]
    rows = len(keys) * piece
    (arrays, k_at), (others, v_at) = split(keys), split(values)
    return pl.pallas_call(
        ordered(functools.partial(sums_kernel, k_at, v_at, heads, dh), len(after), 0),
        out_shape=[
            jax.ShapeDtypeStruct((heads, rows, feat), bf16),
            jax.ShapeDtypeStruct((heads, dh + 8, feat), f32),
        ],
        in_specs=waits(after) + vmem(1 + 2 * len(keys)),
        out_specs=vmem(2),
        compiler_params=params(),
        cost_estimate=busy(0),
        name="early_sums",
    )(*after, maps, *arrays, *others)


def split(pieces):
    return [piece[0] for piece in pieces], [piece[1:] for piece in pieces]


def state_kernel(k_at, v_at, heads, dh, where_ref, maps_ref, *refs):
    count = 2 * len(k_at) + 2
    *ins, feats_ref, sums_ref = refs[:count] + refs[-1:]
    share_refs = refs[count:-1]
    sums_kernel(k_at, v_at, heads, dh, maps_ref, *ins, feats_ref, sums_ref)
    share = heads // GROUP
    pad = jnp.zeros((ROW_TILE - share, feats_ref.shape[-1]), f32)
    states = [sums_ref[i] for i in range(heads)]
    shares = []
    for g in range(GROUP):
        mine = states[g * share : (g + 1) * share]
        shares.append(
            jnp.concatenate([v[:dh] for v in mine] + [v[dh : dh + 1] for v in mine] + [pad], axis=0)
        )
    for m, ref in enumerate(share_refs):
        ref[...] = chosen(shares, where_ref[1] ^ m).astype(ref.dtype)


def chosen(values, index):
    result = values[0]
    for n, value in enumerate(values[1:]):
        result = jnp.where(index == n + 1, value, result)
    return result


def block_state(where, maps, keys, values, before, heads, dh, piece, after, beside):
    feat = maps.shape[2]
    rows = len(keys) * piece
    height = heads // GROUP * dh + ROW_TILE
    (arrays, k_at), (others, v_at) = split(keys), split(values)
    return pl.pallas_call(
        ordered(functools.partial(state_kernel, k_at, v_at, heads, dh), len(after), 0),
        out_shape=[
            jax.ShapeDtypeStruct((heads, rows, feat), bf16),
            jax.ShapeDtypeStruct((height, feat), f32),
        ]
        + [jax.ShapeDtypeStruct((height, feat), bf16)] * (GROUP - 1),
        in_specs=waits(after) + [smem()] + vmem(2 + 2 * len(keys)),
        out_specs=vmem(1 + GROUP),
        scratch_shapes=[pltpu.VMEM(before.shape, f32)],
        compiler_params=params(),
        cost_estimate=busy(beside),
        name="block_state",
    )(*after, where, maps, *arrays, *others, before)


def step_kernel(levels, where_ref, *refs):
    ins = refs[: len(refs) - (1 if len(refs) < 2 * GROUP + levels else GROUP)]
    outs = refs[len(ins) :]
    values = [ref[...].astype(f32) for ref in ins[:GROUP]]
    got = [ref[...].astype(f32) for ref in ins[GROUP:]]
    if len(outs) == 1:
        total = values[0]
        for value in values[1:] + got:
            total = total + value
        outs[0][...] = total.astype(bf16)
        return
    prior = jnp.zeros_like(values[0])
    for level, value in enumerate(got):
        prior = prior + jnp.where(where_ref[2 + level] == 1, value, 0.0)
    mine = where_ref[1]
    for m, out in enumerate(outs):
        result = prior
        for other, value in enumerate(values):
            if other != m:
                result = result + jnp.where((mine ^ other) < (mine ^ m), value, 0.0)
        out[...] = result.astype(bf16)


def chain_step(where, levels, values, after, beside):
    shape = values[0].shape
    count = GROUP if len(values) == GROUP + levels else 1
    return pl.pallas_call(
        ordered(functools.partial(step_kernel, levels), len(after), 0),
        out_shape=[jax.ShapeDtypeStruct(shape, bf16)] * count,
        in_specs=waits(after) + [smem()] + vmem(len(values)),
        out_specs=vmem(count),
        compiler_params=params(),
        cost_estimate=busy(beside),
        name="chain_step",
    )(*after, where, *values)


def local_kernel(first, q_at, v_at, heads, dh, where_ref, maps_ref, early_ref, late_ref, *refs):
    asking, partners = len(q_at), len(v_at)
    q_refs, v_refs = refs[:asking], refs[asking : asking + partners]
    query_feats_ref, local_ref, weights_ref = refs[asking + partners :]
    piece = q_refs[0].shape[2]
    rows = partners * piece
    me = where_ref[0]

    def places(first, count, shape, dim):
        ids = lax.broadcasted_iota(jnp.int32, shape, dim)
        result = ids + (me ^ first) * piece
        for j in range(1, count):
            result = jnp.where(ids >= j * piece, ids + ((me ^ (first + j)) - j) * piece, result)
        return result

    here = places(first, asking, (asking * piece, 1), 0)
    causal = here >= places(0, partners, (1, rows), 1)
    ones = jnp.ones((rows, dh), bf16)
    cuts = [slice(i * dh, (i + 1) * dh) for i in range(heads)]
    features(lambda i: joined(q_refs, q_at, cuts[i]), maps_ref, query_feats_ref)
    for i in range(heads):
        scores = lax.dot_general(
            query_feats_ref[i],
            jnp.concatenate([early_ref[i], late_ref[i]], axis=0),
            (((1,), (1,)), ((), ())),
            preferred_element_type=f32,
        )
        weights_ref[i] = jnp.where(causal, scores, 0.0).astype(bf16)
    for i in range(heads):
        local_ref[i] = jnp.dot(
            weights_ref[i],
            jnp.concatenate([joined(v_refs, v_at, cuts[i]), ones], axis=1),
            preferred_element_type=f32,
        )


def attend_local(where, maps, feats, queries, values, first, heads, dh, piece, after, beside):
    feat = maps.shape[2]
    rows = len(queries) * piece
    (arrays, q_at), (others, v_at) = split(queries), split(values)
    return pl.pallas_call(
        ordered(functools.partial(local_kernel, first, q_at, v_at, heads, dh), len(after), 0),
        out_shape=[
            jax.ShapeDtypeStruct((heads, rows, feat), bf16),
            jax.ShapeDtypeStruct((heads, rows, 2 * dh), f32),
        ],
        in_specs=waits(after) + [smem()] + vmem(1 + len(feats) + len(queries) + len(values)),
        out_specs=vmem(2),
        scratch_shapes=[pltpu.VMEM((heads, rows, len(values) * piece), bf16)],
        compiler_params=params(),
        cost_estimate=busy(beside),
        name="attend_local",
    )(*after, where, maps, *feats, *arrays, *others)


def prior_kernel(pieces, heads, dh, where_ref, *refs):
    parts = len(pieces)
    asked = [(refs[2 * p], refs[2 * p + 1]) for p in range(parts)]
    share_refs, (stay_ref, leave_ref) = refs[2 * parts : 2 * parts + GROUP], refs[-2:]
    piece = stay_ref.shape[1]
    share = heads // GROUP
    priors = []
    for i in range(heads):
        j = i % share
        state, total = slice(j * dh, (j + 1) * dh), slice(share * dh, share * dh + ROW_TILE)
        source = where_ref[1] ^ (i // share)
        prior = chosen([ref[state, :] for ref in share_refs], source)
        tail = chosen([ref[total, :] for ref in share_refs], source)
        tail = jnp.broadcast_to(tail[j : j + 1, :], prior.shape)
        priors.append(jnp.concatenate([prior, tail], axis=0))
    first = 0
    for count, (query_feats_ref, local_ref) in zip(pieces, asked):
        sums = [
            local_ref[i]
            + lax.dot_general(
                query_feats_ref[i], priors[i], (((1,), (1,)), ((), ())), preferred_element_type=f32
            )
            for i in range(heads)
        ]
        for i in range(heads):
            attended = (sums[i][:, :dh] / sums[i][:, dh:]).astype(bf16)
            for n in range(count):
                out = leave_ref if (first + n) & 1 else stay_ref
                out[(first + n) // 2, :, i * dh : (i + 1) * dh] = attended[n * piece : (n + 1) * piece]
        first += count


def attend_prior(where, asked, shares, piece, dh, after, beside):
    heads = asked[0][0].shape[0]
    pieces = [query_feats.shape[1] // piece for query_feats, _ in asked]
    out = jax.ShapeDtypeStruct((sum(pieces) // 2, piece, heads * dh), bf16)
    values = [value for pair in asked for value in pair]
    return pl.pallas_call(
        ordered(functools.partial(prior_kernel, pieces, heads, dh), len(after), 0),
        out_shape=[out, out],
        in_specs=waits(after) + [smem()] + vmem(len(values) + len(shares)),
        out_specs=vmem(2),
        compiler_params=params(),
        cost_estimate=busy(beside),
        name="attend_prior",
    )(*after, where, *values, *shares)


def project_kernel(parts, *refs):
    own_refs, other_refs = refs[:parts], refs[parts : 2 * parts]
    own_w, other_w, stay_ref, *leave_refs = refs[2 * parts :]
    groups, piece, width = own_refs[0].shape
    acc = None
    for lhs_refs, w_ref in ((own_refs, own_w), (other_refs, other_w)):
        for p, ref in enumerate(lhs_refs):
            lhs = ref[...].reshape(groups * piece, width)
            term = jnp.dot(
                lhs, w_ref[p * width : (p + 1) * width, :], preferred_element_type=f32
            )
            acc = term if acc is None else acc + term
    stay_ref[...] = acc[:piece]
    for g, ref in enumerate(leave_refs):
        ref[...] = acc[(g + 1) * piece : (g + 2) * piece].astype(bf16)


def project(own, other, own_w, other_w, slabs, slab, after, beside):
    parts, (groups, piece, width) = len(own), own[0].shape
    depth, cols = own_w.shape
    unit = cols // sum(slabs)
    tile = math.gcd(cols * slabs[slab] // sum(slabs), 1024)
    tile = math.gcd(tile, sum(slabs[:slab]) * unit) if slab else tile
    first, cols = sum(slabs[:slab]) * unit // tile, slabs[slab] * unit
    lhs = pl.BlockSpec((groups, piece, width), lambda n: (0, 0, 0))
    weight = pl.BlockSpec((depth, tile), lambda n: (0, first + n))
    out = pl.BlockSpec((piece, tile), lambda n: (0, n))
    return pl.pallas_call(
        ordered(functools.partial(project_kernel, parts), len(after), 0),
        grid=(cols // tile,),
        out_shape=[jax.ShapeDtypeStruct((piece, cols), f32)]
        + [jax.ShapeDtypeStruct((piece, cols), bf16)] * (groups - 1),
        in_specs=waits(after) + [lhs] * (2 * parts) + [weight, weight],
        out_specs=[out] * groups,
        compiler_params=params(),
        cost_estimate=busy(beside),
        name="project",
    )(*after, *own, *other, own_w, other_w)


def finish_kernel(counts, *refs):
    refs = list(refs)
    out_ref = refs.pop()
    for s, slabs in enumerate(counts):
        at = 0
        for shares in slabs:
            total = refs.pop(0)[...]
            for _ in range(shares):
                total = total + refs.pop(0)[...].astype(f32)
            width = total.shape[1]
            out_ref[s, :, at : at + width] = total.astype(bf16)
            at += width


def finish(sums, piece):
    *slabs, (total, shares) = sums[-1]
    most = [*sums[:-1], slabs]
    counts = [[len(given) for _, given in row] for row in most]
    values = [value for row in most for own, given in row for value in (own, *given)]
    out = jax.ShapeDtypeStruct(
        (len(sums), piece, sum(own.shape[1] for own, _ in sums[-1])), bf16
    )
    begun = pl.pallas_call(
        functools.partial(finish_kernel, counts),
        grid=(1,),
        out_shape=out,
        in_specs=[pl.BlockSpec(value.shape, lambda _: (0, 0)) for value in values],
        out_specs=pl.BlockSpec(out.shape, lambda _: (0, 0, 0)),
        compiler_params=params(),
        cost_estimate=busy(3),
        name="finish",
    )(*values)
    width = total.shape[1]
    place = (len(sums) - 1, 0, out.shape[2] // width - 1)
    return pl.pallas_call(
        ordered(functools.partial(finish_kernel, [[len(shares)]]), 1, 0),
        grid=(1,),
        out_shape=out,
        in_specs=waits([begun])
        + [pl.BlockSpec(value.shape, lambda _: (0, 0)) for value in (total, *shares)],
        out_specs=pl.BlockSpec((1, piece, width), lambda _: place),
        input_output_aliases={0: 0},
        compiler_params=params(),
        cost_estimate=busy(0),
        name="finish_last",
    )(begun, total, *shares)


def nothing(*refs):
    pass


def later_than(value, after):
    anywhere = pl.BlockSpec(memory_space=pl.ANY)
    return pl.pallas_call(
        nothing,
        out_shape=jax.ShapeDtypeStruct(value.shape, value.dtype),
        in_specs=[anywhere] * (1 + len(after)),
        out_specs=anywhere,
        input_output_aliases={0: 0},
        compiler_params=params(1),
        cost_estimate=busy(0),
        name="later_than",
    )(value, *after)


def body(qkv_tokens, sign_bits, out_weight):
    partners, blocks = lax.axis_size("head"), lax.axis_size("seq")
    me, index = lax.axis_index("head"), lax.axis_index("seq")
    seqs = qkv_tokens.shape[0]
    heads, dh = sign_bits.shape[0], sign_bits.shape[-1]
    levels = (blocks // GROUP).bit_length() - 1
    x = qkv_tokens.transpose(0, 2, 1, 3)
    piece = x.shape[2]
    where = jnp.stack(
        [me, index % GROUP] + [(index // GROUP >> l) & 1 for l in range(levels)]
    ).astype(jnp.int32)

    outer, shape = range(2, partners, 2), (piece, x.shape[3] // partners)
    beside = [(s, kind, 1) for s in range(seqs) for kind in (0, 1, 2)]
    beside += [
        (s, kind, k + 1)
        for s in range(seqs)
        for kind in (0, 1, 2)
        for k in outer
        if s > 0 or kind == 0
    ]
    straight = [[[(0, kind, k) for kind in (1, 2)]] for k in range(2, partners)]
    *first, near = first_pack(where, x, [*straight, [beside]], shape)
    first = [swap(value, "head", k + 2) for k, value in enumerate(first)]
    near = swap(near, "head", 1)
    messages = [(s, (1, 2)) for s in range(1, seqs)] + [(s, (0,)) for s in range(seqs)]
    wanted = [
        [
            [(x, s, kind, k) for kind in kinds],
            [(near, 0, beside.index((s, kind, k + 1)), None) for kind in kinds],
        ]
        for s, kinds in messages
        for k in outer
    ]
    wanted.append([[(x, s, kind, 0) for kind in (0, 1, 2)] for s in range(seqs)])
    *packed, own_rows = pack(where, wanted, shape, 20)
    packed = [swap(value, "head", k) for value, k in zip(packed, list(outer) * len(messages))]
    packed = [packed[n * len(outer) : (n + 1) * len(outer)] for n in range(len(messages))]
    asked = packed[seqs - 1 :]

    def pieces(s, kind):
        found = [(own_rows, s, kind), (near, 0, beside.index((s, kind, 1)))]
        if s == 0 and kind > 0:
            return found + [(value, 0, kind - 1) for value in first]
        row, at = (packed[s - 1], kind - 1) if kind > 0 else (asked[s], 0)
        return found + [(value, half, at) for value in row for half in (0, 1)]

    maps = integer_maps(sign_bits)

    last = [own_rows]
    begun, chains, ends, locals_, own, other, totals = {}, {}, {}, {}, {}, {}, {}

    def early(n):
        begun[n] = early_sums(
            maps, pieces(n, 1)[:2], pieces(n, 2)[:2], heads, dh, piece, last
        )
        last[:] = [begun[n][0]]

    def state(n):
        feats, mine, *others = block_state(
            where,
            maps,
            pieces(n, 1)[2:],
            pieces(n, 2)[2:],
            begun[n][1],
            heads,
            dh,
            piece,
            last,
            3 if n else 0,
        )
        begun[n] = begun[n][0], feats
        chains[n] = [mine] + [swap(value, "seq", m + 1) for m, value in enumerate(others)]
        last[:] = [mine]

    def step(n):
        first_out, *others = chain_step(where, levels, chains[n], last, STEP_US if n and len(chains[n]) == GROUP else 0)
        last[:] = [first_out]
        if others:
            ends[n] = [first_out] + [swap(value, "seq", m + 1) for m, value in enumerate(others)]
        else:
            chains[n] = chains[n] + [swap(first_out, "seq", GROUP << (len(chains[n]) - GROUP))]

    def local(n, first, last_row):
        part = attend_local(
            where,
            maps,
            begun[n],
            pieces(n, 0)[first:last_row],
            pieces(n, 2),
            first,
            heads,
            dh,
            piece,
            last,
            3,
        )
        locals_.setdefault(n, []).append(part)
        last[:] = [part[0]]

    def attend(n):
        stay, leave = attend_prior(
            where, locals_[n], ends[n], piece, dh, last, 1 if n + 1 < seqs else 0
        )
        own[n], other[n] = [stay], [swap(leave, "head", 1)]
        last[:] = [stay]

    def multiply(s, slab):
        if slab == 1 and s > 0:
            for key in totals:
                if key[0] < s:
                    last.extend(totals[key][1])
        total, *shares = project(
            own[s], other[s], out_weight, other_weight, slabs[s], slab, last, 6 if slab == len(slabs[s]) - 1 and s < seqs - 1 else 0
        )
        totals[s, slab] = total, [swap(v, "head", 2 * (g + 1)) for g, v in enumerate(shares)]
        last[:] = [total]

    slabs = [SLABS[0]] * (seqs - 1) + [SLABS[1]]
    plan = []
    for n in range(seqs):
        came = 22 * n
        end = came + 22 + 9 * levels
        plan.append((came, state, n))
        if n > 0:
            plan.append((came - 21, early, n))
        plan += [(came + 12 + 9 * j, step, n) for j in range(levels + 1)]
        if n == 0:
            plan += [(came + 12.5, local, n, 0, 2), (end - 7, local, n, 2, partners)]
        else:
            plan.append((end - 7, local, n, 0, partners))
        plan.append((end, attend, n))
        plan += [(end + 6 + (3.5 if n == seqs - 1 else 0.1) * j, multiply, n, j) for j in range(len(slabs[n]))]
    plan = sorted(plan, key=lambda entry: entry[0])
    early(0)
    state(0)
    other_weight = swap(later_than(out_weight, last), "head", 1)
    for _, act, *which in plan:
        if (act, which) != (state, [0]):
            act(*which)

    return finish([[totals[s, n] for n in range(len(slabs[s]))] for s in range(seqs)], piece)


def solution(mesh):
    return jax.shard_map(
        body,
        mesh=mesh,
        in_specs=(
            P(None, ("seq", "head"), None, None),
            P("head", None, None, None),
            P("head", None),
        ),
        out_specs=P(None, ("seq", "head"), None),
        check_vma=False,
    )
```

```python
import functools
import math

import jax
import jax.numpy as jnp
import numpy as np
from jax import lax
from jax.experimental import pallas as pl
from jax.experimental.pallas import tpu as pltpu
from jax.sharding import PartitionSpec as P

logit_divisor = 1.3
norm_epsilon = 1e-06
SLABS = (8,), (4, 3, 1)

bf16, f32 = jnp.bfloat16, jnp.float32
ROW_TILE = 16
STEP_US = 4
GROUP = 4


def params(mebibytes=20):
    return pltpu.CompilerParams(vmem_limit_bytes=mebibytes * 1024 * 1024)


def vmem(count):
    return [pl.BlockSpec(memory_space=pltpu.VMEM)] * count


def smem():
    return pl.BlockSpec(memory_space=pltpu.SMEM)


def ordered(kernel, count, skip):
    return lambda *refs: kernel(*refs[:skip], *refs[skip + count :])


def busy(microseconds):
    return pl.CostEstimate(flops=int(microseconds * 1e9), bytes_accessed=0, transcendentals=0)


def waits(after):
    return [pl.BlockSpec(memory_space=pl.ANY)] * len(after)


def swap(value, axis, bit):
    return lax.ppermute(value, axis, [(j, j ^ bit) for j in range(lax.axis_size(axis))])


def sign_matrix(order):
    ids = np.arange(order)
    common = ids[:, None] & ids[None, :]
    parity = np.zeros_like(common)
    while common.any():
        parity ^= common & 1
        common = common >> 1
    return (1 - 2 * parity).astype(np.float32)


def maps_kernel(bits_ref, had_ref, maps_ref):
    had = had_ref[...]
    dh = had.shape[0]
    for h in range(bits_ref.shape[0]):
        for b in range(bits_ref.shape[1]):
            signs = (2 * bits_ref[h, b] - 1).astype(f32)
            inner = jnp.dot((had * signs[2:3]).astype(bf16), had, preferred_element_type=f32)
            outer = jnp.dot((inner * signs[1:2]).astype(bf16), had, preferred_element_type=f32)
            whole = outer * signs[0:1]
            near = whole.astype(bf16)
            rows = slice(b * dh, (b + 1) * dh)
            maps_ref[h, rows, :dh] = near
            maps_ref[h, rows, dh:] = (whole - near.astype(f32)).astype(bf16)


def integer_maps(sign_bits):
    heads, blocks, _, dh = sign_bits.shape
    return pl.pallas_call(
        maps_kernel,
        out_shape=jax.ShapeDtypeStruct((heads, blocks * dh, 2 * dh), bf16),
        in_specs=vmem(2),
        out_specs=vmem(1)[0],
        compiler_params=params(),
        cost_estimate=busy(0),
        name="integer_maps",
    )(sign_bits, jnp.asarray(sign_matrix(dh), bf16))


def features(rows_of, maps_ref, out_ref):
    heads, _, twice = maps_ref.shape
    dh = twice // 2
    rows = [rows_of(i) for i in range(heads)]
    scales = []
    for i in range(heads):
        wide = rows[i].astype(f32)
        mean = jnp.sum(wide * wide, axis=-1, keepdims=True) * (1.0 / dh)
        scales.append(lax.rsqrt(mean + norm_epsilon) * (logit_divisor / dh**0.25 / dh))
    for i in range(heads):
        product = lax.dot_general(
            jnp.concatenate([rows[i], rows[i]], axis=1),
            maps_ref[i],
            (((1,), (1,)), ((), ())),
            preferred_element_type=f32,
        )
        out_ref[i] = jnp.exp(product * scales[i]).astype(bf16)


def pack_kernel(places, arrays, where_ref, *refs):
    ins, outs, sems = refs[:arrays], refs[arrays:-1], refs[-1]
    copies = []
    for n, (which, first, second, k, out, i, j, count) in enumerate(places):
        width = outs[out].shape[-1]
        start = 0 if k is None else pl.multiple_of((where_ref[0] ^ k) * width, width)
        source = ins[which].at[first, pl.ds(second, count), :, pl.ds(start, width)]
        copies.append(pltpu.make_async_copy(source, outs[out].at[i, pl.ds(j, count)], sems.at[n]))
    for copy in copies:
        copy.start()
    for copy in copies:
        copy.wait()


def pack(where, wanted, shape, mebibytes):
    arrays, places, shapes = [], [], []
    for out, table in enumerate(wanted):
        shapes.append((len(table), len(table[0]), *shape))
        for i, row in enumerate(table):
            for j, (array, first, second, k) in enumerate(row):
                if not any(array is known for known in arrays):
                    arrays.append(array)
                which = [array is known for known in arrays].index(True)
                before = places[-1] if places else None
                if before and before[:6] == (which, first, second - before[7], k, out, i):
                    places[-1] = (*before[:7], before[7] + 1)
                else:
                    places.append((which, first, second, k, out, i, j, 1))
    return pl.pallas_call(
        functools.partial(pack_kernel, places, len(arrays)),
        out_shape=[jax.ShapeDtypeStruct(shape, bf16) for shape in shapes],
        in_specs=[pl.BlockSpec(memory_space=pltpu.SMEM)]
        + [pl.BlockSpec(memory_space=pl.ANY)] * len(arrays),
        out_specs=[pl.BlockSpec(memory_space=pltpu.VMEM)] * len(shapes),
        scratch_shapes=[pltpu.SemaphoreType.DMA((len(places),))],
        compiler_params=params(mebibytes),
        cost_estimate=busy(0),
        name="pack",
    )(where, *arrays)


def joined(refs, places, cut):
    return jnp.concatenate(
        [ref[lead, kind, :, cut] for ref, (lead, kind) in zip(refs, places)], axis=0
    )


def sums_kernel(k_at, v_at, heads, dh, maps_ref, *refs):
    pieces = len(k_at)
    k_refs, v_refs = refs[:pieces], refs[pieces : 2 * pieces]
    *before, feats_ref, sums_ref = refs[2 * pieces :]
    cuts = [slice(i * dh, (i + 1) * dh) for i in range(heads)]
    features(lambda i: joined(k_refs, k_at, cuts[i]), maps_ref, feats_ref)
    for i in range(heads):
        feats = feats_ref[i]
        state = lax.dot_general(
            joined(v_refs, v_at, cuts[i]),
            feats,
            (((0,), (0,)), ((), ())),
            preferred_element_type=f32,
        )
        sums_ref[i, :dh] = before[0][i, :dh] + state if before else state
    for i in range(heads):
        total = jnp.sum(feats_ref[i].astype(f32), axis=0, keepdims=True)
        total = jnp.broadcast_to(total, (sums_ref.shape[1] - dh, total.shape[1]))
        sums_ref[i, dh:] = before[0][i, dh:] + total if before else total


def early_sums(maps, keys, values, heads, dh, piece, after):
    feat = maps.shape[1]
    rows = len(keys) * piece
    (arrays, k_at), (others, v_at) = split(keys), split(values)
    return pl.pallas_call(
        ordered(functools.partial(sums_kernel, k_at, v_at, heads, dh), len(after), 0),
        out_shape=[
            jax.ShapeDtypeStruct((heads, rows, feat), bf16),
            jax.ShapeDtypeStruct((heads, dh + 8, feat), f32),
        ],
        in_specs=waits(after) + vmem(1 + 2 * len(keys)),
        out_specs=vmem(2),
        compiler_params=params(),
        cost_estimate=busy(0),
        name="early_sums",
    )(*after, maps, *arrays, *others)


def split(pieces):
    return [piece[0] for piece in pieces], [piece[1:] for piece in pieces]


def state_kernel(k_at, v_at, heads, dh, where_ref, maps_ref, *refs):
    count = 2 * len(k_at) + 2
    *ins, feats_ref, sums_ref = refs[:count] + refs[-1:]
    share_refs = refs[count:-1]
    sums_kernel(k_at, v_at, heads, dh, maps_ref, *ins, feats_ref, sums_ref)
    share = heads // GROUP
    pad = jnp.zeros((ROW_TILE - share, feats_ref.shape[-1]), f32)
    states = [sums_ref[i] for i in range(heads)]
    shares = []
    for g in range(GROUP):
        mine = states[g * share : (g + 1) * share]
        shares.append(
            jnp.concatenate([v[:dh] for v in mine] + [v[dh : dh + 1] for v in mine] + [pad], axis=0)
        )
    for m, ref in enumerate(share_refs):
        ref[...] = chosen(shares, where_ref[1] ^ m).astype(ref.dtype)


def chosen(values, index):
    result = values[0]
    for n, value in enumerate(values[1:]):
        result = jnp.where(index == n + 1, value, result)
    return result


def block_state(where, maps, keys, values, before, heads, dh, piece, after, beside):
    feat = maps.shape[1]
    rows = len(keys) * piece
    height = heads // GROUP * dh + ROW_TILE
    (arrays, k_at), (others, v_at) = split(keys), split(values)
    return pl.pallas_call(
        ordered(functools.partial(state_kernel, k_at, v_at, heads, dh), len(after), 0),
        out_shape=[
            jax.ShapeDtypeStruct((heads, rows, feat), bf16),
            jax.ShapeDtypeStruct((height, feat), f32),
        ]
        + [jax.ShapeDtypeStruct((height, feat), bf16)] * (GROUP - 1),
        in_specs=waits(after) + [smem()] + vmem(2 + 2 * len(keys)),
        out_specs=vmem(1 + GROUP),
        scratch_shapes=[pltpu.VMEM(before.shape, f32)],
        compiler_params=params(),
        cost_estimate=busy(beside),
        name="block_state",
    )(*after, where, maps, *arrays, *others, before)


def step_kernel(levels, where_ref, *refs):
    ins = refs[: len(refs) - (1 if len(refs) < 2 * GROUP + levels else GROUP)]
    outs = refs[len(ins) :]
    values = [ref[...].astype(f32) for ref in ins[:GROUP]]
    got = [ref[...].astype(f32) for ref in ins[GROUP:]]
    if len(outs) == 1:
        total = values[0]
        for value in values[1:] + got:
            total = total + value
        outs[0][...] = total.astype(bf16)
        return
    prior = jnp.zeros_like(values[0])
    for level, value in enumerate(got):
        prior = prior + jnp.where(where_ref[2 + level] == 1, value, 0.0)
    mine = where_ref[1]
    for m, out in enumerate(outs):
        result = prior
        for other, value in enumerate(values):
            if other != m:
                result = result + jnp.where((mine ^ other) < (mine ^ m), value, 0.0)
        out[...] = result.astype(bf16)


def chain_step(where, levels, values, after, beside):
    shape = values[0].shape
    count = GROUP if len(values) == GROUP + levels else 1
    return pl.pallas_call(
        ordered(functools.partial(step_kernel, levels), len(after), 0),
        out_shape=[jax.ShapeDtypeStruct(shape, bf16)] * count,
        in_specs=waits(after) + [smem()] + vmem(len(values)),
        out_specs=vmem(count),
        compiler_params=params(),
        cost_estimate=busy(beside),
        name="chain_step",
    )(*after, where, *values)


def local_kernel(first, q_at, v_at, heads, dh, where_ref, maps_ref, early_ref, late_ref, *refs):
    asking, partners = len(q_at), len(v_at)
    q_refs, v_refs = refs[:asking], refs[asking : asking + partners]
    query_feats_ref, local_ref, weights_ref = refs[asking + partners :]
    piece = q_refs[0].shape[2]
    rows = partners * piece
    me = where_ref[0]

    def places(first, count, shape, dim):
        ids = lax.broadcasted_iota(jnp.int32, shape, dim)
        result = ids + (me ^ first) * piece
        for j in range(1, count):
            result = jnp.where(ids >= j * piece, ids + ((me ^ (first + j)) - j) * piece, result)
        return result

    here = places(first, asking, (asking * piece, 1), 0)
    causal = here >= places(0, partners, (1, rows), 1)
    ones = jnp.ones((rows, dh), bf16)
    cuts = [slice(i * dh, (i + 1) * dh) for i in range(heads)]
    features(lambda i: joined(q_refs, q_at, cuts[i]), maps_ref, query_feats_ref)
    for i in range(heads):
        scores = lax.dot_general(
            query_feats_ref[i],
            jnp.concatenate([early_ref[i], late_ref[i]], axis=0),
            (((1,), (1,)), ((), ())),
            preferred_element_type=f32,
        )
        weights_ref[i] = jnp.where(causal, scores, 0.0).astype(bf16)
    for i in range(heads):
        local_ref[i] = jnp.dot(
            weights_ref[i],
            jnp.concatenate([joined(v_refs, v_at, cuts[i]), ones], axis=1),
            preferred_element_type=f32,
        )


def attend_local(where, maps, feats, queries, values, first, heads, dh, piece, after, beside):
    feat = maps.shape[1]
    rows = len(queries) * piece
    (arrays, q_at), (others, v_at) = split(queries), split(values)
    return pl.pallas_call(
        ordered(functools.partial(local_kernel, first, q_at, v_at, heads, dh), len(after), 0),
        out_shape=[
            jax.ShapeDtypeStruct((heads, rows, feat), bf16),
            jax.ShapeDtypeStruct((heads, rows, 2 * dh), f32),
        ],
        in_specs=waits(after) + [smem()] + vmem(1 + len(feats) + len(queries) + len(values)),
        out_specs=vmem(2),
        scratch_shapes=[pltpu.VMEM((heads, rows, len(values) * piece), bf16)],
        compiler_params=params(),
        cost_estimate=busy(beside),
        name="attend_local",
    )(*after, where, maps, *feats, *arrays, *others)


def prior_kernel(pieces, heads, dh, where_ref, *refs):
    parts = len(pieces)
    asked = [(refs[2 * p], refs[2 * p + 1]) for p in range(parts)]
    share_refs, (stay_ref, leave_ref) = refs[2 * parts : 2 * parts + GROUP], refs[-2:]
    piece = stay_ref.shape[1]
    share = heads // GROUP
    priors = []
    for i in range(heads):
        j = i % share
        state, total = slice(j * dh, (j + 1) * dh), slice(share * dh, share * dh + ROW_TILE)
        source = where_ref[1] ^ (i // share)
        prior = chosen([ref[state, :] for ref in share_refs], source)
        tail = chosen([ref[total, :] for ref in share_refs], source)
        tail = jnp.broadcast_to(tail[j : j + 1, :], prior.shape)
        priors.append(jnp.concatenate([prior, tail], axis=0))
    first = 0
    for count, (query_feats_ref, local_ref) in zip(pieces, asked):
        sums = [
            local_ref[i]
            + lax.dot_general(
                query_feats_ref[i], priors[i], (((1,), (1,)), ((), ())), preferred_element_type=f32
            )
            for i in range(heads)
        ]
        for i in range(heads):
            attended = (sums[i][:, :dh] / sums[i][:, dh:]).astype(bf16)
            for n in range(count):
                out = leave_ref if (first + n) & 1 else stay_ref
                out[(first + n) // 2, :, i * dh : (i + 1) * dh] = attended[n * piece : (n + 1) * piece]
        first += count


def attend_prior(where, asked, shares, piece, dh, after, beside):
    heads = asked[0][0].shape[0]
    pieces = [query_feats.shape[1] // piece for query_feats, _ in asked]
    out = jax.ShapeDtypeStruct((sum(pieces) // 2, piece, heads * dh), bf16)
    values = [value for pair in asked for value in pair]
    return pl.pallas_call(
        ordered(functools.partial(prior_kernel, pieces, heads, dh), len(after), 0),
        out_shape=[out, out],
        in_specs=waits(after) + [smem()] + vmem(len(values) + len(shares)),
        out_specs=vmem(2),
        compiler_params=params(),
        cost_estimate=busy(beside),
        name="attend_prior",
    )(*after, where, *values, *shares)


def project_kernel(first, tile, own_ref, other_ref, own_w, other_w, stay_ref, *leave_refs):
    groups, piece, width = own_ref.shape
    lhs = [ref[...].reshape(groups * piece, width) for ref in (own_ref, other_ref)]
    for n in range(stay_ref.shape[1] // tile):
        here = slice(n * tile, (n + 1) * tile)
        there = slice(first + n * tile, first + (n + 1) * tile)
        acc = jnp.dot(lhs[0], own_w[:, there], preferred_element_type=f32) + jnp.dot(
            lhs[1], other_w[:, there], preferred_element_type=f32
        )
        stay_ref[:, here] = acc[:piece]
        for g, ref in enumerate(leave_refs):
            ref[:, here] = acc[(g + 1) * piece : (g + 2) * piece].astype(bf16)


def project(own, other, own_w, other_w, slabs, slab, after, beside):
    groups, piece, _ = own.shape
    unit = own_w.shape[1] // sum(slabs)
    first, cols = sum(slabs[:slab]) * unit, slabs[slab] * unit
    return pl.pallas_call(
        ordered(
            functools.partial(project_kernel, first, math.gcd(unit, 512)), len(after), 0
        ),
        out_shape=[jax.ShapeDtypeStruct((piece, cols), f32)]
        + [jax.ShapeDtypeStruct((piece, cols), bf16)] * (groups - 1),
        in_specs=waits(after) + vmem(4),
        out_specs=vmem(groups),
        compiler_params=params(),
        cost_estimate=busy(beside),
        name="project",
    )(*after, own, other, own_w, other_w)


def finish_kernel(counts, *refs):
    refs = list(refs)
    out_ref = refs.pop()
    for s, slabs in enumerate(counts):
        at = 0
        for shares in slabs:
            total = refs.pop(0)[...]
            for _ in range(shares):
                total = total + refs.pop(0)[...].astype(f32)
            width = total.shape[1]
            out_ref[s, :, at : at + width] = total.astype(bf16)
            at += width


def finish(sums, piece):
    *slabs, (total, shares) = sums[-1]
    most = [*sums[:-1], slabs]
    counts = [[len(given) for _, given in row] for row in most]
    values = [value for row in most for own, given in row for value in (own, *given)]
    out = jax.ShapeDtypeStruct(
        (len(sums), piece, sum(own.shape[1] for own, _ in sums[-1])), bf16
    )
    begun = pl.pallas_call(
        functools.partial(finish_kernel, counts),
        grid=(1,),
        out_shape=out,
        in_specs=[pl.BlockSpec(value.shape, lambda _: (0, 0)) for value in values],
        out_specs=pl.BlockSpec(out.shape, lambda _: (0, 0, 0)),
        compiler_params=params(),
        cost_estimate=busy(3),
        name="finish",
    )(*values)
    width = total.shape[1]
    place = (len(sums) - 1, 0, out.shape[2] // width - 1)
    return pl.pallas_call(
        ordered(functools.partial(finish_kernel, [[len(shares)]]), 1, 0),
        grid=(1,),
        out_shape=out,
        in_specs=waits([begun])
        + [pl.BlockSpec(value.shape, lambda _: (0, 0)) for value in (total, *shares)],
        out_specs=pl.BlockSpec((1, piece, width), lambda _: place),
        input_output_aliases={0: 0},
        compiler_params=params(),
        cost_estimate=busy(0),
        name="finish_last",
    )(begun, total, *shares)


def nothing(*refs):
    pass


def later_than(value, after):
    anywhere = pl.BlockSpec(memory_space=pl.ANY)
    return pl.pallas_call(
        nothing,
        out_shape=jax.ShapeDtypeStruct(value.shape, value.dtype),
        in_specs=[anywhere] * (1 + len(after)),
        out_specs=anywhere,
        input_output_aliases={0: 0},
        compiler_params=params(1),
        cost_estimate=busy(0),
        name="later_than",
    )(value, *after)


def body(qkv_tokens, sign_bits, out_weight):
    partners, blocks = lax.axis_size("head"), lax.axis_size("seq")
    me, index = lax.axis_index("head"), lax.axis_index("seq")
    seqs = qkv_tokens.shape[0]
    heads, dh = sign_bits.shape[0], sign_bits.shape[-1]
    levels = (blocks // GROUP).bit_length() - 1
    x = qkv_tokens.transpose(0, 2, 1, 3)
    piece = x.shape[2]
    where = jnp.stack(
        [me, index % GROUP] + [(index // GROUP >> l) & 1 for l in range(levels)]
    ).astype(jnp.int32)

    outer, shape = range(2, partners, 2), (piece, x.shape[3] // partners)
    beside = [(s, kind, 1) for s in range(seqs) for kind in (0, 1, 2)]
    beside += [
        (s, kind, k + 1)
        for s in range(seqs)
        for kind in (0, 1, 2)
        for k in outer
        if s > 0 or kind == 0
    ]
    straight = [[[(x, 0, kind, k) for kind in (1, 2)]] for k in range(2, partners)]
    *first, near = pack(where, [*straight, [[(x, *entry) for entry in beside]]], shape, 60)
    first = [swap(value, "head", k + 2) for k, value in enumerate(first)]
    near = swap(near, "head", 1)
    messages = [(s, (1, 2)) for s in range(1, seqs)] + [(s, (0,)) for s in range(seqs)]
    wanted = [
        [
            [(x, s, kind, k) for kind in kinds],
            [(near, 0, beside.index((s, kind, k + 1)), None) for kind in kinds],
        ]
        for s, kinds in messages
        for k in outer
    ]
    wanted.append([[(x, s, kind, 0) for kind in (0, 1, 2)] for s in range(seqs)])
    *packed, own_rows = pack(where, wanted, shape, 20)
    packed = [swap(value, "head", k) for value, k in zip(packed, list(outer) * len(messages))]
    packed = [packed[n * len(outer) : (n + 1) * len(outer)] for n in range(len(messages))]
    asked = packed[seqs - 1 :]

    def pieces(s, kind):
        found = [(own_rows, s, kind), (near, 0, beside.index((s, kind, 1)))]
        if s == 0 and kind > 0:
            return found + [(value, 0, kind - 1) for value in first]
        row, at = (packed[s - 1], kind - 1) if kind > 0 else (asked[s], 0)
        return found + [(value, half, at) for value in row for half in (0, 1)]

    maps = integer_maps(sign_bits)

    last = [own_rows]
    begun, chains, ends, locals_, own, other, totals = {}, {}, {}, {}, {}, {}, {}

    def early(n):
        begun[n] = early_sums(
            maps, pieces(n, 1)[:2], pieces(n, 2)[:2], heads, dh, piece, last
        )
        last[:] = [begun[n][0]]

    def state(n):
        feats, mine, *others = block_state(
            where,
            maps,
            pieces(n, 1)[2:],
            pieces(n, 2)[2:],
            begun[n][1],
            heads,
            dh,
            piece,
            last,
            3 if n else 0,
        )
        begun[n] = begun[n][0], feats
        chains[n] = [mine] + [swap(value, "seq", m + 1) for m, value in enumerate(others)]
        last[:] = [mine]

    def step(n):
        first_out, *others = chain_step(where, levels, chains[n], last, STEP_US if n and len(chains[n]) == GROUP else 0)
        last[:] = [first_out]
        if others:
            ends[n] = [first_out] + [swap(value, "seq", m + 1) for m, value in enumerate(others)]
        else:
            chains[n] = chains[n] + [swap(first_out, "seq", GROUP << (len(chains[n]) - GROUP))]

    def local(n, first, last_row):
        part = attend_local(
            where,
            maps,
            begun[n],
            pieces(n, 0)[first:last_row],
            pieces(n, 2),
            first,
            heads,
            dh,
            piece,
            last,
            3,
        )
        locals_.setdefault(n, []).append(part)
        last[:] = [part[0]]

    def attend(n):
        stay, leave = attend_prior(
            where, locals_[n], ends[n], piece, dh, last, 1 if n + 1 < seqs else 0
        )
        own[n], other[n] = stay, swap(leave, "head", 1)
        last[:] = [stay]

    def multiply(s, slab):
        if slab == 1:
            for key in totals:
                if key[0] < s:
                    last.extend(totals[key][1])
        total, *shares = project(
            own[s], other[s], out_weight, other_weight, slabs[s], slab, last, 0 if s == seqs - 1 else 6
        )
        totals[s, slab] = total, [swap(v, "head", 2 * (g + 1)) for g, v in enumerate(shares)]
        last[:] = [total]

    slabs = [SLABS[0]] * (seqs - 1) + [SLABS[1]]
    plan = []
    for n in range(seqs):
        came = 22 * n
        end = came + 22 + 9 * levels
        plan.append((came, state, n))
        if n > 0:
            plan.append((came - 21, early, n))
        plan += [(came + 12 + 9 * j, step, n) for j in range(levels + 1)]
        if n == 0:
            plan += [(came + 12.5, local, n, 0, 2), (end - 7, local, n, 2, partners)]
        else:
            plan.append((end - 7, local, n, 0, partners))
        plan.append((end, attend, n))
        plan += [(end + 6 + 3.5 * j, multiply, n, j) for j in range(len(slabs[n]))]
    plan = sorted(plan, key=lambda entry: entry[0])
    early(0)
    state(0)
    other_weight = swap(later_than(out_weight, last), "head", 1)
    for _, act, *which in plan:
        if (act, which) != (state, [0]):
            act(*which)

    return finish([[totals[s, n] for n in range(len(slabs[s]))] for s in range(seqs)], piece)


def solution(mesh):
    return jax.shard_map(
        body,
        mesh=mesh,
        in_specs=(
            P(None, ("seq", "head"), None, None),
            P("head", None, None, None),
            P("head", None),
        ),
        out_specs=P(None, ("seq", "head"), None),
        check_vma=False,
    )
```

```python
import functools
import math

import jax
import jax.numpy as jnp
import numpy as np
from jax import lax
from jax.experimental import pallas as pl
from jax.experimental.pallas import tpu as pltpu
from jax.sharding import PartitionSpec as P

logit_divisor = 1.3
norm_epsilon = 1e-06
SLABS = (8,), (4, 3, 1)

bf16, f32 = jnp.bfloat16, jnp.float32
ROW_TILE = 16
STEP_US = 4
GROUP = 4


def params(mebibytes=20):
    return pltpu.CompilerParams(vmem_limit_bytes=mebibytes * 1024 * 1024)


def vmem(count):
    return [pl.BlockSpec(memory_space=pltpu.VMEM)] * count


def smem():
    return pl.BlockSpec(memory_space=pltpu.SMEM)


def ordered(kernel, count, skip):
    return lambda *refs: kernel(*refs[:skip], *refs[skip + count :])


def busy(microseconds):
    return pl.CostEstimate(flops=int(microseconds * 1e9), bytes_accessed=0, transcendentals=0)


def waits(after):
    return [pl.BlockSpec(memory_space=pl.ANY)] * len(after)


def swap(value, axis, bit):
    return lax.ppermute(value, axis, [(j, j ^ bit) for j in range(lax.axis_size(axis))])


def sign_matrix(order):
    ids = np.arange(order)
    common = ids[:, None] & ids[None, :]
    parity = np.zeros_like(common)
    while common.any():
        parity ^= common & 1
        common = common >> 1
    return (1 - 2 * parity).astype(np.float32)


def maps_kernel(bits_ref, had_ref, maps_ref):
    had = had_ref[...]
    dh = had.shape[0]
    for h in range(bits_ref.shape[0]):
        for b in range(bits_ref.shape[1]):
            signs = (2 * bits_ref[h, b] - 1).astype(f32)
            inner = jnp.dot((had * signs[2:3]).astype(bf16), had, preferred_element_type=f32)
            outer = jnp.dot((inner * signs[1:2]).astype(bf16), had, preferred_element_type=f32)
            whole = outer * signs[0:1]
            near = whole.astype(bf16)
            rows = slice(b * dh, (b + 1) * dh)
            maps_ref[h, rows, :dh] = near
            maps_ref[h, rows, dh:] = (whole - near.astype(f32)).astype(bf16)


def integer_maps(sign_bits):
    heads, blocks, _, dh = sign_bits.shape
    return pl.pallas_call(
        maps_kernel,
        out_shape=jax.ShapeDtypeStruct((heads, blocks * dh, 2 * dh), bf16),
        in_specs=vmem(2),
        out_specs=vmem(1)[0],
        compiler_params=params(),
        cost_estimate=busy(0),
        name="integer_maps",
    )(sign_bits, jnp.asarray(sign_matrix(dh), bf16))


def features(rows_of, maps_ref, out_ref):
    heads, _, twice = maps_ref.shape
    dh = twice // 2
    rows = [rows_of(i) for i in range(heads)]
    scales = []
    for i in range(heads):
        wide = rows[i].astype(f32)
        mean = jnp.sum(wide * wide, axis=-1, keepdims=True) * (1.0 / dh)
        scales.append(lax.rsqrt(mean + norm_epsilon) * (logit_divisor / dh**0.25 / dh))
    for i in range(heads):
        product = lax.dot_general(
            jnp.concatenate([rows[i], rows[i]], axis=1),
            maps_ref[i],
            (((1,), (1,)), ((), ())),
            preferred_element_type=f32,
        )
        out_ref[i] = jnp.exp(product * scales[i]).astype(bf16)


def pack_kernel(places, arrays, where_ref, *refs):
    ins, outs, sems = refs[:arrays], refs[arrays:-1], refs[-1]
    copies = []
    for n, (which, first, second, k, out, i, j, count) in enumerate(places):
        width = outs[out].shape[-1]
        start = 0 if k is None else pl.multiple_of((where_ref[0] ^ k) * width, width)
        source = ins[which].at[first, pl.ds(second, count), :, pl.ds(start, width)]
        copies.append(pltpu.make_async_copy(source, outs[out].at[i, pl.ds(j, count)], sems.at[n]))
    for copy in copies:
        copy.start()
    for copy in copies:
        copy.wait()


def pack(where, wanted, shape, mebibytes):
    arrays, places, shapes = [], [], []
    for out, table in enumerate(wanted):
        shapes.append((len(table), len(table[0]), *shape))
        for i, row in enumerate(table):
            for j, (array, first, second, k) in enumerate(row):
                if not any(array is known for known in arrays):
                    arrays.append(array)
                which = [array is known for known in arrays].index(True)
                before = places[-1] if places else None
                if before and before[:6] == (which, first, second - before[7], k, out, i):
                    places[-1] = (*before[:7], before[7] + 1)
                else:
                    places.append((which, first, second, k, out, i, j, 1))
    return pl.pallas_call(
        functools.partial(pack_kernel, places, len(arrays)),
        out_shape=[jax.ShapeDtypeStruct(shape, bf16) for shape in shapes],
        in_specs=[pl.BlockSpec(memory_space=pltpu.SMEM)]
        + [pl.BlockSpec(memory_space=pl.ANY)] * len(arrays),
        out_specs=[pl.BlockSpec(memory_space=pltpu.VMEM)] * len(shapes),
        scratch_shapes=[pltpu.SemaphoreType.DMA((len(places),))],
        compiler_params=params(mebibytes),
        cost_estimate=busy(0),
        name="pack",
    )(where, *arrays)


def joined(refs, places, cut):
    return jnp.concatenate(
        [ref[lead, kind, :, cut] for ref, (lead, kind) in zip(refs, places)], axis=0
    )


def sums_kernel(k_at, v_at, heads, dh, maps_ref, *refs):
    pieces = len(k_at)
    k_refs, v_refs = refs[:pieces], refs[pieces : 2 * pieces]
    *before, feats_ref, sums_ref = refs[2 * pieces :]
    cuts = [slice(i * dh, (i + 1) * dh) for i in range(heads)]
    features(lambda i: joined(k_refs, k_at, cuts[i]), maps_ref, feats_ref)
    for i in range(heads):
        feats = feats_ref[i]
        state = lax.dot_general(
            joined(v_refs, v_at, cuts[i]),
            feats,
            (((0,), (0,)), ((), ())),
            preferred_element_type=f32,
        )
        sums_ref[i, :dh] = before[0][i, :dh] + state if before else state
    for i in range(heads):
        total = jnp.sum(feats_ref[i].astype(f32), axis=0, keepdims=True)
        total = jnp.broadcast_to(total, (sums_ref.shape[1] - dh, total.shape[1]))
        sums_ref[i, dh:] = before[0][i, dh:] + total if before else total


def early_sums(maps, keys, values, heads, dh, piece, after):
    feat = maps.shape[1]
    rows = len(keys) * piece
    (arrays, k_at), (others, v_at) = split(keys), split(values)
    return pl.pallas_call(
        ordered(functools.partial(sums_kernel, k_at, v_at, heads, dh), len(after), 0),
        out_shape=[
            jax.ShapeDtypeStruct((heads, rows, feat), bf16),
            jax.ShapeDtypeStruct((heads, dh + 8, feat), f32),
        ],
        in_specs=waits(after) + vmem(1 + 2 * len(keys)),
        out_specs=vmem(2),
        compiler_params=params(),
        cost_estimate=busy(0),
        name="early_sums",
    )(*after, maps, *arrays, *others)


def split(pieces):
    return [piece[0] for piece in pieces], [piece[1:] for piece in pieces]


def state_kernel(k_at, v_at, heads, dh, where_ref, maps_ref, *refs):
    count = 2 * len(k_at) + 2
    *ins, feats_ref, sums_ref = refs[:count] + refs[-1:]
    share_refs = refs[count:-1]
    sums_kernel(k_at, v_at, heads, dh, maps_ref, *ins, feats_ref, sums_ref)
    share = heads // GROUP
    pad = jnp.zeros((ROW_TILE - share, feats_ref.shape[-1]), f32)
    states = [sums_ref[i] for i in range(heads)]
    shares = []
    for g in range(GROUP):
        mine = states[g * share : (g + 1) * share]
        shares.append(
            jnp.concatenate([v[:dh] for v in mine] + [v[dh : dh + 1] for v in mine] + [pad], axis=0)
        )
    for m, ref in enumerate(share_refs):
        ref[...] = chosen(shares, where_ref[1] ^ m).astype(ref.dtype)


def chosen(values, index):
    result = values[0]
    for n, value in enumerate(values[1:]):
        result = jnp.where(index == n + 1, value, result)
    return result


def block_state(where, maps, keys, values, before, heads, dh, piece, after, beside):
    feat = maps.shape[1]
    rows = len(keys) * piece
    height = heads // GROUP * dh + ROW_TILE
    (arrays, k_at), (others, v_at) = split(keys), split(values)
    return pl.pallas_call(
        ordered(functools.partial(state_kernel, k_at, v_at, heads, dh), len(after), 0),
        out_shape=[
            jax.ShapeDtypeStruct((heads, rows, feat), bf16),
            jax.ShapeDtypeStruct((height, feat), f32),
        ]
        + [jax.ShapeDtypeStruct((height, feat), bf16)] * (GROUP - 1),
        in_specs=waits(after) + [smem()] + vmem(2 + 2 * len(keys)),
        out_specs=vmem(1 + GROUP),
        scratch_shapes=[pltpu.VMEM(before.shape, f32)],
        compiler_params=params(),
        cost_estimate=busy(beside),
        name="block_state",
    )(*after, where, maps, *arrays, *others, before)


def step_kernel(levels, where_ref, *refs):
    ins = refs[: len(refs) - (1 if len(refs) < 2 * GROUP + levels else GROUP)]
    outs = refs[len(ins) :]
    values = [ref[...].astype(f32) for ref in ins[:GROUP]]
    got = [ref[...].astype(f32) for ref in ins[GROUP:]]
    if len(outs) == 1:
        total = values[0]
        for value in values[1:] + got:
            total = total + value
        outs[0][...] = total.astype(bf16)
        return
    prior = jnp.zeros_like(values[0])
    for level, value in enumerate(got):
        prior = prior + jnp.where(where_ref[2 + level] == 1, value, 0.0)
    mine = where_ref[1]
    for m, out in enumerate(outs):
        result = prior
        for other, value in enumerate(values):
            if other != m:
                result = result + jnp.where((mine ^ other) < (mine ^ m), value, 0.0)
        out[...] = result.astype(bf16)


def chain_step(where, levels, values, after, beside):
    shape = values[0].shape
    count = GROUP if len(values) == GROUP + levels else 1
    return pl.pallas_call(
        ordered(functools.partial(step_kernel, levels), len(after), 0),
        out_shape=[jax.ShapeDtypeStruct(shape, bf16)] * count,
        in_specs=waits(after) + [smem()] + vmem(len(values)),
        out_specs=vmem(count),
        compiler_params=params(),
        cost_estimate=busy(beside),
        name="chain_step",
    )(*after, where, *values)


def local_kernel(first, q_at, v_at, heads, dh, where_ref, maps_ref, early_ref, late_ref, *refs):
    asking, partners = len(q_at), len(v_at)
    q_refs, v_refs = refs[:asking], refs[asking : asking + partners]
    query_feats_ref, local_ref, weights_ref = refs[asking + partners :]
    piece = q_refs[0].shape[2]
    rows = partners * piece
    me = where_ref[0]

    def places(first, count, shape, dim):
        ids = lax.broadcasted_iota(jnp.int32, shape, dim)
        result = ids + (me ^ first) * piece
        for j in range(1, count):
            result = jnp.where(ids >= j * piece, ids + ((me ^ (first + j)) - j) * piece, result)
        return result

    here = places(first, asking, (asking * piece, 1), 0)
    causal = here >= places(0, partners, (1, rows), 1)
    ones = jnp.ones((rows, dh), bf16)
    cuts = [slice(i * dh, (i + 1) * dh) for i in range(heads)]
    features(lambda i: joined(q_refs, q_at, cuts[i]), maps_ref, query_feats_ref)
    for i in range(heads):
        scores = lax.dot_general(
            query_feats_ref[i],
            jnp.concatenate([early_ref[i], late_ref[i]], axis=0),
            (((1,), (1,)), ((), ())),
            preferred_element_type=f32,
        )
        weights_ref[i] = jnp.where(causal, scores, 0.0).astype(bf16)
    for i in range(heads):
        local_ref[i] = jnp.dot(
            weights_ref[i],
            jnp.concatenate([joined(v_refs, v_at, cuts[i]), ones], axis=1),
            preferred_element_type=f32,
        )


def attend_local(where, maps, feats, queries, values, first, heads, dh, piece, after, beside):
    feat = maps.shape[1]
    rows = len(queries) * piece
    (arrays, q_at), (others, v_at) = split(queries), split(values)
    return pl.pallas_call(
        ordered(functools.partial(local_kernel, first, q_at, v_at, heads, dh), len(after), 0),
        out_shape=[
            jax.ShapeDtypeStruct((heads, rows, feat), bf16),
            jax.ShapeDtypeStruct((heads, rows, 2 * dh), f32),
        ],
        in_specs=waits(after) + [smem()] + vmem(1 + len(feats) + len(queries) + len(values)),
        out_specs=vmem(2),
        scratch_shapes=[pltpu.VMEM((heads, rows, len(values) * piece), bf16)],
        compiler_params=params(),
        cost_estimate=busy(beside),
        name="attend_local",
    )(*after, where, maps, *feats, *arrays, *others)


def prior_kernel(pieces, heads, dh, where_ref, *refs):
    parts = len(pieces)
    asked = [(refs[2 * p], refs[2 * p + 1]) for p in range(parts)]
    share_refs, (stay_ref, leave_ref) = refs[2 * parts : 2 * parts + GROUP], refs[-2:]
    piece = stay_ref.shape[1]
    share = heads // GROUP
    priors = []
    for i in range(heads):
        j = i % share
        state, total = slice(j * dh, (j + 1) * dh), slice(share * dh, share * dh + ROW_TILE)
        source = where_ref[1] ^ (i // share)
        prior = chosen([ref[state, :] for ref in share_refs], source)
        tail = chosen([ref[total, :] for ref in share_refs], source)
        tail = jnp.broadcast_to(tail[j : j + 1, :], prior.shape)
        priors.append(jnp.concatenate([prior, tail], axis=0))
    first = 0
    for count, (query_feats_ref, local_ref) in zip(pieces, asked):
        sums = [
            local_ref[i]
            + lax.dot_general(
                query_feats_ref[i], priors[i], (((1,), (1,)), ((), ())), preferred_element_type=f32
            )
            for i in range(heads)
        ]
        for i in range(heads):
            attended = (sums[i][:, :dh] / sums[i][:, dh:]).astype(bf16)
            for n in range(count):
                out = leave_ref if (first + n) & 1 else stay_ref
                out[(first + n) // 2, :, i * dh : (i + 1) * dh] = attended[n * piece : (n + 1) * piece]
        first += count


def attend_prior(where, asked, shares, piece, dh, after, beside):
    heads = asked[0][0].shape[0]
    pieces = [query_feats.shape[1] // piece for query_feats, _ in asked]
    out = jax.ShapeDtypeStruct((sum(pieces) // 2, piece, heads * dh), bf16)
    values = [value for pair in asked for value in pair]
    return pl.pallas_call(
        ordered(functools.partial(prior_kernel, pieces, heads, dh), len(after), 0),
        out_shape=[out, out],
        in_specs=waits(after) + [smem()] + vmem(len(values) + len(shares)),
        out_specs=vmem(2),
        compiler_params=params(),
        cost_estimate=busy(beside),
        name="attend_prior",
    )(*after, where, *values, *shares)


def project_kernel(first, tile, begun, lhs_refs, w_refs, *out_refs):
    groups, piece, width = lhs_refs[0].shape
    lhs = [ref[...].reshape(groups * piece, width) for ref in lhs_refs]
    for n in range(out_refs[0].shape[1] // tile):
        here = slice(n * tile, (n + 1) * tile)
        there = slice(first + n * tile, first + (n + 1) * tile)
        acc = None if begun is None else begun[:, here]
        for value, w_ref in zip(lhs, w_refs):
            term = jnp.dot(value, w_ref[:, there], preferred_element_type=f32)
            acc = term if acc is None else acc + term
        if len(out_refs) == 1:
            out_refs[0][:, here] = acc
        else:
            for g, ref in enumerate(out_refs):
                ref[:, here] = acc[g * piece : (g + 1) * piece].astype(ref.dtype)


def begin_kernel(first, tile, lhs_ref, w_ref, out_ref):
    project_kernel(first, tile, None, [lhs_ref], [w_ref], out_ref)


def whole_kernel(first, tile, own_ref, other_ref, own_w, other_w, *out_refs):
    project_kernel(first, tile, None, [own_ref, other_ref], [own_w, other_w], *out_refs)


def end_kernel(first, tile, begun_ref, other_ref, other_w, *out_refs):
    project_kernel(first, tile, begun_ref, [other_ref], [other_w], *out_refs)


def begin_project(own, own_w, slabs, slab, after):
    groups, piece, _ = own.shape
    unit = own_w.shape[1] // sum(slabs)
    first, cols = sum(slabs[:slab]) * unit, slabs[slab] * unit
    return pl.pallas_call(
        ordered(functools.partial(begin_kernel, first, math.gcd(unit, 512)), len(after), 0),
        out_shape=jax.ShapeDtypeStruct((groups * piece, cols), f32),
        in_specs=waits(after) + vmem(2),
        out_specs=vmem(1)[0],
        compiler_params=params(),
        cost_estimate=busy(3),
        name="begin_project",
    )(*after, own, own_w)


def project(own, other, own_w, other_w, slabs, slab, after, beside, begun=None):
    groups, piece, _ = own.shape
    unit = own_w.shape[1] // sum(slabs)
    first, cols = sum(slabs[:slab]) * unit, slabs[slab] * unit
    kernel, values = whole_kernel, (own, other, own_w, other_w)
    if begun is not None:
        kernel, values = end_kernel, (begun, other, other_w)
    return pl.pallas_call(
        ordered(functools.partial(kernel, first, math.gcd(unit, 512)), len(after), 0),
        out_shape=[jax.ShapeDtypeStruct((piece, cols), f32)]
        + [jax.ShapeDtypeStruct((piece, cols), bf16)] * (groups - 1),
        in_specs=waits(after) + vmem(len(values)),
        out_specs=vmem(groups),
        compiler_params=params(),
        cost_estimate=busy(beside),
        name="project",
    )(*after, *values)


def finish_kernel(counts, *refs):
    refs = list(refs)
    out_ref = refs.pop()
    for s, slabs in enumerate(counts):
        at = 0
        for shares in slabs:
            total = refs.pop(0)[...]
            for _ in range(shares):
                total = total + refs.pop(0)[...].astype(f32)
            width = total.shape[1]
            out_ref[s, :, at : at + width] = total.astype(bf16)
            at += width


def finish(sums, piece):
    *slabs, (total, shares) = sums[-1]
    most = [*sums[:-1], slabs]
    counts = [[len(given) for _, given in row] for row in most]
    values = [value for row in most for own, given in row for value in (own, *given)]
    out = jax.ShapeDtypeStruct(
        (len(sums), piece, sum(own.shape[1] for own, _ in sums[-1])), bf16
    )
    begun = pl.pallas_call(
        functools.partial(finish_kernel, counts),
        grid=(1,),
        out_shape=out,
        in_specs=[pl.BlockSpec(value.shape, lambda _: (0, 0)) for value in values],
        out_specs=pl.BlockSpec(out.shape, lambda _: (0, 0, 0)),
        compiler_params=params(),
        cost_estimate=busy(3),
        name="finish",
    )(*values)
    width = total.shape[1]
    place = (len(sums) - 1, 0, out.shape[2] // width - 1)
    return pl.pallas_call(
        ordered(functools.partial(finish_kernel, [[len(shares)]]), 1, 0),
        grid=(1,),
        out_shape=out,
        in_specs=waits([begun])
        + [pl.BlockSpec(value.shape, lambda _: (0, 0)) for value in (total, *shares)],
        out_specs=pl.BlockSpec((1, piece, width), lambda _: place),
        input_output_aliases={0: 0},
        compiler_params=params(),
        cost_estimate=busy(0),
        name="finish_last",
    )(begun, total, *shares)


def nothing(*refs):
    pass


def later_than(value, after):
    anywhere = pl.BlockSpec(memory_space=pl.ANY)
    return pl.pallas_call(
        nothing,
        out_shape=jax.ShapeDtypeStruct(value.shape, value.dtype),
        in_specs=[anywhere] * (1 + len(after)),
        out_specs=anywhere,
        input_output_aliases={0: 0},
        compiler_params=params(1),
        cost_estimate=busy(0),
        name="later_than",
    )(value, *after)


def body(qkv_tokens, sign_bits, out_weight):
    partners, blocks = lax.axis_size("head"), lax.axis_size("seq")
    me, index = lax.axis_index("head"), lax.axis_index("seq")
    seqs = qkv_tokens.shape[0]
    heads, dh = sign_bits.shape[0], sign_bits.shape[-1]
    levels = (blocks // GROUP).bit_length() - 1
    x = qkv_tokens.transpose(0, 2, 1, 3)
    piece = x.shape[2]
    where = jnp.stack(
        [me, index % GROUP] + [(index // GROUP >> l) & 1 for l in range(levels)]
    ).astype(jnp.int32)

    outer, shape = range(2, partners, 2), (piece, x.shape[3] // partners)
    beside = [(s, kind, 1) for s in range(seqs) for kind in (0, 1, 2)]
    beside += [
        (s, kind, k + 1)
        for s in range(seqs)
        for kind in (0, 1, 2)
        for k in outer
        if s > 0 or kind == 0
    ]
    straight = [[[(x, 0, kind, k) for kind in (1, 2)]] for k in range(2, partners)]
    *first, near = pack(where, [*straight, [[(x, *entry) for entry in beside]]], shape, 60)
    first = [swap(value, "head", k + 2) for k, value in enumerate(first)]
    near = swap(near, "head", 1)
    messages = [(s, (1, 2)) for s in range(1, seqs)] + [(s, (0,)) for s in range(seqs)]
    wanted = [
        [
            [(x, s, kind, k) for kind in kinds],
            [(near, 0, beside.index((s, kind, k + 1)), None) for kind in kinds],
        ]
        for s, kinds in messages
        for k in outer
    ]
    wanted.append([[(x, s, kind, 0) for kind in (0, 1, 2)] for s in range(seqs)])
    *packed, own_rows = pack(where, wanted, shape, 20)
    packed = [swap(value, "head", k) for value, k in zip(packed, list(outer) * len(messages))]
    packed = [packed[n * len(outer) : (n + 1) * len(outer)] for n in range(len(messages))]
    asked = packed[seqs - 1 :]

    def pieces(s, kind):
        found = [(own_rows, s, kind), (near, 0, beside.index((s, kind, 1)))]
        if s == 0 and kind > 0:
            return found + [(value, 0, kind - 1) for value in first]
        row, at = (packed[s - 1], kind - 1) if kind > 0 else (asked[s], 0)
        return found + [(value, half, at) for value in row for half in (0, 1)]

    maps = integer_maps(sign_bits)

    last = [own_rows]
    begun, chains, ends, locals_, own, other, totals = {}, {}, {}, {}, {}, {}, {}

    def early(n):
        begun[n] = early_sums(
            maps, pieces(n, 1)[:2], pieces(n, 2)[:2], heads, dh, piece, last
        )
        last[:] = [begun[n][0]]

    def state(n):
        feats, mine, *others = block_state(
            where,
            maps,
            pieces(n, 1)[2:],
            pieces(n, 2)[2:],
            begun[n][1],
            heads,
            dh,
            piece,
            last,
            3 if n else 0,
        )
        begun[n] = begun[n][0], feats
        chains[n] = [mine] + [swap(value, "seq", m + 1) for m, value in enumerate(others)]
        last[:] = [mine]

    def step(n):
        first_out, *others = chain_step(where, levels, chains[n], last, STEP_US if n and len(chains[n]) == GROUP else 0)
        last[:] = [first_out]
        if others:
            ends[n] = [first_out] + [swap(value, "seq", m + 1) for m, value in enumerate(others)]
        else:
            chains[n] = chains[n] + [swap(first_out, "seq", GROUP << (len(chains[n]) - GROUP))]

    def local(n, first, last_row):
        part = attend_local(
            where,
            maps,
            begun[n],
            pieces(n, 0)[first:last_row],
            pieces(n, 2),
            first,
            heads,
            dh,
            piece,
            last,
            3,
        )
        locals_.setdefault(n, []).append(part)
        last[:] = [part[0]]

    def attend(n):
        stay, leave = attend_prior(
            where, locals_[n], ends[n], piece, dh, last, 1 if n + 1 < seqs else 0
        )
        own[n], other[n] = stay, swap(leave, "head", 1)
        last[:] = [stay]

    def multiply(s, slab):
        if slab == 1:
            for key in totals:
                if key[0] < s:
                    last.extend(totals[key][1])
        begun = None
        if s == seqs - 1 and slab == 0:
            begun = begin_project(own[s], out_weight, slabs[s], slab, last)
            last[:] = [begun]
        total, *shares = project(
            own[s], other[s], out_weight, other_weight, slabs[s], slab, last, 0 if s == seqs - 1 else 6, begun
        )
        totals[s, slab] = total, [swap(v, "head", 2 * (g + 1)) for g, v in enumerate(shares)]
        last[:] = [total]

    slabs = [SLABS[0]] * (seqs - 1) + [SLABS[1]]
    plan = []
    for n in range(seqs):
        came = 22 * n
        end = came + 22 + 9 * levels
        plan.append((came, state, n))
        if n > 0:
            plan.append((came - 21, early, n))
        plan += [(came + 12 + 9 * j, step, n) for j in range(levels + 1)]
        if n == 0:
            plan += [(came + 12.5, local, n, 0, 2), (end - 7, local, n, 2, partners)]
        else:
            plan.append((end - 7, local, n, 0, partners))
        plan.append((end, attend, n))
        plan += [(end + 6 + 3.5 * j, multiply, n, j) for j in range(len(slabs[n]))]
    plan = sorted(plan, key=lambda entry: entry[0])
    early(0)
    state(0)
    other_weight = swap(later_than(out_weight, last), "head", 1)
    for _, act, *which in plan:
        if (act, which) != (state, [0]):
            act(*which)

    return finish([[totals[s, n] for n in range(len(slabs[s]))] for s in range(seqs)], piece)


def solution(mesh):
    return jax.shard_map(
        body,
        mesh=mesh,
        in_specs=(
            P(None, ("seq", "head"), None, None),
            P("head", None, None, None),
            P("head", None),
        ),
        out_specs=P(None, ("seq", "head"), None),
        check_vma=False,
    )
```

```python
import functools
import math

import jax
import jax.numpy as jnp
import numpy as np
from jax import lax
from jax.experimental import pallas as pl
from jax.experimental.pallas import tpu as pltpu
from jax.sharding import PartitionSpec as P

logit_divisor = 1.3
norm_epsilon = 1e-06
SLABS = (8,), (4, 3, 1)

bf16, f32 = jnp.bfloat16, jnp.float32
ROW_TILE = 16
STEP_US = 4
GROUP = 4


def params(mebibytes=20):
    return pltpu.CompilerParams(vmem_limit_bytes=mebibytes * 1024 * 1024)


def vmem(count):
    return [pl.BlockSpec(memory_space=pltpu.VMEM)] * count


def smem():
    return pl.BlockSpec(memory_space=pltpu.SMEM)


def ordered(kernel, count, skip):
    return lambda *refs: kernel(*refs[:skip], *refs[skip + count :])


def busy(microseconds):
    return pl.CostEstimate(flops=int(microseconds * 1e9), bytes_accessed=0, transcendentals=0)


def waits(after):
    return [pl.BlockSpec(memory_space=pl.ANY)] * len(after)


def swap(value, axis, bit):
    return lax.ppermute(value, axis, [(j, j ^ bit) for j in range(lax.axis_size(axis))])


def sign_matrix(order):
    ids = np.arange(order)
    common = ids[:, None] & ids[None, :]
    parity = np.zeros_like(common)
    while common.any():
        parity ^= common & 1
        common = common >> 1
    return (1 - 2 * parity).astype(np.float32)


def maps_kernel(bits_ref, had_ref, maps_ref):
    had = had_ref[...]
    dh = had.shape[0]
    for h in range(bits_ref.shape[0]):
        for b in range(bits_ref.shape[1]):
            signs = (2 * bits_ref[h, b] - 1).astype(f32)
            inner = jnp.dot((had * signs[2:3]).astype(bf16), had, preferred_element_type=f32)
            outer = jnp.dot((inner * signs[1:2]).astype(bf16), had, preferred_element_type=f32)
            whole = outer * signs[0:1]
            near = whole.astype(bf16)
            rows = slice(b * dh, (b + 1) * dh)
            maps_ref[h, rows, :dh] = near
            maps_ref[h, rows, dh:] = (whole - near.astype(f32)).astype(bf16)


def integer_maps(sign_bits):
    heads, blocks, _, dh = sign_bits.shape
    return pl.pallas_call(
        maps_kernel,
        out_shape=jax.ShapeDtypeStruct((heads, blocks * dh, 2 * dh), bf16),
        in_specs=vmem(2),
        out_specs=vmem(1)[0],
        compiler_params=params(),
        cost_estimate=busy(0),
        name="integer_maps",
    )(sign_bits, jnp.asarray(sign_matrix(dh), bf16))


def features(rows_of, maps_ref, out_ref):
    heads, _, twice = maps_ref.shape
    dh = twice // 2
    rows = [rows_of(i) for i in range(heads)]
    scales = []
    for i in range(heads):
        wide = rows[i].astype(f32)
        mean = jnp.sum(wide * wide, axis=-1, keepdims=True) * (1.0 / dh)
        scales.append(lax.rsqrt(mean + norm_epsilon) * (logit_divisor / dh**0.25 / dh))
    for i in range(heads):
        product = lax.dot_general(
            jnp.concatenate([rows[i], rows[i]], axis=1),
            maps_ref[i],
            (((1,), (1,)), ((), ())),
            preferred_element_type=f32,
        )
        out_ref[i] = jnp.exp(product * scales[i]).astype(bf16)


def pack_kernel(places, arrays, *refs):
    me = lax.axis_index("head")
    ins, outs, sems = refs[:arrays], refs[arrays:-1], refs[-1]
    copies = []
    for n, (which, first, second, k, out, i, j, count) in enumerate(places):
        width = outs[out].shape[-1]
        start = 0 if k is None else pl.multiple_of((me ^ k) * width, width)
        source = ins[which].at[first, pl.ds(second, count), :, pl.ds(start, width)]
        copies.append(pltpu.make_async_copy(source, outs[out].at[i, pl.ds(j, count)], sems.at[n]))
    for copy in copies:
        copy.start()
    for copy in copies:
        copy.wait()


def pack(wanted, shape, mebibytes):
    arrays, places, shapes = [], [], []
    for out, table in enumerate(wanted):
        shapes.append((len(table), len(table[0]), *shape))
        for i, row in enumerate(table):
            for j, (array, first, second, k) in enumerate(row):
                if not any(array is known for known in arrays):
                    arrays.append(array)
                which = [array is known for known in arrays].index(True)
                before = places[-1] if places else None
                if before and before[:6] == (which, first, second - before[7], k, out, i):
                    places[-1] = (*before[:7], before[7] + 1)
                else:
                    places.append((which, first, second, k, out, i, j, 1))
    return pl.pallas_call(
        functools.partial(pack_kernel, places, len(arrays)),
        out_shape=[jax.ShapeDtypeStruct(shape, bf16) for shape in shapes],
        in_specs=waits(arrays),
        out_specs=[pl.BlockSpec(memory_space=pltpu.VMEM)] * len(shapes),
        scratch_shapes=[pltpu.SemaphoreType.DMA((len(places),))],
        compiler_params=params(mebibytes),
        cost_estimate=busy(0),
        name="pack",
    )(*arrays)


def joined(refs, places, cut):
    return jnp.concatenate(
        [ref[lead, kind, :, cut] for ref, (lead, kind) in zip(refs, places)], axis=0
    )


def sums_kernel(k_at, v_at, heads, dh, maps_ref, *refs):
    pieces = len(k_at)
    k_refs, v_refs = refs[:pieces], refs[pieces : 2 * pieces]
    *before, feats_ref, sums_ref = refs[2 * pieces :]
    cuts = [slice(i * dh, (i + 1) * dh) for i in range(heads)]
    features(lambda i: joined(k_refs, k_at, cuts[i]), maps_ref, feats_ref)
    for i in range(heads):
        feats = feats_ref[i]
        state = lax.dot_general(
            joined(v_refs, v_at, cuts[i]),
            feats,
            (((0,), (0,)), ((), ())),
            preferred_element_type=f32,
        )
        sums_ref[i, :dh] = before[0][i, :dh] + state if before else state
    for i in range(heads):
        total = jnp.sum(feats_ref[i].astype(f32), axis=0, keepdims=True)
        total = jnp.broadcast_to(total, (sums_ref.shape[1] - dh, total.shape[1]))
        sums_ref[i, dh:] = before[0][i, dh:] + total if before else total


def early_sums(maps, keys, values, heads, dh, piece, after):
    feat = maps.shape[1]
    rows = len(keys) * piece
    (arrays, k_at), (others, v_at) = split(keys), split(values)
    return pl.pallas_call(
        ordered(functools.partial(sums_kernel, k_at, v_at, heads, dh), len(after), 0),
        out_shape=[
            jax.ShapeDtypeStruct((heads, rows, feat), bf16),
            jax.ShapeDtypeStruct((heads, dh + 8, feat), f32),
        ],
        in_specs=waits(after) + vmem(1 + 2 * len(keys)),
        out_specs=vmem(2),
        compiler_params=params(),
        cost_estimate=busy(0),
        name="early_sums",
    )(*after, maps, *arrays, *others)


def split(pieces):
    return [piece[0] for piece in pieces], [piece[1:] for piece in pieces]


def state_kernel(k_at, v_at, heads, dh, where_ref, maps_ref, *refs):
    count = 2 * len(k_at) + 2
    *ins, feats_ref, sums_ref = refs[:count] + refs[-1:]
    share_refs = refs[count:-1]
    sums_kernel(k_at, v_at, heads, dh, maps_ref, *ins, feats_ref, sums_ref)
    share = heads // GROUP
    pad = jnp.zeros((ROW_TILE - share, feats_ref.shape[-1]), f32)
    states = [sums_ref[i] for i in range(heads)]
    shares = []
    for g in range(GROUP):
        mine = states[g * share : (g + 1) * share]
        shares.append(
            jnp.concatenate([v[:dh] for v in mine] + [v[dh : dh + 1] for v in mine] + [pad], axis=0)
        )
    for m, ref in enumerate(share_refs):
        ref[...] = chosen(shares, where_ref[1] ^ m).astype(ref.dtype)


def chosen(values, index):
    result = values[0]
    for n, value in enumerate(values[1:]):
        result = jnp.where(index == n + 1, value, result)
    return result


def block_state(where, maps, keys, values, before, heads, dh, piece, after, beside):
    feat = maps.shape[1]
    rows = len(keys) * piece
    height = heads // GROUP * dh + ROW_TILE
    (arrays, k_at), (others, v_at) = split(keys), split(values)
    return pl.pallas_call(
        ordered(functools.partial(state_kernel, k_at, v_at, heads, dh), len(after), 0),
        out_shape=[
            jax.ShapeDtypeStruct((heads, rows, feat), bf16),
            jax.ShapeDtypeStruct((height, feat), f32),
        ]
        + [jax.ShapeDtypeStruct((height, feat), bf16)] * (GROUP - 1),
        in_specs=waits(after) + [smem()] + vmem(2 + 2 * len(keys)),
        out_specs=vmem(1 + GROUP),
        scratch_shapes=[pltpu.VMEM(before.shape, f32)],
        compiler_params=params(),
        cost_estimate=busy(beside),
        name="block_state",
    )(*after, where, maps, *arrays, *others, before)


def step_kernel(levels, where_ref, *refs):
    ins = refs[: len(refs) - (1 if len(refs) < 2 * GROUP + levels else GROUP)]
    outs = refs[len(ins) :]
    values = [ref[...].astype(f32) for ref in ins[:GROUP]]
    got = [ref[...].astype(f32) for ref in ins[GROUP:]]
    if len(outs) == 1:
        total = values[0]
        for value in values[1:] + got:
            total = total + value
        outs[0][...] = total.astype(bf16)
        return
    prior = jnp.zeros_like(values[0])
    for level, value in enumerate(got):
        prior = prior + jnp.where(where_ref[2 + level] == 1, value, 0.0)
    mine = where_ref[1]
    for m, out in enumerate(outs):
        result = prior
        for other, value in enumerate(values):
            if other != m:
                result = result + jnp.where((mine ^ other) < (mine ^ m), value, 0.0)
        out[...] = result.astype(bf16)


def chain_step(where, levels, values, after, beside):
    shape = values[0].shape
    count = GROUP if len(values) == GROUP + levels else 1
    return pl.pallas_call(
        ordered(functools.partial(step_kernel, levels), len(after), 0),
        out_shape=[jax.ShapeDtypeStruct(shape, bf16)] * count,
        in_specs=waits(after) + [smem()] + vmem(len(values)),
        out_specs=vmem(count),
        compiler_params=params(),
        cost_estimate=busy(beside),
        name="chain_step",
    )(*after, where, *values)


def local_kernel(first, q_at, v_at, heads, dh, where_ref, maps_ref, early_ref, late_ref, *refs):
    asking, partners = len(q_at), len(v_at)
    q_refs, v_refs = refs[:asking], refs[asking : asking + partners]
    query_feats_ref, local_ref, weights_ref = refs[asking + partners :]
    piece = q_refs[0].shape[2]
    rows = partners * piece
    me = where_ref[0]

    def places(first, count, shape, dim):
        ids = lax.broadcasted_iota(jnp.int32, shape, dim)
        result = ids + (me ^ first) * piece
        for j in range(1, count):
            result = jnp.where(ids >= j * piece, ids + ((me ^ (first + j)) - j) * piece, result)
        return result

    here = places(first, asking, (asking * piece, 1), 0)
    causal = here >= places(0, partners, (1, rows), 1)
    ones = jnp.ones((rows, dh), bf16)
    cuts = [slice(i * dh, (i + 1) * dh) for i in range(heads)]
    features(lambda i: joined(q_refs, q_at, cuts[i]), maps_ref, query_feats_ref)
    for i in range(heads):
        scores = lax.dot_general(
            query_feats_ref[i],
            jnp.concatenate([early_ref[i], late_ref[i]], axis=0),
            (((1,), (1,)), ((), ())),
            preferred_element_type=f32,
        )
        weights_ref[i] = jnp.where(causal, scores, 0.0).astype(bf16)
    for i in range(heads):
        local_ref[i] = jnp.dot(
            weights_ref[i],
            jnp.concatenate([joined(v_refs, v_at, cuts[i]), ones], axis=1),
            preferred_element_type=f32,
        )


def attend_local(where, maps, feats, queries, values, first, heads, dh, piece, after, beside):
    feat = maps.shape[1]
    rows = len(queries) * piece
    (arrays, q_at), (others, v_at) = split(queries), split(values)
    return pl.pallas_call(
        ordered(functools.partial(local_kernel, first, q_at, v_at, heads, dh), len(after), 0),
        out_shape=[
            jax.ShapeDtypeStruct((heads, rows, feat), bf16),
            jax.ShapeDtypeStruct((heads, rows, 2 * dh), f32),
        ],
        in_specs=waits(after) + [smem()] + vmem(1 + len(feats) + len(queries) + len(values)),
        out_specs=vmem(2),
        scratch_shapes=[pltpu.VMEM((heads, rows, len(values) * piece), bf16)],
        compiler_params=params(),
        cost_estimate=busy(beside),
        name="attend_local",
    )(*after, where, maps, *feats, *arrays, *others)


def prior_kernel(pieces, heads, dh, where_ref, *refs):
    parts = len(pieces)
    asked = [(refs[2 * p], refs[2 * p + 1]) for p in range(parts)]
    share_refs, (stay_ref, leave_ref) = refs[2 * parts : 2 * parts + GROUP], refs[-2:]
    piece = stay_ref.shape[1]
    share = heads // GROUP
    priors = []
    for i in range(heads):
        j = i % share
        state, total = slice(j * dh, (j + 1) * dh), slice(share * dh, share * dh + ROW_TILE)
        source = where_ref[1] ^ (i // share)
        prior = chosen([ref[state, :] for ref in share_refs], source)
        tail = chosen([ref[total, :] for ref in share_refs], source)
        tail = jnp.broadcast_to(tail[j : j + 1, :], prior.shape)
        priors.append(jnp.concatenate([prior, tail], axis=0))
    first = 0
    for count, (query_feats_ref, local_ref) in zip(pieces, asked):
        sums = [
            local_ref[i]
            + lax.dot_general(
                query_feats_ref[i], priors[i], (((1,), (1,)), ((), ())), preferred_element_type=f32
            )
            for i in range(heads)
        ]
        for i in range(heads):
            attended = (sums[i][:, :dh] / sums[i][:, dh:]).astype(bf16)
            for n in range(count):
                out = leave_ref if (first + n) & 1 else stay_ref
                out[(first + n) // 2, :, i * dh : (i + 1) * dh] = attended[n * piece : (n + 1) * piece]
        first += count


def attend_prior(where, asked, shares, piece, dh, after, beside):
    heads = asked[0][0].shape[0]
    pieces = [query_feats.shape[1] // piece for query_feats, _ in asked]
    out = jax.ShapeDtypeStruct((sum(pieces) // 2, piece, heads * dh), bf16)
    values = [value for pair in asked for value in pair]
    return pl.pallas_call(
        ordered(functools.partial(prior_kernel, pieces, heads, dh), len(after), 0),
        out_shape=[out, out],
        in_specs=waits(after) + [smem()] + vmem(len(values) + len(shares)),
        out_specs=vmem(2),
        compiler_params=params(),
        cost_estimate=busy(beside),
        name="attend_prior",
    )(*after, where, *values, *shares)


def project_kernel(first, tile, begun, lhs_refs, w_refs, *out_refs):
    groups, piece, width = lhs_refs[0].shape
    lhs = [ref[...].reshape(groups * piece, width) for ref in lhs_refs]
    for n in range(out_refs[0].shape[1] // tile):
        here = slice(n * tile, (n + 1) * tile)
        there = slice(first + n * tile, first + (n + 1) * tile)
        acc = None if begun is None else begun[:, here]
        for value, w_ref in zip(lhs, w_refs):
            term = jnp.dot(value, w_ref[:, there], preferred_element_type=f32)
            acc = term if acc is None else acc + term
        if len(out_refs) == 1:
            out_refs[0][:, here] = acc
        else:
            for g, ref in enumerate(out_refs):
                ref[:, here] = acc[g * piece : (g + 1) * piece].astype(ref.dtype)


def begin_kernel(first, tile, lhs_ref, w_ref, out_ref):
    project_kernel(first, tile, None, [lhs_ref], [w_ref], out_ref)


def whole_kernel(first, tile, own_ref, other_ref, own_w, other_w, *out_refs):
    project_kernel(first, tile, None, [own_ref, other_ref], [own_w, other_w], *out_refs)


def end_kernel(first, tile, begun_ref, other_ref, other_w, *out_refs):
    project_kernel(first, tile, begun_ref, [other_ref], [other_w], *out_refs)


def begin_project(own, own_w, slabs, slab, after):
    groups, piece, _ = own.shape
    unit = own_w.shape[1] // sum(slabs)
    first, cols = sum(slabs[:slab]) * unit, slabs[slab] * unit
    return pl.pallas_call(
        ordered(functools.partial(begin_kernel, first, math.gcd(unit, 512)), len(after), 0),
        out_shape=jax.ShapeDtypeStruct((groups * piece, cols), f32),
        in_specs=waits(after) + vmem(2),
        out_specs=vmem(1)[0],
        compiler_params=params(),
        cost_estimate=busy(3),
        name="begin_project",
    )(*after, own, own_w)


def project(own, other, own_w, other_w, slabs, slab, after, beside, begun=None):
    groups, piece, _ = own.shape
    unit = own_w.shape[1] // sum(slabs)
    first, cols = sum(slabs[:slab]) * unit, slabs[slab] * unit
    kernel, values = whole_kernel, (own, other, own_w, other_w)
    if begun is not None:
        kernel, values = end_kernel, (begun, other, other_w)
    return pl.pallas_call(
        ordered(functools.partial(kernel, first, math.gcd(unit, 512)), len(after), 0),
        out_shape=[jax.ShapeDtypeStruct((piece, cols), f32)]
        + [jax.ShapeDtypeStruct((piece, cols), bf16)] * (groups - 1),
        in_specs=waits(after) + vmem(len(values)),
        out_specs=vmem(groups),
        compiler_params=params(),
        cost_estimate=busy(beside),
        name="project",
    )(*after, *values)


def finish_kernel(counts, *refs):
    refs = list(refs)
    out_ref = refs.pop()
    for s, slabs in enumerate(counts):
        at = 0
        for shares in slabs:
            total = refs.pop(0)[...]
            for _ in range(shares):
                total = total + refs.pop(0)[...].astype(f32)
            width = total.shape[1]
            out_ref[s, :, at : at + width] = total.astype(bf16)
            at += width


def finish(sums, piece):
    *slabs, (total, shares) = sums[-1]
    most = [*sums[:-1], slabs]
    counts = [[len(given) for _, given in row] for row in most]
    values = [value for row in most for own, given in row for value in (own, *given)]
    out = jax.ShapeDtypeStruct(
        (len(sums), piece, sum(own.shape[1] for own, _ in sums[-1])), bf16
    )
    begun = pl.pallas_call(
        functools.partial(finish_kernel, counts),
        grid=(1,),
        out_shape=out,
        in_specs=[pl.BlockSpec(value.shape, lambda _: (0, 0)) for value in values],
        out_specs=pl.BlockSpec(out.shape, lambda _: (0, 0, 0)),
        compiler_params=params(),
        cost_estimate=busy(3),
        name="finish",
    )(*values)
    width = total.shape[1]
    place = (len(sums) - 1, 0, out.shape[2] // width - 1)
    return pl.pallas_call(
        ordered(functools.partial(finish_kernel, [[len(shares)]]), 1, 0),
        grid=(1,),
        out_shape=out,
        in_specs=waits([begun])
        + [pl.BlockSpec(value.shape, lambda _: (0, 0)) for value in (total, *shares)],
        out_specs=pl.BlockSpec((1, piece, width), lambda _: place),
        input_output_aliases={0: 0},
        compiler_params=params(),
        cost_estimate=busy(0),
        name="finish_last",
    )(begun, total, *shares)


def nothing(*refs):
    pass


def later_than(value, after):
    anywhere = pl.BlockSpec(memory_space=pl.ANY)
    return pl.pallas_call(
        nothing,
        out_shape=jax.ShapeDtypeStruct(value.shape, value.dtype),
        in_specs=[anywhere] * (1 + len(after)),
        out_specs=anywhere,
        input_output_aliases={0: 0},
        compiler_params=params(1),
        cost_estimate=busy(0),
        name="later_than",
    )(value, *after)


def body(qkv_tokens, sign_bits, out_weight):
    partners, blocks = lax.axis_size("head"), lax.axis_size("seq")
    me, index = lax.axis_index("head"), lax.axis_index("seq")
    seqs = qkv_tokens.shape[0]
    heads, dh = sign_bits.shape[0], sign_bits.shape[-1]
    levels = (blocks // GROUP).bit_length() - 1
    x = qkv_tokens.transpose(0, 2, 1, 3)
    piece = x.shape[2]
    where = jnp.stack(
        [me, index % GROUP] + [(index // GROUP >> l) & 1 for l in range(levels)]
    ).astype(jnp.int32)

    outer, shape = range(2, partners, 2), (piece, x.shape[3] // partners)
    beside = [(s, kind, 1) for s in range(seqs) for kind in (0, 1, 2)]
    beside += [
        (s, kind, k + 1)
        for s in range(seqs)
        for kind in (0, 1, 2)
        for k in outer
        if s > 0 or kind == 0
    ]
    straight = [[[(x, 0, kind, k) for kind in (1, 2)]] for k in range(2, partners)]
    *first, near = pack([*straight, [[(x, *entry) for entry in beside]]], shape, 60)
    first = [swap(value, "head", k + 2) for k, value in enumerate(first)]
    near = swap(near, "head", 1)
    messages = [(s, (1, 2)) for s in range(1, seqs)] + [(s, (0,)) for s in range(seqs)]
    wanted = [
        [
            [(x, s, kind, k) for kind in kinds],
            [(near, 0, beside.index((s, kind, k + 1)), None) for kind in kinds],
        ]
        for s, kinds in messages
        for k in outer
    ]
    wanted.append([[(x, s, kind, 0) for kind in (0, 1, 2)] for s in range(seqs)])
    *packed, own_rows = pack(wanted, shape, 20)
    packed = [swap(value, "head", k) for value, k in zip(packed, list(outer) * len(messages))]
    packed = [packed[n * len(outer) : (n + 1) * len(outer)] for n in range(len(messages))]
    asked = packed[seqs - 1 :]

    def pieces(s, kind):
        found = [(own_rows, s, kind), (near, 0, beside.index((s, kind, 1)))]
        if s == 0 and kind > 0:
            return found + [(value, 0, kind - 1) for value in first]
        row, at = (packed[s - 1], kind - 1) if kind > 0 else (asked[s], 0)
        return found + [(value, half, at) for value in row for half in (0, 1)]

    maps = integer_maps(sign_bits)

    last = [own_rows]
    begun, chains, ends, locals_, own, other, totals = {}, {}, {}, {}, {}, {}, {}

    def early(n):
        begun[n] = early_sums(
            maps, pieces(n, 1)[:2], pieces(n, 2)[:2], heads, dh, piece, last
        )
        last[:] = [begun[n][0]]

    def state(n):
        feats, mine, *others = block_state(
            where,
            maps,
            pieces(n, 1)[2:],
            pieces(n, 2)[2:],
            begun[n][1],
            heads,
            dh,
            piece,
            last,
            3 if n else 0,
        )
        begun[n] = begun[n][0], feats
        chains[n] = [mine] + [swap(value, "seq", m + 1) for m, value in enumerate(others)]
        last[:] = [mine]

    def step(n):
        first_out, *others = chain_step(where, levels, chains[n], last, STEP_US if n and len(chains[n]) == GROUP else 0)
        last[:] = [first_out]
        if others:
            ends[n] = [first_out] + [swap(value, "seq", m + 1) for m, value in enumerate(others)]
        else:
            chains[n] = chains[n] + [swap(first_out, "seq", GROUP << (len(chains[n]) - GROUP))]

    def local(n, first, last_row):
        part = attend_local(
            where,
            maps,
            begun[n],
            pieces(n, 0)[first:last_row],
            pieces(n, 2),
            first,
            heads,
            dh,
            piece,
            last,
            3,
        )
        locals_.setdefault(n, []).append(part)
        last[:] = [part[0]]

    def attend(n):
        stay, leave = attend_prior(
            where, locals_[n], ends[n], piece, dh, last, 1 if n + 1 < seqs else 0
        )
        own[n], other[n] = stay, swap(leave, "head", 1)
        last[:] = [stay]

    def multiply(s, slab):
        if slab == 1:
            for key in totals:
                if key[0] < s:
                    last.extend(totals[key][1])
        begun = None
        if s == seqs - 1 and slab == 0:
            begun = begin_project(own[s], out_weight, slabs[s], slab, last)
            last[:] = [begun]
        total, *shares = project(
            own[s], other[s], out_weight, other_weight, slabs[s], slab, last, 0 if s == seqs - 1 else 6, begun
        )
        totals[s, slab] = total, [swap(v, "head", 2 * (g + 1)) for g, v in enumerate(shares)]
        last[:] = [total]

    slabs = [SLABS[0]] * (seqs - 1) + [SLABS[1]]
    plan = []
    for n in range(seqs):
        came = 22 * n
        end = came + 22 + 9 * levels
        plan.append((came, state, n))
        if n > 0:
            plan.append((came - 21, early, n))
        plan += [(came + 12 + 9 * j, step, n) for j in range(levels + 1)]
        if n == 0:
            plan += [(came + 12.5, local, n, 0, 2), (end - 7, local, n, 2, partners)]
        else:
            plan.append((end - 7, local, n, 0, partners))
        plan.append((end, attend, n))
        plan += [(end + 6 + 3.5 * j, multiply, n, j) for j in range(len(slabs[n]))]
    plan = sorted(plan, key=lambda entry: entry[0])
    early(0)
    state(0)
    other_weight = swap(later_than(out_weight, last), "head", 1)
    for _, act, *which in plan:
        if (act, which) != (state, [0]):
            act(*which)

    return finish([[totals[s, n] for n in range(len(slabs[s]))] for s in range(seqs)], piece)


def solution(mesh):
    return jax.shard_map(
        body,
        mesh=mesh,
        in_specs=(
            P(None, ("seq", "head"), None, None),
            P("head", None, None, None),
            P("head", None),
        ),
        out_specs=P(None, ("seq", "head"), None),
        check_vma=False,
    )
```

```python
import functools
import math

import jax
import jax.numpy as jnp
import numpy as np
from jax import lax
from jax.experimental import pallas as pl
from jax.experimental.pallas import tpu as pltpu
from jax.sharding import PartitionSpec as P

logit_divisor = 1.3
norm_epsilon = 1e-06
SLABS = (8,), (4, 3, 1)

bf16, f32 = jnp.bfloat16, jnp.float32
ROW_TILE = 16
STEP_US = 4
GROUP = 4


def params(mebibytes=20):
    return pltpu.CompilerParams(vmem_limit_bytes=mebibytes * 1024 * 1024)


def vmem(count):
    return [pl.BlockSpec(memory_space=pltpu.VMEM)] * count


def smem():
    return pl.BlockSpec(memory_space=pltpu.SMEM)


def ordered(kernel, count, skip):
    return lambda *refs: kernel(*refs[:skip], *refs[skip + count :])


def busy(microseconds):
    return pl.CostEstimate(flops=int(microseconds * 1e9), bytes_accessed=0, transcendentals=0)


def waits(after):
    return [pl.BlockSpec(memory_space=pl.ANY)] * len(after)


def swap(value, axis, bit):
    return lax.ppermute(value, axis, [(j, j ^ bit) for j in range(lax.axis_size(axis))])


def sign_matrix(order):
    ids = np.arange(order)
    common = ids[:, None] & ids[None, :]
    parity = np.zeros_like(common)
    while common.any():
        parity ^= common & 1
        common = common >> 1
    return (1 - 2 * parity).astype(np.float32)


def maps_kernel(bits_ref, had_ref, maps_ref):
    had = had_ref[...]
    dh = had.shape[0]
    for h in range(bits_ref.shape[0]):
        for b in range(bits_ref.shape[1]):
            signs = (2 * bits_ref[h, b] - 1).astype(f32)
            inner = jnp.dot((had * signs[2:3]).astype(bf16), had, preferred_element_type=f32)
            outer = jnp.dot((inner * signs[1:2]).astype(bf16), had, preferred_element_type=f32)
            whole = outer * signs[0:1]
            near = whole.astype(bf16)
            rows = slice(b * dh, (b + 1) * dh)
            maps_ref[h, rows, :dh] = near
            maps_ref[h, rows, dh:] = (whole - near.astype(f32)).astype(bf16)


def integer_maps(sign_bits):
    heads, blocks, _, dh = sign_bits.shape
    return pl.pallas_call(
        maps_kernel,
        out_shape=jax.ShapeDtypeStruct((heads, blocks * dh, 2 * dh), bf16),
        in_specs=vmem(2),
        out_specs=vmem(1)[0],
        compiler_params=params(),
        cost_estimate=busy(0),
        name="integer_maps",
    )(sign_bits, jnp.asarray(sign_matrix(dh), bf16))


def features(rows_of, maps_ref, out_ref):
    heads, _, twice = maps_ref.shape
    dh = twice // 2
    rows = [rows_of(i) for i in range(heads)]
    scales = []
    for i in range(heads):
        wide = rows[i].astype(f32)
        mean = jnp.sum(wide * wide, axis=-1, keepdims=True) * (1.0 / dh)
        scales.append(lax.rsqrt(mean + norm_epsilon) * (logit_divisor / dh**0.25 / dh))
    for i in range(heads):
        product = lax.dot_general(
            jnp.concatenate([rows[i], rows[i]], axis=1),
            maps_ref[i],
            (((1,), (1,)), ((), ())),
            preferred_element_type=f32,
        )
        out_ref[i] = jnp.exp(product * scales[i]).astype(bf16)


def pack_kernel(places, arrays, *refs):
    me = lax.axis_index("head")
    ins, outs, sems = refs[:arrays], refs[arrays:-1], refs[-1]
    copies = []
    for n, (which, first, second, k, out, i, j, count) in enumerate(places):
        width = outs[out].shape[-1]
        start = 0 if k is None else pl.multiple_of((me ^ k) * width, width)
        source = ins[which].at[first, pl.ds(second, count), :, pl.ds(start, width)]
        copies.append(pltpu.make_async_copy(source, outs[out].at[i, pl.ds(j, count)], sems.at[n]))
    for copy in copies:
        copy.start()
    for copy in copies:
        copy.wait()


def pack(wanted, shape, mebibytes):
    arrays, places, shapes = [], [], []
    for out, table in enumerate(wanted):
        shapes.append((len(table), len(table[0]), *shape))
        for i, row in enumerate(table):
            for j, (array, first, second, k) in enumerate(row):
                if not any(array is known for known in arrays):
                    arrays.append(array)
                which = [array is known for known in arrays].index(True)
                before = places[-1] if places else None
                if before and before[:6] == (which, first, second - before[7], k, out, i):
                    places[-1] = (*before[:7], before[7] + 1)
                else:
                    places.append((which, first, second, k, out, i, j, 1))
    return pl.pallas_call(
        functools.partial(pack_kernel, places, len(arrays)),
        out_shape=[jax.ShapeDtypeStruct(shape, bf16) for shape in shapes],
        in_specs=waits(arrays),
        out_specs=[pl.BlockSpec(memory_space=pltpu.VMEM)] * len(shapes),
        scratch_shapes=[pltpu.SemaphoreType.DMA((len(places),))],
        compiler_params=params(mebibytes),
        cost_estimate=busy(0),
        name="pack",
    )(*arrays)


def joined(refs, places, cut):
    return jnp.concatenate(
        [ref[lead, kind, :, cut] for ref, (lead, kind) in zip(refs, places)], axis=0
    )


def sums_kernel(k_at, v_at, heads, dh, maps_ref, *refs):
    pieces = len(k_at)
    k_refs, v_refs = refs[:pieces], refs[pieces : 2 * pieces]
    *before, feats_ref, sums_ref = refs[2 * pieces :]
    cuts = [slice(i * dh, (i + 1) * dh) for i in range(heads)]
    features(lambda i: joined(k_refs, k_at, cuts[i]), maps_ref, feats_ref)
    for i in range(heads):
        feats = feats_ref[i]
        state = lax.dot_general(
            joined(v_refs, v_at, cuts[i]),
            feats,
            (((0,), (0,)), ((), ())),
            preferred_element_type=f32,
        )
        sums_ref[i, :dh] = before[0][i, :dh] + state if before else state
    for i in range(heads):
        total = jnp.sum(feats_ref[i].astype(f32), axis=0, keepdims=True)
        total = jnp.broadcast_to(total, (sums_ref.shape[1] - dh, total.shape[1]))
        sums_ref[i, dh:] = before[0][i, dh:] + total if before else total


def early_sums(maps, keys, values, heads, dh, piece, after):
    feat = maps.shape[1]
    rows = len(keys) * piece
    (arrays, k_at), (others, v_at) = split(keys), split(values)
    return pl.pallas_call(
        ordered(functools.partial(sums_kernel, k_at, v_at, heads, dh), len(after), 0),
        out_shape=[
            jax.ShapeDtypeStruct((heads, rows, feat), bf16),
            jax.ShapeDtypeStruct((heads, dh + 8, feat), f32),
        ],
        in_specs=waits(after) + vmem(1 + 2 * len(keys)),
        out_specs=vmem(2),
        compiler_params=params(),
        cost_estimate=busy(0),
        name="early_sums",
    )(*after, maps, *arrays, *others)


def split(pieces):
    return [piece[0] for piece in pieces], [piece[1:] for piece in pieces]


def state_kernel(k_at, v_at, heads, dh, where_ref, maps_ref, *refs):
    count = 2 * len(k_at) + 2
    *ins, feats_ref, sums_ref = refs[:count] + refs[-1:]
    share_refs = refs[count:-1]
    sums_kernel(k_at, v_at, heads, dh, maps_ref, *ins, feats_ref, sums_ref)
    share = heads // GROUP
    pad = jnp.zeros((ROW_TILE - share, feats_ref.shape[-1]), f32)
    states = [sums_ref[i] for i in range(heads)]
    shares = []
    for g in range(GROUP):
        mine = states[g * share : (g + 1) * share]
        shares.append(
            jnp.concatenate([v[:dh] for v in mine] + [v[dh : dh + 1] for v in mine] + [pad], axis=0)
        )
    for m, ref in enumerate(share_refs):
        ref[...] = chosen(shares, where_ref[1] ^ m).astype(ref.dtype)


def chosen(values, index):
    result = values[0]
    for n, value in enumerate(values[1:]):
        result = jnp.where(index == n + 1, value, result)
    return result


def block_state(where, maps, keys, values, before, heads, dh, piece, after, beside):
    feat = maps.shape[1]
    rows = len(keys) * piece
    height = heads // GROUP * dh + ROW_TILE
    (arrays, k_at), (others, v_at) = split(keys), split(values)
    return pl.pallas_call(
        ordered(functools.partial(state_kernel, k_at, v_at, heads, dh), len(after), 0),
        out_shape=[
            jax.ShapeDtypeStruct((heads, rows, feat), bf16),
            jax.ShapeDtypeStruct((height, feat), f32),
        ]
        + [jax.ShapeDtypeStruct((height, feat), bf16)] * (GROUP - 1),
        in_specs=waits(after) + [smem()] + vmem(2 + 2 * len(keys)),
        out_specs=vmem(1 + GROUP),
        scratch_shapes=[pltpu.VMEM(before.shape, f32)],
        compiler_params=params(),
        cost_estimate=busy(beside),
        name="block_state",
    )(*after, where, maps, *arrays, *others, before)


def step_kernel(levels, where_ref, *refs):
    ins = refs[: len(refs) - (1 if len(refs) < 2 * GROUP + levels else GROUP)]
    outs = refs[len(ins) :]
    values = [ref[...].astype(f32) for ref in ins[:GROUP]]
    got = [ref[...].astype(f32) for ref in ins[GROUP:]]
    if len(outs) == 1:
        total = values[0]
        for value in values[1:] + got:
            total = total + value
        outs[0][...] = total.astype(bf16)
        return
    prior = jnp.zeros_like(values[0])
    for level, value in enumerate(got):
        prior = prior + jnp.where(where_ref[2 + level] == 1, value, 0.0)
    mine = where_ref[1]
    for m, out in enumerate(outs):
        result = prior
        for other, value in enumerate(values):
            if other != m:
                result = result + jnp.where((mine ^ other) < (mine ^ m), value, 0.0)
        out[...] = result.astype(bf16)


def chain_step(where, levels, values, after, beside):
    shape = values[0].shape
    count = GROUP if len(values) == GROUP + levels else 1
    return pl.pallas_call(
        ordered(functools.partial(step_kernel, levels), len(after), 0),
        out_shape=[jax.ShapeDtypeStruct(shape, bf16)] * count,
        in_specs=waits(after) + [smem()] + vmem(len(values)),
        out_specs=vmem(count),
        compiler_params=params(),
        cost_estimate=busy(beside),
        name="chain_step",
    )(*after, where, *values)


def local_kernel(first, q_at, v_at, heads, dh, where_ref, maps_ref, early_ref, late_ref, *refs):
    asking, partners = len(q_at), len(v_at)
    q_refs, v_refs = refs[:asking], refs[asking : asking + partners]
    query_feats_ref, local_ref, weights_ref = refs[asking + partners :]
    piece = q_refs[0].shape[2]
    rows = partners * piece
    me = where_ref[0]

    def places(first, count, shape, dim):
        ids = lax.broadcasted_iota(jnp.int32, shape, dim)
        result = ids + (me ^ first) * piece
        for j in range(1, count):
            result = jnp.where(ids >= j * piece, ids + ((me ^ (first + j)) - j) * piece, result)
        return result

    here = places(first, asking, (asking * piece, 1), 0)
    causal = here >= places(0, partners, (1, rows), 1)
    ones = jnp.ones((rows, dh), bf16)
    cuts = [slice(i * dh, (i + 1) * dh) for i in range(heads)]
    features(lambda i: joined(q_refs, q_at, cuts[i]), maps_ref, query_feats_ref)
    for i in range(heads):
        scores = lax.dot_general(
            query_feats_ref[i],
            jnp.concatenate([early_ref[i], late_ref[i]], axis=0),
            (((1,), (1,)), ((), ())),
            preferred_element_type=f32,
        )
        weights_ref[i] = jnp.where(causal, scores, 0.0).astype(bf16)
    for i in range(heads):
        local_ref[i] = jnp.dot(
            weights_ref[i],
            jnp.concatenate([joined(v_refs, v_at, cuts[i]), ones], axis=1),
            preferred_element_type=f32,
        )


def attend_local(where, maps, feats, queries, values, first, heads, dh, piece, after, beside):
    feat = maps.shape[1]
    rows = len(queries) * piece
    (arrays, q_at), (others, v_at) = split(queries), split(values)
    return pl.pallas_call(
        ordered(functools.partial(local_kernel, first, q_at, v_at, heads, dh), len(after), 0),
        out_shape=[
            jax.ShapeDtypeStruct((heads, rows, feat), bf16),
            jax.ShapeDtypeStruct((heads, rows, 2 * dh), f32),
        ],
        in_specs=waits(after) + [smem()] + vmem(1 + len(feats) + len(queries) + len(values)),
        out_specs=vmem(2),
        scratch_shapes=[pltpu.VMEM((heads, rows, len(values) * piece), bf16)],
        compiler_params=params(),
        cost_estimate=busy(beside),
        name="attend_local",
    )(*after, where, maps, *feats, *arrays, *others)


def prior_kernel(pieces, heads, dh, where_ref, *refs):
    parts = len(pieces)
    asked = [(refs[2 * p], refs[2 * p + 1]) for p in range(parts)]
    share_refs, (stay_ref, leave_ref) = refs[2 * parts : 2 * parts + GROUP], refs[-2:]
    piece = stay_ref.shape[1]
    share = heads // GROUP
    priors = []
    for i in range(heads):
        j = i % share
        state, total = slice(j * dh, (j + 1) * dh), slice(share * dh, share * dh + ROW_TILE)
        source = where_ref[1] ^ (i // share)
        prior = chosen([ref[state, :] for ref in share_refs], source)
        tail = chosen([ref[total, :] for ref in share_refs], source)
        tail = jnp.broadcast_to(tail[j : j + 1, :], prior.shape)
        priors.append(jnp.concatenate([prior, tail], axis=0))
    first = 0
    for count, (query_feats_ref, local_ref) in zip(pieces, asked):
        sums = [
            local_ref[i]
            + lax.dot_general(
                query_feats_ref[i], priors[i], (((1,), (1,)), ((), ())), preferred_element_type=f32
            )
            for i in range(heads)
        ]
        for i in range(heads):
            attended = (sums[i][:, :dh] / sums[i][:, dh:]).astype(bf16)
            for n in range(count):
                out = leave_ref if (first + n) & 1 else stay_ref
                out[(first + n) // 2, :, i * dh : (i + 1) * dh] = attended[n * piece : (n + 1) * piece]
        first += count


def attend_prior(where, asked, shares, piece, dh, after, beside):
    heads = asked[0][0].shape[0]
    pieces = [query_feats.shape[1] // piece for query_feats, _ in asked]
    out = jax.ShapeDtypeStruct((sum(pieces) // 2, piece, heads * dh), bf16)
    values = [value for pair in asked for value in pair]
    return pl.pallas_call(
        ordered(functools.partial(prior_kernel, pieces, heads, dh), len(after), 0),
        out_shape=[out, out],
        in_specs=waits(after) + [smem()] + vmem(len(values) + len(shares)),
        out_specs=vmem(2),
        compiler_params=params(),
        cost_estimate=busy(beside),
        name="attend_prior",
    )(*after, where, *values, *shares)


def project_kernel(first, tile, begun, lhs_refs, w_refs, *out_refs):
    groups, piece, width = lhs_refs[0].shape
    lhs = [ref[...].reshape(groups * piece, width) for ref in lhs_refs]
    for n in range(out_refs[0].shape[1] // tile):
        here = slice(n * tile, (n + 1) * tile)
        there = slice(first + n * tile, first + (n + 1) * tile)
        acc = None if begun is None else begun[:, here]
        for value, w_ref in zip(lhs, w_refs):
            term = jnp.dot(value, w_ref[:, there], preferred_element_type=f32)
            acc = term if acc is None else acc + term
        if len(out_refs) == 1:
            out_refs[0][:, here] = acc
        else:
            for g, ref in enumerate(out_refs):
                ref[:, here] = acc[g * piece : (g + 1) * piece].astype(ref.dtype)


def begin_kernel(first, tile, lhs_ref, w_ref, out_ref):
    project_kernel(first, tile, None, [lhs_ref], [w_ref], out_ref)


def whole_kernel(first, tile, own_ref, other_ref, own_w, other_w, *out_refs):
    project_kernel(first, tile, None, [own_ref, other_ref], [own_w, other_w], *out_refs)


def end_kernel(first, tile, begun_ref, other_ref, other_w, *out_refs):
    project_kernel(first, tile, begun_ref, [other_ref], [other_w], *out_refs)


def begin_project(own, own_w, slabs, slab, after):
    groups, piece, _ = own.shape
    unit = own_w.shape[1] // sum(slabs)
    first, cols = sum(slabs[:slab]) * unit, slabs[slab] * unit
    return pl.pallas_call(
        ordered(functools.partial(begin_kernel, first, math.gcd(unit, 512)), len(after), 0),
        out_shape=jax.ShapeDtypeStruct((groups * piece, cols), f32),
        in_specs=waits(after) + vmem(2),
        out_specs=vmem(1)[0],
        compiler_params=params(),
        cost_estimate=busy(3),
        name="begin_project",
    )(*after, own, own_w)


def project(own, other, own_w, other_w, slabs, slab, after, beside, begun=None):
    groups, piece, _ = own.shape
    unit = own_w.shape[1] // sum(slabs)
    first, cols = sum(slabs[:slab]) * unit, slabs[slab] * unit
    kernel, values = whole_kernel, (own, other, own_w, other_w)
    if begun is not None:
        kernel, values = end_kernel, (begun, other, other_w)
    return pl.pallas_call(
        ordered(functools.partial(kernel, first, math.gcd(unit, 512)), len(after), 0),
        out_shape=[jax.ShapeDtypeStruct((piece, cols), f32)]
        + [jax.ShapeDtypeStruct((piece, cols), bf16)] * (groups - 1),
        in_specs=waits(after) + vmem(len(values)),
        out_specs=vmem(groups),
        compiler_params=params(),
        cost_estimate=busy(beside),
        name="project",
    )(*after, *values)


def finish_kernel(counts, *refs):
    refs = list(refs)
    out_ref = refs.pop()
    for s, slabs in enumerate(counts):
        at = 0
        for shares in slabs:
            total = refs.pop(0)[...]
            for _ in range(shares):
                total = total + refs.pop(0)[...].astype(f32)
            width = total.shape[1]
            out_ref[s, :, at : at + width] = total.astype(bf16)
            at += width


def finish(sums, piece):
    *slabs, (total, shares) = sums[-1]
    most = [*sums[:-1], slabs]
    counts = [[len(given) for _, given in row] for row in most]
    values = [value for row in most for own, given in row for value in (own, *given)]
    out = jax.ShapeDtypeStruct(
        (len(sums), piece, sum(own.shape[1] for own, _ in sums[-1])), bf16
    )
    begun = pl.pallas_call(
        functools.partial(finish_kernel, counts),
        grid=(1,),
        out_shape=out,
        in_specs=[pl.BlockSpec(value.shape, lambda _: (0, 0)) for value in values],
        out_specs=pl.BlockSpec(out.shape, lambda _: (0, 0, 0)),
        compiler_params=params(),
        cost_estimate=busy(3),
        name="finish",
    )(*values)
    width = total.shape[1]
    place = (len(sums) - 1, 0, out.shape[2] // width - 1)
    return pl.pallas_call(
        ordered(functools.partial(finish_kernel, [[len(shares)]]), 1, 0),
        grid=(1,),
        out_shape=out,
        in_specs=waits([begun])
        + [pl.BlockSpec(value.shape, lambda _: (0, 0)) for value in (total, *shares)],
        out_specs=pl.BlockSpec((1, piece, width), lambda _: place),
        input_output_aliases={0: 0},
        compiler_params=params(),
        cost_estimate=busy(0),
        name="finish_last",
    )(begun, total, *shares)


def nothing(*refs):
    pass


def later_than(value, after):
    anywhere = pl.BlockSpec(memory_space=pl.ANY)
    return pl.pallas_call(
        nothing,
        out_shape=jax.ShapeDtypeStruct(value.shape, value.dtype),
        in_specs=[anywhere] * (1 + len(after)),
        out_specs=anywhere,
        input_output_aliases={0: 0},
        compiler_params=params(1),
        cost_estimate=busy(0),
        name="later_than",
    )(value, *after)


def body(qkv_tokens, sign_bits, out_weight):
    partners, blocks = lax.axis_size("head"), lax.axis_size("seq")
    me, index = lax.axis_index("head"), lax.axis_index("seq")
    seqs = qkv_tokens.shape[0]
    heads, dh = sign_bits.shape[0], sign_bits.shape[-1]
    levels = (blocks // GROUP).bit_length() - 1
    x = qkv_tokens.transpose(0, 2, 1, 3)
    piece = x.shape[2]
    where = jnp.stack(
        [me, index % GROUP] + [(index // GROUP >> l) & 1 for l in range(levels)]
    ).astype(jnp.int32)

    outer, shape = range(2, partners, 2), (piece, x.shape[3] // partners)
    beside = [(s, kind, 1) for s in range(seqs) for kind in (0, 1, 2)]
    beside += [
        (s, kind, k + 1)
        for s in range(seqs)
        for kind in (0, 1, 2)
        for k in outer
        if s > 0 or kind == 0
    ]
    straight = [[[(x, 0, kind, k) for kind in (1, 2)]] for k in range(2, partners)]
    *first, near = pack([*straight, [[(x, *entry) for entry in beside]]], shape, 60)
    first = [swap(value, "head", k + 2) for k, value in enumerate(first)]
    near = swap(near, "head", 1)
    messages = [(s, (1, 2)) for s in range(1, seqs)] + [(s, (0,)) for s in range(seqs)]
    wanted = [
        [
            [(x, s, kind, k) for kind in kinds],
            [(near, 0, beside.index((s, kind, k + 1)), None) for kind in kinds],
        ]
        for s, kinds in messages
        for k in outer
    ]
    wanted.append([[(x, s, kind, 0) for kind in (0, 1, 2)] for s in range(seqs)])
    *packed, own_rows = pack(wanted, shape, 20)
    packed = [swap(value, "head", k) for value, k in zip(packed, list(outer) * len(messages))]
    packed = [packed[n * len(outer) : (n + 1) * len(outer)] for n in range(len(messages))]
    asked = packed[seqs - 1 :]

    def pieces(s, kind):
        found = [(own_rows, s, kind), (near, 0, beside.index((s, kind, 1)))]
        if s == 0 and kind > 0:
            return found + [(value, 0, kind - 1) for value in first]
        row, at = (packed[s - 1], kind - 1) if kind > 0 else (asked[s], 0)
        return found + [(value, half, at) for value in row for half in (0, 1)]

    maps = integer_maps(sign_bits)

    last = [own_rows]
    begun, chains, ends, locals_, own, other, totals = {}, {}, {}, {}, {}, {}, {}

    def early(n):
        begun[n] = early_sums(
            maps, pieces(n, 1)[:2], pieces(n, 2)[:2], heads, dh, piece, last
        )
        last[:] = [begun[n][0]]

    def state(n):
        feats, mine, *others = block_state(
            where,
            maps,
            pieces(n, 1)[2:],
            pieces(n, 2)[2:],
            begun[n][1],
            heads,
            dh,
            piece,
            last,
            3 if n else 0,
        )
        begun[n] = begun[n][0], feats
        chains[n] = [mine] + [swap(value, "seq", m + 1) for m, value in enumerate(others)]
        last[:] = [mine]

    def step(n):
        first_out, *others = chain_step(where, levels, chains[n], last, STEP_US if n and len(chains[n]) == GROUP else 0)
        last[:] = [first_out]
        if others:
            ends[n] = [first_out] + [swap(value, "seq", m + 1) for m, value in enumerate(others)]
        else:
            chains[n] = chains[n] + [swap(first_out, "seq", GROUP << (len(chains[n]) - GROUP))]

    def local(n, first, last_row):
        part = attend_local(
            where,
            maps,
            begun[n],
            pieces(n, 0)[first:last_row],
            pieces(n, 2),
            first,
            heads,
            dh,
            piece,
            last,
            3,
        )
        locals_.setdefault(n, []).append(part)
        last[:] = [part[0]]

    def attend(n):
        stay, leave = attend_prior(
            where, locals_[n], ends[n], piece, dh, last, 1 if n + 1 < seqs else 0
        )
        own[n], other[n] = stay, swap(leave, "head", 1)
        last[:] = [stay]

    def multiply(s, slab):
        if slab == 1:
            for key in totals:
                if key[0] < s:
                    last.extend(totals[key][1])
        begun = None
        if s == seqs - 1 and slab == 0:
            begun = begin_project(own[s], out_weight, slabs[s], slab, last)
            last[:] = [begun]
        total, *shares = project(
            own[s], other[s], out_weight, other_weight, slabs[s], slab, last, 0 if s == seqs - 1 else 6, begun
        )
        totals[s, slab] = total, [swap(v, "head", 2 * (g + 1)) for g, v in enumerate(shares)]
        last[:] = [total]

    slabs = [SLABS[0]] * (seqs - 1) + [SLABS[1]]
    plan = []
    for n in range(seqs):
        came = 20.9 * n
        end = came + 22 + 9 * levels
        plan.append((came, state, n))
        if n > 0:
            plan.append((came - 21, early, n))
        plan += [(came + 12 + 9 * j, step, n) for j in range(levels + 1)]
        if n == 0:
            plan += [(came + 12.5, local, n, 0, 2), (end - 7, local, n, 2, partners)]
        else:
            plan.append((end - 7, local, n, 0, partners))
        plan.append((end, attend, n))
        plan += [(end + 6 + 3.5 * j, multiply, n, j) for j in range(len(slabs[n]))]
    plan = sorted(plan, key=lambda entry: entry[0])
    early(0)
    state(0)
    other_weight = swap(later_than(out_weight, last), "head", 1)
    for _, act, *which in plan:
        if (act, which) != (state, [0]):
            act(*which)

    return finish([[totals[s, n] for n in range(len(slabs[s]))] for s in range(seqs)], piece)


def solution(mesh):
    return jax.shard_map(
        body,
        mesh=mesh,
        in_specs=(
            P(None, ("seq", "head"), None, None),
            P("head", None, None, None),
            P("head", None),
        ),
        out_specs=P(None, ("seq", "head"), None),
        check_vma=False,
    )
```
